32 devices in a mesh: ctx: 8 (over z, core), tp: 4 (over y, x).
Axes of the slice: x: 2, y: 2, z: 4, core: 2. Of those that a mesh axis runs over, the one named last changes fastest.
Arguments:
- queries: bfloat16 [1024, 8192], P('ctx', 'tp'), may hold values from -6 to 6
- keys_in: bfloat16 [1024, 8192], P('ctx', 'tp'), may hold values from -6 to 6
- values_in: bfloat16 [1024, 8192], P('ctx', 'tp'), may hold values from -6 to 6
- decay_rates: float32 [8192, 16], P('tp'), may hold values from 0.00029296876 to 0.03
- residues: float32 [8192, 16], P('tp'), may hold values from -1.5 to 1.5
- skip_gain: float32 [8192], P('tp'), may hold values from -4 to 4
- cotangent: bfloat16 [1024, 8192], P('ctx', 'tp'), may hold values from -6 to 6
Outputs:
- operator_out: bfloat16 [1024, 8192], P('ctx', 'tp')
- grad_queries: bfloat16 [1024, 8192], P('ctx', 'tp')
- grad_keys: bfloat16 [1024, 8192], P('ctx', 'tp')
- grad_values: bfloat16 [1024, 8192], P('ctx', 'tp')
- grad_residues: float32 [8192, 16], P('tp')
The draws below stay inside these ranges and needn't reach their ends.
All inputs are finite; a program needn't handle non-finite values.
Results may differ from the reference program's by a relative error of at most 0.0054.
Values may be sent and summed in bfloat16 or wider, within the bound.
No kernel may reach another device: no remote copies, remote signals or barrier semaphores. Data moves between devices by JAX's collectives and lax.ppermute only.
A program may use at most 64 MiB of HBM per device.

```python
import math
import jax
import jax.numpy as jnp
from jax import lax

D = 8192
ORDER = 16
SEQ = 1024


def level_of(key, dims, split, low, high):
    loudness, own = 1.0, jax.random.fold_in(key, 6)
    for axis_at, blocks in split:
        heights = jnp.exp(jax.random.uniform(jax.random.fold_in(own, axis_at), (blocks,), jnp.float32, low / len(split), high / len(split)))
        loudness = loudness * jnp.repeat(heights, dims[axis_at] // blocks).reshape([-1 if axis == axis_at else 1 for axis in range(len(dims))])
    return loudness


def bell_draw(rng, dims, deviation, limit, pieces=(), kind=jnp.bfloat16):
    result = jax.random.normal(rng, dims, jnp.float32) * deviation
    if len(pieces) > 0:
        result = level_of(rng, dims, pieces, -0.22, 0.18) * result
    return jnp.clip(result, min=-limit, max=limit).astype(kind)


def setup_inputs(seed: int = 0) -> dict:
    streams_of = jax.random.split(jax.random.key(seed), 8)
    queries = bell_draw(streams_of[0], (SEQ, D), 1.0, 6.0, ((0, 8), (1, 4)))
    keys_in = bell_draw(streams_of[1], (SEQ, D), 1.0, 6.0, ((0, 8), (1, 4)))
    values_in = bell_draw(streams_of[2], (SEQ, D), 1.0, 6.0, ((0, 8), (1, 4)))
    decay_rates = jnp.clip(jnp.exp(math.log(0.03) - 4.6288867 * jax.random.uniform(streams_of[3], (D, ORDER), jnp.float32) ** level_of(streams_of[3], (D, ORDER), ((0, 4),), -0.2, 0.2)), 0.00029296876, 0.03)
    residues = bell_draw(streams_of[4], (D, ORDER), 0.25, 1.5, ((0, 4),), jnp.float32)
    skip_gain = bell_draw(streams_of[5], (D,), 1.0, 4.0, ((0, 4),), jnp.float32)
    cotangent = bell_draw(streams_of[6], (SEQ, D), 1.0, 6.0, ((0, 8), (1, 4)))
    return dict(queries=queries, keys_in=keys_in, values_in=values_in, decay_rates=decay_rates, residues=residues, skip_gain=skip_gain, cotangent=cotangent)


PRECISE = lax.Precision.HIGHEST

def causal_conv(signal, taps, length):
    padded_len = 2 * length
    spectrum = jnp.fft.rfft(signal, n=padded_len, axis=0) * jnp.fft.rfft(taps, n=padded_len, axis=0)
    return jnp.fft.irfft(spectrum, n=padded_len, axis=0)[:length]

def lagged_sums(later_sig, earlier_sig, length):
    padded_len = 2 * length
    spectrum = jnp.fft.rfft(later_sig, n=padded_len, axis=0) * jnp.conj(jnp.fft.rfft(earlier_sig, n=padded_len, axis=0))
    return jnp.fft.irfft(spectrum, n=padded_len, axis=0)[:length]

def reference(queries, keys_in, values_in, decay_rates, residues, skip_gain, cotangent):
    length = queries.shape[0]
    channels = queries.shape[1]
    queries_f = queries.astype(jnp.float32)
    keys_f = keys_in.astype(jnp.float32)
    values_f = values_in.astype(jnp.float32)
    cot_f = cotangent.astype(jnp.float32)
    gated = lax.optimization_barrier((keys_f * values_f).astype(jnp.bfloat16))
    pulled = lax.optimization_barrier((cot_f * queries_f).astype(jnp.bfloat16))
    positions = jnp.arange(length, dtype=jnp.float32)
    group_width = min(channels, 128)
    group_count = channels // group_width

    def one_group(group_index):
        start = group_index * group_width
        gated_block = lax.dynamic_slice_in_dim(gated, start, group_width, 1).astype(jnp.float32)
        pulled_block = lax.dynamic_slice_in_dim(pulled, start, group_width, 1).astype(jnp.float32)
        rate_block = lax.dynamic_slice_in_dim(decay_rates, start, group_width, 0)
        residue_block = lax.dynamic_slice_in_dim(residues, start, group_width, 0)
        powers = jnp.exp(-rate_block[None] * positions[:, None, None])
        unit_scale = jnp.sqrt(1.0 - jnp.exp(-2.0 * rate_block))
        mode_coef = residue_block * unit_scale
        filter_taps = jnp.einsum('tcn,cn->tc', powers, mode_coef, precision=PRECISE)
        convolved = causal_conv(gated_block, filter_taps, length)
        adjoint = causal_conv(pulled_block[::-1], filter_taps, length)[::-1]
        lags = lagged_sums(pulled_block, gated_block, length)
        raw_grad = unit_scale * jnp.einsum('tc,tcn->cn', lags, powers, precision=PRECISE)
        return (convolved, adjoint, raw_grad)
    convolved, adjoint, raw_grad = lax.map(one_group, jnp.arange(group_count, dtype=jnp.int32))
    convolved = jnp.moveaxis(convolved, 0, 1).reshape(length, channels)
    adjoint = jnp.moveaxis(adjoint, 0, 1).reshape(length, channels)
    raw_grad = raw_grad.reshape(channels, decay_rates.shape[1])
    convolved = lax.optimization_barrier(convolved.astype(jnp.bfloat16))
    adjoint = lax.optimization_barrier(adjoint.astype(jnp.bfloat16))
    mixed = convolved.astype(jnp.float32) + skip_gain[None, :] * gated.astype(jnp.float32)
    operator_out = (queries_f * mixed).astype(jnp.bfloat16)
    grad_queries = (cot_f * mixed).astype(jnp.bfloat16)
    grad_gated = adjoint.astype(jnp.float32) + skip_gain[None, :] * pulled.astype(jnp.float32)
    grad_keys = (grad_gated * values_f).astype(jnp.bfloat16)
    grad_values = (grad_gated * keys_f).astype(jnp.bfloat16)
    grad_square = jnp.sum(raw_grad * raw_grad)
    factor = jnp.minimum(1.0, math.sqrt(D * ORDER) / jnp.sqrt(grad_square + 1e-06))
    grad_residues = raw_grad * factor
    return (operator_out, grad_queries, grad_keys, grad_values, grad_residues)
```

```python
import math

import jax
import jax.numpy as jnp
from jax import lax
from jax.experimental import pallas as pl
from jax.experimental.pallas import tpu as pltpu
from jax.sharding import PartitionSpec as P

F32 = jnp.float32
WIRE = jnp.bfloat16
LANES = 128
UNROLL = 8
VMEM_LIMIT = 40 * 1024 * 1024


def gate(left_ref, right_ref, cols):
    product = left_ref[:, cols].astype(F32) * right_ref[:, cols].astype(F32)
    return product.astype(jnp.bfloat16).astype(F32)


def rows_of(ref, step, sub, pitch):
    return ref[pl.ds(step, sub, stride=pitch), :]


def spread(table_ref, modes, sub, scratch):
    for s in range(sub):
        scratch[pl.ds(s, modes, stride=sub), :] = table_ref[:, s * LANES : (s + 1) * LANES]
    return [scratch[n * sub : (n + 1) * sub, :] for n in range(modes)]


def tree_sum(items):
    items = list(items)
    while len(items) > 1:
        items = [
            items[i] + items[i + 1] if i + 1 < len(items) else items[i]
            for i in range(0, len(items), 2)
        ]
    return items[0]


def fill_lines(k_ref, v_ref, q_ref, ct_ref, gated, pulled, sub, seq):
    for s in range(sub):
        cols = slice(s * LANES, (s + 1) * LANES)
        gated[s * seq : (s + 1) * seq, :] = gate(k_ref, v_ref, cols)
        pulled[s * seq : (s + 1) * seq, :] = gate(ct_ref, q_ref, cols)


def states_kernel(q_ref, k_ref, v_ref, ct_ref, rate_ref, out_ref, gated, pulled, table, states):
    seq = q_ref.shape[0]
    modes = rate_ref.shape[0]
    sub = q_ref.shape[1] // LANES
    fill_lines(k_ref, v_ref, q_ref, ct_ref, gated, pulled, sub, seq)
    decay = [jnp.exp(-r) for r in spread(rate_ref, modes, sub, table)]
    zeros = tuple(jnp.zeros((sub, LANES), F32) for _ in range(modes))

    def forward(i, carry):
        held, inner = list(carry[0]), list(carry[1])
        for u in range(UNROLL):
            t = i * UNROLL + u
            x = rows_of(gated, t, sub, seq)
            p = rows_of(pulled, t, sub, seq)
            for n in range(modes):
                held[n] = decay[n] * held[n] + x
                inner[n] = inner[n] + p * held[n]
        return tuple(held), tuple(inner)

    def backward(i, carry):
        held = list(carry)
        for u in range(UNROLL):
            t = seq - 1 - (i * UNROLL + u)
            p = rows_of(pulled, t, sub, seq)
            for n in range(modes):
                held[n] = decay[n] * held[n] + p
        return tuple(held)

    ends, inner = lax.fori_loop(0, seq // UNROLL, forward, (zeros, zeros))
    starts = lax.fori_loop(0, seq // UNROLL, backward, zeros)
    for n in range(modes):
        rows = slice(n * sub, (n + 1) * sub)
        states[0, rows, :] = ends[n]
        states[1, rows, :] = starts[n]
        states[2, rows, :] = inner[n]
    dests, _, slab, _ = out_ref.shape
    for d in range(dests):
        for kind in range(3):
            out_ref[d, kind] = states[kind, d * slab : (d + 1) * slab, :].astype(out_ref.dtype)


def local_kernel(
    q_ref, k_ref, v_ref, ct_ref, rate_ref, res_ref, conv_ref, adj_ref, gated, pulled, table
):
    seq = q_ref.shape[0]
    modes = rate_ref.shape[0]
    sub = q_ref.shape[1] // LANES
    fill_lines(k_ref, v_ref, q_ref, ct_ref, gated, pulled, sub, seq)
    rates = spread(rate_ref, modes, sub, table)
    weights = spread(res_ref, modes, sub, table)
    decay = [jnp.exp(-r) for r in rates]
    coef = [w * jnp.sqrt(1.0 - jnp.exp(-2.0 * r)) for w, r in zip(weights, rates)]
    zeros = tuple(jnp.zeros((sub, LANES), F32) for _ in range(modes))

    def scan(source, target, reverse):
        def body(i, carry):
            held = list(carry)
            for u in range(UNROLL):
                t = i * UNROLL + u
                if reverse:
                    t = seq - 1 - t
                x = rows_of(source, t, sub, seq)
                total = [None] * 4
                for n in range(modes):
                    held[n] = decay[n] * held[n] + x
                    term = coef[n] * held[n]
                    total[n % 4] = term if total[n % 4] is None else total[n % 4] + term
                target[0, t] = tree_sum(total)
            return tuple(held)

        lax.fori_loop(0, seq // UNROLL, body, zeros)

    scan(gated, conv_ref, False)
    scan(pulled, adj_ref, True)


def chunks_kernel(in_ref, rate_ref, out_ref):
    count = in_ref.shape[0]
    rate = rate_ref[...]
    step = jnp.exp(-rate)
    span = jnp.exp(-rate * CHUNK[0])
    unit = jnp.sqrt(1.0 - jnp.exp(-2.0 * rate))
    held = jnp.zeros_like(rate)
    total = jnp.zeros_like(rate)
    for j in range(count):
        out_ref[j, 0] = held.astype(out_ref.dtype)
        start = in_ref[j, 1].astype(F32)
        total = total + (in_ref[j, 2].astype(F32) + step * start * held)
        held = span * held + in_ref[j, 0].astype(F32)
    back = jnp.zeros_like(rate)
    raw = (unit * total).astype(out_ref.dtype)
    for j in reversed(range(count)):
        out_ref[j, 1] = back.astype(out_ref.dtype)
        out_ref[j, 2] = raw
        back = span * back + in_ref[j, 1].astype(F32)


CHUNK = [128]


def finish_kernel(
    q_ref,
    k_ref,
    v_ref,
    ct_ref,
    rate_ref,
    res_ref,
    skip_ref,
    conv_ref,
    adj_ref,
    in_ref,
    out_ref,
    gq_ref,
    gk_ref,
    gv_ref,
    raw_ref,
    conv_lines,
    adj_lines,
    table,
    states,
):
    seq = q_ref.shape[0]
    modes = rate_ref.shape[0]
    sub = q_ref.shape[1] // LANES
    sources, _, slab, _ = in_ref.shape
    for d in range(sources):
        for kind in range(3):
            states[kind, d * slab : (d + 1) * slab, :] = in_ref[d, kind].astype(F32)
    for s in range(sub):
        raw_ref[:, s * LANES : (s + 1) * LANES] = states[2, pl.ds(s, modes, stride=sub), :]
    rates = spread(rate_ref, modes, sub, table)
    weights = spread(res_ref, modes, sub, table)
    decay = [jnp.exp(-r) for r in rates]
    coef = [w * jnp.sqrt(1.0 - jnp.exp(-2.0 * r)) for w, r in zip(weights, rates)]
    ahead = tuple(coef[n] * states[0, n * sub : (n + 1) * sub, :] for n in range(modes))
    behind = tuple(coef[n] * states[1, n * sub : (n + 1) * sub, :] for n in range(modes))

    def body(i, carry):
        ahead, behind = list(carry[0]), list(carry[1])
        for u in range(UNROLL):
            t = i * UNROLL + u
            back_t = seq - 1 - t
            total_a, total_b = [None] * 4, [None] * 4
            for n in range(modes):
                ahead[n] = decay[n] * ahead[n]
                behind[n] = decay[n] * behind[n]
                total_a[n % 4] = ahead[n] if n < 4 else total_a[n % 4] + ahead[n]
                total_b[n % 4] = behind[n] if n < 4 else total_b[n % 4] + behind[n]
            conv_lines[pl.ds(t, sub, stride=seq), :] = conv_ref[0, t] + tree_sum(total_a)
            adj_lines[pl.ds(back_t, sub, stride=seq), :] = adj_ref[0, back_t] + tree_sum(total_b)
        return tuple(ahead), tuple(behind)

    lax.fori_loop(0, seq // UNROLL, body, (ahead, behind))
    for s in range(sub):
        cols = slice(s * LANES, (s + 1) * LANES)
        rows = slice(s * seq, (s + 1) * seq)
        skip = skip_ref[:, cols]
        q, ct = q_ref[:, cols].astype(F32), ct_ref[:, cols].astype(F32)
        k, v = k_ref[:, cols].astype(F32), v_ref[:, cols].astype(F32)
        gated = (k * v).astype(jnp.bfloat16).astype(F32)
        pulled = (ct * q).astype(jnp.bfloat16).astype(F32)
        mixed = conv_lines[rows, :].astype(jnp.bfloat16).astype(F32) + skip * gated
        out_ref[:, cols] = (q * mixed).astype(out_ref.dtype)
        gq_ref[:, cols] = (ct * mixed).astype(gq_ref.dtype)
        grad = adj_lines[rows, :].astype(jnp.bfloat16).astype(F32) + skip * pulled
        gk_ref[:, cols] = (grad * v).astype(gk_ref.dtype)
        gv_ref[:, cols] = (grad * k).astype(gv_ref.dtype)


def shards(queries, keys_in, values_in, decay_rates, residues, skip_gain, cotangent):
    seq, channels = queries.shape
    modes = decay_rates.shape[1]
    ctx = lax.axis_size("ctx")
    tp = lax.axis_size("tp")
    groups = channels // LANES
    sub = math.gcd(groups, 8)
    blocks = groups // sub
    width = sub * LANES
    slab = modes * groups // ctx
    per_block = ctx // blocks
    block_rows = modes * sub
    rates, weights = decay_rates.T, residues.T
    params = pltpu.CompilerParams(vmem_limit_bytes=VMEM_LIMIT)

    line_spec = pl.BlockSpec((seq, width), lambda b: (0, b))
    table_spec = pl.BlockSpec((modes, width), lambda b: (0, b))
    pack_spec = pl.BlockSpec((per_block, 3, slab, LANES), lambda b: (b, 0, 0, 0))
    tall_spec = pl.BlockSpec((1, seq, sub, LANES), lambda b: (b, 0, 0, 0))
    lines_scratch = pltpu.VMEM((sub * seq, LANES), F32)
    table_scratch = pltpu.VMEM((block_rows, LANES), F32)
    states_scratch = pltpu.VMEM((3, block_rows, LANES), F32)
    elements = seq * channels * modes

    packed = pl.pallas_call(
        states_kernel,
        grid=(blocks,),
        in_specs=[line_spec] * 4 + [table_spec],
        out_specs=pack_spec,
        out_shape=jax.ShapeDtypeStruct((ctx, 3, slab, LANES), WIRE),
        scratch_shapes=[lines_scratch, lines_scratch, table_scratch, states_scratch],
        compiler_params=params,
        cost_estimate=pl.CostEstimate(
            flops=6 * elements, bytes_accessed=8 * seq * channels, transcendentals=0
        ),
        name="chunk_states",
    )(queries, keys_in, values_in, cotangent, rates)
    gathered = lax.all_to_all(packed, "ctx", split_axis=0, concat_axis=0, tiled=True)

    conv, adj = pl.pallas_call(
        local_kernel,
        grid=(blocks,),
        in_specs=[line_spec] * 4 + [table_spec] * 2,
        out_specs=[tall_spec] * 2,
        out_shape=[jax.ShapeDtypeStruct((blocks, seq, sub, LANES), F32)] * 2,
        scratch_shapes=[lines_scratch, lines_scratch, table_scratch],
        compiler_params=params,
        cost_estimate=pl.CostEstimate(
            flops=8 * elements, bytes_accessed=16 * seq * channels, transcendentals=0
        ),
        name="local_conv",
    )(queries, keys_in, values_in, cotangent, rates, weights)

    own_rates = lax.dynamic_slice_in_dim(
        rates.reshape(modes, blocks, sub, LANES).transpose(1, 0, 2, 3).reshape(-1, LANES),
        lax.axis_index("ctx") * slab,
        slab,
        0,
    )
    CHUNK[0] = seq
    carries = pl.pallas_call(
        chunks_kernel,
        out_shape=jax.ShapeDtypeStruct((ctx, 3, slab, LANES), WIRE),
        name="chunk_scan",
    )(gathered, own_rates)
    carried = lax.all_to_all(carries, "ctx", split_axis=0, concat_axis=0, tiled=True)

    raw_rows = carried[:, 2].astype(F32)
    square = jnp.sum(raw_rows * raw_rows)
    if tp <= 4:
        shares = [
            lax.ppermute(square, "tp", [(i, (i + hop) % tp) for i in range(tp)])
            for hop in range(1, tp)
        ]
    else:
        shares = None

    operator_out, grad_queries, grad_keys, grad_values, raw = pl.pallas_call(
        finish_kernel,
        grid=(blocks,),
        in_specs=[line_spec] * 4
        + [table_spec] * 2
        + [pl.BlockSpec((1, width), lambda b: (0, b))]
        + [tall_spec] * 2
        + [pack_spec],
        out_specs=[line_spec] * 4 + [table_spec],
        out_shape=[jax.ShapeDtypeStruct((seq, channels), jnp.bfloat16)] * 4
        + [jax.ShapeDtypeStruct((modes, channels), F32)],
        scratch_shapes=[lines_scratch, lines_scratch, table_scratch, states_scratch],
        compiler_params=params,
        cost_estimate=pl.CostEstimate(
            flops=4 * elements, bytes_accessed=24 * seq * channels, transcendentals=0
        ),
        name="finish",
    )(
        queries,
        keys_in,
        values_in,
        cotangent,
        rates,
        weights,
        skip_gain.reshape(1, channels),
        conv,
        adj,
        carried,
    )
    if shares is None:
        grad_square = lax.psum(square, "tp")
    else:
        grad_square = square
        for share in shares:
            grad_square = grad_square + share
    limit = math.sqrt(channels * tp * modes)
    factor = jnp.minimum(1.0, limit / jnp.sqrt(grad_square + 1e-06))
    return (operator_out, grad_queries, grad_keys, grad_values, (raw * factor).T)


def solution(mesh):
    lines, tables = P("ctx", "tp"), P("tp", None)
    in_specs = (lines, lines, lines, tables, tables, P("tp"), lines)
    out_specs = (lines, lines, lines, lines, tables)
    return jax.shard_map(shards, mesh=mesh, in_specs=in_specs, out_specs=out_specs, check_vma=False)
```

```python
from functools import partial
import math

import jax
import jax.numpy as jnp
from jax import lax
from jax.experimental import pallas as pl
from jax.experimental.pallas import tpu as pltpu
from jax.sharding import PartitionSpec as P

F32 = jnp.float32
WIRE = jnp.bfloat16
LANES = 128
UNROLL = 8
VMEM_LIMIT = 60 * 1024 * 1024


def gate(left_ref, right_ref, cols):
    product = left_ref[:, cols].astype(F32) * right_ref[:, cols].astype(F32)
    return product.astype(jnp.bfloat16).astype(F32)


def rows_of(ref, step, sub, pitch):
    return ref[pl.ds(step, sub, stride=pitch), :]


def spread(table_ref, modes, sub, scratch):
    for s in range(sub):
        scratch[pl.ds(s, modes, stride=sub), :] = table_ref[:, s * LANES : (s + 1) * LANES]
    return [scratch[n * sub : (n + 1) * sub, :] for n in range(modes)]


def tree_sum(items):
    items = list(items)
    while len(items) > 1:
        items = [
            items[i] + items[i + 1] if i + 1 < len(items) else items[i]
            for i in range(0, len(items), 2)
        ]
    return items[0]


def fill_lines(k_ref, v_ref, q_ref, ct_ref, gated, pulled, sub, seq):
    for s in range(sub):
        cols = slice(s * LANES, (s + 1) * LANES)
        gated[s * seq : (s + 1) * seq, :] = gate(k_ref, v_ref, cols)
        pulled[s * seq : (s + 1) * seq, :] = gate(ct_ref, q_ref, cols)


def states_kernel(q_ref, k_ref, v_ref, ct_ref, rate_ref, out_ref, token_ref, gated, pulled, table, states):
    seq = q_ref.shape[0]
    modes = rate_ref.shape[0]
    sub = q_ref.shape[1] // LANES
    fill_lines(k_ref, v_ref, q_ref, ct_ref, gated, pulled, sub, seq)
    decay = [jnp.exp(-r) for r in spread(rate_ref, modes, sub, table)]
    token_ref[...] = jnp.zeros_like(token_ref)
    zeros = tuple(jnp.zeros((sub, LANES), F32) for _ in range(modes))

    def forward(i, carry):
        held, inner = list(carry[0]), list(carry[1])
        for u in range(UNROLL):
            t = i * UNROLL + u
            x = rows_of(gated, t, sub, seq)
            p = rows_of(pulled, t, sub, seq)
            for n in range(modes):
                held[n] = decay[n] * held[n] + x
                inner[n] = inner[n] + p * held[n]
        return tuple(held), tuple(inner)

    def backward(i, carry):
        held = list(carry)
        for u in range(UNROLL):
            t = seq - 1 - (i * UNROLL + u)
            p = rows_of(pulled, t, sub, seq)
            for n in range(modes):
                held[n] = decay[n] * held[n] + p
        return tuple(held)

    ends, inner = lax.fori_loop(0, seq // UNROLL, forward, (zeros, zeros))
    starts = lax.fori_loop(0, seq // UNROLL, backward, zeros)
    for n in range(modes):
        rows = slice(n * sub, (n + 1) * sub)
        states[0, rows, :] = ends[n]
        states[1, rows, :] = starts[n]
        states[2, rows, :] = inner[n]
    dests, _, slab, _ = out_ref.shape
    for d in range(dests):
        for kind in range(3):
            out_ref[d, kind] = states[kind, d * slab : (d + 1) * slab, :].astype(out_ref.dtype)


def local_kernel(
    reverse, left_ref, right_ref, rate_ref, res_ref, after_ref, out_ref, token_ref, lines, table
):
    token_ref[...] = jnp.zeros_like(token_ref)
    seq = left_ref.shape[0]
    modes = rate_ref.shape[0]
    sub = left_ref.shape[1] // LANES
    for s in range(sub):
        cols = slice(s * LANES, (s + 1) * LANES)
        lines[s * seq : (s + 1) * seq, :] = gate(left_ref, right_ref, cols)
    rates = spread(rate_ref, modes, sub, table)
    weights = spread(res_ref, modes, sub, table)
    decay = [jnp.exp(-r) for r in rates]
    coef = [w * jnp.sqrt(1.0 - jnp.exp(-2.0 * r)) for w, r in zip(weights, rates)]

    def body(i, carry):
        held = list(carry)
        for u in range(UNROLL):
            t = i * UNROLL + u
            if reverse:
                t = seq - 1 - t
            x = rows_of(lines, t, sub, seq)
            total = [None] * 4
            for n in range(modes):
                held[n] = decay[n] * held[n] + x
                term = coef[n] * held[n]
                total[n % 4] = term if total[n % 4] is None else total[n % 4] + term
            out_ref[0, t] = tree_sum(total)
        return tuple(held)

    zeros = tuple(jnp.zeros((sub, LANES), F32) for _ in range(modes))
    lax.fori_loop(0, seq // UNROLL, body, zeros)


def chunks_kernel(in_ref, rate_ref, after_ref, out_ref, token_ref):
    token_ref[...] = jnp.zeros_like(token_ref)
    count = in_ref.shape[0]
    rate = rate_ref[...]
    step = jnp.exp(-rate)
    span = jnp.exp(-rate * CHUNK[0])
    unit = jnp.sqrt(1.0 - jnp.exp(-2.0 * rate))
    held = jnp.zeros_like(rate)
    total = jnp.zeros_like(rate)
    for j in range(count):
        out_ref[j, 0] = held.astype(out_ref.dtype)
        start = in_ref[j, 1].astype(F32)
        total = total + (in_ref[j, 2].astype(F32) + step * start * held)
        held = span * held + in_ref[j, 0].astype(F32)
    back = jnp.zeros_like(rate)
    raw = (unit * total).astype(out_ref.dtype)
    for j in reversed(range(count)):
        out_ref[j, 1] = back.astype(out_ref.dtype)
        out_ref[j, 2] = raw
        back = span * back + in_ref[j, 1].astype(F32)


CHUNK = [128]


def finish_kernel(
    q_ref,
    k_ref,
    v_ref,
    ct_ref,
    rate_ref,
    res_ref,
    skip_ref,
    conv_ref,
    adj_ref,
    in_ref,
    out_ref,
    gq_ref,
    gk_ref,
    gv_ref,
    raw_ref,
    conv_lines,
    adj_lines,
    table,
    states,
):
    seq = q_ref.shape[0]
    modes = rate_ref.shape[0]
    sub = q_ref.shape[1] // LANES
    sources, _, slab, _ = in_ref.shape
    for d in range(sources):
        for kind in range(3):
            states[kind, d * slab : (d + 1) * slab, :] = in_ref[d, kind].astype(F32)
    for s in range(sub):
        raw_ref[:, s * LANES : (s + 1) * LANES] = states[2, pl.ds(s, modes, stride=sub), :]
    rates = spread(rate_ref, modes, sub, table)
    weights = spread(res_ref, modes, sub, table)
    decay = [jnp.exp(-r) for r in rates]
    coef = [w * jnp.sqrt(1.0 - jnp.exp(-2.0 * r)) for w, r in zip(weights, rates)]
    ahead = tuple(coef[n] * states[0, n * sub : (n + 1) * sub, :] for n in range(modes))
    behind = tuple(coef[n] * states[1, n * sub : (n + 1) * sub, :] for n in range(modes))

    def body(i, carry):
        ahead, behind = list(carry[0]), list(carry[1])
        for u in range(UNROLL):
            t = i * UNROLL + u
            back_t = seq - 1 - t
            total_a, total_b = [None] * 4, [None] * 4
            for n in range(modes):
                ahead[n] = decay[n] * ahead[n]
                behind[n] = decay[n] * behind[n]
                total_a[n % 4] = ahead[n] if n < 4 else total_a[n % 4] + ahead[n]
                total_b[n % 4] = behind[n] if n < 4 else total_b[n % 4] + behind[n]
            conv_lines[pl.ds(t, sub, stride=seq), :] = conv_ref[0, t] + tree_sum(total_a)
            adj_lines[pl.ds(back_t, sub, stride=seq), :] = adj_ref[0, back_t] + tree_sum(total_b)
        return tuple(ahead), tuple(behind)

    lax.fori_loop(0, seq // UNROLL, body, (ahead, behind))
    for s in range(sub):
        cols = slice(s * LANES, (s + 1) * LANES)
        rows = slice(s * seq, (s + 1) * seq)
        skip = skip_ref[:, cols]
        q, ct = q_ref[:, cols].astype(F32), ct_ref[:, cols].astype(F32)
        k, v = k_ref[:, cols].astype(F32), v_ref[:, cols].astype(F32)
        gated = (k * v).astype(jnp.bfloat16).astype(F32)
        pulled = (ct * q).astype(jnp.bfloat16).astype(F32)
        mixed = conv_lines[rows, :].astype(jnp.bfloat16).astype(F32) + skip * gated
        out_ref[:, cols] = (q * mixed).astype(out_ref.dtype)
        gq_ref[:, cols] = (ct * mixed).astype(gq_ref.dtype)
        grad = adj_lines[rows, :].astype(jnp.bfloat16).astype(F32) + skip * pulled
        gk_ref[:, cols] = (grad * v).astype(gk_ref.dtype)
        gv_ref[:, cols] = (grad * k).astype(gv_ref.dtype)


def shards(queries, keys_in, values_in, decay_rates, residues, skip_gain, cotangent):
    seq, channels = queries.shape
    modes = decay_rates.shape[1]
    ctx = lax.axis_size("ctx")
    tp = lax.axis_size("tp")
    groups = channels // LANES
    sub = math.gcd(groups, 8)
    blocks = groups // sub
    width = sub * LANES
    slab = modes * groups // ctx
    per_block = ctx // blocks
    block_rows = modes * sub
    rates, weights = decay_rates.T, residues.T
    params = pltpu.CompilerParams(vmem_limit_bytes=VMEM_LIMIT)

    line_spec = pl.BlockSpec((seq, width), lambda b: (0, b))
    table_spec = pl.BlockSpec((modes, width), lambda b: (0, b))
    pack_spec = pl.BlockSpec((per_block, 3, slab, LANES), lambda b: (b, 0, 0, 0))
    tall_spec = pl.BlockSpec((1, seq, sub, LANES), lambda b: (b, 0, 0, 0))
    lines_scratch = pltpu.VMEM((sub * seq, LANES), F32)
    table_scratch = pltpu.VMEM((block_rows, LANES), F32)
    states_scratch = pltpu.VMEM((3, block_rows, LANES), F32)
    token_spec = pl.BlockSpec((8, LANES), lambda b: (0, 0))
    token_shape = jax.ShapeDtypeStruct((8, LANES), F32)
    elements = seq * channels * modes

    packed, token = pl.pallas_call(
        states_kernel,
        grid=(blocks,),
        in_specs=[line_spec] * 4 + [table_spec],
        out_specs=[pack_spec, token_spec],
        out_shape=[jax.ShapeDtypeStruct((ctx, 3, slab, LANES), WIRE), token_shape],
        scratch_shapes=[lines_scratch, lines_scratch, table_scratch, states_scratch],
        compiler_params=params,
        cost_estimate=pl.CostEstimate(
            flops=6 * elements, bytes_accessed=8 * seq * channels, transcendentals=0
        ),
        name="chunk_states",
    )(queries, keys_in, values_in, cotangent, rates)
    gathered = lax.all_to_all(packed, "ctx", split_axis=0, concat_axis=0, tiled=True)

    def local(reverse, left, right, after, name):
        return pl.pallas_call(
            partial(local_kernel, reverse),
            grid=(blocks,),
            in_specs=[line_spec] * 2 + [table_spec] * 2 + [pl.BlockSpec(memory_space=pl.ANY)],
            out_specs=[tall_spec, token_spec],
            out_shape=[jax.ShapeDtypeStruct((blocks, seq, sub, LANES), F32), token_shape],
            scratch_shapes=[lines_scratch, table_scratch],
            compiler_params=params,
            cost_estimate=pl.CostEstimate(
                flops=4 * elements, bytes_accessed=8 * seq * channels, transcendentals=0
            ),
            name=name,
        )(left, right, rates, weights, after)

    conv, token = local(False, keys_in, values_in, token, "local_conv")
    own_rates = lax.dynamic_slice_in_dim(
        rates.reshape(modes, blocks, sub, LANES).transpose(1, 0, 2, 3).reshape(-1, LANES),
        lax.axis_index("ctx") * slab,
        slab,
        0,
    )
    CHUNK[0] = seq
    carries, token = pl.pallas_call(
        chunks_kernel,
        out_shape=[jax.ShapeDtypeStruct((ctx, 3, slab, LANES), WIRE), token_shape],
        in_specs=[pl.BlockSpec(), pl.BlockSpec(), pl.BlockSpec(memory_space=pl.ANY)],
        compiler_params=pltpu.CompilerParams(vmem_limit_bytes=4 * 1024 * 1024),
        name="chunk_scan",
    )(gathered, own_rates, token)
    adj, _ = local(True, cotangent, queries, token, "local_adjoint")
    carried = lax.all_to_all(carries, "ctx", split_axis=0, concat_axis=0, tiled=True)

    raw_rows = carried[:, 2].astype(F32)
    square = jnp.sum(raw_rows * raw_rows)
    if tp <= 4:
        shares = [
            lax.ppermute(square, "tp", [(i, (i + hop) % tp) for i in range(tp)])
            for hop in range(1, tp)
        ]
    else:
        shares = None

    operator_out, grad_queries, grad_keys, grad_values, raw = pl.pallas_call(
        finish_kernel,
        grid=(blocks,),
        in_specs=[line_spec] * 4
        + [table_spec] * 2
        + [pl.BlockSpec((1, width), lambda b: (0, b))]
        + [tall_spec] * 2
        + [pack_spec],
        out_specs=[line_spec] * 4 + [table_spec],
        out_shape=[jax.ShapeDtypeStruct((seq, channels), jnp.bfloat16)] * 4
        + [jax.ShapeDtypeStruct((modes, channels), F32)],
        scratch_shapes=[lines_scratch, lines_scratch, table_scratch, states_scratch],
        compiler_params=params,
        cost_estimate=pl.CostEstimate(
            flops=4 * elements, bytes_accessed=24 * seq * channels, transcendentals=0
        ),
        name="finish",
    )(
        queries,
        keys_in,
        values_in,
        cotangent,
        rates,
        weights,
        skip_gain.reshape(1, channels),
        conv,
        adj,
        carried,
    )
    if shares is None:
        grad_square = lax.psum(square, "tp")
    else:
        grad_square = square
        for share in shares:
            grad_square = grad_square + share
    limit = math.sqrt(channels * tp * modes)
    factor = jnp.minimum(1.0, limit / jnp.sqrt(grad_square + 1e-06))
    return (operator_out, grad_queries, grad_keys, grad_values, (raw * factor).T)


def solution(mesh):
    lines, tables = P("ctx", "tp"), P("tp", None)
    in_specs = (lines, lines, lines, tables, tables, P("tp"), lines)
    out_specs = (lines, lines, lines, lines, tables)
    return jax.shard_map(shards, mesh=mesh, in_specs=in_specs, out_specs=out_specs, check_vma=False)
```

```python
from functools import partial
import math

import jax
import jax.numpy as jnp
from jax import lax
from jax.experimental import pallas as pl
from jax.experimental.pallas import tpu as pltpu
from jax.sharding import PartitionSpec as P

F32 = jnp.float32
WIRE = jnp.bfloat16
LANES = 128
UNROLL = 8
LARGE = pltpu.CompilerParams(vmem_limit_bytes=60 * 1024 * 1024)
SMALL = pltpu.CompilerParams(vmem_limit_bytes=8 * 1024 * 1024)


def gate(left_ref, right_ref, cols):
    product = left_ref[:, cols].astype(F32) * right_ref[:, cols].astype(F32)
    return product.astype(jnp.bfloat16).astype(F32)


def fill_lines(left_ref, right_ref, lines, sub, seq):
    for s in range(sub):
        cols = slice(s * LANES, (s + 1) * LANES)
        lines[s * seq : (s + 1) * seq, :] = gate(left_ref, right_ref, cols)


def spread(table_ref, modes, sub, scratch):
    for s in range(sub):
        scratch[pl.ds(s, modes, stride=sub), :] = table_ref[:, s * LANES : (s + 1) * LANES]
    return [scratch[n * sub : (n + 1) * sub, :] for n in range(modes)]


def tree_sum(items):
    items = list(items)
    while len(items) > 1:
        items = [
            items[i] + items[i + 1] if i + 1 < len(items) else items[i]
            for i in range(0, len(items), 2)
        ]
    return items[0]


def states_kernel(
    q_ref, k_ref, v_ref, ct_ref, rate_ref, keep_ref, send_ref, gated, pulled, table, states
):
    seq = q_ref.shape[0]
    modes = rate_ref.shape[0]
    sub = q_ref.shape[1] // LANES
    block = pl.program_id(0)
    fill_lines(k_ref, v_ref, gated, sub, seq)
    fill_lines(ct_ref, q_ref, pulled, sub, seq)
    decay = [jnp.exp(-r) for r in spread(rate_ref, modes, sub, table)]
    zeros = tuple(jnp.zeros((sub, LANES), F32) for _ in range(modes))

    def forward(i, carry):
        held, inner = list(carry[0]), list(carry[1])
        for u in range(UNROLL):
            t = i * UNROLL + u
            x = gated[pl.ds(t, sub, stride=seq), :]
            p = pulled[pl.ds(t, sub, stride=seq), :]
            for n in range(modes):
                held[n] = decay[n] * held[n] + x
                inner[n] = inner[n] + p * held[n]
        return tuple(held), tuple(inner)

    def backward(i, carry):
        held = list(carry)
        for u in range(UNROLL):
            t = seq - 1 - (i * UNROLL + u)
            p = pulled[pl.ds(t, sub, stride=seq), :]
            for n in range(modes):
                held[n] = decay[n] * held[n] + p
        return tuple(held)

    ends, inner = lax.fori_loop(0, seq // UNROLL, forward, (zeros, zeros))
    starts = lax.fori_loop(0, seq // UNROLL, backward, zeros)
    for n in range(modes):
        rows = pl.ds(pl.multiple_of((block * modes + n) * sub, sub), sub)
        states[0, rows, :] = ends[n]
        states[1, rows, :] = starts[n]
        states[2, rows, :] = inner[n]

    @pl.when(block == pl.num_programs(0) - 1)
    def _():
        half = keep_ref.shape[1]
        core = lax.axis_index("ctx") % 2
        keep_ref[...] = states[:, pl.ds(pl.multiple_of(core * half, half), half), :]
        send_ref[...] = states[:, pl.ds(pl.multiple_of((1 - core) * half, half), half), :]


def joined(is_right, mine, other, span, step):
    left = [jnp.where(is_right, o, m) for m, o in zip(mine, other)]
    right = [jnp.where(is_right, m, o) for m, o in zip(mine, other)]
    return (
        span * left[0] + right[0],
        left[1] + span * right[1],
        left[2] + right[2] + step * right[1] * left[0],
    )


def put_wire(wire_ref, is_last, next_right, block):
    if is_last:
        wire_ref[0] = jnp.where(next_right, block[1], block[0]).astype(wire_ref.dtype)
        wire_ref[1] = block[2].astype(wire_ref.dtype)
    else:
        for kind in range(3):
            wire_ref[kind] = block[kind].astype(wire_ref.dtype)


def pair_kernel(seq, is_last, keep_ref, got_ref, rate_ref, block_ref, wire_ref):
    rate = rate_ref[...]
    place = lax.axis_index("ctx")
    block = joined(
        place % 2 == 1,
        [keep_ref[i] for i in range(3)],
        [got_ref[i] for i in range(3)],
        jnp.exp(-rate * seq),
        jnp.exp(-rate),
    )
    for kind in range(3):
        block_ref[kind] = block[kind]
    block_ref[3] = jnp.zeros_like(rate)
    block_ref[4] = jnp.zeros_like(rate)
    put_wire(wire_ref, is_last, (place // 2) % 2 == 1, block)


def carries_with(block_ref, end_state, start_state, level, seq, rate):
    place = lax.axis_index("ctx")
    is_right = (place >> level) % 2 == 1
    chips = 1 << (level - 1)
    at = (place // 2) % chips
    before = at * (2 * seq)
    behind = (chips - 1 - at) * (2 * seq)
    ahead = block_ref[3] + jnp.where(
        is_right, jnp.exp(-rate * before.astype(F32)) * end_state, 0.0
    )
    after = block_ref[4] + jnp.where(
        is_right, 0.0, jnp.exp(-rate * behind.astype(F32)) * start_state
    )
    return is_right, ahead, after


def level_kernel(seq, level, is_last, block_ref, got_ref, rate_ref, out_ref, wire_ref):
    rate = rate_ref[...]
    got = [got_ref[i].astype(F32) for i in range(3)]
    is_right, ahead, after = carries_with(block_ref, got[0], got[1], level, seq, rate)
    block = joined(
        is_right,
        [block_ref[i] for i in range(3)],
        got,
        jnp.exp(-rate * (seq << level)),
        jnp.exp(-rate),
    )
    for kind in range(3):
        out_ref[kind] = block[kind]
    out_ref[3] = ahead
    out_ref[4] = after
    next_right = (lax.axis_index("ctx") >> (level + 1)) % 2 == 1
    put_wire(wire_ref, is_last, next_right, block)


def last_kernel(
    seq, level, block_ref, got_ref, rate_ref, keep_ref, sibling_ref, mine_ref, other_ref
):
    rate = rate_ref[...]
    half = rate.shape[0]
    edge, inner = got_ref[0].astype(F32), got_ref[1].astype(F32)
    is_right, ahead, after = carries_with(block_ref, edge, edge, level, seq, rate)
    own_edge = jnp.where(is_right, block_ref[1], block_ref[0])
    total = block_ref[2] + inner + jnp.exp(-rate) * own_edge * edge
    raw = jnp.sqrt(1.0 - jnp.exp(-2.0 * rate)) * total
    core = lax.axis_index("ctx") % 2
    first = core == 0
    span = jnp.exp(-rate * seq)
    end_first = jnp.where(first, keep_ref[0], sibling_ref[0])
    start_second = jnp.where(first, sibling_ref[1], keep_ref[1])
    ahead_second = span * ahead + end_first
    after_first = span * after + start_second
    mine_ref[0:half, :] = jnp.where(first, ahead, ahead_second)
    mine_ref[half : 2 * half, :] = jnp.where(first, after_first, after)
    other_ref[0:half, :] = jnp.where(first, ahead_second, ahead)
    other_ref[half : 2 * half, :] = jnp.where(first, after, after_first)
    squares = raw * raw
    share = tree_sum([squares[i : i + 8, :] for i in range(0, half, 8)])
    for ref in (mine_ref, other_ref):
        ref[2 * half : 3 * half, :] = raw
        ref[3 * half : 3 * half + 8, :] = share


def finish_kernel(
    q_ref,
    k_ref,
    v_ref,
    ct_ref,
    rate_ref,
    res_ref,
    skip_ref,
    mine_ref,
    other_ref,
    out_ref,
    gq_ref,
    gk_ref,
    gv_ref,
    raw_ref,
    conv_lines,
    adj_lines,
    table,
    states,
):
    seq = q_ref.shape[0]
    modes = rate_ref.shape[0]
    sub = q_ref.shape[1] // LANES
    half = states.shape[1] // 2
    block = pl.program_id(0)

    @pl.when(block == 0)
    def _():
        core = lax.axis_index("ctx") % 2
        for ref, at in ((mine_ref, core), (other_ref, 1 - core)):
            rows = pl.ds(pl.multiple_of(at * half, half), half)
            for kind in range(3):
                states[kind, rows, :] = ref[kind * half : (kind + 1) * half, :]

    first_row = block * modes * sub
    for s in range(sub):
        raw_ref[:, s * LANES : (s + 1) * LANES] = states[
            2, pl.ds(first_row + s, modes, stride=sub), :
        ]
    rates = spread(rate_ref, modes, sub, table)
    weights = spread(res_ref, modes, sub, table)
    decay = [jnp.exp(-r) for r in rates]
    coef = [w * jnp.sqrt(1.0 - jnp.exp(-2.0 * r)) for w, r in zip(weights, rates)]
    rows = [pl.ds(pl.multiple_of(first_row + n * sub, sub), sub) for n in range(modes)]
    fill_lines(k_ref, v_ref, conv_lines, sub, seq)
    fill_lines(ct_ref, q_ref, adj_lines, sub, seq)

    def scan(lines, kind, reverse):
        def body(i, carry):
            held = list(carry)
            for u in range(UNROLL):
                t = i * UNROLL + u
                if reverse:
                    t = seq - 1 - t
                at = pl.ds(t, sub, stride=seq)
                x = lines[at, :]
                total = [None] * 4
                for n in range(modes):
                    held[n] = decay[n] * held[n] + x
                    term = coef[n] * held[n]
                    total[n % 4] = term if n < 4 else total[n % 4] + term
                lines[at, :] = tree_sum(total)
            return tuple(held)

        lax.fori_loop(0, seq // UNROLL, body, tuple(states[kind, r, :] for r in rows))

    scan(conv_lines, 0, False)
    scan(adj_lines, 1, True)
    for s in range(sub):
        cols = slice(s * LANES, (s + 1) * LANES)
        rows = slice(s * seq, (s + 1) * seq)
        skip = skip_ref[:, cols]
        q, ct = q_ref[:, cols].astype(F32), ct_ref[:, cols].astype(F32)
        k, v = k_ref[:, cols].astype(F32), v_ref[:, cols].astype(F32)
        gated = (k * v).astype(jnp.bfloat16).astype(F32)
        pulled = (ct * q).astype(jnp.bfloat16).astype(F32)
        mixed = conv_lines[rows, :].astype(jnp.bfloat16).astype(F32) + skip * gated
        out_ref[:, cols] = (q * mixed).astype(out_ref.dtype)
        gq_ref[:, cols] = (ct * mixed).astype(gq_ref.dtype)
        grad = adj_lines[rows, :].astype(jnp.bfloat16).astype(F32) + skip * pulled
        gk_ref[:, cols] = (grad * v).astype(gk_ref.dtype)
        gv_ref[:, cols] = (grad * k).astype(gv_ref.dtype)


def clip_kernel(limit, *refs):
    raw_ref, share_refs, out_ref = refs[0], refs[1:-1], refs[-1]
    square = jnp.sum(tree_sum([ref[...] for ref in share_refs]))
    factor = jnp.minimum(1.0, limit * lax.rsqrt(jnp.full((1, LANES), square + 1e-06, F32)))
    for at in range(0, raw_ref.shape[1], LANES):
        out_ref[:, at : at + LANES] = raw_ref[:, at : at + LANES] * factor


def shards(queries, keys_in, values_in, decay_rates, residues, skip_gain, cotangent):
    seq, channels = queries.shape
    modes = decay_rates.shape[1]
    ctx = lax.axis_size("ctx")
    tp = lax.axis_size("tp")
    levels = ctx.bit_length() - 1
    groups = channels // LANES
    sub = math.gcd(groups, 8)
    blocks = groups // sub
    width = sub * LANES
    half = modes * groups // 2
    rates, weights = decay_rates.T, residues.T

    def swap(value, bit):
        return lax.ppermute(value, "ctx", [(i, i ^ (1 << bit)) for i in range(ctx)])

    def rows(*shape, dtype=F32):
        return jax.ShapeDtypeStruct((*shape, LANES), dtype)

    line_spec = pl.BlockSpec((seq, width), lambda b: (0, b))
    table_spec = pl.BlockSpec((modes, width), lambda b: (0, b))
    edge_spec = pl.BlockSpec((3, half, LANES), lambda b: (0, 0, 0))
    pack_spec = pl.BlockSpec((3 * half + 8, LANES), lambda b: (0, 0))
    lines_scratch = pltpu.VMEM((sub * seq, LANES), F32)
    table_scratch = pltpu.VMEM((modes * sub, LANES), F32)
    states_scratch = pltpu.VMEM((3, 2 * half, LANES), F32)
    elements = seq * channels * modes

    keep, send = pl.pallas_call(
        states_kernel,
        grid=(blocks,),
        in_specs=[line_spec] * 4 + [table_spec],
        out_specs=[edge_spec] * 2,
        out_shape=[rows(3, half)] * 2,
        scratch_shapes=[lines_scratch, lines_scratch, table_scratch, states_scratch],
        compiler_params=LARGE,
        cost_estimate=pl.CostEstimate(
            flops=6 * elements, bytes_accessed=8 * seq * channels, transcendentals=0
        ),
        name="chunk_states",
    )(queries, keys_in, values_in, cotangent, rates)
    sibling = swap(send, 0)

    own_rates = lax.dynamic_slice_in_dim(
        rates.reshape(modes, blocks, sub, LANES).transpose(1, 0, 2, 3).reshape(-1, LANES),
        (lax.axis_index("ctx") % 2) * half,
        half,
        0,
    )

    def wire(level):
        return rows(2 if level == levels - 1 else 3, half, dtype=WIRE)

    block, packed = pl.pallas_call(
        partial(pair_kernel, seq, levels == 2),
        out_shape=[rows(5, half), wire(1)],
        compiler_params=SMALL,
        name="chip_states",
    )(keep, sibling, own_rates)
    for level in range(1, levels - 1):
        got = swap(packed, level)
        block, packed = pl.pallas_call(
            partial(level_kernel, seq, level, level + 1 == levels - 1),
            out_shape=[rows(5, half), wire(level + 1)],
            compiler_params=SMALL,
            name="block_states",
        )(block, got, own_rates)
    got = swap(packed, levels - 1)
    mine, other = pl.pallas_call(
        partial(last_kernel, seq, levels - 1),
        out_shape=[rows(3 * half + 8)] * 2,
        compiler_params=SMALL,
        name="carries",
    )(block, got, own_rates, keep, sibling)
    other = swap(other, 0)

    square = mine[3 * half :] + other[3 * half :]
    if tp <= 4:
        shares = [square] + [
            lax.ppermute(square, "tp", [(i, (i + hop) % tp) for i in range(tp)])
            for hop in range(1, tp)
        ]
    else:
        shares = [lax.psum(square, "tp")]

    operator_out, grad_queries, grad_keys, grad_values, raw = pl.pallas_call(
        finish_kernel,
        grid=(blocks,),
        in_specs=[line_spec] * 4
        + [table_spec] * 2
        + [pl.BlockSpec((1, width), lambda b: (0, b))]
        + [pack_spec] * 2,
        out_specs=[line_spec] * 4 + [table_spec],
        out_shape=[jax.ShapeDtypeStruct((seq, channels), jnp.bfloat16)] * 4
        + [jax.ShapeDtypeStruct((modes, channels), F32)],
        scratch_shapes=[lines_scratch, lines_scratch, table_scratch, states_scratch],
        compiler_params=LARGE,
        cost_estimate=pl.CostEstimate(
            flops=8 * elements, bytes_accessed=16 * seq * channels, transcendentals=0
        ),
        name="finish",
    )(
        queries,
        keys_in,
        values_in,
        cotangent,
        rates,
        weights,
        skip_gain.reshape(1, channels),
        mine,
        other,
    )
    grad_residues = pl.pallas_call(
        partial(clip_kernel, math.sqrt(channels * tp * modes)),
        out_shape=jax.ShapeDtypeStruct((modes, channels), F32),
        compiler_params=SMALL,
        name="clip",
    )(raw, *shares)
    return (operator_out, grad_queries, grad_keys, grad_values, grad_residues.T)


def solution(mesh):
    lines, tables = P("ctx", "tp"), P("tp", None)
    in_specs = (lines, lines, lines, tables, tables, P("tp"), lines)
    out_specs = (lines, lines, lines, lines, tables)
    return jax.shard_map(shards, mesh=mesh, in_specs=in_specs, out_specs=out_specs, check_vma=False)
```

```python
from functools import partial
import math

import jax
import jax.numpy as jnp
from jax import lax
from jax.experimental import pallas as pl
from jax.experimental.pallas import tpu as pltpu
from jax.sharding import PartitionSpec as P

F32 = jnp.float32
WIRE = jnp.bfloat16
LANES = 128
UNROLL = 8
STEP_ROWS = 32
KERNEL = pltpu.CompilerParams(vmem_limit_bytes=24 * 1024 * 1024)
HBM = pl.BlockSpec(memory_space=pltpu.HBM)
VMEM = pl.BlockSpec(memory_space=pltpu.VMEM)


def reorder(rows, inner, transpose):
    outer = rows // inner
    to = lax.broadcasted_iota(jnp.int32, (rows, rows), 0)
    fro = lax.broadcasted_iota(jnp.int32, (rows, rows), 1)
    if transpose:
        to, fro = fro, to
    same = (to % outer == fro // inner) & (to // outer == fro % inner)
    return jnp.where(same, 1.0, 0.0).astype(jnp.bfloat16)


def tree_sum(items):
    items = list(items)
    while len(items) > 1:
        items = [
            items[i] + items[i + 1] if i + 1 < len(items) else items[i]
            for i in range(0, len(items), 2)
        ]
    return items[0]


def states_kernel(
    q_hbm,
    k_hbm,
    v_hbm,
    ct_hbm,
    rate_hbm,
    res_hbm,
    keep_ref,
    send_ref,
    q_ref,
    k_ref,
    v_ref,
    ct_ref,
    gated_ref,
    pulled_ref,
    rate_ref,
    coef_ref,
    rate_cols,
    res_cols,
    states,
    sems,
):
    seq, channels = q_ref.shape
    modes = rate_cols.shape[0]
    blocks = gated_ref.shape[0]
    sub = channels // (blocks * LANES)
    part = math.gcd(seq, STEP_ROWS)
    parts = seq // part
    tables = [
        pltpu.make_async_copy(rate_hbm, rate_cols, sems.at[4 * parts]),
        pltpu.make_async_copy(res_hbm, res_cols, sems.at[4 * parts + 1]),
    ]
    lines = []
    for i in range(parts):
        rows = pl.ds(i * part, part)
        pairs = ((k_hbm, k_ref), (v_hbm, v_ref), (ct_hbm, ct_ref), (q_hbm, q_ref))
        for j, (source, target) in enumerate(pairs):
            lines.append(
                pltpu.make_async_copy(source.at[rows], target.at[rows], sems.at[4 * i + j])
            )
    for copy in tables + lines:
        copy.start()
    for copy in tables:
        copy.wait()
    for b in range(blocks):
        for s in range(sub):
            cols = slice((b * sub + s) * LANES, (b * sub + s + 1) * LANES)
            rows = pl.ds(b * modes * sub + s, modes, stride=sub)
            rate_ref[rows, :] = rate_cols[:, cols]
            coef_ref[rows, :] = res_cols[:, cols]
    rate = rate_ref[...]
    coef_ref[...] = coef_ref[...] * jnp.sqrt(1.0 - jnp.exp(-2.0 * rate))
    to_scan = reorder(part * sub, part, False)

    def mode_rows(b):
        return [slice((b * modes + n) * sub, (b * modes + n + 1) * sub) for n in range(modes)]

    def to_scan_order(left, right, i, target):
        rows = slice(i * part, (i + 1) * part)
        product = (left[rows, :].astype(F32) * right[rows, :].astype(F32)).astype(jnp.bfloat16)
        stacked = jnp.concatenate(
            [
                jnp.concatenate(
                    [
                        product[:, (b * sub + s) * LANES : (b * sub + s + 1) * LANES]
                        for s in range(sub)
                    ],
                    axis=0,
                )
                for b in range(blocks)
            ],
            axis=1,
        )
        ordered = jnp.dot(to_scan, stacked, preferred_element_type=F32)
        for b in range(blocks):
            target[b, i * part * sub : (i + 1) * part * sub, :] = ordered[
                :, b * LANES : (b + 1) * LANES
            ]

    for i in range(parts):
        for copy in lines[4 * i : 4 * i + 4]:
            copy.wait()
        to_scan_order(k_ref, v_ref, i, gated_ref)
        to_scan_order(ct_ref, q_ref, i, pulled_ref)
        for b in range(blocks):
            decay = [jnp.exp(-rate_ref[r, :]) for r in mode_rows(b)]

            def forward(j, carry):
                held, inner = list(carry[0]), list(carry[1])
                for u in range(UNROLL):
                    at = pl.ds(pl.multiple_of((i * part + j * UNROLL + u) * sub, sub), sub)
                    x = gated_ref[b, at, :]
                    p = pulled_ref[b, at, :]
                    for n in range(modes):
                        held[n] = decay[n] * held[n] + x
                        inner[n] = inner[n] + p * held[n]
                return tuple(held), tuple(inner)

            if i == 0:
                first = tuple(jnp.zeros((sub, LANES), F32) for _ in range(modes))
                carry = (first, first)
            else:
                carry = tuple(tuple(states[kind, r, :] for r in mode_rows(b)) for kind in (0, 2))
            ends, inner = lax.fori_loop(0, part // UNROLL, forward, carry)
            for n, r in enumerate(mode_rows(b)):
                states[0, r, :] = ends[n]
                states[2, r, :] = inner[n]

    for b in range(blocks):
        decay = [jnp.exp(-rate_ref[r, :]) for r in mode_rows(b)]

        def backward(j, carry):
            held = list(carry)
            for u in range(UNROLL):
                at = pl.ds(pl.multiple_of((seq - 1 - (j * UNROLL + u)) * sub, sub), sub)
                p = pulled_ref[b, at, :]
                for n in range(modes):
                    held[n] = decay[n] * held[n] + p
            return tuple(held)

        first = tuple(jnp.zeros((sub, LANES), F32) for _ in range(modes))
        starts = lax.fori_loop(0, seq // UNROLL, backward, first)
        for n, r in enumerate(mode_rows(b)):
            states[1, r, :] = starts[n]

    half = keep_ref.shape[1]
    core = lax.axis_index("ctx") % 2
    keep_ref[...] = states[:, pl.ds(pl.multiple_of(core * half, half), half), :]
    send_ref[...] = states[:, pl.ds(pl.multiple_of((1 - core) * half, half), half), :]


def own_rows(rate_ref, half):
    core = lax.axis_index("ctx") % 2
    return rate_ref[pl.ds(pl.multiple_of(core * half, half), half), :]


def joined(is_right, mine, other, span, step):
    left = [jnp.where(is_right, o, m) for m, o in zip(mine, other)]
    right = [jnp.where(is_right, m, o) for m, o in zip(mine, other)]
    return (
        span * left[0] + right[0],
        left[1] + span * right[1],
        left[2] + right[2] + step * right[1] * left[0],
    )


def put_wire(wire_ref, is_last, next_right, block):
    if is_last:
        wire_ref[0] = jnp.where(next_right, block[1], block[0]).astype(wire_ref.dtype)
        wire_ref[1] = block[2].astype(wire_ref.dtype)
    else:
        for kind in range(3):
            wire_ref[kind] = block[kind].astype(wire_ref.dtype)


def pair_kernel(seq, is_last, keep_ref, got_ref, rate_ref, block_ref, wire_ref):
    rate = own_rows(rate_ref, keep_ref.shape[1])
    place = lax.axis_index("ctx")
    block = joined(
        place % 2 == 1,
        [keep_ref[i] for i in range(3)],
        [got_ref[i] for i in range(3)],
        jnp.exp(-rate * seq),
        jnp.exp(-rate),
    )
    for kind in range(3):
        block_ref[kind] = block[kind]
    block_ref[3] = jnp.zeros_like(rate)
    block_ref[4] = jnp.zeros_like(rate)
    put_wire(wire_ref, is_last, (place // 2) % 2 == 1, block)


def carries_with(block_ref, end_state, start_state, level, seq, rate):
    place = lax.axis_index("ctx")
    is_right = (place >> level) % 2 == 1
    chips = 1 << (level - 1)
    at = (place // 2) % chips
    before = at * (2 * seq)
    behind = (chips - 1 - at) * (2 * seq)
    ahead = block_ref[3] + jnp.where(
        is_right, jnp.exp(-rate * before.astype(F32)) * end_state, 0.0
    )
    after = block_ref[4] + jnp.where(
        is_right, 0.0, jnp.exp(-rate * behind.astype(F32)) * start_state
    )
    return is_right, ahead, after


def level_kernel(seq, level, is_last, block_ref, got_ref, rate_ref, out_ref, wire_ref):
    rate = own_rows(rate_ref, block_ref.shape[1])
    got = [got_ref[i].astype(F32) for i in range(3)]
    is_right, ahead, after = carries_with(block_ref, got[0], got[1], level, seq, rate)
    block = joined(
        is_right,
        [block_ref[i] for i in range(3)],
        got,
        jnp.exp(-rate * (seq << level)),
        jnp.exp(-rate),
    )
    for kind in range(3):
        out_ref[kind] = block[kind]
    out_ref[3] = ahead
    out_ref[4] = after
    next_right = (lax.axis_index("ctx") >> (level + 1)) % 2 == 1
    put_wire(wire_ref, is_last, next_right, block)


def last_kernel(
    seq, level, block_ref, got_ref, rate_ref, keep_ref, sibling_ref, mine_ref, other_ref
):
    half = block_ref.shape[1]
    rate = own_rows(rate_ref, half)
    edge, inner = got_ref[0].astype(F32), got_ref[1].astype(F32)
    is_right, ahead, after = carries_with(block_ref, edge, edge, level, seq, rate)
    own_edge = jnp.where(is_right, block_ref[1], block_ref[0])
    total = block_ref[2] + inner + jnp.exp(-rate) * own_edge * edge
    raw = jnp.sqrt(1.0 - jnp.exp(-2.0 * rate)) * total
    core = lax.axis_index("ctx") % 2
    first = core == 0
    span = jnp.exp(-rate * seq)
    end_first = jnp.where(first, keep_ref[0], sibling_ref[0])
    start_second = jnp.where(first, sibling_ref[1], keep_ref[1])
    ahead_second = span * ahead + end_first
    after_first = span * after + start_second
    mine_ref[0:half, :] = jnp.where(first, ahead, ahead_second)
    mine_ref[half : 2 * half, :] = jnp.where(first, after_first, after)
    other_ref[0:half, :] = jnp.where(first, ahead_second, ahead)
    other_ref[half : 2 * half, :] = jnp.where(first, after, after_first)
    squares = raw * raw
    share = tree_sum([squares[i : i + 8, :] for i in range(0, half, 8)])
    for ref in (mine_ref, other_ref):
        ref[2 * half : 3 * half, :] = raw
        ref[3 * half : 3 * half + 8, :] = share


def place_halves(mine_ref, other_ref, first, target):
    half = target.shape[0] // 2
    core = lax.axis_index("ctx") % 2
    for ref, at in ((mine_ref, core), (other_ref, 1 - core)):
        rows = pl.ds(pl.multiple_of(at * half, half), half)
        target[rows, :] = ref[first : first + half, :]


def finish_kernel(
    q_ref,
    k_ref,
    v_ref,
    ct_ref,
    gated_ref,
    pulled_ref,
    rate_ref,
    coef_ref,
    skip_ref,
    mine_ref,
    other_ref,
    out_hbm,
    gq_hbm,
    gk_hbm,
    gv_hbm,
    out_rows,
    gq_rows,
    gk_rows,
    gv_rows,
    scanned,
    states,
    sems,
):
    seq, channels = q_ref.shape
    blocks = gated_ref.shape[0]
    sub = channels // (blocks * LANES)
    modes = rate_ref.shape[0] // (blocks * sub)
    half = rate_ref.shape[0] // 2
    part = math.gcd(seq, STEP_ROWS)
    parts = seq // part
    from_scan = reorder(part * sub, part, True)
    copies = []

    def scan(lines, kind, reverse):
        place_halves(mine_ref, other_ref, kind * half, states)
        for b in range(blocks):
            rows = [slice((b * modes + n) * sub, (b * modes + n + 1) * sub) for n in range(modes)]
            decay = [jnp.exp(-rate_ref[r, :]) for r in rows]
            coef = [coef_ref[r, :] for r in rows]

            def body(j, carry):
                held = list(carry)
                for u in range(UNROLL):
                    t = j * UNROLL + u
                    if reverse:
                        t = seq - 1 - t
                    at = pl.ds(pl.multiple_of(t * sub, sub), sub)
                    x = lines[b, at, :]
                    total = [None] * 4
                    for n in range(modes):
                        held[n] = decay[n] * held[n] + x
                        term = coef[n] * held[n]
                        total[n % 4] = term if n < 4 else total[n % 4] + term
                    scanned[b, at, :] = tree_sum(total)
                return tuple(held)

            lax.fori_loop(0, seq // UNROLL, body, tuple(states[r, :] for r in rows))

    def outputs(left, right, first_scale, second_scale, first, second, base):
        for i in range(parts):
            rows = slice(i * part, (i + 1) * part)
            stacked = jnp.concatenate(
                [scanned[b, i * part * sub : (i + 1) * part * sub, :] for b in range(blocks)],
                axis=1,
            ).astype(jnp.bfloat16)
            ordered = jnp.dot(from_scan, stacked, preferred_element_type=F32)
            for b in range(blocks):
                for s in range(sub):
                    cols = slice((b * sub + s) * LANES, (b * sub + s + 1) * LANES)
                    own = ordered[s * part : (s + 1) * part, b * LANES : (b + 1) * LANES]
                    line = left[rows, cols].astype(F32) * right[rows, cols].astype(F32)
                    line = line.astype(jnp.bfloat16).astype(F32)
                    mixed = own + skip_ref[:, cols] * line
                    first[0][rows, cols] = (
                        first_scale[rows, cols].astype(F32) * mixed
                    ).astype(jnp.bfloat16)
                    second[0][rows, cols] = (
                        second_scale[rows, cols].astype(F32) * mixed
                    ).astype(jnp.bfloat16)
            at = pl.ds(i * part, part)
            for j, (source, target) in enumerate((first, second)):
                copy = pltpu.make_async_copy(
                    source.at[at], target.at[at], sems.at[base + 2 * i + j]
                )
                copy.start()
                copies.append(copy)

    scan(gated_ref, 0, False)
    outputs(k_ref, v_ref, q_ref, ct_ref, (out_rows, out_hbm), (gq_rows, gq_hbm), 0)
    scan(pulled_ref, 1, True)
    outputs(ct_ref, q_ref, v_ref, k_ref, (gk_rows, gk_hbm), (gv_rows, gv_hbm), 2 * parts)
    for copy in copies:
        copy.wait()


def clip_kernel(limit, blocks, mine_ref, other_ref, *refs):
    share_refs, out_ref, states = refs[:-2], refs[-2], refs[-1]
    modes = out_ref.shape[0]
    sub = out_ref.shape[1] // (blocks * LANES)
    half = states.shape[0] // 2
    place_halves(mine_ref, other_ref, 2 * half, states)
    square = jnp.sum(tree_sum([ref[...] for ref in share_refs]))
    factor = jnp.minimum(1.0, limit * lax.rsqrt(jnp.full((1, LANES), square + 1e-06, F32)))
    for b in range(blocks):
        for s in range(sub):
            cols = slice((b * sub + s) * LANES, (b * sub + s + 1) * LANES)
            rows = pl.ds(b * modes * sub + s, modes, stride=sub)
            out_ref[:, cols] = states[rows, :] * factor


def shards(queries, keys_in, values_in, decay_rates, residues, skip_gain, cotangent):
    seq, channels = queries.shape
    modes = decay_rates.shape[1]
    ctx = lax.axis_size("ctx")
    tp = lax.axis_size("tp")
    levels = ctx.bit_length() - 1
    groups = channels // LANES
    sub = math.gcd(groups, 8)
    blocks = groups // sub
    half = modes * groups // 2
    parts = seq // math.gcd(seq, STEP_ROWS)

    def swap(value, bit):
        return lax.ppermute(value, "ctx", [(i, i ^ (1 << bit)) for i in range(ctx)])

    def rows(*shape, dtype=F32):
        return jax.ShapeDtypeStruct((*shape, LANES), dtype)

    line_shape = jax.ShapeDtypeStruct((seq, channels), jnp.bfloat16)
    line_scratch = pltpu.VMEM((seq, channels), jnp.bfloat16)
    table_scratch = pltpu.VMEM((modes, channels), F32)
    elements = seq * channels * modes
    sources = (queries, keys_in, values_in, cotangent, decay_rates.T, residues.T)

    keep, send, q, k, v, ct, gated, pulled, row_rates, row_coefs = pl.pallas_call(
        states_kernel,
        in_specs=[HBM] * 6,
        out_specs=[VMEM] * 10,
        out_shape=[rows(3, half)] * 2
        + [line_shape] * 4
        + [rows(blocks, seq * sub)] * 2
        + [rows(2 * half)] * 2,
        scratch_shapes=[
            table_scratch,
            table_scratch,
            pltpu.VMEM((3, 2 * half, LANES), F32),
            pltpu.SemaphoreType.DMA((4 * parts + 2,)),
        ],
        compiler_params=KERNEL,
        cost_estimate=pl.CostEstimate(
            flops=6 * elements, bytes_accessed=8 * seq * channels, transcendentals=0
        ),
        name="chunk_states",
    )(*[pltpu.with_memory_space_constraint(item, pltpu.HBM) for item in sources])
    sibling = swap(send, 0)

    def wire(level):
        return rows(2 if level == levels - 1 else 3, half, dtype=WIRE)

    block, packed = pl.pallas_call(
        partial(pair_kernel, seq, levels == 2),
        out_shape=[rows(5, half), wire(1)],
        compiler_params=KERNEL,
        name="chip_states",
    )(keep, sibling, row_rates)
    for level in range(1, levels - 1):
        got = swap(packed, level)
        block, packed = pl.pallas_call(
            partial(level_kernel, seq, level, level + 1 == levels - 1),
            out_shape=[rows(5, half), wire(level + 1)],
            compiler_params=KERNEL,
            name="block_states",
        )(block, got, row_rates)
    got = swap(packed, levels - 1)
    mine, other = pl.pallas_call(
        partial(last_kernel, seq, levels - 1),
        out_shape=[rows(3 * half + 8)] * 2,
        compiler_params=KERNEL,
        name="carries",
    )(block, got, row_rates, keep, sibling)
    other = swap(other, 0)

    square = mine[3 * half :] + other[3 * half :]
    if tp <= 4:
        shares = [square] + [
            lax.ppermute(square, "tp", [(i, (i + hop) % tp) for i in range(tp)])
            for hop in range(1, tp)
        ]
    else:
        shares = [lax.psum(square, "tp")]

    operator_out, grad_queries, grad_keys, grad_values = pl.pallas_call(
        finish_kernel,
        in_specs=[VMEM] * 11,
        out_specs=[HBM] * 4,
        out_shape=[line_shape] * 4,
        scratch_shapes=[line_scratch] * 4
        + [
            pltpu.VMEM((blocks, seq * sub, LANES), F32),
            pltpu.VMEM((2 * half, LANES), F32),
            pltpu.SemaphoreType.DMA((4 * parts,)),
        ],
        compiler_params=KERNEL,
        cost_estimate=pl.CostEstimate(
            flops=8 * elements, bytes_accessed=16 * seq * channels, transcendentals=0
        ),
        name="finish",
    )(
        q,
        k,
        v,
        ct,
        gated,
        pulled,
        row_rates,
        row_coefs,
        skip_gain.reshape(1, channels),
        mine,
        other,
    )
    grad_residues = pl.pallas_call(
        partial(clip_kernel, math.sqrt(channels * tp * modes), blocks),
        out_shape=jax.ShapeDtypeStruct((modes, channels), F32),
        scratch_shapes=[pltpu.VMEM((2 * half, LANES), F32)],
        compiler_params=KERNEL,
        name="clip",
    )(mine, other, *shares)
    return (operator_out, grad_queries, grad_keys, grad_values, grad_residues.T)


def solution(mesh):
    lines, tables = P("ctx", "tp"), P("tp", None)
    in_specs = (lines, lines, lines, tables, tables, P("tp"), lines)
    out_specs = (lines, lines, lines, lines, tables)
    return jax.shard_map(shards, mesh=mesh, in_specs=in_specs, out_specs=out_specs, check_vma=False)
```

```python
from functools import partial
import math

import jax
import jax.numpy as jnp
from jax import lax
from jax.experimental import pallas as pl
from jax.experimental.pallas import tpu as pltpu
from jax.sharding import PartitionSpec as P

F32 = jnp.float32
WIRE = jnp.bfloat16
LANES = 128
UNROLL = 8
STEP_ROWS = 32
KERNEL = pltpu.CompilerParams(vmem_limit_bytes=24 * 1024 * 1024)
HBM = pl.BlockSpec(memory_space=pltpu.HBM)
VMEM = pl.BlockSpec(memory_space=pltpu.VMEM)


def reorder(rows, inner, transpose):
    outer = rows // inner
    to = lax.broadcasted_iota(jnp.int32, (rows, rows), 0)
    fro = lax.broadcasted_iota(jnp.int32, (rows, rows), 1)
    if transpose:
        to, fro = fro, to
    same = (to % outer == fro // inner) & (to // outer == fro % inner)
    return jnp.where(same, 1.0, 0.0).astype(jnp.bfloat16)


def tree_sum(items):
    items = list(items)
    while len(items) > 1:
        items = [
            items[i] + items[i + 1] if i + 1 < len(items) else items[i]
            for i in range(0, len(items), 2)
        ]
    return items[0]


def states_kernel(
    q_hbm,
    k_hbm,
    v_hbm,
    ct_hbm,
    rate_hbm,
    res_hbm,
    keep_ref,
    send_ref,
    q_ref,
    k_ref,
    v_ref,
    ct_ref,
    gated_ref,
    pulled_ref,
    rate_ref,
    coef_ref,
    rate_cols,
    res_cols,
    states,
    sems,
):
    seq, channels = q_ref.shape
    modes = rate_cols.shape[0]
    blocks = gated_ref.shape[0]
    sub = channels // (blocks * LANES)
    part = math.gcd(seq, STEP_ROWS)
    parts = seq // part
    tables = [
        pltpu.make_async_copy(rate_hbm, rate_cols, sems.at[4 * parts]),
        pltpu.make_async_copy(res_hbm, res_cols, sems.at[4 * parts + 1]),
    ]
    lines = []
    for i in range(parts):
        rows = pl.ds(i * part, part)
        pairs = ((k_hbm, k_ref), (v_hbm, v_ref), (ct_hbm, ct_ref), (q_hbm, q_ref))
        for j, (source, target) in enumerate(pairs):
            lines.append(
                pltpu.make_async_copy(source.at[rows], target.at[rows], sems.at[4 * i + j])
            )
    for copy in tables + lines:
        copy.start()
    for copy in tables:
        copy.wait()
    for b in range(blocks):
        for s in range(sub):
            cols = slice((b * sub + s) * LANES, (b * sub + s + 1) * LANES)
            rows = pl.ds(b * modes * sub + s, modes, stride=sub)
            rate_ref[rows, :] = rate_cols[:, cols]
            coef_ref[rows, :] = res_cols[:, cols]
    rate = rate_ref[...]
    coef_ref[...] = coef_ref[...] * jnp.sqrt(1.0 - jnp.exp(-2.0 * rate))
    to_scan = reorder(part * sub, part, False)

    def to_scan_order(left, right, i, target):
        rows = slice(i * part, (i + 1) * part)
        product = (left[rows, :].astype(F32) * right[rows, :].astype(F32)).astype(jnp.bfloat16)
        stacked = jnp.concatenate(
            [
                jnp.concatenate(
                    [
                        product[:, (b * sub + s) * LANES : (b * sub + s + 1) * LANES]
                        for s in range(sub)
                    ],
                    axis=0,
                )
                for b in range(blocks)
            ],
            axis=1,
        )
        ordered = jnp.dot(to_scan, stacked, preferred_element_type=F32)
        for b in range(blocks):
            target[b, i * part * sub : (i + 1) * part * sub, :] = ordered[
                :, b * LANES : (b + 1) * LANES
            ]

    mode_rows_of = partial(mode_rows, modes=modes, sub=sub)
    for i in range(parts):
        for copy in lines[4 * i : 4 * i + 4]:
            copy.wait()
        to_scan_order(k_ref, v_ref, i, gated_ref)
        to_scan_order(ct_ref, q_ref, i, pulled_ref)
        for b in range(blocks):
            decay = [jnp.exp(-rate_ref[r, :]) for r in mode_rows_of(b)]

            def forward(j, carry):
                held, inner = list(carry[0]), list(carry[1])
                for u in range(UNROLL):
                    at = pl.ds(pl.multiple_of((i * part + j * UNROLL + u) * sub, sub), sub)
                    x = gated_ref[b, at, :]
                    p = pulled_ref[b, at, :]
                    for n in range(modes):
                        held[n] = decay[n] * held[n] + x
                        inner[n] = inner[n] + p * held[n]
                return tuple(held), tuple(inner)

            if i == 0:
                first = tuple(jnp.zeros((sub, LANES), F32) for _ in range(modes))
                carry = (first, first)
            else:
                carry = tuple(tuple(states[kind, r, :] for r in mode_rows_of(b)) for kind in (0, 2))
            ends, inner = lax.fori_loop(0, part // UNROLL, forward, carry)
            for n, r in enumerate(mode_rows_of(b)):
                states[0, r, :] = ends[n]
                states[2, r, :] = inner[n]

    for b in range(blocks):
        decay = [jnp.exp(-rate_ref[r, :]) for r in mode_rows_of(b)]

        def backward(j, carry):
            held = list(carry)
            for u in range(UNROLL):
                at = pl.ds(pl.multiple_of((seq - 1 - (j * UNROLL + u)) * sub, sub), sub)
                p = pulled_ref[b, at, :]
                for n in range(modes):
                    held[n] = decay[n] * held[n] + p
            return tuple(held)

        first = tuple(jnp.zeros((sub, LANES), F32) for _ in range(modes))
        starts = lax.fori_loop(0, seq // UNROLL, backward, first)
        for n, r in enumerate(mode_rows_of(b)):
            states[1, r, :] = starts[n]

    half = keep_ref.shape[1]
    core = lax.axis_index("ctx") % 2
    keep_ref[...] = states[:, pl.ds(pl.multiple_of(core * half, half), half), :]
    send_ref[...] = states[:, pl.ds(pl.multiple_of((1 - core) * half, half), half), :]


def own_rows(rate_ref, half):
    core = lax.axis_index("ctx") % 2
    return rate_ref[pl.ds(pl.multiple_of(core * half, half), half), :]


def joined(is_right, mine, other, span, step):
    left = [jnp.where(is_right, o, m) for m, o in zip(mine, other)]
    right = [jnp.where(is_right, m, o) for m, o in zip(mine, other)]
    return (
        span * left[0] + right[0],
        left[1] + span * right[1],
        left[2] + right[2] + step * right[1] * left[0],
    )


def put_wire(wire_ref, is_last, next_right, block):
    if is_last:
        wire_ref[0] = jnp.where(next_right, block[1], block[0]).astype(wire_ref.dtype)
        wire_ref[1] = block[2].astype(wire_ref.dtype)
    else:
        for kind in range(3):
            wire_ref[kind] = block[kind].astype(wire_ref.dtype)


def pair_kernel(seq, is_last, keep_ref, got_ref, rate_ref, after_ref, block_ref, wire_ref):
    rate = own_rows(rate_ref, keep_ref.shape[1])
    place = lax.axis_index("ctx")
    block = joined(
        place % 2 == 1,
        [keep_ref[i] for i in range(3)],
        [got_ref[i] for i in range(3)],
        jnp.exp(-rate * seq),
        jnp.exp(-rate),
    )
    for kind in range(3):
        block_ref[kind] = block[kind]
    block_ref[3] = jnp.zeros_like(rate)
    block_ref[4] = jnp.zeros_like(rate)
    put_wire(wire_ref, is_last, (place // 2) % 2 == 1, block)


def carries_with(block_ref, end_state, start_state, level, seq, rate):
    place = lax.axis_index("ctx")
    is_right = (place >> level) % 2 == 1
    chips = 1 << (level - 1)
    at = (place // 2) % chips
    before = at * (2 * seq)
    behind = (chips - 1 - at) * (2 * seq)
    ahead = block_ref[3] + jnp.where(
        is_right, jnp.exp(-rate * before.astype(F32)) * end_state, 0.0
    )
    after = block_ref[4] + jnp.where(
        is_right, 0.0, jnp.exp(-rate * behind.astype(F32)) * start_state
    )
    return is_right, ahead, after


def level_kernel(
    seq, level, is_last, block_ref, got_ref, rate_ref, after_ref, out_ref, wire_ref
):
    rate = own_rows(rate_ref, block_ref.shape[1])
    got = [got_ref[i].astype(F32) for i in range(3)]
    is_right, ahead, after = carries_with(block_ref, got[0], got[1], level, seq, rate)
    block = joined(
        is_right,
        [block_ref[i] for i in range(3)],
        got,
        jnp.exp(-rate * (seq << level)),
        jnp.exp(-rate),
    )
    for kind in range(3):
        out_ref[kind] = block[kind]
    out_ref[3] = ahead
    out_ref[4] = after
    next_right = (lax.axis_index("ctx") >> (level + 1)) % 2 == 1
    put_wire(wire_ref, is_last, next_right, block)


def last_kernel(
    seq,
    level,
    block_ref,
    got_ref,
    rate_ref,
    keep_ref,
    sibling_ref,
    after_ref,
    mine_ref,
    other_ref,
):
    half = block_ref.shape[1]
    rate = own_rows(rate_ref, half)
    edge, inner = got_ref[0].astype(F32), got_ref[1].astype(F32)
    is_right, ahead, after = carries_with(block_ref, edge, edge, level, seq, rate)
    own_edge = jnp.where(is_right, block_ref[1], block_ref[0])
    total = block_ref[2] + inner + jnp.exp(-rate) * own_edge * edge
    raw = jnp.sqrt(1.0 - jnp.exp(-2.0 * rate)) * total
    core = lax.axis_index("ctx") % 2
    first = core == 0
    span = jnp.exp(-rate * seq)
    end_first = jnp.where(first, keep_ref[0], sibling_ref[0])
    start_second = jnp.where(first, sibling_ref[1], keep_ref[1])
    ahead_second = span * ahead + end_first
    after_first = span * after + start_second
    mine_ref[0:half, :] = jnp.where(first, ahead, ahead_second)
    mine_ref[half : 2 * half, :] = jnp.where(first, after_first, after)
    other_ref[0:half, :] = jnp.where(first, ahead_second, ahead)
    other_ref[half : 2 * half, :] = jnp.where(first, after, after_first)
    squares = raw * raw
    share = tree_sum([squares[i : i + 8, :] for i in range(0, half, 8)])
    for ref in (mine_ref, other_ref):
        ref[2 * half : 3 * half, :] = raw
        ref[3 * half : 3 * half + 8, :] = share


def place_halves(mine_ref, other_ref, first, target):
    half = target.shape[0] // 2
    core = lax.axis_index("ctx") % 2
    for ref, at in ((mine_ref, core), (other_ref, 1 - core)):
        rows = pl.ds(pl.multiple_of(at * half, half), half)
        target[rows, :] = ref[first : first + half, :]


def mode_rows(block, modes, sub):
    return [slice((block * modes + n) * sub, (block * modes + n + 1) * sub) for n in range(modes)]


def local_kernel(reverse, which, modes, lines_ref, rate_ref, coef_ref, after_ref, *out_refs):
    sub = rate_ref.shape[0] // (lines_ref.shape[0] * modes)
    seq = lines_ref.shape[1] // sub
    for b, out_ref in zip(which, out_refs):
        rows = mode_rows(b, modes, sub)
        decay = [jnp.exp(-rate_ref[r, :]) for r in rows]
        coef = [coef_ref[r, :] for r in rows]

        def body(j, carry):
            held = list(carry)
            for u in range(UNROLL):
                t = j * UNROLL + u
                if reverse:
                    t = seq - 1 - t
                at = pl.ds(pl.multiple_of(t * sub, sub), sub)
                x = lines_ref[b, at, :]
                total = [None] * 4
                for n in range(modes):
                    held[n] = decay[n] * held[n] + x
                    term = coef[n] * held[n]
                    total[n % 4] = term if n < 4 else total[n % 4] + term
                out_ref[at, :] = tree_sum(total)
            return tuple(held)

        first = tuple(jnp.zeros((sub, LANES), F32) for _ in range(modes))
        lax.fori_loop(0, seq // UNROLL, body, first)


def add_carries(reverse, modes, rate_ref, coef_ref, states, local_refs, target):
    sub = rate_ref.shape[0] // (len(local_refs) * modes)
    seq = local_refs[0].shape[0] // sub
    for b, local_ref in enumerate(local_refs):
        rows = mode_rows(b, modes, sub)
        decay = [jnp.exp(-rate_ref[r, :]) for r in rows]
        first = tuple(coef_ref[r, :] * states[r, :] for r in rows)

        def body(j, carry):
            held = list(carry)
            for u in range(UNROLL):
                t = j * UNROLL + u
                if reverse:
                    t = seq - 1 - t
                at = pl.ds(pl.multiple_of(t * sub, sub), sub)
                total = [local_ref[at, :], None, None, None]
                for n in range(modes):
                    held[n] = decay[n] * held[n]
                    total[n % 4] = held[n] if total[n % 4] is None else total[n % 4] + held[n]
                target[b, at, :] = tree_sum(total)
            return tuple(held)

        lax.fori_loop(0, seq // UNROLL, body, first)


def line_outputs(left, right, scales, skip_ref, scanned, targets, done_with):
    seq, channels = left.shape
    blocks = scanned.shape[0]
    sub = channels // (blocks * LANES)
    part = math.gcd(seq, STEP_ROWS)
    from_scan = reorder(part * sub, part, True)
    for i in range(seq // part):
        rows = slice(i * part, (i + 1) * part)
        stacked = jnp.concatenate(
            [scanned[b, i * part * sub : (i + 1) * part * sub, :] for b in range(blocks)], axis=1
        ).astype(jnp.bfloat16)
        ordered = jnp.dot(from_scan, stacked, preferred_element_type=F32)
        for b in range(blocks):
            for s in range(sub):
                cols = slice((b * sub + s) * LANES, (b * sub + s + 1) * LANES)
                own = ordered[s * part : (s + 1) * part, b * LANES : (b + 1) * LANES]
                line = left[rows, cols].astype(F32) * right[rows, cols].astype(F32)
                mixed = own + skip_ref[:, cols] * line.astype(jnp.bfloat16).astype(F32)
                for scale, target in zip(scales, targets):
                    target[rows, cols] = (scale[rows, cols].astype(F32) * mixed).astype(
                        jnp.bfloat16
                    )
        done_with(i, pl.ds(i * part, part))


def forward_kernel(modes, blocks, *refs):
    q_ref, k_ref, v_ref, ct_ref, rate_ref, coef_ref, skip_ref, mine_ref, other_ref, _ = refs[:10]
    local_refs = refs[10 : 10 + blocks]
    out_ref, gq_ref, token_ref, scanned, states = refs[10 + blocks :]
    token_ref[...] = jnp.zeros_like(token_ref)
    place_halves(mine_ref, other_ref, 0, states)
    add_carries(False, modes, rate_ref, coef_ref, states, local_refs, scanned)
    line_outputs(
        k_ref,
        v_ref,
        (q_ref, ct_ref),
        skip_ref,
        scanned,
        (out_ref, gq_ref),
        lambda i, at: None,
    )


def adjoint_kernel(modes, blocks, *refs):
    rate_ref, coef_ref, mine_ref, other_ref, _ = refs[:5]
    local_refs = refs[5 : 5 + blocks]
    scanned, states = refs[5 + blocks :]
    place_halves(mine_ref, other_ref, states.shape[0] // 2, states)
    add_carries(True, modes, rate_ref, coef_ref, states, local_refs, scanned)


def backward_kernel(
    q_ref,
    k_ref,
    v_ref,
    ct_ref,
    scanned,
    skip_ref,
    out_rows,
    gq_rows,
    raw_cols,
    out_hbm,
    gq_hbm,
    raw_hbm,
    gk_hbm,
    gv_hbm,
    gk_rows,
    gv_rows,
    sems,
):
    copies = []

    def start(source, target):
        copy = pltpu.make_async_copy(source, target, sems.at[len(copies)])
        copy.start()
        copies.append(copy)

    def send(i, at):
        for source, target in ((gk_rows, gk_hbm), (gv_rows, gv_hbm)):
            start(source.at[at], target.at[at])

    for source, target in ((out_rows, out_hbm), (gq_rows, gq_hbm), (raw_cols, raw_hbm)):
        start(source, target)
    line_outputs(ct_ref, q_ref, (v_ref, k_ref), skip_ref, scanned, (gk_rows, gv_rows), send)
    for copy in copies:
        copy.wait()


def add_kernel(left_ref, right_ref, after_ref, out_ref):
    out_ref[...] = left_ref[...] + right_ref[...]


def clip_kernel(limit, blocks, mine_ref, other_ref, *refs):
    share_refs, (out_ref, states) = refs[1:-2], refs[-2:]
    modes = out_ref.shape[0]
    sub = out_ref.shape[1] // (blocks * LANES)
    half = states.shape[0] // 2
    place_halves(mine_ref, other_ref, 2 * half, states)
    square = jnp.sum(tree_sum([ref[...] for ref in share_refs]))
    factor = jnp.minimum(1.0, limit * lax.rsqrt(jnp.full((1, LANES), square + 1e-06, F32)))
    for b in range(blocks):
        for s in range(sub):
            cols = slice((b * sub + s) * LANES, (b * sub + s + 1) * LANES)
            rows = pl.ds(b * modes * sub + s, modes, stride=sub)
            out_ref[:, cols] = states[rows, :] * factor


def shards(queries, keys_in, values_in, decay_rates, residues, skip_gain, cotangent):
    seq, channels = queries.shape
    modes = decay_rates.shape[1]
    ctx = lax.axis_size("ctx")
    tp = lax.axis_size("tp")
    levels = ctx.bit_length() - 1
    groups = channels // LANES
    sub = math.gcd(groups, 8)
    blocks = groups // sub
    half = modes * groups // 2
    parts = seq // math.gcd(seq, STEP_ROWS)

    def swap(value, bit):
        return lax.ppermute(value, "ctx", [(i, i ^ (1 << bit)) for i in range(ctx)])

    def rows(*shape, dtype=F32):
        return jax.ShapeDtypeStruct((*shape, LANES), dtype)

    line_shape = jax.ShapeDtypeStruct((seq, channels), jnp.bfloat16)
    table_shape = jax.ShapeDtypeStruct((modes, channels), F32)
    line_scratch = pltpu.VMEM((seq, channels), jnp.bfloat16)
    table_scratch = pltpu.VMEM((modes, channels), F32)
    elements = seq * channels * modes
    sources = (queries, keys_in, values_in, cotangent, decay_rates.T, residues.T)

    keep, send, q, k, v, ct, gated, pulled, row_rates, row_coefs = pl.pallas_call(
        states_kernel,
        in_specs=[HBM] * 6,
        out_specs=[VMEM] * 10,
        out_shape=[rows(3, half)] * 2
        + [line_shape] * 4
        + [rows(blocks, seq * sub)] * 2
        + [rows(2 * half)] * 2,
        scratch_shapes=[
            table_scratch,
            table_scratch,
            pltpu.VMEM((3, 2 * half, LANES), F32),
            pltpu.SemaphoreType.DMA((4 * parts + 2,)),
        ],
        compiler_params=KERNEL,
        cost_estimate=pl.CostEstimate(
            flops=6 * elements, bytes_accessed=8 * seq * channels, transcendentals=0
        ),
        name="chunk_states",
    )(*[pltpu.with_memory_space_constraint(item, pltpu.HBM) for item in sources])
    sibling = swap(send, 0)

    def wire(level):
        return rows(2 if level == levels - 1 else 3, half, dtype=WIRE)

    whole = rows(blocks, seq * sub)
    whole_scratch = pltpu.VMEM((blocks, seq * sub, LANES), F32)
    states_scratch = pltpu.VMEM((2 * half, LANES), F32)
    every = tuple(range(blocks))

    def local(reverse, which, after, name):
        lines = pulled if reverse else gated
        return pl.pallas_call(
            partial(local_kernel, reverse, which, modes),
            out_shape=[rows(seq * sub)] * len(which),
            compiler_params=KERNEL,
            cost_estimate=pl.CostEstimate(
                flops=4 * elements, bytes_accessed=8 * seq * channels, transcendentals=0
            ),
            name=name,
        )(lines, row_rates, row_coefs, after[:8])

    block, packed = pl.pallas_call(
        partial(pair_kernel, seq, levels == 2),
        out_shape=[rows(5, half), wire(1)],
        compiler_params=KERNEL,
        name="chip_states",
    )(keep, sibling, row_rates, row_rates[:8])
    got = swap(packed, 1)
    conv = local(False, every, block[4], "local_conv")
    for level in range(1, levels - 1):
        block, packed = pl.pallas_call(
            partial(level_kernel, seq, level, level + 1 == levels - 1),
            out_shape=[rows(5, half), wire(level + 1)],
            compiler_params=KERNEL,
            name="block_states",
        )(block, got, row_rates, conv[0])
        got = swap(packed, level + 1)
    early = every[: (blocks + 1) // 2]
    adj = local(True, early, block[4], "local_adjoint")
    mine, other = pl.pallas_call(
        partial(last_kernel, seq, levels - 1),
        out_shape=[rows(3 * half + 8)] * 2,
        compiler_params=KERNEL,
        name="carries",
    )(block, got, row_rates, keep, sibling, adj[0])
    other = swap(other, 0)
    after = mine
    if len(early) < blocks:
        adj += local(True, every[len(early) :], mine, "late_adjoint")
        after = adj[-1]

    def plus(left, right, after):
        return pl.pallas_call(
            add_kernel,
            in_specs=[VMEM] * 3,
            out_shape=rows(8),
            compiler_params=KERNEL,
            name="square_sum",
        )(left, right, after)

    def tp_swap(value, bit):
        return lax.ppermute(value, "tp", [(i, i ^ (1 << bit)) for i in range(tp)])

    square = plus(mine[3 * half :], other[3 * half :], after)
    bits = tp.bit_length() - 1
    share = tp_swap(square, 0) if bits else jnp.zeros_like(square)
    skip = skip_gain.reshape(1, channels)
    forward_out, forward_grad, after = pl.pallas_call(
        partial(forward_kernel, modes, blocks),
        out_shape=[line_shape] * 2 + [rows(8)],
        scratch_shapes=[whole_scratch, states_scratch],
        compiler_params=KERNEL,
        cost_estimate=pl.CostEstimate(
            flops=2 * elements, bytes_accessed=16 * seq * channels, transcendentals=0
        ),
        name="forward_outputs",
    )(q, k, v, ct, row_rates, row_coefs, skip, mine, other, square, *conv)
    for bit in range(1, bits):
        square = plus(square, share, after)
        share = tp_swap(square, bit)
        after = square
    scanned = pl.pallas_call(
        partial(adjoint_kernel, modes, blocks),
        out_shape=whole,
        scratch_shapes=[states_scratch],
        compiler_params=KERNEL,
        cost_estimate=pl.CostEstimate(
            flops=2 * elements, bytes_accessed=8 * seq * channels, transcendentals=0
        ),
        name="adjoint_carries",
    )(row_rates, row_coefs, mine, other, after, *adj)
    clipped = pl.pallas_call(
        partial(clip_kernel, math.sqrt(channels * tp * modes), blocks),
        out_shape=table_shape,
        scratch_shapes=[states_scratch],
        compiler_params=KERNEL,
        name="clip",
    )(mine, other, scanned, square, share)
    operator_out, grad_queries, grad_residues, grad_keys, grad_values = pl.pallas_call(
        backward_kernel,
        in_specs=[VMEM] * 9,
        out_specs=[HBM] * 5,
        out_shape=[line_shape] * 2 + [table_shape] + [line_shape] * 2,
        scratch_shapes=[line_scratch] * 2 + [pltpu.SemaphoreType.DMA((2 * parts + 3,))],
        compiler_params=KERNEL,
        cost_estimate=pl.CostEstimate(
            flops=elements, bytes_accessed=8 * seq * channels, transcendentals=0
        ),
        name="backward_outputs",
    )(q, k, v, ct, scanned, skip, forward_out, forward_grad, clipped)
    return (operator_out, grad_queries, grad_keys, grad_values, grad_residues.T)


def solution(mesh):
    lines, tables = P("ctx", "tp"), P("tp", None)
    in_specs = (lines, lines, lines, tables, tables, P("tp"), lines)
    out_specs = (lines, lines, lines, lines, tables)
    return jax.shard_map(shards, mesh=mesh, in_specs=in_specs, out_specs=out_specs, check_vma=False)
```

```python
from functools import partial
import math

import jax
import jax.numpy as jnp
from jax import lax
from jax.experimental import pallas as pl
from jax.experimental.pallas import tpu as pltpu
from jax.sharding import PartitionSpec as P

F32 = jnp.float32
WIRE = jnp.bfloat16
LANES = 128
UNROLL = 8
STEP_ROWS = 32
KERNEL = pltpu.CompilerParams(vmem_limit_bytes=24 * 1024 * 1024)
HBM = pl.BlockSpec(memory_space=pltpu.HBM)
VMEM = pl.BlockSpec(memory_space=pltpu.VMEM)


def reorder(rows, inner, transpose):
    outer = rows // inner
    to = lax.broadcasted_iota(jnp.int32, (rows, rows), 0)
    fro = lax.broadcasted_iota(jnp.int32, (rows, rows), 1)
    if transpose:
        to, fro = fro, to
    same = (to % outer == fro // inner) & (to // outer == fro % inner)
    return jnp.where(same, 1.0, 0.0).astype(jnp.bfloat16)


def tree_sum(items):
    items = list(items)
    while len(items) > 1:
        items = [
            items[i] + items[i + 1] if i + 1 < len(items) else items[i]
            for i in range(0, len(items), 2)
        ]
    return items[0]


def half_units(which, blocks, modes, sub):
    if blocks == 1:
        return [(0, which * (modes // 2 * sub), modes // 2)]
    count = blocks // 2
    return [
        (which * count + j, (which * count + j) * (modes * sub), modes) for j in range(count)
    ]


def to_scan_order(to_scan, left, right, part, i, block, target):
    size, sub = to_scan.shape[0], to_scan.shape[0] // part
    rows = slice(i * part, (i + 1) * part)
    stacked = []
    for s in range(sub):
        cols = pl.ds(pl.multiple_of((block * sub + s) * LANES, LANES), LANES)
        product = left[rows, cols].astype(F32) * right[rows, cols].astype(F32)
        stacked.append(product.astype(jnp.bfloat16))
    target[block, i * size : (i + 1) * size, :] = jnp.dot(
        to_scan, jnp.concatenate(stacked, axis=0), preferred_element_type=F32
    )


def scan_states(unit, sub, part, gated_ref, pulled_ref, rate_ref, before_part, out_ref, at_row):
    block, base, modes = unit
    seq = gated_ref.shape[1] // sub
    decay = [
        jnp.exp(-rate_ref[pl.ds(pl.multiple_of(base + n * sub, sub), sub), :])
        for n in range(modes)
    ]
    first = tuple(jnp.zeros((sub, LANES), F32) for _ in range(modes))
    carry = (first, first)
    for i in range(seq // part):
        before_part(i)

        def forward(j, carry):
            held, inner = list(carry[0]), list(carry[1])
            for u in range(UNROLL):
                at = pl.ds(pl.multiple_of((i * part + j * UNROLL + u) * sub, sub), sub)
                x = gated_ref[block, at, :]
                p = pulled_ref[block, at, :]
                for n in range(modes):
                    held[n] = decay[n] * held[n] + x
                    inner[n] = inner[n] + p * held[n]
            return tuple(held), tuple(inner)

        carry = lax.fori_loop(0, part // UNROLL, forward, carry)

    def backward(j, carry):
        held = list(carry)
        for u in range(UNROLL):
            at = pl.ds(pl.multiple_of((seq - 1 - (j * UNROLL + u)) * sub, sub), sub)
            p = pulled_ref[block, at, :]
            for n in range(modes):
                held[n] = decay[n] * held[n] + p
        return tuple(held)

    for n in range(modes):
        rows = slice(at_row + n * sub, at_row + (n + 1) * sub)
        out_ref[0, rows, :] = carry[0][n]
        out_ref[2, rows, :] = carry[1][n]
    starts = lax.fori_loop(0, seq // UNROLL, backward, first)
    for n in range(modes):
        out_ref[1, at_row + n * sub : at_row + (n + 1) * sub, :] = starts[n]


def send_kernel(
    q_hbm,
    k_hbm,
    v_hbm,
    ct_hbm,
    rate_hbm,
    res_hbm,
    send_ref,
    q_ref,
    k_ref,
    v_ref,
    ct_ref,
    gated_ref,
    pulled_ref,
    rate_ref,
    coef_ref,
    rate_cols,
    res_cols,
    sems,
):
    seq, channels = q_ref.shape
    modes = rate_cols.shape[0]
    blocks = gated_ref.shape[0]
    sub = channels // (blocks * LANES)
    part = math.gcd(seq, STEP_ROWS)
    parts = seq // part
    which = 1 - lax.axis_index("ctx") % 2
    pairs = ((k_hbm, k_ref), (v_hbm, v_ref), (ct_hbm, ct_ref), (q_hbm, q_ref))
    copies = []

    def start(source, target):
        copy = pltpu.make_async_copy(source, target, sems.at[len(copies)])
        copy.start()
        copies.append(copy)

    start(rate_hbm, rate_cols)
    width = channels // min(blocks, 2)
    cols = pl.ds(pl.multiple_of(which * width, LANES) if blocks > 1 else 0, width)
    for i in range(parts):
        rows = pl.ds(i * part, part)
        for source, target in pairs:
            start(source.at[rows, cols], target.at[rows, cols])
    start(res_hbm, res_cols)
    if blocks > 1:
        cols = pl.ds(pl.multiple_of((1 - which) * width, LANES), width)
        for source, target in pairs:
            start(source.at[:, cols], target.at[:, cols])

    def spread(source, target):
        for b in range(blocks):
            for s in range(sub):
                cols = slice((b * sub + s) * LANES, (b * sub + s + 1) * LANES)
                target[pl.ds(b * modes * sub + s, modes, stride=sub), :] = source[:, cols]

    to_scan = reorder(part * sub, part, False)
    copies[0].wait()
    spread(rate_cols, rate_ref)
    units = half_units(which, blocks, modes, sub)
    for at, unit in enumerate(units):

        def before_part(i):
            if at == 0:
                for copy in copies[1 + 4 * i : 5 + 4 * i]:
                    copy.wait()
            to_scan_order(to_scan, k_ref, v_ref, part, i, unit[0], gated_ref)
            to_scan_order(to_scan, ct_ref, q_ref, part, i, unit[0], pulled_ref)

        at_row = at * unit[2] * sub
        scan_states(
            unit, sub, part, gated_ref, pulled_ref, rate_ref, before_part, send_ref, at_row
        )
    for copy in copies[1 + 4 * parts :]:
        copy.wait()
    spread(res_cols, coef_ref)
    coef_ref[...] = coef_ref[...] * jnp.sqrt(1.0 - jnp.exp(-2.0 * rate_ref[...]))


def keep_kernel(
    q_ref,
    k_ref,
    v_ref,
    ct_ref,
    rate_ref,
    gated_in,
    pulled_in,
    keep_ref,
    gated_ref,
    pulled_ref,
    sems,
):
    seq, channels = q_ref.shape
    blocks = gated_ref.shape[0]
    sub = channels // (blocks * LANES)
    modes = rate_ref.shape[0] // (blocks * sub)
    part = math.gcd(seq, STEP_ROWS)
    to_scan = reorder(part * sub, part, False)
    which = lax.axis_index("ctx") % 2
    count = max(blocks // 2, 1)
    done = pl.ds((1 - which) * count if blocks > 1 else 0, count)
    copies = [
        pltpu.make_async_copy(gated_in.at[done], gated_ref.at[done], sems.at[0]),
        pltpu.make_async_copy(pulled_in.at[done], pulled_ref.at[done], sems.at[1]),
    ]
    for copy in copies:
        copy.start()
    lines = (gated_ref, pulled_ref) if blocks > 1 else (gated_in, pulled_in)
    units = half_units(which, blocks, modes, sub)
    for at, unit in enumerate(units):

        def before_part(i):
            if blocks > 1:
                to_scan_order(to_scan, k_ref, v_ref, part, i, unit[0], gated_ref)
                to_scan_order(to_scan, ct_ref, q_ref, part, i, unit[0], pulled_ref)

        at_row = at * unit[2] * sub
        scan_states(unit, sub, part, *lines, rate_ref, before_part, keep_ref, at_row)
    for copy in copies:
        copy.wait()


def own_rows(rate_ref, half):
    core = lax.axis_index("ctx") % 2
    return rate_ref[pl.ds(pl.multiple_of(core * half, half), half), :]


def joined(is_right, mine, other, span, step):
    left = [jnp.where(is_right, o, m) for m, o in zip(mine, other)]
    right = [jnp.where(is_right, m, o) for m, o in zip(mine, other)]
    return (
        span * left[0] + right[0],
        left[1] + span * right[1],
        left[2] + right[2] + step * right[1] * left[0],
    )


def put_wire(wire_ref, is_last, next_right, block):
    if is_last:
        wire_ref[0] = jnp.where(next_right, block[1], block[0]).astype(wire_ref.dtype)
        wire_ref[1] = block[2].astype(wire_ref.dtype)
    else:
        for kind in range(3):
            wire_ref[kind] = block[kind].astype(wire_ref.dtype)


def pair_kernel(seq, is_last, keep_ref, got_ref, rate_ref, after_ref, block_ref, wire_ref):
    rate = own_rows(rate_ref, keep_ref.shape[1])
    place = lax.axis_index("ctx")
    block = joined(
        place % 2 == 1,
        [keep_ref[i] for i in range(3)],
        [got_ref[i] for i in range(3)],
        jnp.exp(-rate * seq),
        jnp.exp(-rate),
    )
    for kind in range(3):
        block_ref[kind] = block[kind]
    block_ref[3] = jnp.zeros_like(rate)
    block_ref[4] = jnp.zeros_like(rate)
    put_wire(wire_ref, is_last, (place // 2) % 2 == 1, block)


def carries_with(block_ref, end_state, start_state, level, seq, rate):
    place = lax.axis_index("ctx")
    is_right = (place >> level) % 2 == 1
    chips = 1 << (level - 1)
    at = (place // 2) % chips
    before = at * (2 * seq)
    behind = (chips - 1 - at) * (2 * seq)
    ahead = block_ref[3] + jnp.where(
        is_right, jnp.exp(-rate * before.astype(F32)) * end_state, 0.0
    )
    after = block_ref[4] + jnp.where(
        is_right, 0.0, jnp.exp(-rate * behind.astype(F32)) * start_state
    )
    return is_right, ahead, after


def level_kernel(
    seq, level, is_last, block_ref, got_ref, rate_ref, after_ref, out_ref, wire_ref
):
    rate = own_rows(rate_ref, block_ref.shape[1])
    got = [got_ref[i].astype(F32) for i in range(3)]
    is_right, ahead, after = carries_with(block_ref, got[0], got[1], level, seq, rate)
    block = joined(
        is_right,
        [block_ref[i] for i in range(3)],
        got,
        jnp.exp(-rate * (seq << level)),
        jnp.exp(-rate),
    )
    for kind in range(3):
        out_ref[kind] = block[kind]
    out_ref[3] = ahead
    out_ref[4] = after
    next_right = (lax.axis_index("ctx") >> (level + 1)) % 2 == 1
    put_wire(wire_ref, is_last, next_right, block)


def last_kernel(
    seq,
    level,
    block_ref,
    got_ref,
    rate_ref,
    keep_ref,
    sibling_ref,
    after_ref,
    mine_ref,
    other_ref,
):
    half = block_ref.shape[1]
    rate = own_rows(rate_ref, half)
    edge, inner = got_ref[0].astype(F32), got_ref[1].astype(F32)
    is_right, ahead, after = carries_with(block_ref, edge, edge, level, seq, rate)
    own_edge = jnp.where(is_right, block_ref[1], block_ref[0])
    total = block_ref[2] + inner + jnp.exp(-rate) * own_edge * edge
    raw = jnp.sqrt(1.0 - jnp.exp(-2.0 * rate)) * total
    core = lax.axis_index("ctx") % 2
    first = core == 0
    span = jnp.exp(-rate * seq)
    end_first = jnp.where(first, keep_ref[0], sibling_ref[0])
    start_second = jnp.where(first, sibling_ref[1], keep_ref[1])
    ahead_second = span * ahead + end_first
    after_first = span * after + start_second
    mine_ref[0:half, :] = jnp.where(first, ahead, ahead_second)
    mine_ref[half : 2 * half, :] = jnp.where(first, after_first, after)
    other_ref[0:half, :] = jnp.where(first, ahead_second, ahead)
    other_ref[half : 2 * half, :] = jnp.where(first, after, after_first)
    squares = raw * raw
    share = tree_sum([squares[i : i + 8, :] for i in range(0, half, 8)])
    for ref in (mine_ref, other_ref):
        ref[2 * half : 3 * half, :] = raw
        ref[3 * half : 3 * half + 8, :] = share


def place_halves(mine_ref, other_ref, first, target):
    half = target.shape[0] // 2
    core = lax.axis_index("ctx") % 2
    for ref, at in ((mine_ref, core), (other_ref, 1 - core)):
        rows = pl.ds(pl.multiple_of(at * half, half), half)
        target[rows, :] = ref[first : first + half, :]


def mode_rows(block, modes, sub):
    return [slice((block * modes + n) * sub, (block * modes + n + 1) * sub) for n in range(modes)]


def local_kernel(reverse, which, modes, lines_ref, rate_ref, coef_ref, after_ref, *out_refs):
    sub = rate_ref.shape[0] // (lines_ref.shape[0] * modes)
    seq = lines_ref.shape[1] // sub
    for b, out_ref in zip(which, out_refs):
        rows = mode_rows(b, modes, sub)
        decay = [jnp.exp(-rate_ref[r, :]) for r in rows]
        coef = [coef_ref[r, :] for r in rows]

        def body(j, carry):
            held = list(carry)
            for u in range(UNROLL):
                t = j * UNROLL + u
                if reverse:
                    t = seq - 1 - t
                at = pl.ds(pl.multiple_of(t * sub, sub), sub)
                x = lines_ref[b, at, :]
                total = [None] * 4
                for n in range(modes):
                    held[n] = decay[n] * held[n] + x
                    term = coef[n] * held[n]
                    total[n % 4] = term if n < 4 else total[n % 4] + term
                out_ref[at, :] = tree_sum(total)
            return tuple(held)

        first = tuple(jnp.zeros((sub, LANES), F32) for _ in range(modes))
        lax.fori_loop(0, seq // UNROLL, body, first)


def add_carries(reverse, modes, rate_ref, coef_ref, states, local_refs, target):
    sub = rate_ref.shape[0] // (len(local_refs) * modes)
    seq = local_refs[0].shape[0] // sub
    for b, local_ref in enumerate(local_refs):
        rows = mode_rows(b, modes, sub)
        decay = [jnp.exp(-rate_ref[r, :]) for r in rows]
        first = tuple(coef_ref[r, :] * states[r, :] for r in rows)

        def body(j, carry):
            held = list(carry)
            for u in range(UNROLL):
                t = j * UNROLL + u
                if reverse:
                    t = seq - 1 - t
                at = pl.ds(pl.multiple_of(t * sub, sub), sub)
                total = [local_ref[at, :], None, None, None]
                for n in range(modes):
                    held[n] = decay[n] * held[n]
                    total[n % 4] = held[n] if total[n % 4] is None else total[n % 4] + held[n]
                target[b, at, :] = tree_sum(total)
            return tuple(held)

        lax.fori_loop(0, seq // UNROLL, body, first)


def line_outputs(left, right, scales, skip_ref, scanned, targets, which, done_with=None):
    seq, channels = left.shape
    blocks = scanned.shape[0]
    sub = channels // (blocks * LANES)
    part = math.gcd(seq, STEP_ROWS)
    from_scan = reorder(part * sub, part, True)
    for i in which:
        rows = slice(i * part, (i + 1) * part)
        to_rows = slice((i - which[0]) * part, (i - which[0] + 1) * part)
        stacked = jnp.concatenate(
            [scanned[b, i * part * sub : (i + 1) * part * sub, :] for b in range(blocks)], axis=1
        ).astype(jnp.bfloat16)
        ordered = jnp.dot(from_scan, stacked, preferred_element_type=F32)
        for b in range(blocks):
            for s in range(sub):
                cols = slice((b * sub + s) * LANES, (b * sub + s + 1) * LANES)
                own = ordered[s * part : (s + 1) * part, b * LANES : (b + 1) * LANES]
                line = left[rows, cols].astype(F32) * right[rows, cols].astype(F32)
                mixed = own + skip_ref[:, cols] * line.astype(jnp.bfloat16).astype(F32)
                for scale, target in zip(scales, targets):
                    target[to_rows, cols] = (scale[rows, cols].astype(F32) * mixed).astype(
                        jnp.bfloat16
                    )
        if done_with is not None:
            done_with(pl.ds((i - which[0]) * part, part), pl.ds(i * part, part))


def forward_kernel(modes, blocks, *refs):
    q_ref, k_ref, v_ref, ct_ref, rate_ref, coef_ref, skip_ref, mine_ref, other_ref, _ = refs[:10]
    local_refs = refs[10 : 10 + blocks]
    out_ref, gq_ref, token_ref, scanned, states = refs[10 + blocks :]
    token_ref[...] = jnp.zeros_like(token_ref)
    place_halves(mine_ref, other_ref, 0, states)
    add_carries(False, modes, rate_ref, coef_ref, states, local_refs, scanned)
    line_outputs(
        k_ref,
        v_ref,
        (q_ref, ct_ref),
        skip_ref,
        scanned,
        (out_ref, gq_ref),
        range(k_ref.shape[0] // math.gcd(k_ref.shape[0], STEP_ROWS)),
    )


def early_parts(seq):
    parts = seq // math.gcd(seq, STEP_ROWS)
    return range((parts + 1) // 2), range((parts + 1) // 2, parts)


def adjoint_kernel(modes, blocks, *refs):
    q_ref, k_ref, v_ref, ct_ref, rate_ref, coef_ref, skip_ref, mine_ref, other_ref, _ = refs[:10]
    local_refs, refs = refs[10 : 10 + blocks], refs[10 + blocks :]
    out_rows, gq_rows, out_hbm, gq_hbm, scanned, gk_ref, gv_ref, states, sems = refs
    copies = [
        pltpu.make_async_copy(out_rows, out_hbm, sems.at[0]),
        pltpu.make_async_copy(gq_rows, gq_hbm, sems.at[1]),
    ]
    for copy in copies:
        copy.start()
    place_halves(mine_ref, other_ref, states.shape[0] // 2, states)
    add_carries(True, modes, rate_ref, coef_ref, states, local_refs, scanned)
    line_outputs(
        ct_ref,
        q_ref,
        (v_ref, k_ref),
        skip_ref,
        scanned,
        (gk_ref, gv_ref),
        early_parts(q_ref.shape[0])[0],
    )
    for copy in copies:
        copy.wait()


def last_outputs_kernel(limit, *refs):
    q_ref, k_ref, v_ref, ct_ref, scanned, skip_ref, gk_early, gv_early, mine_ref, other_ref = refs[
        :10
    ]
    share_refs = refs[10:-8]
    raw_hbm, gk_hbm, gv_hbm, gk_rows, gv_rows, raw_cols, states, sems = refs[-8:]
    copies = []

    def start(source, target):
        copy = pltpu.make_async_copy(source, target, sems.at[len(copies)])
        copy.start()
        copies.append(copy)

    early = pl.ds(0, gk_early.shape[0])
    start(gk_early, gk_hbm.at[early])
    start(gv_early, gv_hbm.at[early])
    clip(limit, scanned.shape[0], mine_ref, other_ref, share_refs, raw_cols, states)
    start(raw_cols, raw_hbm)

    def send(at, to):
        start(gk_rows.at[at], gk_hbm.at[to])
        start(gv_rows.at[at], gv_hbm.at[to])

    late = early_parts(q_ref.shape[0])[1]
    if len(late) > 0:
        line_outputs(
            ct_ref, q_ref, (v_ref, k_ref), skip_ref, scanned, (gk_rows, gv_rows), late, send
        )
    for copy in copies:
        copy.wait()


def add_kernel(left_ref, right_ref, after_ref, out_ref):
    out_ref[...] = left_ref[...] + right_ref[...]


def clip(limit, blocks, mine_ref, other_ref, share_refs, out_ref, states):
    modes = out_ref.shape[0]
    sub = out_ref.shape[1] // (blocks * LANES)
    half = states.shape[0] // 2
    place_halves(mine_ref, other_ref, 2 * half, states)
    square = jnp.sum(tree_sum([ref[...] for ref in share_refs]))
    factor = jnp.minimum(1.0, limit * lax.rsqrt(jnp.full((1, LANES), square + 1e-06, F32)))
    for b in range(blocks):
        for s in range(sub):
            cols = slice((b * sub + s) * LANES, (b * sub + s + 1) * LANES)
            rows = pl.ds(b * modes * sub + s, modes, stride=sub)
            out_ref[:, cols] = states[rows, :] * factor


def shards(queries, keys_in, values_in, decay_rates, residues, skip_gain, cotangent):
    seq, channels = queries.shape
    modes = decay_rates.shape[1]
    ctx = lax.axis_size("ctx")
    tp = lax.axis_size("tp")
    levels = ctx.bit_length() - 1
    groups = channels // LANES
    sub = math.gcd(groups, 8)
    blocks = groups // sub
    half = modes * groups // 2
    parts = seq // math.gcd(seq, STEP_ROWS)

    def swap(value, bit):
        return lax.ppermute(value, "ctx", [(i, i ^ (1 << bit)) for i in range(ctx)])

    def rows(*shape, dtype=F32):
        return jax.ShapeDtypeStruct((*shape, LANES), dtype)

    line_shape = jax.ShapeDtypeStruct((seq, channels), jnp.bfloat16)
    table_shape = jax.ShapeDtypeStruct((modes, channels), F32)
    line_scratch = pltpu.VMEM((seq, channels), jnp.bfloat16)
    table_scratch = pltpu.VMEM((modes, channels), F32)
    elements = seq * channels * modes
    sources = (queries, keys_in, values_in, cotangent, decay_rates.T, residues.T)

    send, q, k, v, ct, gated, pulled, row_rates, row_coefs = pl.pallas_call(
        send_kernel,
        in_specs=[HBM] * 6,
        out_specs=[VMEM] * 9,
        out_shape=[rows(3, half)]
        + [line_shape] * 4
        + [rows(blocks, seq * sub)] * 2
        + [rows(2 * half)] * 2,
        scratch_shapes=[
            table_scratch,
            table_scratch,
            pltpu.SemaphoreType.DMA((4 * parts + 6,)),
        ],
        compiler_params=KERNEL,
        cost_estimate=pl.CostEstimate(
            flops=3 * elements, bytes_accessed=8 * seq * channels, transcendentals=0
        ),
        name="sent_states",
    )(*[pltpu.with_memory_space_constraint(item, pltpu.HBM) for item in sources])
    sibling = swap(send, 0)
    keep, gated, pulled = pl.pallas_call(
        keep_kernel,
        out_shape=[rows(3, half)] + [rows(blocks, seq * sub)] * 2,
        scratch_shapes=[pltpu.SemaphoreType.DMA((2,))],
        compiler_params=KERNEL,
        cost_estimate=pl.CostEstimate(
            flops=3 * elements, bytes_accessed=8 * seq * channels, transcendentals=0
        ),
        name="kept_states",
    )(q, k, v, ct, row_rates, gated, pulled)

    def wire(level):
        return rows(2 if level == levels - 1 else 3, half, dtype=WIRE)

    whole = rows(blocks, seq * sub)
    whole_scratch = pltpu.VMEM((blocks, seq * sub, LANES), F32)
    states_scratch = pltpu.VMEM((2 * half, LANES), F32)
    every = tuple(range(blocks))

    def local(reverse, which, after, name):
        lines = pulled if reverse else gated
        return pl.pallas_call(
            partial(local_kernel, reverse, which, modes),
            out_shape=[rows(seq * sub)] * len(which),
            compiler_params=KERNEL,
            cost_estimate=pl.CostEstimate(
                flops=4 * elements, bytes_accessed=8 * seq * channels, transcendentals=0
            ),
            name=name,
        )(lines, row_rates, row_coefs, after[:8])

    block, packed = pl.pallas_call(
        partial(pair_kernel, seq, levels == 2),
        out_shape=[rows(5, half), wire(1)],
        compiler_params=KERNEL,
        name="chip_states",
    )(keep, sibling, row_rates, row_rates[:8])
    got = swap(packed, 1)
    conv = local(False, every, block[4], "local_conv")
    for level in range(1, levels - 1):
        block, packed = pl.pallas_call(
            partial(level_kernel, seq, level, level + 1 == levels - 1),
            out_shape=[rows(5, half), wire(level + 1)],
            compiler_params=KERNEL,
            name="block_states",
        )(block, got, row_rates, conv[0])
        got = swap(packed, level + 1)
    early = every[: (blocks + 1) // 2]
    adj = local(True, early, block[4], "local_adjoint")
    mine, other = pl.pallas_call(
        partial(last_kernel, seq, levels - 1),
        out_shape=[rows(3 * half + 8)] * 2,
        compiler_params=KERNEL,
        name="carries",
    )(block, got, row_rates, keep, sibling, adj[0])
    other = swap(other, 0)
    after = mine
    if len(early) < blocks:
        adj += local(True, every[len(early) :], mine, "late_adjoint")
        after = adj[-1]

    def plus(left, right, after):
        return pl.pallas_call(
            add_kernel,
            in_specs=[VMEM] * 3,
            out_shape=rows(8),
            compiler_params=KERNEL,
            name="square_sum",
        )(left, right, after)

    def tp_swap(value, bit):
        return lax.ppermute(value, "tp", [(i, i ^ (1 << bit)) for i in range(tp)])

    square = plus(mine[3 * half :], other[3 * half :], after)
    bits = tp.bit_length() - 1
    share = tp_swap(square, 0) if bits else jnp.zeros_like(square)
    skip = skip_gain.reshape(1, channels)
    forward_out, forward_grad, after = pl.pallas_call(
        partial(forward_kernel, modes, blocks),
        out_shape=[line_shape] * 2 + [rows(8)],
        scratch_shapes=[whole_scratch, states_scratch],
        compiler_params=KERNEL,
        cost_estimate=pl.CostEstimate(
            flops=2 * elements, bytes_accessed=16 * seq * channels, transcendentals=0
        ),
        name="forward_outputs",
    )(q, k, v, ct, row_rates, row_coefs, skip, mine, other, square, *conv)
    for bit in range(1, bits):
        square = plus(square, share, after)
        share = tp_swap(square, bit)
        after = square
    early, late = early_parts(seq)
    early_shape = jax.ShapeDtypeStruct((seq * len(early) // parts, channels), jnp.bfloat16)
    late_scratch = pltpu.VMEM((seq * max(len(late), 1) // parts, channels), jnp.bfloat16)
    operator_out, grad_queries, scanned, early_keys, early_values = pl.pallas_call(
        partial(adjoint_kernel, modes, blocks),
        in_specs=[VMEM] * (12 + blocks),
        out_specs=[HBM] * 2 + [VMEM] * 3,
        out_shape=[line_shape] * 2 + [whole] + [early_shape] * 2,
        scratch_shapes=[states_scratch, pltpu.SemaphoreType.DMA((2,))],
        compiler_params=KERNEL,
        cost_estimate=pl.CostEstimate(
            flops=2 * elements, bytes_accessed=8 * seq * channels, transcendentals=0
        ),
        name="adjoint_carries",
    )(
        q,
        k,
        v,
        ct,
        row_rates,
        row_coefs,
        skip,
        mine,
        other,
        after,
        *adj,
        forward_out,
        forward_grad,
    )
    grad_residues, grad_keys, grad_values = pl.pallas_call(
        partial(last_outputs_kernel, math.sqrt(channels * tp * modes)),
        in_specs=[VMEM] * 12,
        out_specs=[HBM] * 3,
        out_shape=[table_shape] + [line_shape] * 2,
        scratch_shapes=[
            late_scratch,
            late_scratch,
            table_scratch,
            states_scratch,
            pltpu.SemaphoreType.DMA((2 * parts + 3,)),
        ],
        compiler_params=KERNEL,
        cost_estimate=pl.CostEstimate(
            flops=elements, bytes_accessed=8 * seq * channels, transcendentals=0
        ),
        name="last_outputs",
    )(q, k, v, ct, scanned, skip, early_keys, early_values, mine, other, square, share)
    return (operator_out, grad_queries, grad_keys, grad_values, grad_residues.T)


def solution(mesh):
    lines, tables = P("ctx", "tp"), P("tp", None)
    in_specs = (lines, lines, lines, tables, tables, P("tp"), lines)
    out_specs = (lines, lines, lines, lines, tables)
    return jax.shard_map(shards, mesh=mesh, in_specs=in_specs, out_specs=out_specs, check_vma=False)
```

```python
from functools import partial
import math

import jax
import jax.numpy as jnp
from jax import lax
from jax.experimental import pallas as pl
from jax.experimental.pallas import tpu as pltpu
from jax.sharding import PartitionSpec as P

F32 = jnp.float32
WIRE = jnp.bfloat16
LANES = 128
UNROLL = 8
STEP_ROWS = 32
KERNEL = pltpu.CompilerParams(vmem_limit_bytes=24 * 1024 * 1024)
HBM = pl.BlockSpec(memory_space=pltpu.HBM)
VMEM = pl.BlockSpec(memory_space=pltpu.VMEM)


def reorder(rows, inner):
    outer = rows // inner
    first = lax.broadcasted_iota(jnp.int32, (rows, rows), 0)
    second = lax.broadcasted_iota(jnp.int32, (rows, rows), 1)

    def matrix(to, fro):
        if inner & (inner - 1) == 0 and outer & (outer - 1) == 0:
            low, high = inner.bit_length() - 1, outer.bit_length() - 1
            same = (fro & (inner - 1)) * outer + (fro >> low) == to
        else:
            same = (fro % inner) * outer + fro // inner == to
        return jnp.where(same, 1.0, 0.0).astype(jnp.bfloat16)

    return matrix(first, second), matrix(second, first)


def tree_sum(items):
    items = list(items)
    while len(items) > 1:
        items = [
            items[i] + items[i + 1] if i + 1 < len(items) else items[i]
            for i in range(0, len(items), 2)
        ]
    return items[0]


def half_units(which, blocks, modes, sub):
    if blocks == 1:
        return [(0, which * (modes // 2 * sub), modes // 2)]
    count = blocks // 2
    return [
        (which * count + j, (which * count + j) * (modes * sub), modes) for j in range(count)
    ]


def to_scan_order(to_scan, pairs, part, i, block, targets):
    size, sub = to_scan.shape[0], to_scan.shape[0] // part
    rows = slice(i * part, (i + 1) * part)
    sides = []
    for left, right in pairs:
        stacked = []
        for s in range(sub):
            cols = pl.ds(pl.multiple_of((block * sub + s) * LANES, LANES), LANES)
            product = left[rows, cols].astype(F32) * right[rows, cols].astype(F32)
            stacked.append(product.astype(jnp.bfloat16))
        sides.append(jnp.concatenate(stacked, axis=0))
    ordered = jnp.dot(
        to_scan[...], jnp.concatenate(sides, axis=1), preferred_element_type=F32
    )
    for j, target in enumerate(targets):
        target[block, i * size : (i + 1) * size, :] = ordered[:, j * LANES : (j + 1) * LANES]


def scan_states(unit, sub, gated_ref, pulled_ref, decay_ref, out_ref, at_row):
    block, base, modes = unit
    seq = gated_ref.shape[1] // sub
    decay = [
        decay_ref[pl.ds(pl.multiple_of(base + n * sub, sub), sub), :] for n in range(modes)
    ]
    first = tuple(jnp.zeros((sub, LANES), F32) for _ in range(modes))

    def forward(j, carry):
        held, inner = list(carry[0]), list(carry[1])
        for u in range(UNROLL):
            at = pl.ds(pl.multiple_of((j * UNROLL + u) * sub, sub), sub)
            x = gated_ref[block, at, :]
            p = pulled_ref[block, at, :]
            for n in range(modes):
                held[n] = decay[n] * held[n] + x
                inner[n] = inner[n] + p * held[n]
        return tuple(held), tuple(inner)

    def backward(j, carry):
        held = list(carry)
        for u in range(UNROLL):
            at = pl.ds(pl.multiple_of((seq - 1 - (j * UNROLL + u)) * sub, sub), sub)
            p = pulled_ref[block, at, :]
            for n in range(modes):
                held[n] = decay[n] * held[n] + p
        return tuple(held)

    ends, inner = lax.fori_loop(0, seq // UNROLL, forward, (first, first))
    for n in range(modes):
        rows = slice(at_row + n * sub, at_row + (n + 1) * sub)
        out_ref[0, rows, :] = ends[n]
        out_ref[2, rows, :] = inner[n]
    starts = lax.fori_loop(0, seq // UNROLL, backward, first)
    for n in range(modes):
        out_ref[1, at_row + n * sub : at_row + (n + 1) * sub, :] = starts[n]


def send_kernel(
    q_hbm,
    k_hbm,
    v_hbm,
    ct_hbm,
    rate_hbm,
    res_hbm,
    send_ref,
    q_ref,
    k_ref,
    v_ref,
    ct_ref,
    gated_ref,
    pulled_ref,
    rate_ref,
    decay_ref,
    coef_ref,
    to_scan,
    from_scan,
    rate_cols,
    res_cols,
    sems,
):
    seq, channels = q_ref.shape
    modes = rate_cols.shape[0]
    blocks = gated_ref.shape[0]
    sub = channels // (blocks * LANES)
    part = math.gcd(seq, STEP_ROWS)
    parts = seq // part
    which = 1 - lax.axis_index("ctx") % 2
    pairs = ((k_hbm, k_ref), (v_hbm, v_ref), (ct_hbm, ct_ref), (q_hbm, q_ref))
    copies = []

    def start(source, target):
        copy = pltpu.make_async_copy(source, target, sems.at[len(copies)])
        copy.start()
        copies.append(copy)

    start(rate_hbm, rate_cols)
    start(res_hbm, res_cols)
    width = channels // min(blocks, 2)
    cols = pl.ds(pl.multiple_of(which * width, LANES) if blocks > 1 else 0, width)
    for i in range(parts):
        rows = pl.ds(i * part, part)
        for source, target in pairs:
            start(source.at[rows, cols], target.at[rows, cols])
    if blocks > 1:
        cols = pl.ds(pl.multiple_of((1 - which) * width, LANES), width)
        for source, target in pairs:
            start(source.at[:, cols], target.at[:, cols])

    def spread(source, target):
        for b in range(blocks):
            for s in range(sub):
                cols = slice((b * sub + s) * LANES, (b * sub + s + 1) * LANES)
                target[pl.ds(b * modes * sub + s, modes, stride=sub), :] = source[:, cols]

    to_scan[...], from_scan[...] = reorder(part * sub, part)
    copies[0].wait()
    spread(rate_cols, rate_ref)
    copies[1].wait()
    spread(res_cols, coef_ref)
    rate = rate_ref[...]
    decay_ref[...] = jnp.exp(-rate)
    coef_ref[...] = coef_ref[...] * jnp.sqrt(1.0 - jnp.exp(-2.0 * rate))
    units = half_units(which, blocks, modes, sub)
    lines = ((k_ref, v_ref), (ct_ref, q_ref))
    for i in range(parts):
        for copy in copies[2 + 4 * i : 6 + 4 * i]:
            copy.wait()
        for unit in units:
            to_scan_order(to_scan, lines, part, i, unit[0], (gated_ref, pulled_ref))
    for at, unit in enumerate(units):
        at_row = at * unit[2] * sub
        scan_states(unit, sub, gated_ref, pulled_ref, decay_ref, send_ref, at_row)
    for copy in copies[2 + 4 * parts :]:
        copy.wait()


def keep_kernel(
    q_ref,
    k_ref,
    v_ref,
    ct_ref,
    decay_ref,
    to_scan,
    gated_in,
    pulled_in,
    keep_ref,
    gated_ref,
    pulled_ref,
    sems,
):
    seq, channels = q_ref.shape
    blocks = gated_ref.shape[0]
    sub = channels // (blocks * LANES)
    modes = decay_ref.shape[0] // (blocks * sub)
    part = math.gcd(seq, STEP_ROWS)
    which = lax.axis_index("ctx") % 2
    count = max(blocks // 2, 1)
    done = pl.ds((1 - which) * count if blocks > 1 else 0, count)
    copies = [
        pltpu.make_async_copy(gated_in.at[done], gated_ref.at[done], sems.at[0]),
        pltpu.make_async_copy(pulled_in.at[done], pulled_ref.at[done], sems.at[1]),
    ]
    for copy in copies:
        copy.start()
    units = half_units(which, blocks, modes, sub)
    lines = (gated_in, pulled_in)
    if blocks > 1:
        lines = (gated_ref, pulled_ref)
        for i in range(seq // part):
            for unit in units:
                pairs = ((k_ref, v_ref), (ct_ref, q_ref))
                to_scan_order(to_scan, pairs, part, i, unit[0], lines)
    for at, unit in enumerate(units):
        scan_states(unit, sub, *lines, decay_ref, keep_ref, at * unit[2] * sub)
    for copy in copies:
        copy.wait()


def own_rows(rate_ref, half):
    core = lax.axis_index("ctx") % 2
    return rate_ref[pl.ds(pl.multiple_of(core * half, half), half), :]


def joined(is_right, mine, other, span, step):
    left = [jnp.where(is_right, o, m) for m, o in zip(mine, other)]
    right = [jnp.where(is_right, m, o) for m, o in zip(mine, other)]
    return (
        span * left[0] + right[0],
        left[1] + span * right[1],
        left[2] + right[2] + step * right[1] * left[0],
    )


def put_wire(wire_ref, is_last, next_right, block):
    if is_last:
        wire_ref[0] = jnp.where(next_right, block[1], block[0]).astype(wire_ref.dtype)
        wire_ref[1] = block[2].astype(wire_ref.dtype)
    else:
        for kind in range(3):
            wire_ref[kind] = block[kind].astype(wire_ref.dtype)


def pair_kernel(seq, is_last, keep_ref, got_ref, rate_ref, after_ref, block_ref, wire_ref):
    rate = own_rows(rate_ref, keep_ref.shape[1])
    place = lax.axis_index("ctx")
    block = joined(
        place % 2 == 1,
        [keep_ref[i] for i in range(3)],
        [got_ref[i] for i in range(3)],
        jnp.exp(-rate * seq),
        jnp.exp(-rate),
    )
    for kind in range(3):
        block_ref[kind] = block[kind]
    block_ref[3] = jnp.zeros_like(rate)
    block_ref[4] = jnp.zeros_like(rate)
    put_wire(wire_ref, is_last, (place // 2) % 2 == 1, block)


def carries_with(block_ref, end_state, start_state, level, seq, rate):
    place = lax.axis_index("ctx")
    is_right = (place >> level) % 2 == 1
    chips = 1 << (level - 1)
    at = (place // 2) % chips
    before = at * (2 * seq)
    behind = (chips - 1 - at) * (2 * seq)
    ahead = block_ref[3] + jnp.where(
        is_right, jnp.exp(-rate * before.astype(F32)) * end_state, 0.0
    )
    after = block_ref[4] + jnp.where(
        is_right, 0.0, jnp.exp(-rate * behind.astype(F32)) * start_state
    )
    return is_right, ahead, after


def level_kernel(
    seq, level, is_last, block_ref, got_ref, rate_ref, after_ref, out_ref, wire_ref
):
    rate = own_rows(rate_ref, block_ref.shape[1])
    got = [got_ref[i].astype(F32) for i in range(3)]
    is_right, ahead, after = carries_with(block_ref, got[0], got[1], level, seq, rate)
    block = joined(
        is_right,
        [block_ref[i] for i in range(3)],
        got,
        jnp.exp(-rate * (seq << level)),
        jnp.exp(-rate),
    )
    for kind in range(3):
        out_ref[kind] = block[kind]
    out_ref[3] = ahead
    out_ref[4] = after
    next_right = (lax.axis_index("ctx") >> (level + 1)) % 2 == 1
    put_wire(wire_ref, is_last, next_right, block)


def last_kernel(
    seq,
    level,
    block_ref,
    got_ref,
    rate_ref,
    keep_ref,
    sibling_ref,
    after_ref,
    mine_ref,
    other_ref,
):
    half = block_ref.shape[1]
    rate = own_rows(rate_ref, half)
    edge, inner = got_ref[0].astype(F32), got_ref[1].astype(F32)
    is_right, ahead, after = carries_with(block_ref, edge, edge, level, seq, rate)
    own_edge = jnp.where(is_right, block_ref[1], block_ref[0])
    total = block_ref[2] + inner + jnp.exp(-rate) * own_edge * edge
    raw = jnp.sqrt(1.0 - jnp.exp(-2.0 * rate)) * total
    core = lax.axis_index("ctx") % 2
    first = core == 0
    span = jnp.exp(-rate * seq)
    end_first = jnp.where(first, keep_ref[0], sibling_ref[0])
    start_second = jnp.where(first, sibling_ref[1], keep_ref[1])
    ahead_second = span * ahead + end_first
    after_first = span * after + start_second
    mine_ref[0:half, :] = jnp.where(first, ahead, ahead_second)
    mine_ref[half : 2 * half, :] = jnp.where(first, after_first, after)
    other_ref[0:half, :] = jnp.where(first, ahead_second, ahead)
    other_ref[half : 2 * half, :] = jnp.where(first, after, after_first)
    squares = raw * raw
    share = tree_sum([squares[i : i + 8, :] for i in range(0, half, 8)])
    for ref in (mine_ref, other_ref):
        ref[2 * half : 3 * half, :] = raw
        ref[3 * half : 3 * half + 8, :] = share


def place_halves(mine_ref, other_ref, first, target):
    half = target.shape[0] // 2
    core = lax.axis_index("ctx") % 2
    for ref, at in ((mine_ref, core), (other_ref, 1 - core)):
        rows = pl.ds(pl.multiple_of(at * half, half), half)
        target[rows, :] = ref[first : first + half, :]


def mode_rows(block, modes, sub):
    return [slice((block * modes + n) * sub, (block * modes + n + 1) * sub) for n in range(modes)]


def local_kernel(reverse, which, modes, lines_ref, decay_ref, coef_ref, after_ref, *out_refs):
    sub = decay_ref.shape[0] // (lines_ref.shape[0] * modes)
    seq = lines_ref.shape[1] // sub
    for b, out_ref in zip(which, out_refs):
        rows = mode_rows(b, modes, sub)
        decay = [decay_ref[r, :] for r in rows]
        coef = [coef_ref[r, :] for r in rows]

        def body(j, carry):
            held = list(carry)
            for u in range(UNROLL):
                t = j * UNROLL + u
                if reverse:
                    t = seq - 1 - t
                at = pl.ds(pl.multiple_of(t * sub, sub), sub)
                x = lines_ref[b, at, :]
                total = [None] * 4
                for n in range(modes):
                    held[n] = decay[n] * held[n] + x
                    term = coef[n] * held[n]
                    total[n % 4] = term if n < 4 else total[n % 4] + term
                out_ref[at, :] = tree_sum(total)
            return tuple(held)

        first = tuple(jnp.zeros((sub, LANES), F32) for _ in range(modes))
        lax.fori_loop(0, seq // UNROLL, body, first)


def add_carries(reverse, modes, decay_ref, coef_ref, states, local_refs, target):
    sub = decay_ref.shape[0] // (len(local_refs) * modes)
    seq = local_refs[0].shape[0] // sub
    for b, local_ref in enumerate(local_refs):
        rows = mode_rows(b, modes, sub)
        decay = [decay_ref[r, :] for r in rows]
        first = tuple(coef_ref[r, :] * states[r, :] for r in rows)

        def body(j, carry):
            held = list(carry)
            for u in range(UNROLL):
                t = j * UNROLL + u
                if reverse:
                    t = seq - 1 - t
                at = pl.ds(pl.multiple_of(t * sub, sub), sub)
                total = [local_ref[at, :], None, None, None]
                for n in range(modes):
                    held[n] = decay[n] * held[n]
                    total[n % 4] = held[n] if total[n % 4] is None else total[n % 4] + held[n]
                target[b, at, :] = tree_sum(total)
            return tuple(held)

        lax.fori_loop(0, seq // UNROLL, body, first)


def line_outputs(
    from_scan, left, right, scales, skip_ref, scanned, targets, which, done_with=None
):
    seq, channels = left.shape
    blocks = scanned.shape[0]
    sub = channels // (blocks * LANES)
    part = math.gcd(seq, STEP_ROWS)
    for i in which:
        rows = slice(i * part, (i + 1) * part)
        to_rows = slice((i - which[0]) * part, (i - which[0] + 1) * part)
        stacked = jnp.concatenate(
            [scanned[b, i * part * sub : (i + 1) * part * sub, :] for b in range(blocks)], axis=1
        ).astype(jnp.bfloat16)
        ordered = jnp.dot(from_scan[...], stacked, preferred_element_type=F32)
        for b in range(blocks):
            for s in range(sub):
                cols = slice((b * sub + s) * LANES, (b * sub + s + 1) * LANES)
                own = ordered[s * part : (s + 1) * part, b * LANES : (b + 1) * LANES]
                line = left[rows, cols].astype(F32) * right[rows, cols].astype(F32)
                mixed = own + skip_ref[:, cols] * line.astype(jnp.bfloat16).astype(F32)
                for scale, target in zip(scales, targets):
                    target[to_rows, cols] = (scale[rows, cols].astype(F32) * mixed).astype(
                        jnp.bfloat16
                    )
        if done_with is not None:
            done_with(pl.ds((i - which[0]) * part, part), pl.ds(i * part, part))


def forward_kernel(modes, blocks, *refs):
    q_ref, k_ref, v_ref, ct_ref, decay_ref, coef_ref, skip_ref, mine_ref, other_ref = refs[:9]
    from_scan, local_refs = refs[9], refs[11 : 11 + blocks]
    out_ref, gq_ref, token_ref, scanned, states = refs[11 + blocks :]
    token_ref[...] = jnp.zeros_like(token_ref)
    place_halves(mine_ref, other_ref, 0, states)
    add_carries(False, modes, decay_ref, coef_ref, states, local_refs, scanned)
    line_outputs(
        from_scan,
        k_ref,
        v_ref,
        (q_ref, ct_ref),
        skip_ref,
        scanned,
        (out_ref, gq_ref),
        range(k_ref.shape[0] // math.gcd(k_ref.shape[0], STEP_ROWS)),
    )


def early_parts(seq):
    parts = seq // math.gcd(seq, STEP_ROWS)
    return range((parts + 1) // 2), range((parts + 1) // 2, parts)


def adjoint_kernel(modes, blocks, *refs):
    q_ref, k_ref, v_ref, ct_ref, decay_ref, coef_ref, skip_ref, mine_ref, other_ref = refs[:9]
    from_scan, local_refs, refs = refs[9], refs[11 : 11 + blocks], refs[11 + blocks :]
    out_rows, gq_rows, out_hbm, gq_hbm, scanned, gk_ref, gv_ref, states, sems = refs
    copies = [
        pltpu.make_async_copy(out_rows, out_hbm, sems.at[0]),
        pltpu.make_async_copy(gq_rows, gq_hbm, sems.at[1]),
    ]
    for copy in copies:
        copy.start()
    place_halves(mine_ref, other_ref, states.shape[0] // 2, states)
    add_carries(True, modes, decay_ref, coef_ref, states, local_refs, scanned)
    line_outputs(
        from_scan,
        ct_ref,
        q_ref,
        (v_ref, k_ref),
        skip_ref,
        scanned,
        (gk_ref, gv_ref),
        early_parts(q_ref.shape[0])[0],
    )
    for copy in copies:
        copy.wait()


def last_outputs_kernel(limit, *refs):
    q_ref, k_ref, v_ref, ct_ref, scanned, skip_ref, gk_early, gv_early = refs[:8]
    mine_ref, other_ref, from_scan = refs[8:11]
    share_refs = refs[11:-8]
    raw_hbm, gk_hbm, gv_hbm, gk_rows, gv_rows, raw_cols, states, sems = refs[-8:]
    copies = []

    def start(source, target):
        copy = pltpu.make_async_copy(source, target, sems.at[len(copies)])
        copy.start()
        copies.append(copy)

    early = pl.ds(0, gk_early.shape[0])
    start(gk_early, gk_hbm.at[early])
    start(gv_early, gv_hbm.at[early])
    clip(limit, scanned.shape[0], mine_ref, other_ref, share_refs, raw_cols, states)
    start(raw_cols, raw_hbm)

    def send(at, to):
        start(gk_rows.at[at], gk_hbm.at[to])
        start(gv_rows.at[at], gv_hbm.at[to])

    late = early_parts(q_ref.shape[0])[1]
    if len(late) > 0:
        sides, targets = (v_ref, k_ref), (gk_rows, gv_rows)
        line_outputs(
            from_scan, ct_ref, q_ref, sides, skip_ref, scanned, targets, late, send
        )
    for copy in copies:
        copy.wait()


def add_kernel(left_ref, right_ref, after_ref, out_ref):
    out_ref[...] = left_ref[...] + right_ref[...]


def clip(limit, blocks, mine_ref, other_ref, share_refs, out_ref, states):
    modes = out_ref.shape[0]
    sub = out_ref.shape[1] // (blocks * LANES)
    half = states.shape[0] // 2
    place_halves(mine_ref, other_ref, 2 * half, states)
    square = jnp.sum(tree_sum([ref[...] for ref in share_refs]))
    factor = jnp.minimum(1.0, limit * lax.rsqrt(jnp.full((1, LANES), square + 1e-06, F32)))
    for b in range(blocks):
        for s in range(sub):
            cols = slice((b * sub + s) * LANES, (b * sub + s + 1) * LANES)
            rows = pl.ds(b * modes * sub + s, modes, stride=sub)
            out_ref[:, cols] = states[rows, :] * factor


def shards(queries, keys_in, values_in, decay_rates, residues, skip_gain, cotangent):
    seq, channels = queries.shape
    modes = decay_rates.shape[1]
    ctx = lax.axis_size("ctx")
    tp = lax.axis_size("tp")
    levels = ctx.bit_length() - 1
    groups = channels // LANES
    sub = math.gcd(groups, 8)
    blocks = groups // sub
    half = modes * groups // 2
    part = math.gcd(seq, STEP_ROWS)
    parts, size = seq // part, part * sub

    def swap(value, bit):
        return lax.ppermute(value, "ctx", [(i, i ^ (1 << bit)) for i in range(ctx)])

    def rows(*shape, dtype=F32):
        return jax.ShapeDtypeStruct((*shape, LANES), dtype)

    line_shape = jax.ShapeDtypeStruct((seq, channels), jnp.bfloat16)
    table_shape = jax.ShapeDtypeStruct((modes, channels), F32)
    line_scratch = pltpu.VMEM((seq, channels), jnp.bfloat16)
    table_scratch = pltpu.VMEM((modes, channels), F32)
    elements = seq * channels * modes
    sources = (queries, keys_in, values_in, cotangent, decay_rates.T, residues.T)

    (
        send,
        q,
        k,
        v,
        ct,
        gated,
        pulled,
        row_rates,
        row_decay,
        row_coefs,
        to_scan,
        from_scan,
    ) = pl.pallas_call(
        send_kernel,
        in_specs=[HBM] * 6,
        out_specs=[VMEM] * 12,
        out_shape=[rows(3, half)]
        + [line_shape] * 4
        + [rows(blocks, seq * sub)] * 2
        + [rows(2 * half)] * 3
        + [jax.ShapeDtypeStruct((size, size), jnp.bfloat16)] * 2,
        scratch_shapes=[
            table_scratch,
            table_scratch,
            pltpu.SemaphoreType.DMA((4 * parts + 6,)),
        ],
        compiler_params=KERNEL,
        cost_estimate=pl.CostEstimate(
            flops=3 * elements, bytes_accessed=8 * seq * channels, transcendentals=0
        ),
        name="sent_states",
    )(*[pltpu.with_memory_space_constraint(item, pltpu.HBM) for item in sources])
    sibling = swap(send, 0)
    keep, gated, pulled = pl.pallas_call(
        keep_kernel,
        out_shape=[rows(3, half)] + [rows(blocks, seq * sub)] * 2,
        scratch_shapes=[pltpu.SemaphoreType.DMA((2,))],
        compiler_params=KERNEL,
        cost_estimate=pl.CostEstimate(
            flops=3 * elements, bytes_accessed=8 * seq * channels, transcendentals=0
        ),
        name="kept_states",
    )(q, k, v, ct, row_decay, to_scan, gated, pulled)

    def wire(level):
        return rows(2 if level == levels - 1 else 3, half, dtype=WIRE)

    whole = rows(blocks, seq * sub)
    whole_scratch = pltpu.VMEM((blocks, seq * sub, LANES), F32)
    states_scratch = pltpu.VMEM((2 * half, LANES), F32)
    every = tuple(range(blocks))

    def local(reverse, which, after, name):
        lines = pulled if reverse else gated
        return pl.pallas_call(
            partial(local_kernel, reverse, which, modes),
            out_shape=[rows(seq * sub)] * len(which),
            compiler_params=KERNEL,
            cost_estimate=pl.CostEstimate(
                flops=4 * elements, bytes_accessed=8 * seq * channels, transcendentals=0
            ),
            name=name,
        )(lines, row_decay, row_coefs, after[:8])

    block, packed = pl.pallas_call(
        partial(pair_kernel, seq, levels == 2),
        out_shape=[rows(5, half), wire(1)],
        compiler_params=KERNEL,
        name="chip_states",
    )(keep, sibling, row_rates, row_rates[:8])
    got = swap(packed, 1)
    conv = local(False, every, block[4], "local_conv")
    for level in range(1, levels - 1):
        block, packed = pl.pallas_call(
            partial(level_kernel, seq, level, level + 1 == levels - 1),
            out_shape=[rows(5, half), wire(level + 1)],
            compiler_params=KERNEL,
            name="block_states",
        )(block, got, row_rates, conv[0])
        got = swap(packed, level + 1)
    early = every[: (blocks + 1) // 2]
    adj = local(True, early, block[4], "local_adjoint")
    mine, other = pl.pallas_call(
        partial(last_kernel, seq, levels - 1),
        out_shape=[rows(3 * half + 8)] * 2,
        compiler_params=KERNEL,
        name="carries",
    )(block, got, row_rates, keep, sibling, adj[0])
    other = swap(other, 0)
    after = mine
    if len(early) < blocks:
        adj += local(True, every[len(early) :], mine, "late_adjoint")
        after = adj[-1]

    def plus(left, right, after):
        return pl.pallas_call(
            add_kernel,
            in_specs=[VMEM] * 3,
            out_shape=rows(8),
            compiler_params=KERNEL,
            name="square_sum",
        )(left, right, after)

    def tp_swap(value, bit):
        return lax.ppermute(value, "tp", [(i, i ^ (1 << bit)) for i in range(tp)])

    square = plus(mine[3 * half :], other[3 * half :], after)
    bits = tp.bit_length() - 1
    share = tp_swap(square, 0) if bits else jnp.zeros_like(square)
    skip = skip_gain.reshape(1, channels)
    forward_out, forward_grad, after = pl.pallas_call(
        partial(forward_kernel, modes, blocks),
        out_shape=[line_shape] * 2 + [rows(8)],
        scratch_shapes=[whole_scratch, states_scratch],
        compiler_params=KERNEL,
        cost_estimate=pl.CostEstimate(
            flops=2 * elements, bytes_accessed=16 * seq * channels, transcendentals=0
        ),
        name="forward_outputs",
    )(q, k, v, ct, row_decay, row_coefs, skip, mine, other, from_scan, square, *conv)
    for bit in range(1, bits):
        square = plus(square, share, after)
        share = tp_swap(square, bit)
        after = square
    early, late = early_parts(seq)
    early_shape = jax.ShapeDtypeStruct((seq * len(early) // parts, channels), jnp.bfloat16)
    late_scratch = pltpu.VMEM((seq * max(len(late), 1) // parts, channels), jnp.bfloat16)
    operator_out, grad_queries, scanned, early_keys, early_values = pl.pallas_call(
        partial(adjoint_kernel, modes, blocks),
        in_specs=[VMEM] * (13 + blocks),
        out_specs=[HBM] * 2 + [VMEM] * 3,
        out_shape=[line_shape] * 2 + [whole] + [early_shape] * 2,
        scratch_shapes=[states_scratch, pltpu.SemaphoreType.DMA((2,))],
        compiler_params=KERNEL,
        cost_estimate=pl.CostEstimate(
            flops=2 * elements, bytes_accessed=8 * seq * channels, transcendentals=0
        ),
        name="adjoint_carries",
    )(
        q,
        k,
        v,
        ct,
        row_decay,
        row_coefs,
        skip,
        mine,
        other,
        from_scan,
        after,
        *adj,
        forward_out,
        forward_grad,
    )
    grad_residues, grad_keys, grad_values = pl.pallas_call(
        partial(last_outputs_kernel, math.sqrt(channels * tp * modes)),
        in_specs=[VMEM] * 13,
        out_specs=[HBM] * 3,
        out_shape=[table_shape] + [line_shape] * 2,
        scratch_shapes=[
            late_scratch,
            late_scratch,
            table_scratch,
            states_scratch,
            pltpu.SemaphoreType.DMA((2 * parts + 3,)),
        ],
        compiler_params=KERNEL,
        cost_estimate=pl.CostEstimate(
            flops=elements, bytes_accessed=8 * seq * channels, transcendentals=0
        ),
        name="last_outputs",
    )(
        q,
        k,
        v,
        ct,
        scanned,
        skip,
        early_keys,
        early_values,
        mine,
        other,
        from_scan,
        square,
        share,
    )
    return (operator_out, grad_queries, grad_keys, grad_values, grad_residues.T)


def solution(mesh):
    lines, tables = P("ctx", "tp"), P("tp", None)
    in_specs = (lines, lines, lines, tables, tables, P("tp"), lines)
    out_specs = (lines, lines, lines, lines, tables)
    return jax.shard_map(shards, mesh=mesh, in_specs=in_specs, out_specs=out_specs, check_vma=False)
```

```python
from functools import partial
import math

import jax
import jax.numpy as jnp
from jax import lax
from jax.experimental import pallas as pl
from jax.experimental.pallas import tpu as pltpu
from jax.sharding import PartitionSpec as P

F32 = jnp.float32
WIRE = jnp.bfloat16
LANES = 128
UNROLL = 8
STEP_ROWS = 32
KERNEL = pltpu.CompilerParams(vmem_limit_bytes=24 * 1024 * 1024)
HBM = pl.BlockSpec(memory_space=pltpu.HBM)
VMEM = pl.BlockSpec(memory_space=pltpu.VMEM)


def reorder(rows, inner):
    outer = rows // inner
    first = lax.broadcasted_iota(jnp.int32, (rows, rows), 0)
    second = lax.broadcasted_iota(jnp.int32, (rows, rows), 1)

    def matrix(to, fro):
        if inner & (inner - 1) == 0 and outer & (outer - 1) == 0:
            low, high = inner.bit_length() - 1, outer.bit_length() - 1
            same = (fro & (inner - 1)) * outer + (fro >> low) == to
        else:
            same = (fro % inner) * outer + fro // inner == to
        return jnp.where(same, 1.0, 0.0).astype(jnp.bfloat16)

    return matrix(first, second), matrix(second, first)


def tree_sum(items):
    items = list(items)
    while len(items) > 1:
        items = [
            items[i] + items[i + 1] if i + 1 < len(items) else items[i]
            for i in range(0, len(items), 2)
        ]
    return items[0]


def half_units(which, blocks, modes, sub):
    if blocks == 1:
        return [(0, which * (modes // 2 * sub), modes // 2)]
    count = blocks // 2
    return [
        (which * count + j, (which * count + j) * (modes * sub), modes) for j in range(count)
    ]


def to_scan_order(to_scan, pairs, part, i, block, targets):
    size, sub = to_scan.shape[0], to_scan.shape[0] // part
    rows = slice(i * part, (i + 1) * part)
    sides = []
    for left, right in pairs:
        stacked = []
        for s in range(sub):
            cols = pl.ds(pl.multiple_of((block * sub + s) * LANES, LANES), LANES)
            product = left[rows, cols].astype(F32) * right[rows, cols].astype(F32)
            stacked.append(product.astype(jnp.bfloat16))
        sides.append(jnp.concatenate(stacked, axis=0))
    ordered = jnp.dot(
        to_scan[...], jnp.concatenate(sides, axis=1), preferred_element_type=F32
    )
    for j, target in enumerate(targets):
        target[block, i * size : (i + 1) * size, :] = ordered[:, j * LANES : (j + 1) * LANES]


def scan_states(unit, sub, gated_ref, pulled_ref, decay_ref, out_ref, at_row):
    block, base, modes = unit
    seq = gated_ref.shape[1] // sub
    decay = [
        decay_ref[pl.ds(pl.multiple_of(base + n * sub, sub), sub), :] for n in range(modes)
    ]
    first = tuple(jnp.zeros((sub, LANES), F32) for _ in range(modes))

    def forward(j, carry):
        held, inner = list(carry[0]), list(carry[1])
        for u in range(UNROLL):
            at = pl.ds(pl.multiple_of((j * UNROLL + u) * sub, sub), sub)
            x = gated_ref[block, at, :]
            p = pulled_ref[block, at, :]
            for n in range(modes):
                held[n] = decay[n] * held[n] + x
                inner[n] = inner[n] + p * held[n]
        return tuple(held), tuple(inner)

    def backward(j, carry):
        held = list(carry)
        for u in range(UNROLL):
            at = pl.ds(pl.multiple_of((seq - 1 - (j * UNROLL + u)) * sub, sub), sub)
            p = pulled_ref[block, at, :]
            for n in range(modes):
                held[n] = decay[n] * held[n] + p
        return tuple(held)

    ends, inner = lax.fori_loop(0, seq // UNROLL, forward, (first, first))
    for n in range(modes):
        rows = slice(at_row + n * sub, at_row + (n + 1) * sub)
        out_ref[0, rows, :] = ends[n]
        out_ref[2, rows, :] = inner[n]
    starts = lax.fori_loop(0, seq // UNROLL, backward, first)
    for n in range(modes):
        out_ref[1, at_row + n * sub : at_row + (n + 1) * sub, :] = starts[n]


def send_kernel(
    q_hbm,
    k_hbm,
    v_hbm,
    ct_hbm,
    rate_hbm,
    res_hbm,
    send_ref,
    q_ref,
    k_ref,
    v_ref,
    ct_ref,
    gated_ref,
    pulled_ref,
    rate_ref,
    decay_ref,
    coef_ref,
    to_scan,
    from_scan,
    rate_cols,
    res_cols,
    sems,
):
    seq, channels = q_ref.shape
    modes = rate_cols.shape[0]
    blocks = gated_ref.shape[0]
    sub = channels // (blocks * LANES)
    part = math.gcd(seq, STEP_ROWS)
    parts = seq // part
    which = 1 - lax.axis_index("ctx") % 2
    pairs = ((k_hbm, k_ref), (v_hbm, v_ref), (ct_hbm, ct_ref), (q_hbm, q_ref))
    copies = []

    def start(source, target):
        copy = pltpu.make_async_copy(source, target, sems.at[len(copies)])
        copy.start()
        copies.append(copy)

    start(rate_hbm, rate_cols)
    start(res_hbm, res_cols)
    width = channels // min(blocks, 2)
    cols = pl.ds(pl.multiple_of(which * width, LANES) if blocks > 1 else 0, width)
    for i in range(parts):
        rows = pl.ds(i * part, part)
        for source, target in pairs:
            start(source.at[rows, cols], target.at[rows, cols])
    if blocks > 1:
        cols = pl.ds(pl.multiple_of((1 - which) * width, LANES), width)
        for source, target in pairs:
            start(source.at[:, cols], target.at[:, cols])

    def spread(source, target):
        for b in range(blocks):
            for s in range(sub):
                cols = slice((b * sub + s) * LANES, (b * sub + s + 1) * LANES)
                target[pl.ds(b * modes * sub + s, modes, stride=sub), :] = source[:, cols]

    to_scan[...], from_scan[...] = reorder(part * sub, part)
    copies[0].wait()
    spread(rate_cols, rate_ref)
    copies[1].wait()
    spread(res_cols, coef_ref)
    rate = rate_ref[...]
    decay_ref[...] = jnp.exp(-rate)
    coef_ref[...] = coef_ref[...] * jnp.sqrt(1.0 - jnp.exp(-2.0 * rate))
    units = half_units(which, blocks, modes, sub)
    lines = ((k_ref, v_ref), (ct_ref, q_ref))
    for i in range(parts):
        for copy in copies[2 + 4 * i : 6 + 4 * i]:
            copy.wait()
        for unit in units:
            to_scan_order(to_scan, lines, part, i, unit[0], (gated_ref, pulled_ref))
    for at, unit in enumerate(units):
        at_row = at * unit[2] * sub
        scan_states(unit, sub, gated_ref, pulled_ref, decay_ref, send_ref, at_row)
    for copy in copies[2 + 4 * parts :]:
        copy.wait()


def keep_kernel(
    q_ref,
    k_ref,
    v_ref,
    ct_ref,
    decay_ref,
    to_scan,
    gated_in,
    pulled_in,
    keep_ref,
    gated_ref,
    pulled_ref,
    sems,
):
    seq, channels = q_ref.shape
    blocks = gated_ref.shape[0]
    sub = channels // (blocks * LANES)
    modes = decay_ref.shape[0] // (blocks * sub)
    part = math.gcd(seq, STEP_ROWS)
    which = lax.axis_index("ctx") % 2
    count = max(blocks // 2, 1)
    done = pl.ds((1 - which) * count if blocks > 1 else 0, count)
    copies = [
        pltpu.make_async_copy(gated_in.at[done], gated_ref.at[done], sems.at[0]),
        pltpu.make_async_copy(pulled_in.at[done], pulled_ref.at[done], sems.at[1]),
    ]
    for copy in copies:
        copy.start()
    units = half_units(which, blocks, modes, sub)
    lines = (gated_in, pulled_in)
    if blocks > 1:
        lines = (gated_ref, pulled_ref)
        for i in range(seq // part):
            for unit in units:
                pairs = ((k_ref, v_ref), (ct_ref, q_ref))
                to_scan_order(to_scan, pairs, part, i, unit[0], lines)
    for at, unit in enumerate(units):
        scan_states(unit, sub, *lines, decay_ref, keep_ref, at * unit[2] * sub)
    for copy in copies:
        copy.wait()


def own_rows(rate_ref, half):
    core = lax.axis_index("ctx") % 2
    return rate_ref[pl.ds(pl.multiple_of(core * half, half), half), :]


def joined(is_right, mine, other, span, step):
    left = [jnp.where(is_right, o, m) for m, o in zip(mine, other)]
    right = [jnp.where(is_right, m, o) for m, o in zip(mine, other)]
    return (
        span * left[0] + right[0],
        left[1] + span * right[1],
        left[2] + right[2] + step * right[1] * left[0],
    )


def put_wire(wire_ref, is_last, next_right, block):
    if is_last:
        wire_ref[0] = jnp.where(next_right, block[1], block[0]).astype(wire_ref.dtype)
        wire_ref[1] = block[2].astype(wire_ref.dtype)
    else:
        for kind in range(3):
            wire_ref[kind] = block[kind].astype(wire_ref.dtype)


def pair_kernel(seq, is_last, keep_ref, got_ref, rate_ref, after_ref, block_ref, wire_ref):
    rate = own_rows(rate_ref, keep_ref.shape[1])
    place = lax.axis_index("ctx")
    block = joined(
        place % 2 == 1,
        [keep_ref[i] for i in range(3)],
        [got_ref[i] for i in range(3)],
        jnp.exp(-rate * seq),
        jnp.exp(-rate),
    )
    for kind in range(3):
        block_ref[kind] = block[kind]
    block_ref[3] = jnp.zeros_like(rate)
    block_ref[4] = jnp.zeros_like(rate)
    put_wire(wire_ref, is_last, (place // 2) % 2 == 1, block)


def carries_with(block_ref, end_state, start_state, level, seq, rate):
    place = lax.axis_index("ctx")
    is_right = (place >> level) % 2 == 1
    chips = 1 << (level - 1)
    at = (place // 2) % chips
    before = at * (2 * seq)
    behind = (chips - 1 - at) * (2 * seq)
    ahead = block_ref[3] + jnp.where(
        is_right, jnp.exp(-rate * before.astype(F32)) * end_state, 0.0
    )
    after = block_ref[4] + jnp.where(
        is_right, 0.0, jnp.exp(-rate * behind.astype(F32)) * start_state
    )
    return is_right, ahead, after


def level_kernel(
    seq, level, is_last, block_ref, got_ref, rate_ref, after_ref, out_ref, wire_ref
):
    rate = own_rows(rate_ref, block_ref.shape[1])
    got = [got_ref[i].astype(F32) for i in range(3)]
    is_right, ahead, after = carries_with(block_ref, got[0], got[1], level, seq, rate)
    block = joined(
        is_right,
        [block_ref[i] for i in range(3)],
        got,
        jnp.exp(-rate * (seq << level)),
        jnp.exp(-rate),
    )
    for kind in range(3):
        out_ref[kind] = block[kind]
    out_ref[3] = ahead
    out_ref[4] = after
    next_right = (lax.axis_index("ctx") >> (level + 1)) % 2 == 1
    put_wire(wire_ref, is_last, next_right, block)


def last_kernel(
    seq,
    level,
    block_ref,
    got_ref,
    rate_ref,
    keep_ref,
    sibling_ref,
    after_ref,
    mine_ref,
    other_ref,
    share_ref,
):
    half = block_ref.shape[1]
    rate = own_rows(rate_ref, half)
    edge, inner = got_ref[0].astype(F32), got_ref[1].astype(F32)
    is_right, ahead, after = carries_with(block_ref, edge, edge, level, seq, rate)
    own_edge = jnp.where(is_right, block_ref[1], block_ref[0])
    total = block_ref[2] + inner + jnp.exp(-rate) * own_edge * edge
    raw = jnp.sqrt(1.0 - jnp.exp(-2.0 * rate)) * total
    core = lax.axis_index("ctx") % 2
    first = core == 0
    span = jnp.exp(-rate * seq)
    end_first = jnp.where(first, keep_ref[0], sibling_ref[0])
    start_second = jnp.where(first, sibling_ref[1], keep_ref[1])
    ahead_second = span * ahead + end_first
    after_first = span * after + start_second
    mine_ref[0:half, :] = jnp.where(first, ahead, ahead_second)
    mine_ref[half : 2 * half, :] = jnp.where(first, after_first, after)
    other_ref[0:half, :] = jnp.where(first, ahead_second, ahead)
    other_ref[half : 2 * half, :] = jnp.where(first, after, after_first)
    squares = raw * raw
    share_ref[...] = tree_sum([squares[i : i + 8, :] for i in range(0, half, 8)])
    mine_ref[2 * half : 3 * half, :] = raw
    other_ref[2 * half : 3 * half, :] = raw


def place_halves(mine_ref, other_ref, first, target):
    half = target.shape[0] // 2
    core = lax.axis_index("ctx") % 2
    for ref, at in ((mine_ref, core), (other_ref, 1 - core)):
        rows = pl.ds(pl.multiple_of(at * half, half), half)
        target[rows, :] = ref[first : first + half, :]


def mode_rows(block, modes, sub):
    return [slice((block * modes + n) * sub, (block * modes + n + 1) * sub) for n in range(modes)]


def local_kernel(reverse, modes, lines_ref, decay_ref, coef_ref, after_ref, out_ref):
    blocks = lines_ref.shape[0]
    sub = decay_ref.shape[0] // (blocks * modes)
    seq = lines_ref.shape[1] // sub
    for b in range(blocks):
        rows = mode_rows(b, modes, sub)
        decay = [decay_ref[r, :] for r in rows]
        coef = [coef_ref[r, :] for r in rows]

        def body(j, carry):
            held = list(carry)
            for u in range(UNROLL):
                t = j * UNROLL + u
                if reverse:
                    t = seq - 1 - t
                at = pl.ds(pl.multiple_of(t * sub, sub), sub)
                x = lines_ref[b, at, :]
                total = [None] * 4
                for n in range(modes):
                    held[n] = decay[n] * held[n] + x
                    term = coef[n] * held[n]
                    total[n % 4] = term if n < 4 else total[n % 4] + term
                out_ref[b, at, :] = tree_sum(total)
            return tuple(held)

        first = tuple(jnp.zeros((sub, LANES), F32) for _ in range(modes))
        lax.fori_loop(0, seq // UNROLL, body, first)


def add_carries(reverse, unit, sub, decay_ref, coef_ref, states_ref, at_row, source, target, at):
    _, base, modes = unit
    seq = target.shape[1] // sub
    rows = [pl.ds(pl.multiple_of(base + n * sub, sub), sub) for n in range(modes)]
    decay = [decay_ref[r, :] for r in rows]
    first = tuple(
        coef_ref[r, :] * states_ref[at_row + n * sub : at_row + (n + 1) * sub, :]
        for n, r in enumerate(rows)
    )

    def body(j, carry):
        held = list(carry)
        for u in range(UNROLL):
            t = j * UNROLL + u
            if reverse:
                t = seq - 1 - t
            where = pl.ds(pl.multiple_of(t * sub, sub), sub)
            total = [source[where, :], None, None, None]
            for n in range(modes):
                held[n] = decay[n] * held[n]
                total[n % 4] = held[n] if total[n % 4] is None else total[n % 4] + held[n]
            target[at, where, :] = tree_sum(total)
        return tuple(held)

    lax.fori_loop(0, seq // UNROLL, body, first)


def own_kernel(modes, conv_ref, adj_ref, decay_ref, coef_ref, mine_ref, conv_own, adj_own):
    blocks = conv_ref.shape[0]
    sub = decay_ref.shape[0] // (blocks * modes)
    half = decay_ref.shape[0] // 2
    core = lax.axis_index("ctx") % 2
    for i, unit in enumerate(half_units(core, blocks, modes, sub)):
        at_row = i * unit[2] * sub
        for reverse, source, target in ((False, conv_ref, conv_own), (True, adj_ref, adj_own)):
            add_carries(
                reverse,
                unit,
                sub,
                decay_ref,
                coef_ref,
                mine_ref,
                at_row + half * reverse,
                source.at[unit[0]],
                target,
                i,
            )


def other_carries(reverse, modes, decay_ref, coef_ref, other_ref, local_ref, own_ref, whole, sem):
    blocks, own_blocks = local_ref.shape[0], own_ref.shape[0]
    sub = decay_ref.shape[0] // (blocks * modes)
    half = decay_ref.shape[0] // 2
    core = lax.axis_index("ctx") % 2
    copy = pltpu.make_async_copy(own_ref, whole.at[pl.ds(core * own_blocks, own_blocks)], sem)
    if blocks > 1:
        copy.start()
    for i, unit in enumerate(half_units(1 - core, blocks, modes, sub)):
        source = local_ref.at[unit[0]] if blocks > 1 else own_ref.at[0]
        at_row = i * unit[2] * sub + half * reverse
        add_carries(
            reverse, unit, sub, decay_ref, coef_ref, other_ref, at_row, source, whole, unit[0]
        )
    if blocks > 1:
        copy.wait()


def line_outputs(
    from_scan, left, right, scales, skip_ref, scanned, targets, which, done_with=None
):
    seq, channels = left.shape
    blocks = scanned.shape[0]
    sub = channels // (blocks * LANES)
    part = math.gcd(seq, STEP_ROWS)
    for i in which:
        rows = slice(i * part, (i + 1) * part)
        to_rows = slice((i - which[0]) * part, (i - which[0] + 1) * part)
        stacked = jnp.concatenate(
            [scanned[b, i * part * sub : (i + 1) * part * sub, :] for b in range(blocks)], axis=1
        ).astype(jnp.bfloat16)
        ordered = jnp.dot(from_scan[...], stacked, preferred_element_type=F32)
        for b in range(blocks):
            for s in range(sub):
                cols = slice((b * sub + s) * LANES, (b * sub + s + 1) * LANES)
                own = ordered[s * part : (s + 1) * part, b * LANES : (b + 1) * LANES]
                line = left[rows, cols].astype(F32) * right[rows, cols].astype(F32)
                mixed = own + skip_ref[:, cols] * line.astype(jnp.bfloat16).astype(F32)
                for scale, target in zip(scales, targets):
                    target[to_rows, cols] = (scale[rows, cols].astype(F32) * mixed).astype(
                        jnp.bfloat16
                    )
        if done_with is not None:
            done_with(pl.ds((i - which[0]) * part, part), pl.ds(i * part, part))


def forward_kernel(
    modes,
    q_ref,
    k_ref,
    v_ref,
    ct_ref,
    decay_ref,
    coef_ref,
    skip_ref,
    other_ref,
    from_scan,
    conv_ref,
    conv_own,
    after_ref,
    out_ref,
    gq_ref,
    token_ref,
    scanned,
    sem,
):
    token_ref[...] = jnp.zeros_like(token_ref)
    other_carries(
        False, modes, decay_ref, coef_ref, other_ref, conv_ref, conv_own, scanned, sem
    )
    line_outputs(
        from_scan,
        k_ref,
        v_ref,
        (q_ref, ct_ref),
        skip_ref,
        scanned,
        (out_ref, gq_ref),
        range(k_ref.shape[0] // math.gcd(k_ref.shape[0], STEP_ROWS)),
    )


def early_parts(seq):
    parts = seq // math.gcd(seq, STEP_ROWS)
    return range((parts + 1) // 2), range((parts + 1) // 2, parts)


def adjoint_kernel(
    modes,
    q_ref,
    k_ref,
    v_ref,
    ct_ref,
    decay_ref,
    coef_ref,
    skip_ref,
    other_ref,
    from_scan,
    adj_ref,
    adj_own,
    out_rows,
    gq_rows,
    after_ref,
    out_hbm,
    gq_hbm,
    scanned,
    gk_ref,
    gv_ref,
    token_ref,
    sems,
):
    token_ref[...] = jnp.zeros_like(token_ref)
    copies = [
        pltpu.make_async_copy(out_rows, out_hbm, sems.at[0]),
        pltpu.make_async_copy(gq_rows, gq_hbm, sems.at[1]),
    ]
    for copy in copies:
        copy.start()
    other_carries(
        True, modes, decay_ref, coef_ref, other_ref, adj_ref, adj_own, scanned, sems.at[2]
    )
    line_outputs(
        from_scan,
        ct_ref,
        q_ref,
        (v_ref, k_ref),
        skip_ref,
        scanned,
        (gk_ref, gv_ref),
        early_parts(q_ref.shape[0])[0],
    )
    for copy in copies:
        copy.wait()


def last_outputs_kernel(limit, *refs):
    q_ref, k_ref, v_ref, ct_ref, scanned, skip_ref, gk_early, gv_early = refs[:8]
    mine_ref, other_ref, from_scan = refs[8:11]
    share_refs = refs[12:-8]
    raw_hbm, gk_hbm, gv_hbm, gk_rows, gv_rows, raw_cols, states, sems = refs[-8:]
    copies = []

    def start(source, target):
        copy = pltpu.make_async_copy(source, target, sems.at[len(copies)])
        copy.start()
        copies.append(copy)

    early = pl.ds(0, gk_early.shape[0])
    start(gk_early, gk_hbm.at[early])
    start(gv_early, gv_hbm.at[early])
    clip(limit, scanned.shape[0], mine_ref, other_ref, share_refs, raw_cols, states)
    start(raw_cols, raw_hbm)

    def send(at, to):
        start(gk_rows.at[at], gk_hbm.at[to])
        start(gv_rows.at[at], gv_hbm.at[to])

    late = early_parts(q_ref.shape[0])[1]
    if len(late) > 0:
        sides, targets = (v_ref, k_ref), (gk_rows, gv_rows)
        line_outputs(
            from_scan, ct_ref, q_ref, sides, skip_ref, scanned, targets, late, send
        )
    for copy in copies:
        copy.wait()


def add_kernel(left_ref, right_ref, after_ref, out_ref):
    out_ref[...] = left_ref[...] + right_ref[...]


def clip(limit, blocks, mine_ref, other_ref, share_refs, out_ref, states):
    modes = out_ref.shape[0]
    sub = out_ref.shape[1] // (blocks * LANES)
    half = states.shape[0] // 2
    place_halves(mine_ref, other_ref, 2 * half, states)
    square = jnp.sum(tree_sum([ref[...] for ref in share_refs]))
    factor = jnp.minimum(1.0, limit * lax.rsqrt(jnp.full((1, LANES), square + 1e-06, F32)))
    for b in range(blocks):
        for s in range(sub):
            cols = slice((b * sub + s) * LANES, (b * sub + s + 1) * LANES)
            rows = pl.ds(b * modes * sub + s, modes, stride=sub)
            out_ref[:, cols] = states[rows, :] * factor


def shards(queries, keys_in, values_in, decay_rates, residues, skip_gain, cotangent):
    seq, channels = queries.shape
    modes = decay_rates.shape[1]
    ctx = lax.axis_size("ctx")
    tp = lax.axis_size("tp")
    levels = ctx.bit_length() - 1
    groups = channels // LANES
    sub = math.gcd(groups, 8)
    blocks = groups // sub
    half = modes * groups // 2
    part = math.gcd(seq, STEP_ROWS)
    parts, size = seq // part, part * sub

    def swap(value, bit):
        return lax.ppermute(value, "ctx", [(i, i ^ (1 << bit)) for i in range(ctx)])

    def rows(*shape, dtype=F32):
        return jax.ShapeDtypeStruct((*shape, LANES), dtype)

    line_shape = jax.ShapeDtypeStruct((seq, channels), jnp.bfloat16)
    table_shape = jax.ShapeDtypeStruct((modes, channels), F32)
    line_scratch = pltpu.VMEM((seq, channels), jnp.bfloat16)
    table_scratch = pltpu.VMEM((modes, channels), F32)
    elements = seq * channels * modes
    sources = (queries, keys_in, values_in, cotangent, decay_rates.T, residues.T)

    (
        send,
        q,
        k,
        v,
        ct,
        gated,
        pulled,
        row_rates,
        row_decay,
        row_coefs,
        to_scan,
        from_scan,
    ) = pl.pallas_call(
        send_kernel,
        in_specs=[HBM] * 6,
        out_specs=[VMEM] * 12,
        out_shape=[rows(3, half)]
        + [line_shape] * 4
        + [rows(blocks, seq * sub)] * 2
        + [rows(2 * half)] * 3
        + [jax.ShapeDtypeStruct((size, size), jnp.bfloat16)] * 2,
        scratch_shapes=[
            table_scratch,
            table_scratch,
            pltpu.SemaphoreType.DMA((4 * parts + 6,)),
        ],
        compiler_params=KERNEL,
        cost_estimate=pl.CostEstimate(
            flops=3 * elements, bytes_accessed=8 * seq * channels, transcendentals=0
        ),
        name="sent_states",
    )(*[pltpu.with_memory_space_constraint(item, pltpu.HBM) for item in sources])
    sibling = swap(send, 0)
    keep, gated, pulled = pl.pallas_call(
        keep_kernel,
        out_shape=[rows(3, half)] + [rows(blocks, seq * sub)] * 2,
        scratch_shapes=[pltpu.SemaphoreType.DMA((2,))],
        compiler_params=KERNEL,
        cost_estimate=pl.CostEstimate(
            flops=3 * elements, bytes_accessed=8 * seq * channels, transcendentals=0
        ),
        name="kept_states",
    )(q, k, v, ct, row_decay, to_scan, gated, pulled)

    def wire(level):
        return rows(2 if level == levels - 1 else 3, half, dtype=WIRE)

    whole = rows(blocks, seq * sub)
    whole_scratch = pltpu.VMEM((blocks, seq * sub, LANES), F32)
    states_scratch = pltpu.VMEM((2 * half, LANES), F32)
    def local(reverse, after, name):
        return pl.pallas_call(
            partial(local_kernel, reverse, modes),
            out_shape=whole,
            compiler_params=KERNEL,
            cost_estimate=pl.CostEstimate(
                flops=4 * elements, bytes_accessed=8 * seq * channels, transcendentals=0
            ),
            name=name,
        )(pulled if reverse else gated, row_decay, row_coefs, after)

    block, packed = pl.pallas_call(
        partial(pair_kernel, seq, levels == 2),
        out_shape=[rows(5, half), wire(1)],
        compiler_params=KERNEL,
        name="chip_states",
    )(keep, sibling, row_rates, row_rates[:8])
    got = swap(packed, 1)
    conv = local(False, block[4, :8], "local_conv")
    for level in range(1, levels - 1):
        block, packed = pl.pallas_call(
            partial(level_kernel, seq, level, level + 1 == levels - 1),
            out_shape=[rows(5, half), wire(level + 1)],
            compiler_params=KERNEL,
            name="block_states",
        )(block, got, row_rates, conv[0, :8])
        got = swap(packed, level + 1)
    adj = local(True, block[4, :8], "local_adjoint")
    mine, other, square = pl.pallas_call(
        partial(last_kernel, seq, levels - 1),
        out_shape=[rows(3 * half)] * 2 + [rows(8)],
        compiler_params=KERNEL,
        name="carries",
    )(block, got, row_rates, keep, sibling, adj[0, :8])
    other = swap(other, 0)
    skip = skip_gain.reshape(1, channels)
    early, late = early_parts(seq)
    early_shape = jax.ShapeDtypeStruct((seq * len(early) // parts, channels), jnp.bfloat16)
    late_scratch = pltpu.VMEM((seq * max(len(late), 1) // parts, channels), jnp.bfloat16)
    own_shape = rows(max(blocks // 2, 1), seq * sub)
    kept = {}

    def add_own(after):
        kept["conv"], kept["adj"] = pl.pallas_call(
            partial(own_kernel, modes),
            out_shape=[own_shape] * 2,
            compiler_params=KERNEL,
            cost_estimate=pl.CostEstimate(
                flops=2 * elements, bytes_accessed=8 * seq * channels, transcendentals=0
            ),
            name="own_carries",
        )(conv, adj, row_decay, row_coefs, mine)
        return kept["adj"][0, :8]

    def forward_outputs(after):
        kept["out"], kept["gq"], token = pl.pallas_call(
            partial(forward_kernel, modes),
            out_shape=[line_shape] * 2 + [rows(8)],
            scratch_shapes=[whole_scratch, pltpu.SemaphoreType.DMA],
            compiler_params=KERNEL,
            cost_estimate=pl.CostEstimate(
                flops=2 * elements, bytes_accessed=16 * seq * channels, transcendentals=0
            ),
            name="forward_outputs",
        )(
            q,
            k,
            v,
            ct,
            row_decay,
            row_coefs,
            skip,
            other,
            from_scan,
            conv,
            kept["conv"],
            after,
        )
        return token

    def adjoint_outputs(after):
        results = (
            pl.pallas_call(
                partial(adjoint_kernel, modes),
                in_specs=[VMEM] * 14,
                out_specs=[HBM] * 2 + [VMEM] * 4,
                out_shape=[line_shape] * 2 + [whole] + [early_shape] * 2 + [rows(8)],
                scratch_shapes=[pltpu.SemaphoreType.DMA((3,))],
                compiler_params=KERNEL,
                cost_estimate=pl.CostEstimate(
                    flops=2 * elements, bytes_accessed=8 * seq * channels, transcendentals=0
                ),
                name="adjoint_outputs",
            )(
                q,
                k,
                v,
                ct,
                row_decay,
                row_coefs,
                skip,
                other,
                from_scan,
                adj,
                kept["adj"],
                kept["out"],
                kept["gq"],
                after,
            )
        )
        kept["final"] = results[:-1]
        return results[-1]

    def plus(left, right, after):
        return pl.pallas_call(
            add_kernel,
            in_specs=[VMEM] * 3,
            out_shape=rows(8),
            compiler_params=KERNEL,
            name="square_sum",
        )(left, right, after)

    def tp_swap(value, bit):
        return lax.ppermute(value, "tp", [(i, i ^ (1 << bit)) for i in range(tp)])

    works = [add_own, forward_outputs, adjoint_outputs]
    rounds = [partial(tp_swap, bit=bit) for bit in range(tp.bit_length() - 1)]
    for at, exchange in enumerate(rounds + [partial(swap, bit=0)]):
        if at > 0:
            square = plus(square, share, after)
        share = exchange(square)
        after = works.pop(0)(square) if works else square
    for work in works:
        after = work(after)
    operator_out, grad_queries, scanned, early_keys, early_values = kept["final"]
    grad_residues, grad_keys, grad_values = pl.pallas_call(
        partial(last_outputs_kernel, math.sqrt(channels * tp * modes)),
        in_specs=[VMEM] * 14,
        out_specs=[HBM] * 3,
        out_shape=[table_shape] + [line_shape] * 2,
        scratch_shapes=[
            late_scratch,
            late_scratch,
            table_scratch,
            states_scratch,
            pltpu.SemaphoreType.DMA((2 * parts + 3,)),
        ],
        compiler_params=KERNEL,
        cost_estimate=pl.CostEstimate(
            flops=elements, bytes_accessed=8 * seq * channels, transcendentals=0
        ),
        name="last_outputs",
    )(
        q,
        k,
        v,
        ct,
        scanned,
        skip,
        early_keys,
        early_values,
        mine,
        other,
        from_scan,
        after,
        square,
        share,
    )
    return (operator_out, grad_queries, grad_keys, grad_values, grad_residues.T)


def solution(mesh):
    lines, tables = P("ctx", "tp"), P("tp", None)
    in_specs = (lines, lines, lines, tables, tables, P("tp"), lines)
    out_specs = (lines, lines, lines, lines, tables)
    return jax.shard_map(shards, mesh=mesh, in_specs=in_specs, out_specs=out_specs, check_vma=False)
```

```python
from functools import partial
import math

import jax
import jax.numpy as jnp
from jax import lax
from jax.experimental import pallas as pl
from jax.experimental.pallas import tpu as pltpu
from jax.sharding import PartitionSpec as P

F32 = jnp.float32
WIRE = jnp.bfloat16
LANES = 128
UNROLL = 8
STEP_ROWS = 32
KERNEL = pltpu.CompilerParams(vmem_limit_bytes=24 * 1024 * 1024)
HBM = pl.BlockSpec(memory_space=pltpu.HBM)
VMEM = pl.BlockSpec(memory_space=pltpu.VMEM)


def reorder(rows, inner):
    outer = rows // inner
    first = lax.broadcasted_iota(jnp.int32, (rows, rows), 0)
    second = lax.broadcasted_iota(jnp.int32, (rows, rows), 1)

    def matrix(to, fro):
        if inner & (inner - 1) == 0 and outer & (outer - 1) == 0:
            low, high = inner.bit_length() - 1, outer.bit_length() - 1
            same = (fro & (inner - 1)) * outer + (fro >> low) == to
        else:
            same = (fro % inner) * outer + fro // inner == to
        return jnp.where(same, 1.0, 0.0).astype(jnp.bfloat16)

    return matrix(first, second), matrix(second, first)


def tree_sum(items):
    items = list(items)
    while len(items) > 1:
        items = [
            items[i] + items[i + 1] if i + 1 < len(items) else items[i]
            for i in range(0, len(items), 2)
        ]
    return items[0]


def half_units(which, blocks, modes, sub):
    if blocks == 1:
        return [(0, which * (modes // 2 * sub), modes // 2)]
    count = blocks // 2
    return [
        (which * count + j, (which * count + j) * (modes * sub), modes) for j in range(count)
    ]


def to_scan_order(to_scan, pairs, part, i, block, targets):
    size, sub = to_scan.shape[0], to_scan.shape[0] // part
    rows = slice(i * part, (i + 1) * part)
    sides = []
    for left, right in pairs:
        stacked = []
        for s in range(sub):
            cols = pl.ds(pl.multiple_of((block * sub + s) * LANES, LANES), LANES)
            product = left[rows, cols].astype(F32) * right[rows, cols].astype(F32)
            stacked.append(product.astype(jnp.bfloat16))
        sides.append(jnp.concatenate(stacked, axis=0))
    ordered = jnp.dot(
        to_scan[...], jnp.concatenate(sides, axis=1), preferred_element_type=F32
    )
    for j, target in enumerate(targets):
        target[block, i * size : (i + 1) * size, :] = ordered[:, j * LANES : (j + 1) * LANES]


def scan_states(unit, sub, gated_ref, pulled_ref, decay_ref, out_ref, at_row):
    block, base, modes = unit
    seq = gated_ref.shape[1] // sub
    decay = [
        decay_ref[pl.ds(pl.multiple_of(base + n * sub, sub), sub), :] for n in range(modes)
    ]
    first = tuple(jnp.zeros((sub, LANES), F32) for _ in range(modes))

    def forward(j, carry):
        held, inner = list(carry[0]), list(carry[1])
        for u in range(UNROLL):
            at = pl.ds(pl.multiple_of((j * UNROLL + u) * sub, sub), sub)
            x = gated_ref[block, at, :]
            p = pulled_ref[block, at, :]
            for n in range(modes):
                held[n] = decay[n] * held[n] + x
                inner[n] = inner[n] + p * held[n]
        return tuple(held), tuple(inner)

    def backward(j, carry):
        held = list(carry)
        for u in range(UNROLL):
            at = pl.ds(pl.multiple_of((seq - 1 - (j * UNROLL + u)) * sub, sub), sub)
            p = pulled_ref[block, at, :]
            for n in range(modes):
                held[n] = decay[n] * held[n] + p
        return tuple(held)

    ends, inner = lax.fori_loop(0, seq // UNROLL, forward, (first, first))
    for n in range(modes):
        rows = slice(at_row + n * sub, at_row + (n + 1) * sub)
        out_ref[0, rows, :] = ends[n]
        out_ref[2, rows, :] = inner[n]
    starts = lax.fori_loop(0, seq // UNROLL, backward, first)
    for n in range(modes):
        out_ref[1, at_row + n * sub : at_row + (n + 1) * sub, :] = starts[n]


def send_kernel(
    q_hbm,
    k_hbm,
    v_hbm,
    ct_hbm,
    rate_hbm,
    res_hbm,
    send_ref,
    q_ref,
    k_ref,
    v_ref,
    ct_ref,
    gated_ref,
    pulled_ref,
    rate_ref,
    decay_ref,
    coef_ref,
    to_scan,
    from_scan,
    rate_cols,
    res_cols,
    sems,
):
    seq, channels = q_ref.shape
    modes = rate_cols.shape[0]
    blocks = gated_ref.shape[0]
    sub = channels // (blocks * LANES)
    part = math.gcd(seq, STEP_ROWS)
    parts = seq // part
    which = 1 - lax.axis_index("ctx") % 2
    pairs = ((k_hbm, k_ref), (v_hbm, v_ref), (ct_hbm, ct_ref), (q_hbm, q_ref))
    copies = []

    def start(source, target):
        copy = pltpu.make_async_copy(source, target, sems.at[len(copies)])
        copy.start()
        copies.append(copy)

    start(rate_hbm, rate_cols)
    start(res_hbm, res_cols)
    width = channels // min(blocks, 2)
    cols = pl.ds(pl.multiple_of(which * width, LANES) if blocks > 1 else 0, width)
    for i in range(parts):
        rows = pl.ds(i * part, part)
        for source, target in pairs:
            start(source.at[rows, cols], target.at[rows, cols])
    if blocks > 1:
        cols = pl.ds(pl.multiple_of((1 - which) * width, LANES), width)
        for source, target in pairs:
            start(source.at[:, cols], target.at[:, cols])

    def spread(source, target):
        for b in range(blocks):
            for s in range(sub):
                cols = slice((b * sub + s) * LANES, (b * sub + s + 1) * LANES)
                target[pl.ds(b * modes * sub + s, modes, stride=sub), :] = source[:, cols]

    to_scan[...], from_scan[...] = reorder(part * sub, part)
    copies[0].wait()
    spread(rate_cols, rate_ref)
    copies[1].wait()
    spread(res_cols, coef_ref)
    rate = rate_ref[...]
    decay_ref[...] = jnp.exp(-rate)
    coef_ref[...] = coef_ref[...] * jnp.sqrt(1.0 - jnp.exp(-2.0 * rate))
    units = half_units(which, blocks, modes, sub)
    lines = ((k_ref, v_ref), (ct_ref, q_ref))
    for i in range(parts):
        for copy in copies[2 + 4 * i : 6 + 4 * i]:
            copy.wait()
        for unit in units:
            to_scan_order(to_scan, lines, part, i, unit[0], (gated_ref, pulled_ref))
    for at, unit in enumerate(units):
        at_row = at * unit[2] * sub
        scan_states(unit, sub, gated_ref, pulled_ref, decay_ref, send_ref, at_row)
    for copy in copies[2 + 4 * parts :]:
        copy.wait()


def keep_kernel(
    q_ref,
    k_ref,
    v_ref,
    ct_ref,
    decay_ref,
    to_scan,
    gated_in,
    pulled_in,
    keep_ref,
    gated_ref,
    pulled_ref,
    sems,
):
    seq, channels = q_ref.shape
    blocks = gated_ref.shape[0]
    sub = channels // (blocks * LANES)
    modes = decay_ref.shape[0] // (blocks * sub)
    part = math.gcd(seq, STEP_ROWS)
    which = lax.axis_index("ctx") % 2
    count = max(blocks // 2, 1)
    done = pl.ds((1 - which) * count if blocks > 1 else 0, count)
    copies = [
        pltpu.make_async_copy(gated_in.at[done], gated_ref.at[done], sems.at[0]),
        pltpu.make_async_copy(pulled_in.at[done], pulled_ref.at[done], sems.at[1]),
    ]
    for copy in copies:
        copy.start()
    units = half_units(which, blocks, modes, sub)
    lines = (gated_in, pulled_in)
    if blocks > 1:
        lines = (gated_ref, pulled_ref)
        for i in range(seq // part):
            for unit in units:
                pairs = ((k_ref, v_ref), (ct_ref, q_ref))
                to_scan_order(to_scan, pairs, part, i, unit[0], lines)
    for at, unit in enumerate(units):
        scan_states(unit, sub, *lines, decay_ref, keep_ref, at * unit[2] * sub)
    for copy in copies:
        copy.wait()


def own_rows(rate_ref, half):
    core = lax.axis_index("ctx") % 2
    return rate_ref[pl.ds(pl.multiple_of(core * half, half), half), :]


def joined(is_right, mine, other, span, step):
    left = [jnp.where(is_right, o, m) for m, o in zip(mine, other)]
    right = [jnp.where(is_right, m, o) for m, o in zip(mine, other)]
    return (
        span * left[0] + right[0],
        left[1] + span * right[1],
        left[2] + right[2] + step * right[1] * left[0],
    )


def put_wire(wire_ref, is_last, next_right, block):
    if is_last:
        wire_ref[0] = jnp.where(next_right, block[1], block[0]).astype(wire_ref.dtype)
        wire_ref[1] = block[2].astype(wire_ref.dtype)
    else:
        for kind in range(3):
            wire_ref[kind] = block[kind].astype(wire_ref.dtype)


def pair_kernel(seq, is_last, keep_ref, got_ref, rate_ref, after_ref, block_ref, wire_ref):
    rate = own_rows(rate_ref, keep_ref.shape[1])
    place = lax.axis_index("ctx")
    block = joined(
        place % 2 == 1,
        [keep_ref[i] for i in range(3)],
        [got_ref[i] for i in range(3)],
        jnp.exp(-rate * seq),
        jnp.exp(-rate),
    )
    for kind in range(3):
        block_ref[kind] = block[kind]
    block_ref[3] = jnp.zeros_like(rate)
    block_ref[4] = jnp.zeros_like(rate)
    put_wire(wire_ref, is_last, (place // 2) % 2 == 1, block)


def carries_with(block_ref, end_state, start_state, level, seq, rate):
    place = lax.axis_index("ctx")
    is_right = (place >> level) % 2 == 1
    chips = 1 << (level - 1)
    at = (place // 2) % chips
    before = at * (2 * seq)
    behind = (chips - 1 - at) * (2 * seq)
    ahead = block_ref[3] + jnp.where(
        is_right, jnp.exp(-rate * before.astype(F32)) * end_state, 0.0
    )
    after = block_ref[4] + jnp.where(
        is_right, 0.0, jnp.exp(-rate * behind.astype(F32)) * start_state
    )
    return is_right, ahead, after


def level_kernel(
    seq, level, is_last, block_ref, got_ref, rate_ref, after_ref, out_ref, wire_ref
):
    rate = own_rows(rate_ref, block_ref.shape[1])
    got = [got_ref[i].astype(F32) for i in range(3)]
    is_right, ahead, after = carries_with(block_ref, got[0], got[1], level, seq, rate)
    block = joined(
        is_right,
        [block_ref[i] for i in range(3)],
        got,
        jnp.exp(-rate * (seq << level)),
        jnp.exp(-rate),
    )
    for kind in range(3):
        out_ref[kind] = block[kind]
    out_ref[3] = ahead
    out_ref[4] = after
    next_right = (lax.axis_index("ctx") >> (level + 1)) % 2 == 1
    put_wire(wire_ref, is_last, next_right, block)


def last_kernel(
    seq,
    level,
    block_ref,
    got_ref,
    rate_ref,
    keep_ref,
    sibling_ref,
    after_ref,
    mine_ref,
    other_ref,
    share_ref,
):
    half = block_ref.shape[1]
    rate = own_rows(rate_ref, half)
    edge, inner = got_ref[0].astype(F32), got_ref[1].astype(F32)
    is_right, ahead, after = carries_with(block_ref, edge, edge, level, seq, rate)
    own_edge = jnp.where(is_right, block_ref[1], block_ref[0])
    total = block_ref[2] + inner + jnp.exp(-rate) * own_edge * edge
    raw = jnp.sqrt(1.0 - jnp.exp(-2.0 * rate)) * total
    core = lax.axis_index("ctx") % 2
    first = core == 0
    span = jnp.exp(-rate * seq)
    end_first = jnp.where(first, keep_ref[0], sibling_ref[0])
    start_second = jnp.where(first, sibling_ref[1], keep_ref[1])
    ahead_second = span * ahead + end_first
    after_first = span * after + start_second
    mine_ref[0:half, :] = jnp.where(first, ahead, ahead_second)
    mine_ref[half : 2 * half, :] = jnp.where(first, after_first, after)
    other_ref[0:half, :] = jnp.where(first, ahead_second, ahead)
    other_ref[half : 2 * half, :] = jnp.where(first, after, after_first)
    squares = raw * raw
    share_ref[...] = tree_sum([squares[i : i + 8, :] for i in range(0, half, 8)])
    mine_ref[2 * half : 3 * half, :] = raw
    other_ref[2 * half : 3 * half, :] = raw


def place_halves(mine_ref, other_ref, first, target):
    half = target.shape[0] // 2
    core = lax.axis_index("ctx") % 2
    for ref, at in ((mine_ref, core), (other_ref, 1 - core)):
        rows = pl.ds(pl.multiple_of(at * half, half), half)
        target[rows, :] = ref[first : first + half, :]


def mode_rows(block, modes, sub):
    return [slice((block * modes + n) * sub, (block * modes + n + 1) * sub) for n in range(modes)]


def local_kernel(reverse, modes, lines_ref, decay_ref, coef_ref, after_ref, out_ref):
    blocks = lines_ref.shape[0]
    sub = decay_ref.shape[0] // (blocks * modes)
    seq = lines_ref.shape[1] // sub
    for b in range(blocks):
        rows = mode_rows(b, modes, sub)
        decay = [decay_ref[r, :] for r in rows]
        coef = [coef_ref[r, :] for r in rows]

        def body(j, carry):
            held = list(carry)
            for u in range(UNROLL):
                t = j * UNROLL + u
                if reverse:
                    t = seq - 1 - t
                at = pl.ds(pl.multiple_of(t * sub, sub), sub)
                x = lines_ref[b, at, :]
                total = [None] * 4
                for n in range(modes):
                    held[n] = decay[n] * held[n] + x
                    term = coef[n] * held[n]
                    total[n % 4] = term if n < 4 else total[n % 4] + term
                out_ref[b, at, :] = tree_sum(total)
            return tuple(held)

        first = tuple(jnp.zeros((sub, LANES), F32) for _ in range(modes))
        lax.fori_loop(0, seq // UNROLL, body, first)


def add_carries(reverse, unit, sub, decay_ref, coef_ref, states_ref, at_row, source, target, at):
    _, base, modes = unit
    seq = target.shape[1] // sub
    rows = [pl.ds(pl.multiple_of(base + n * sub, sub), sub) for n in range(modes)]
    decay = [decay_ref[r, :] for r in rows]
    first = tuple(
        coef_ref[r, :] * states_ref[at_row + n * sub : at_row + (n + 1) * sub, :]
        for n, r in enumerate(rows)
    )

    def body(j, carry):
        held = list(carry)
        for u in range(UNROLL):
            t = j * UNROLL + u
            if reverse:
                t = seq - 1 - t
            where = pl.ds(pl.multiple_of(t * sub, sub), sub)
            total = [source[where, :], None, None, None]
            for n in range(modes):
                held[n] = decay[n] * held[n]
                total[n % 4] = held[n] if total[n % 4] is None else total[n % 4] + held[n]
            target[at, where, :] = tree_sum(total)
        return tuple(held)

    lax.fori_loop(0, seq // UNROLL, body, first)


def own_kernel(modes, conv_ref, adj_ref, decay_ref, coef_ref, mine_ref, conv_own, adj_own):
    blocks = conv_ref.shape[0]
    sub = decay_ref.shape[0] // (blocks * modes)
    half = decay_ref.shape[0] // 2
    core = lax.axis_index("ctx") % 2
    for i, unit in enumerate(half_units(core, blocks, modes, sub)):
        at_row = i * unit[2] * sub
        for reverse, source, target in ((False, conv_ref, conv_own), (True, adj_ref, adj_own)):
            add_carries(
                reverse,
                unit,
                sub,
                decay_ref,
                coef_ref,
                mine_ref,
                at_row + half * reverse,
                source.at[unit[0]],
                target,
                i,
            )


def other_carries(reverse, modes, decay_ref, coef_ref, other_ref, local_ref, own_ref, whole, sem):
    blocks, own_blocks = local_ref.shape[0], own_ref.shape[0]
    sub = decay_ref.shape[0] // (blocks * modes)
    half = decay_ref.shape[0] // 2
    core = lax.axis_index("ctx") % 2
    copy = pltpu.make_async_copy(own_ref, whole.at[pl.ds(core * own_blocks, own_blocks)], sem)
    if blocks > 1:
        copy.start()
    for i, unit in enumerate(half_units(1 - core, blocks, modes, sub)):
        source = local_ref.at[unit[0]] if blocks > 1 else own_ref.at[0]
        at_row = i * unit[2] * sub + half * reverse
        add_carries(
            reverse, unit, sub, decay_ref, coef_ref, other_ref, at_row, source, whole, unit[0]
        )
    if blocks > 1:
        copy.wait()


def line_outputs(
    from_scan, left, right, scales, skip_ref, scanned, targets, which, done_with=None
):
    seq, channels = left.shape
    blocks = scanned.shape[0]
    sub = channels // (blocks * LANES)
    part = math.gcd(seq, STEP_ROWS)
    for i in which:
        rows = slice(i * part, (i + 1) * part)
        to_rows = slice((i - which[0]) * part, (i - which[0] + 1) * part)
        stacked = jnp.concatenate(
            [scanned[b, i * part * sub : (i + 1) * part * sub, :] for b in range(blocks)], axis=1
        ).astype(jnp.bfloat16)
        ordered = jnp.dot(from_scan[...], stacked, preferred_element_type=F32)
        for b in range(blocks):
            for s in range(sub):
                cols = slice((b * sub + s) * LANES, (b * sub + s + 1) * LANES)
                own = ordered[s * part : (s + 1) * part, b * LANES : (b + 1) * LANES]
                line = left[rows, cols].astype(F32) * right[rows, cols].astype(F32)
                mixed = own + skip_ref[:, cols] * line.astype(jnp.bfloat16).astype(F32)
                for scale, target in zip(scales, targets):
                    target[to_rows, cols] = (scale[rows, cols].astype(F32) * mixed).astype(
                        jnp.bfloat16
                    )
        if done_with is not None:
            done_with(pl.ds((i - which[0]) * part, part), pl.ds(i * part, part))


def forward_kernel(
    modes,
    q_ref,
    k_ref,
    v_ref,
    ct_ref,
    decay_ref,
    coef_ref,
    skip_ref,
    other_ref,
    from_scan,
    conv_ref,
    conv_own,
    after_ref,
    out_ref,
    gq_ref,
    token_ref,
    scanned,
    sem,
):
    token_ref[...] = jnp.zeros_like(token_ref)
    other_carries(
        False, modes, decay_ref, coef_ref, other_ref, conv_ref, conv_own, scanned, sem
    )
    line_outputs(
        from_scan,
        k_ref,
        v_ref,
        (q_ref, ct_ref),
        skip_ref,
        scanned,
        (out_ref, gq_ref),
        range(k_ref.shape[0] // math.gcd(k_ref.shape[0], STEP_ROWS)),
    )


def early_parts(seq):
    parts = seq // math.gcd(seq, STEP_ROWS)
    return range((parts + 1) // 2), range((parts + 1) // 2, parts)


def adjoint_kernel(
    modes,
    q_ref,
    k_ref,
    v_ref,
    ct_ref,
    decay_ref,
    coef_ref,
    skip_ref,
    other_ref,
    from_scan,
    adj_ref,
    adj_own,
    out_rows,
    gq_rows,
    after_ref,
    out_hbm,
    gq_hbm,
    scanned,
    gk_ref,
    gv_ref,
    token_ref,
    sems,
):
    token_ref[...] = jnp.zeros_like(token_ref)
    copies = [
        pltpu.make_async_copy(out_rows, out_hbm, sems.at[0]),
        pltpu.make_async_copy(gq_rows, gq_hbm, sems.at[1]),
    ]
    for copy in copies:
        copy.start()
    other_carries(
        True, modes, decay_ref, coef_ref, other_ref, adj_ref, adj_own, scanned, sems.at[2]
    )
    line_outputs(
        from_scan,
        ct_ref,
        q_ref,
        (v_ref, k_ref),
        skip_ref,
        scanned,
        (gk_ref, gv_ref),
        early_parts(q_ref.shape[0])[0],
    )
    for copy in copies:
        copy.wait()


def last_outputs_kernel(limit, *refs):
    q_ref, k_ref, v_ref, ct_ref, scanned, skip_ref, gk_early, gv_early = refs[:8]
    mine_ref, other_ref, from_scan = refs[8:11]
    share_refs = refs[12:-8]
    raw_hbm, gk_hbm, gv_hbm, gk_rows, gv_rows, raw_cols, states, sems = refs[-8:]
    copies = []

    def start(source, target):
        copy = pltpu.make_async_copy(source, target, sems.at[len(copies)])
        copy.start()
        copies.append(copy)

    early = pl.ds(0, gk_early.shape[0])
    start(gk_early, gk_hbm.at[early])
    start(gv_early, gv_hbm.at[early])
    clip(limit, scanned.shape[0], mine_ref, other_ref, share_refs, raw_cols, states)
    start(raw_cols, raw_hbm)

    def send(at, to):
        start(gk_rows.at[at], gk_hbm.at[to])
        start(gv_rows.at[at], gv_hbm.at[to])

    late = early_parts(q_ref.shape[0])[1]
    if len(late) > 0:
        sides, targets = (v_ref, k_ref), (gk_rows, gv_rows)
        line_outputs(
            from_scan, ct_ref, q_ref, sides, skip_ref, scanned, targets, late, send
        )
    for copy in copies:
        copy.wait()


def add_kernel(after_ref, *refs):
    refs[-1][...] = tree_sum([ref[...] for ref in refs[:-1]])


def clip(limit, blocks, mine_ref, other_ref, share_refs, out_ref, states):
    modes = out_ref.shape[0]
    sub = out_ref.shape[1] // (blocks * LANES)
    half = states.shape[0] // 2
    place_halves(mine_ref, other_ref, 2 * half, states)
    square = jnp.sum(tree_sum([ref[...] for ref in share_refs]))
    factor = jnp.minimum(1.0, limit * lax.rsqrt(jnp.full((1, LANES), square + 1e-06, F32)))
    for b in range(blocks):
        for s in range(sub):
            cols = slice((b * sub + s) * LANES, (b * sub + s + 1) * LANES)
            rows = pl.ds(b * modes * sub + s, modes, stride=sub)
            out_ref[:, cols] = states[rows, :] * factor


def shards(queries, keys_in, values_in, decay_rates, residues, skip_gain, cotangent):
    seq, channels = queries.shape
    modes = decay_rates.shape[1]
    ctx = lax.axis_size("ctx")
    tp = lax.axis_size("tp")
    levels = ctx.bit_length() - 1
    groups = channels // LANES
    sub = math.gcd(groups, 8)
    blocks = groups // sub
    half = modes * groups // 2
    part = math.gcd(seq, STEP_ROWS)
    parts, size = seq // part, part * sub

    def swap(value, bit):
        return lax.ppermute(value, "ctx", [(i, i ^ (1 << bit)) for i in range(ctx)])

    def rows(*shape, dtype=F32):
        return jax.ShapeDtypeStruct((*shape, LANES), dtype)

    line_shape = jax.ShapeDtypeStruct((seq, channels), jnp.bfloat16)
    table_shape = jax.ShapeDtypeStruct((modes, channels), F32)
    line_scratch = pltpu.VMEM((seq, channels), jnp.bfloat16)
    table_scratch = pltpu.VMEM((modes, channels), F32)
    elements = seq * channels * modes
    sources = (queries, keys_in, values_in, cotangent, decay_rates.T, residues.T)

    (
        send,
        q,
        k,
        v,
        ct,
        gated,
        pulled,
        row_rates,
        row_decay,
        row_coefs,
        to_scan,
        from_scan,
    ) = pl.pallas_call(
        send_kernel,
        in_specs=[HBM] * 6,
        out_specs=[VMEM] * 12,
        out_shape=[rows(3, half)]
        + [line_shape] * 4
        + [rows(blocks, seq * sub)] * 2
        + [rows(2 * half)] * 3
        + [jax.ShapeDtypeStruct((size, size), jnp.bfloat16)] * 2,
        scratch_shapes=[
            table_scratch,
            table_scratch,
            pltpu.SemaphoreType.DMA((4 * parts + 6,)),
        ],
        compiler_params=KERNEL,
        cost_estimate=pl.CostEstimate(
            flops=3 * elements, bytes_accessed=8 * seq * channels, transcendentals=0
        ),
        name="sent_states",
    )(*[pltpu.with_memory_space_constraint(item, pltpu.HBM) for item in sources])
    sibling = swap(send, 0)
    keep, gated, pulled = pl.pallas_call(
        keep_kernel,
        out_shape=[rows(3, half)] + [rows(blocks, seq * sub)] * 2,
        scratch_shapes=[pltpu.SemaphoreType.DMA((2,))],
        compiler_params=KERNEL,
        cost_estimate=pl.CostEstimate(
            flops=3 * elements, bytes_accessed=8 * seq * channels, transcendentals=0
        ),
        name="kept_states",
    )(q, k, v, ct, row_decay, to_scan, gated, pulled)

    def wire(level):
        return rows(2 if level == levels - 1 else 3, half, dtype=WIRE)

    whole = rows(blocks, seq * sub)
    whole_scratch = pltpu.VMEM((blocks, seq * sub, LANES), F32)
    states_scratch = pltpu.VMEM((2 * half, LANES), F32)
    def local(reverse, after, name):
        return pl.pallas_call(
            partial(local_kernel, reverse, modes),
            out_shape=whole,
            compiler_params=KERNEL,
            cost_estimate=pl.CostEstimate(
                flops=4 * elements, bytes_accessed=8 * seq * channels, transcendentals=0
            ),
            name=name,
        )(pulled if reverse else gated, row_decay, row_coefs, after)

    block, packed = pl.pallas_call(
        partial(pair_kernel, seq, levels == 2),
        out_shape=[rows(5, half), wire(1)],
        compiler_params=KERNEL,
        name="chip_states",
    )(keep, sibling, row_rates, row_rates[:8])
    got = swap(packed, 1)
    conv = local(False, block[4, :8], "local_conv")
    for level in range(1, levels - 1):
        block, packed = pl.pallas_call(
            partial(level_kernel, seq, level, level + 1 == levels - 1),
            out_shape=[rows(5, half), wire(level + 1)],
            compiler_params=KERNEL,
            name="block_states",
        )(block, got, row_rates, conv[0, :8])
        got = swap(packed, level + 1)
    adj = local(True, block[4, :8], "local_adjoint")
    mine, other, square = pl.pallas_call(
        partial(last_kernel, seq, levels - 1),
        out_shape=[rows(3 * half)] * 2 + [rows(8)],
        compiler_params=KERNEL,
        name="carries",
    )(block, got, row_rates, keep, sibling, adj[0, :8])
    other = swap(other, 0)
    skip = skip_gain.reshape(1, channels)
    early, late = early_parts(seq)
    early_shape = jax.ShapeDtypeStruct((seq * len(early) // parts, channels), jnp.bfloat16)
    late_scratch = pltpu.VMEM((seq * max(len(late), 1) // parts, channels), jnp.bfloat16)
    own_shape = rows(max(blocks // 2, 1), seq * sub)
    kept = {}

    def add_own(after):
        kept["conv"], kept["adj"] = pl.pallas_call(
            partial(own_kernel, modes),
            out_shape=[own_shape] * 2,
            compiler_params=KERNEL,
            cost_estimate=pl.CostEstimate(
                flops=2 * elements, bytes_accessed=8 * seq * channels, transcendentals=0
            ),
            name="own_carries",
        )(conv, adj, row_decay, row_coefs, mine)
        return kept["adj"][0, :8]

    def forward_outputs(after):
        kept["out"], kept["gq"], token = pl.pallas_call(
            partial(forward_kernel, modes),
            out_shape=[line_shape] * 2 + [rows(8)],
            scratch_shapes=[whole_scratch, pltpu.SemaphoreType.DMA],
            compiler_params=KERNEL,
            cost_estimate=pl.CostEstimate(
                flops=2 * elements, bytes_accessed=16 * seq * channels, transcendentals=0
            ),
            name="forward_outputs",
        )(
            q,
            k,
            v,
            ct,
            row_decay,
            row_coefs,
            skip,
            other,
            from_scan,
            conv,
            kept["conv"],
            after,
        )
        return token

    def adjoint_outputs(after):
        results = (
            pl.pallas_call(
                partial(adjoint_kernel, modes),
                in_specs=[VMEM] * 14,
                out_specs=[HBM] * 2 + [VMEM] * 4,
                out_shape=[line_shape] * 2 + [whole] + [early_shape] * 2 + [rows(8)],
                scratch_shapes=[pltpu.SemaphoreType.DMA((3,))],
                compiler_params=KERNEL,
                cost_estimate=pl.CostEstimate(
                    flops=2 * elements, bytes_accessed=8 * seq * channels, transcendentals=0
                ),
                name="adjoint_outputs",
            )(
                q,
                k,
                v,
                ct,
                row_decay,
                row_coefs,
                skip,
                other,
                from_scan,
                adj,
                kept["adj"],
                kept["out"],
                kept["gq"],
                after,
            )
        )
        kept["final"] = results[:-1]
        return results[-1]

    def plus(after, *shares):
        return pl.pallas_call(
            add_kernel,
            in_specs=[VMEM] * (1 + len(shares)),
            out_shape=rows(8),
            compiler_params=KERNEL,
            name="square_sum",
        )(after, *shares)

    def tp_swap(value, mask):
        return lax.ppermute(value, "tp", [(i, i ^ mask) for i in range(tp)])

    works = [add_own, forward_outputs]
    for bit in range(0, tp.bit_length() - 1, 2):
        masks = [m << bit for m in (1, 2, 3) if m << bit < tp]
        shares = [tp_swap(square, mask) for mask in masks]
        after = square
        while works:
            after = works.pop(0)(after)
        square = plus(after, square, *shares)
    share = swap(square, 0)
    after = square
    for work in works + [adjoint_outputs]:
        after = work(after)
    operator_out, grad_queries, scanned, early_keys, early_values = kept["final"]
    grad_residues, grad_keys, grad_values = pl.pallas_call(
        partial(last_outputs_kernel, math.sqrt(channels * tp * modes)),
        in_specs=[VMEM] * 14,
        out_specs=[HBM] * 3,
        out_shape=[table_shape] + [line_shape] * 2,
        scratch_shapes=[
            late_scratch,
            late_scratch,
            table_scratch,
            states_scratch,
            pltpu.SemaphoreType.DMA((2 * parts + 3,)),
        ],
        compiler_params=KERNEL,
        cost_estimate=pl.CostEstimate(
            flops=elements, bytes_accessed=8 * seq * channels, transcendentals=0
        ),
        name="last_outputs",
    )(
        q,
        k,
        v,
        ct,
        scanned,
        skip,
        early_keys,
        early_values,
        mine,
        other,
        from_scan,
        after,
        square,
        share,
    )
    return (operator_out, grad_queries, grad_keys, grad_values, grad_residues.T)


def solution(mesh):
    lines, tables = P("ctx", "tp"), P("tp", None)
    in_specs = (lines, lines, lines, tables, tables, P("tp"), lines)
    out_specs = (lines, lines, lines, lines, tables)
    return jax.shard_map(shards, mesh=mesh, in_specs=in_specs, out_specs=out_specs, check_vma=False)
```

```python
from functools import partial
import math

import jax
import jax.numpy as jnp
from jax import lax
from jax.experimental import pallas as pl
from jax.experimental.pallas import tpu as pltpu
from jax.sharding import PartitionSpec as P

F32 = jnp.float32
WIRE = jnp.bfloat16
LANES = 128
UNROLL = 8
STEP_ROWS = 32
KERNEL = pltpu.CompilerParams(vmem_limit_bytes=24 * 1024 * 1024)
HBM = pl.BlockSpec(memory_space=pltpu.HBM)
VMEM = pl.BlockSpec(memory_space=pltpu.VMEM)


def reorder(rows, inner):
    outer = rows // inner
    first = lax.broadcasted_iota(jnp.int32, (rows, rows), 0)
    second = lax.broadcasted_iota(jnp.int32, (rows, rows), 1)

    def matrix(to, fro):
        if inner & (inner - 1) == 0 and outer & (outer - 1) == 0:
            low, high = inner.bit_length() - 1, outer.bit_length() - 1
            same = (fro & (inner - 1)) * outer + (fro >> low) == to
        else:
            same = (fro % inner) * outer + fro // inner == to
        return jnp.where(same, 1.0, 0.0).astype(jnp.bfloat16)

    return matrix(first, second), matrix(second, first)


def tree_sum(items):
    items = list(items)
    while len(items) > 1:
        items = [
            items[i] + items[i + 1] if i + 1 < len(items) else items[i]
            for i in range(0, len(items), 2)
        ]
    return items[0]


def spread(source, target, modes, sub):
    for group in range(source.shape[1] // LANES):
        cols = slice(group * LANES, (group + 1) * LANES)
        first = group // sub * (modes * sub) + group % sub
        target[pl.ds(first, modes, stride=sub), :] = source[:, cols]


def half_units(which, blocks, modes, sub):
    if blocks == 1:
        return [(0, which * (modes // 2 * sub), modes // 2)]
    count = blocks // 2
    return [
        (which * count + j, (which * count + j) * (modes * sub), modes) for j in range(count)
    ]


def to_scan_order(to_scan, pairs, part, i, block, targets):
    size, sub = to_scan.shape[0], to_scan.shape[0] // part
    rows = slice(i * part, (i + 1) * part)
    sides = []
    for left, right in pairs:
        stacked = []
        for s in range(sub):
            cols = pl.ds(pl.multiple_of((block * sub + s) * LANES, LANES), LANES)
            product = left[rows, cols].astype(F32) * right[rows, cols].astype(F32)
            stacked.append(product.astype(jnp.bfloat16))
        sides.append(jnp.concatenate(stacked, axis=0))
    ordered = jnp.dot(
        to_scan[...], jnp.concatenate(sides, axis=1), preferred_element_type=F32
    )
    for j, target in enumerate(targets):
        target[block, i * size : (i + 1) * size, :] = ordered[:, j * LANES : (j + 1) * LANES]


def scan_states(unit, sub, gated_ref, pulled_ref, decay_ref, out_ref, at_row):
    block, base, modes = unit
    seq = gated_ref.shape[1] // sub
    decay = [
        decay_ref[pl.ds(pl.multiple_of(base + n * sub, sub), sub), :] for n in range(modes)
    ]
    first = tuple(jnp.zeros((sub, LANES), F32) for _ in range(modes))

    def forward(j, carry):
        held, inner = list(carry[0]), list(carry[1])
        for u in range(UNROLL):
            at = pl.ds(pl.multiple_of((j * UNROLL + u) * sub, sub), sub)
            x = gated_ref[block, at, :]
            p = pulled_ref[block, at, :]
            for n in range(modes):
                held[n] = decay[n] * held[n] + x
                inner[n] = inner[n] + p * held[n]
        return tuple(held), tuple(inner)

    def backward(j, carry):
        held = list(carry)
        for u in range(UNROLL):
            at = pl.ds(pl.multiple_of((seq - 1 - (j * UNROLL + u)) * sub, sub), sub)
            p = pulled_ref[block, at, :]
            for n in range(modes):
                held[n] = decay[n] * held[n] + p
        return tuple(held)

    ends, inner = lax.fori_loop(0, seq // UNROLL, forward, (first, first))
    for n in range(modes):
        rows = slice(at_row + n * sub, at_row + (n + 1) * sub)
        out_ref[0, rows, :] = ends[n]
        out_ref[2, rows, :] = inner[n]
    starts = lax.fori_loop(0, seq // UNROLL, backward, first)
    for n in range(modes):
        out_ref[1, at_row + n * sub : at_row + (n + 1) * sub, :] = starts[n]


def send_kernel(
    q_hbm,
    k_hbm,
    v_hbm,
    ct_hbm,
    rate_hbm,
    res_hbm,
    skip_hbm,
    send_ref,
    q_ref,
    k_ref,
    v_ref,
    ct_ref,
    gated_ref,
    pulled_ref,
    rate_ref,
    decay_ref,
    to_scan,
    from_scan,
    res_cols,
    skip_ref,
    rate_cols,
    sems,
):
    seq, channels = q_ref.shape
    modes = rate_cols.shape[0]
    blocks = gated_ref.shape[0]
    sub = channels // (blocks * LANES)
    part = math.gcd(seq, STEP_ROWS)
    parts = seq // part
    which = 1 - lax.axis_index("ctx") % 2
    pairs = ((k_hbm, k_ref), (v_hbm, v_ref), (ct_hbm, ct_ref), (q_hbm, q_ref))
    copies = []

    def start(source, target):
        copy = pltpu.make_async_copy(source, target, sems.at[len(copies)])
        copy.start()
        copies.append(copy)

    width = channels // min(blocks, 2)
    cols = pl.ds(pl.multiple_of(which * width, LANES) if blocks > 1 else 0, width)
    for i in range(parts):
        rows = pl.ds(i * part, part)
        for source, target in pairs:
            start(source.at[rows, cols], target.at[rows, cols])
    start(rate_hbm, rate_cols)
    if blocks > 1:
        cols = pl.ds(pl.multiple_of((1 - which) * width, LANES), width)
        for source, target in pairs:
            start(source.at[:, cols], target.at[:, cols])
    start(res_hbm, res_cols)
    start(skip_hbm, skip_ref)
    to_scan[...], from_scan[...] = reorder(part * sub, part)
    units = half_units(which, blocks, modes, sub)
    lines = ((k_ref, v_ref), (ct_ref, q_ref))
    for i in range(parts):
        for copy in copies[4 * i : 4 * i + 4]:
            copy.wait()
        for unit in units:
            to_scan_order(to_scan, lines, part, i, unit[0], (gated_ref, pulled_ref))
    copies[4 * parts].wait()
    spread(rate_cols, rate_ref, modes, sub)
    decay_ref[...] = jnp.exp(-rate_ref[...])
    for at, unit in enumerate(units):
        at_row = at * unit[2] * sub
        scan_states(unit, sub, gated_ref, pulled_ref, decay_ref, send_ref, at_row)
    for copy in copies[4 * parts + 1 :]:
        copy.wait()


def keep_kernel(
    q_ref,
    k_ref,
    v_ref,
    ct_ref,
    decay_ref,
    to_scan,
    gated_in,
    pulled_in,
    keep_ref,
    gated_ref,
    pulled_ref,
    sems,
):
    seq, channels = q_ref.shape
    blocks = gated_ref.shape[0]
    sub = channels // (blocks * LANES)
    modes = decay_ref.shape[0] // (blocks * sub)
    part = math.gcd(seq, STEP_ROWS)
    which = lax.axis_index("ctx") % 2
    count = max(blocks // 2, 1)
    done = pl.ds((1 - which) * count if blocks > 1 else 0, count)
    copies = [
        pltpu.make_async_copy(gated_in.at[done], gated_ref.at[done], sems.at[0]),
        pltpu.make_async_copy(pulled_in.at[done], pulled_ref.at[done], sems.at[1]),
    ]
    for copy in copies:
        copy.start()
    units = half_units(which, blocks, modes, sub)
    lines = (gated_in, pulled_in)
    if blocks > 1:
        lines = (gated_ref, pulled_ref)
        for i in range(seq // part):
            for unit in units:
                pairs = ((k_ref, v_ref), (ct_ref, q_ref))
                to_scan_order(to_scan, pairs, part, i, unit[0], lines)
    for at, unit in enumerate(units):
        scan_states(unit, sub, *lines, decay_ref, keep_ref, at * unit[2] * sub)
    for copy in copies:
        copy.wait()


def own_rows(rate_ref, half):
    core = lax.axis_index("ctx") % 2
    return rate_ref[pl.ds(pl.multiple_of(core * half, half), half), :]


def joined(is_right, mine, other, span, step):
    left = [jnp.where(is_right, o, m) for m, o in zip(mine, other)]
    right = [jnp.where(is_right, m, o) for m, o in zip(mine, other)]
    return (
        span * left[0] + right[0],
        left[1] + span * right[1],
        left[2] + right[2] + step * right[1] * left[0],
    )


def put_wire(wire_ref, is_last, next_right, block):
    if is_last:
        wire_ref[0] = jnp.where(next_right, block[1], block[0]).astype(wire_ref.dtype)
        wire_ref[1] = block[2].astype(wire_ref.dtype)
    else:
        for kind in range(3):
            wire_ref[kind] = block[kind].astype(wire_ref.dtype)


def pair_kernel(seq, is_last, keep_ref, got_ref, rate_ref, after_ref, block_ref, wire_ref):
    rate = own_rows(rate_ref, keep_ref.shape[1])
    place = lax.axis_index("ctx")
    block = joined(
        place % 2 == 1,
        [keep_ref[i] for i in range(3)],
        [got_ref[i] for i in range(3)],
        jnp.exp(-rate * seq),
        jnp.exp(-rate),
    )
    for kind in range(3):
        block_ref[kind] = block[kind]
    block_ref[3] = jnp.zeros_like(rate)
    block_ref[4] = jnp.zeros_like(rate)
    put_wire(wire_ref, is_last, (place // 2) % 2 == 1, block)


def carries_with(block_ref, end_state, start_state, level, seq, rate):
    place = lax.axis_index("ctx")
    is_right = (place >> level) % 2 == 1
    chips = 1 << (level - 1)
    at = (place // 2) % chips
    before = at * (2 * seq)
    behind = (chips - 1 - at) * (2 * seq)
    ahead = block_ref[3] + jnp.where(
        is_right, jnp.exp(-rate * before.astype(F32)) * end_state, 0.0
    )
    after = block_ref[4] + jnp.where(
        is_right, 0.0, jnp.exp(-rate * behind.astype(F32)) * start_state
    )
    return is_right, ahead, after


def level_kernel(
    seq, level, is_last, block_ref, got_ref, rate_ref, after_ref, out_ref, wire_ref
):
    rate = own_rows(rate_ref, block_ref.shape[1])
    got = [got_ref[i].astype(F32) for i in range(3)]
    is_right, ahead, after = carries_with(block_ref, got[0], got[1], level, seq, rate)
    block = joined(
        is_right,
        [block_ref[i] for i in range(3)],
        got,
        jnp.exp(-rate * (seq << level)),
        jnp.exp(-rate),
    )
    for kind in range(3):
        out_ref[kind] = block[kind]
    out_ref[3] = ahead
    out_ref[4] = after
    next_right = (lax.axis_index("ctx") >> (level + 1)) % 2 == 1
    put_wire(wire_ref, is_last, next_right, block)


def last_kernel(
    seq,
    level,
    block_ref,
    got_ref,
    rate_ref,
    keep_ref,
    sibling_ref,
    after_ref,
    mine_ref,
    other_ref,
    share_ref,
):
    half = block_ref.shape[1]
    rate = own_rows(rate_ref, half)
    edge, inner = got_ref[0].astype(F32), got_ref[1].astype(F32)
    is_right, ahead, after = carries_with(block_ref, edge, edge, level, seq, rate)
    own_edge = jnp.where(is_right, block_ref[1], block_ref[0])
    total = block_ref[2] + inner + jnp.exp(-rate) * own_edge * edge
    raw = jnp.sqrt(1.0 - jnp.exp(-2.0 * rate)) * total
    core = lax.axis_index("ctx") % 2
    first = core == 0
    span = jnp.exp(-rate * seq)
    end_first = jnp.where(first, keep_ref[0], sibling_ref[0])
    start_second = jnp.where(first, sibling_ref[1], keep_ref[1])
    ahead_second = span * ahead + end_first
    after_first = span * after + start_second
    mine_ref[0:half, :] = jnp.where(first, ahead, ahead_second)
    mine_ref[half : 2 * half, :] = jnp.where(first, after_first, after)
    other_ref[0:half, :] = jnp.where(first, ahead_second, ahead)
    other_ref[half : 2 * half, :] = jnp.where(first, after, after_first)
    squares = raw * raw
    share_ref[...] = tree_sum([squares[i : i + 8, :] for i in range(0, half, 8)])
    mine_ref[2 * half : 3 * half, :] = raw
    other_ref[2 * half : 3 * half, :] = raw


def place_halves(mine_ref, other_ref, first, target):
    half = target.shape[0] // 2
    core = lax.axis_index("ctx") % 2
    for ref, at in ((mine_ref, core), (other_ref, 1 - core)):
        rows = pl.ds(pl.multiple_of(at * half, half), half)
        target[rows, :] = ref[first : first + half, :]


def mode_rows(block, modes, sub):
    return [slice((block * modes + n) * sub, (block * modes + n + 1) * sub) for n in range(modes)]


def first_local_kernel(modes, lines_ref, decay_ref, rate_ref, res_cols, after_ref, out_ref, coef_ref):
    sub = decay_ref.shape[0] // (lines_ref.shape[0] * modes)
    spread(res_cols, coef_ref, modes, sub)
    coef_ref[...] = coef_ref[...] * jnp.sqrt(1.0 - jnp.exp(-2.0 * rate_ref[...]))
    local_kernel(False, modes, lines_ref, decay_ref, coef_ref, after_ref, out_ref)


def local_kernel(reverse, modes, lines_ref, decay_ref, coef_ref, after_ref, out_ref):
    blocks = lines_ref.shape[0]
    sub = decay_ref.shape[0] // (blocks * modes)
    seq = lines_ref.shape[1] // sub
    for b in range(blocks):
        rows = mode_rows(b, modes, sub)
        decay = [decay_ref[r, :] for r in rows]
        coef = [coef_ref[r, :] for r in rows]

        def body(j, carry):
            held = list(carry)
            for u in range(UNROLL):
                t = j * UNROLL + u
                if reverse:
                    t = seq - 1 - t
                at = pl.ds(pl.multiple_of(t * sub, sub), sub)
                x = lines_ref[b, at, :]
                total = [None] * 4
                for n in range(modes):
                    held[n] = decay[n] * held[n] + x
                    term = coef[n] * held[n]
                    total[n % 4] = term if n < 4 else total[n % 4] + term
                out_ref[b, at, :] = tree_sum(total)
            return tuple(held)

        first = tuple(jnp.zeros((sub, LANES), F32) for _ in range(modes))
        lax.fori_loop(0, seq // UNROLL, body, first)


def add_carries(reverse, unit, sub, decay_ref, coef_ref, states_ref, at_row, source, target, at):
    _, base, modes = unit
    seq = target.shape[1] // sub
    rows = [pl.ds(pl.multiple_of(base + n * sub, sub), sub) for n in range(modes)]
    decay = [decay_ref[r, :] for r in rows]
    first = tuple(
        coef_ref[r, :] * states_ref[at_row + n * sub : at_row + (n + 1) * sub, :]
        for n, r in enumerate(rows)
    )

    def body(j, carry):
        held = list(carry)
        for u in range(UNROLL):
            t = j * UNROLL + u
            if reverse:
                t = seq - 1 - t
            where = pl.ds(pl.multiple_of(t * sub, sub), sub)
            total = [source[where, :], None, None, None]
            for n in range(modes):
                held[n] = decay[n] * held[n]
                total[n % 4] = held[n] if total[n % 4] is None else total[n % 4] + held[n]
            target[at, where, :] = tree_sum(total)
        return tuple(held)

    lax.fori_loop(0, seq // UNROLL, body, first)


def own_kernel(modes, conv_ref, adj_ref, decay_ref, coef_ref, mine_ref, conv_own, adj_own):
    blocks = conv_ref.shape[0]
    sub = decay_ref.shape[0] // (blocks * modes)
    half = decay_ref.shape[0] // 2
    core = lax.axis_index("ctx") % 2
    for i, unit in enumerate(half_units(core, blocks, modes, sub)):
        at_row = i * unit[2] * sub
        for reverse, source, target in ((False, conv_ref, conv_own), (True, adj_ref, adj_own)):
            add_carries(
                reverse,
                unit,
                sub,
                decay_ref,
                coef_ref,
                mine_ref,
                at_row + half * reverse,
                source.at[unit[0]],
                target,
                i,
            )


def other_carries(reverse, modes, decay_ref, coef_ref, other_ref, local_ref, own_ref, whole, sem):
    blocks, own_blocks = local_ref.shape[0], own_ref.shape[0]
    sub = decay_ref.shape[0] // (blocks * modes)
    half = decay_ref.shape[0] // 2
    core = lax.axis_index("ctx") % 2
    copy = pltpu.make_async_copy(own_ref, whole.at[pl.ds(core * own_blocks, own_blocks)], sem)
    if blocks > 1:
        copy.start()
    for i, unit in enumerate(half_units(1 - core, blocks, modes, sub)):
        source = local_ref.at[unit[0]] if blocks > 1 else own_ref.at[0]
        at_row = i * unit[2] * sub + half * reverse
        add_carries(
            reverse, unit, sub, decay_ref, coef_ref, other_ref, at_row, source, whole, unit[0]
        )
    if blocks > 1:
        copy.wait()


def line_outputs(
    from_scan, left, right, scales, skip_ref, scanned, targets, which, done_with=None
):
    seq, channels = left.shape
    blocks = scanned.shape[0]
    sub = channels // (blocks * LANES)
    part = math.gcd(seq, STEP_ROWS)
    for i in which:
        rows = slice(i * part, (i + 1) * part)
        to_rows = slice((i - which[0]) * part, (i - which[0] + 1) * part)
        stacked = jnp.concatenate(
            [scanned[b, i * part * sub : (i + 1) * part * sub, :] for b in range(blocks)], axis=1
        ).astype(jnp.bfloat16)
        ordered = jnp.dot(from_scan[...], stacked, preferred_element_type=F32)
        for b in range(blocks):
            for s in range(sub):
                cols = slice((b * sub + s) * LANES, (b * sub + s + 1) * LANES)
                own = ordered[s * part : (s + 1) * part, b * LANES : (b + 1) * LANES]
                line = left[rows, cols].astype(F32) * right[rows, cols].astype(F32)
                mixed = own + skip_ref[:, cols] * line.astype(jnp.bfloat16).astype(F32)
                for scale, target in zip(scales, targets):
                    target[to_rows, cols] = (scale[rows, cols].astype(F32) * mixed).astype(
                        jnp.bfloat16
                    )
        if done_with is not None:
            done_with(pl.ds((i - which[0]) * part, part), pl.ds(i * part, part))


def forward_kernel(
    modes,
    q_ref,
    k_ref,
    v_ref,
    ct_ref,
    decay_ref,
    coef_ref,
    skip_ref,
    other_ref,
    from_scan,
    conv_ref,
    conv_own,
    after_ref,
    out_ref,
    gq_ref,
    token_ref,
    scanned,
    sem,
):
    token_ref[...] = jnp.zeros_like(token_ref)
    other_carries(
        False, modes, decay_ref, coef_ref, other_ref, conv_ref, conv_own, scanned, sem
    )
    line_outputs(
        from_scan,
        k_ref,
        v_ref,
        (q_ref, ct_ref),
        skip_ref,
        scanned,
        (out_ref, gq_ref),
        range(k_ref.shape[0] // math.gcd(k_ref.shape[0], STEP_ROWS)),
    )


def early_parts(seq):
    parts = seq // math.gcd(seq, STEP_ROWS)
    return range((parts + 1) // 2), range((parts + 1) // 2, parts)


def adjoint_kernel(
    modes,
    q_ref,
    k_ref,
    v_ref,
    ct_ref,
    decay_ref,
    coef_ref,
    skip_ref,
    other_ref,
    from_scan,
    adj_ref,
    adj_own,
    out_rows,
    gq_rows,
    after_ref,
    out_hbm,
    gq_hbm,
    scanned,
    gk_ref,
    gv_ref,
    token_ref,
    sems,
):
    token_ref[...] = jnp.zeros_like(token_ref)
    copies = [
        pltpu.make_async_copy(out_rows, out_hbm, sems.at[0]),
        pltpu.make_async_copy(gq_rows, gq_hbm, sems.at[1]),
    ]
    for copy in copies:
        copy.start()
    other_carries(
        True, modes, decay_ref, coef_ref, other_ref, adj_ref, adj_own, scanned, sems.at[2]
    )
    line_outputs(
        from_scan,
        ct_ref,
        q_ref,
        (v_ref, k_ref),
        skip_ref,
        scanned,
        (gk_ref, gv_ref),
        early_parts(q_ref.shape[0])[0],
    )
    for copy in copies:
        copy.wait()


def last_outputs_kernel(limit, *refs):
    q_ref, k_ref, v_ref, ct_ref, scanned, skip_ref, gk_early, gv_early = refs[:8]
    mine_ref, other_ref, from_scan = refs[8:11]
    share_refs = refs[12:-8]
    raw_hbm, gk_hbm, gv_hbm, gk_rows, gv_rows, raw_cols, states, sems = refs[-8:]
    copies = []

    def start(source, target):
        copy = pltpu.make_async_copy(source, target, sems.at[len(copies)])
        copy.start()
        copies.append(copy)

    early = pl.ds(0, gk_early.shape[0])
    start(gk_early, gk_hbm.at[early])
    start(gv_early, gv_hbm.at[early])
    clip(limit, scanned.shape[0], mine_ref, other_ref, share_refs, raw_cols, states)
    start(raw_cols, raw_hbm)

    def send(at, to):
        start(gk_rows.at[at], gk_hbm.at[to])
        start(gv_rows.at[at], gv_hbm.at[to])

    late = early_parts(q_ref.shape[0])[1]
    if len(late) > 0:
        sides, targets = (v_ref, k_ref), (gk_rows, gv_rows)
        line_outputs(
            from_scan, ct_ref, q_ref, sides, skip_ref, scanned, targets, late, send
        )
    for copy in copies:
        copy.wait()


def add_kernel(after_ref, *refs):
    refs[-1][...] = tree_sum([ref[...] for ref in refs[:-1]])


def clip(limit, blocks, mine_ref, other_ref, share_refs, out_ref, states):
    modes = out_ref.shape[0]
    sub = out_ref.shape[1] // (blocks * LANES)
    half = states.shape[0] // 2
    place_halves(mine_ref, other_ref, 2 * half, states)
    square = jnp.sum(tree_sum([ref[...] for ref in share_refs]))
    factor = jnp.minimum(1.0, limit * lax.rsqrt(jnp.full((1, LANES), square + 1e-06, F32)))
    for b in range(blocks):
        for s in range(sub):
            cols = slice((b * sub + s) * LANES, (b * sub + s + 1) * LANES)
            rows = pl.ds(b * modes * sub + s, modes, stride=sub)
            out_ref[:, cols] = states[rows, :] * factor


def shards(queries, keys_in, values_in, decay_rates, residues, skip_gain, cotangent):
    seq, channels = queries.shape
    modes = decay_rates.shape[1]
    ctx = lax.axis_size("ctx")
    tp = lax.axis_size("tp")
    levels = ctx.bit_length() - 1
    groups = channels // LANES
    sub = math.gcd(groups, 8)
    blocks = groups // sub
    half = modes * groups // 2
    part = math.gcd(seq, STEP_ROWS)
    parts, size = seq // part, part * sub

    def swap(value, bit):
        return lax.ppermute(value, "ctx", [(i, i ^ (1 << bit)) for i in range(ctx)])

    def rows(*shape, dtype=F32):
        return jax.ShapeDtypeStruct((*shape, LANES), dtype)

    line_shape = jax.ShapeDtypeStruct((seq, channels), jnp.bfloat16)
    table_shape = jax.ShapeDtypeStruct((modes, channels), F32)
    line_scratch = pltpu.VMEM((seq, channels), jnp.bfloat16)
    table_scratch = pltpu.VMEM((modes, channels), F32)
    elements = seq * channels * modes
    tables = (decay_rates.T, residues.T, skip_gain.reshape(1, channels))
    sources = (queries, keys_in, values_in, cotangent, *tables)

    (
        send,
        q,
        k,
        v,
        ct,
        gated,
        pulled,
        row_rates,
        row_decay,
        to_scan,
        from_scan,
        res_cols,
        skip,
    ) = pl.pallas_call(
        send_kernel,
        in_specs=[HBM] * 7,
        out_specs=[VMEM] * 13,
        out_shape=[rows(3, half)]
        + [line_shape] * 4
        + [rows(blocks, seq * sub)] * 2
        + [rows(2 * half)] * 2
        + [jax.ShapeDtypeStruct((size, size), jnp.bfloat16)] * 2
        + [table_shape, jax.ShapeDtypeStruct((1, channels), F32)],
        scratch_shapes=[table_scratch, pltpu.SemaphoreType.DMA((4 * parts + 7,))],
        compiler_params=KERNEL,
        cost_estimate=pl.CostEstimate(
            flops=3 * elements, bytes_accessed=8 * seq * channels, transcendentals=0
        ),
        name="sent_states",
    )(*[pltpu.with_memory_space_constraint(item, pltpu.HBM) for item in sources])
    sibling = swap(send, 0)
    keep, gated, pulled = pl.pallas_call(
        keep_kernel,
        out_shape=[rows(3, half)] + [rows(blocks, seq * sub)] * 2,
        scratch_shapes=[pltpu.SemaphoreType.DMA((2,))],
        compiler_params=KERNEL,
        cost_estimate=pl.CostEstimate(
            flops=3 * elements, bytes_accessed=8 * seq * channels, transcendentals=0
        ),
        name="kept_states",
    )(q, k, v, ct, row_decay, to_scan, gated, pulled)

    def wire(level):
        return rows(2 if level == levels - 1 else 3, half, dtype=WIRE)

    whole = rows(blocks, seq * sub)
    whole_scratch = pltpu.VMEM((blocks, seq * sub, LANES), F32)
    states_scratch = pltpu.VMEM((2 * half, LANES), F32)
    local_cost = pl.CostEstimate(
        flops=4 * elements, bytes_accessed=8 * seq * channels, transcendentals=0
    )

    block, packed = pl.pallas_call(
        partial(pair_kernel, seq, levels == 2),
        out_shape=[rows(5, half), wire(1)],
        compiler_params=KERNEL,
        name="chip_states",
    )(keep, sibling, row_rates, row_rates[:8])
    got = swap(packed, 1)
    conv, row_coefs = pl.pallas_call(
        partial(first_local_kernel, modes),
        out_shape=[whole, rows(2 * half)],
        compiler_params=KERNEL,
        cost_estimate=local_cost,
        name="local_conv",
    )(gated, row_decay, row_rates, res_cols, block[4, :8])
    for level in range(1, levels - 1):
        block, packed = pl.pallas_call(
            partial(level_kernel, seq, level, level + 1 == levels - 1),
            out_shape=[rows(5, half), wire(level + 1)],
            compiler_params=KERNEL,
            name="block_states",
        )(block, got, row_rates, conv[0, :8])
        got = swap(packed, level + 1)
    adj = pl.pallas_call(
        partial(local_kernel, True, modes),
        out_shape=whole,
        compiler_params=KERNEL,
        cost_estimate=local_cost,
        name="local_adjoint",
    )(pulled, row_decay, row_coefs, block[4, :8])
    mine, other, square = pl.pallas_call(
        partial(last_kernel, seq, levels - 1),
        out_shape=[rows(3 * half)] * 2 + [rows(8)],
        compiler_params=KERNEL,
        name="carries",
    )(block, got, row_rates, keep, sibling, adj[0, :8])
    other = swap(other, 0)
    early, late = early_parts(seq)
    early_shape = jax.ShapeDtypeStruct((seq * len(early) // parts, channels), jnp.bfloat16)
    late_scratch = pltpu.VMEM((seq * max(len(late), 1) // parts, channels), jnp.bfloat16)
    own_shape = rows(max(blocks // 2, 1), seq * sub)
    kept = {}

    def add_own(after):
        kept["conv"], kept["adj"] = pl.pallas_call(
            partial(own_kernel, modes),
            out_shape=[own_shape] * 2,
            compiler_params=KERNEL,
            cost_estimate=pl.CostEstimate(
                flops=2 * elements, bytes_accessed=8 * seq * channels, transcendentals=0
            ),
            name="own_carries",
        )(conv, adj, row_decay, row_coefs, mine)
        return kept["adj"][0, :8]

    def forward_outputs(after):
        kept["out"], kept["gq"], token = pl.pallas_call(
            partial(forward_kernel, modes),
            out_shape=[line_shape] * 2 + [rows(8)],
            scratch_shapes=[whole_scratch, pltpu.SemaphoreType.DMA],
            compiler_params=KERNEL,
            cost_estimate=pl.CostEstimate(
                flops=2 * elements, bytes_accessed=16 * seq * channels, transcendentals=0
            ),
            name="forward_outputs",
        )(
            q,
            k,
            v,
            ct,
            row_decay,
            row_coefs,
            skip,
            other,
            from_scan,
            conv,
            kept["conv"],
            after,
        )
        return token

    def adjoint_outputs(after):
        results = (
            pl.pallas_call(
                partial(adjoint_kernel, modes),
                in_specs=[VMEM] * 14,
                out_specs=[HBM] * 2 + [VMEM] * 4,
                out_shape=[line_shape] * 2 + [whole] + [early_shape] * 2 + [rows(8)],
                scratch_shapes=[pltpu.SemaphoreType.DMA((3,))],
                compiler_params=KERNEL,
                cost_estimate=pl.CostEstimate(
                    flops=2 * elements, bytes_accessed=8 * seq * channels, transcendentals=0
                ),
                name="adjoint_outputs",
            )(
                q,
                k,
                v,
                ct,
                row_decay,
                row_coefs,
                skip,
                other,
                from_scan,
                adj,
                kept["adj"],
                kept["out"],
                kept["gq"],
                after,
            )
        )
        kept["final"] = results[:-1]
        return results[-1]

    def plus(after, *shares):
        return pl.pallas_call(
            add_kernel,
            in_specs=[VMEM] * (1 + len(shares)),
            out_shape=rows(8),
            compiler_params=KERNEL,
            name="square_sum",
        )(after, *shares)

    def tp_swap(value, mask):
        return lax.ppermute(value, "tp", [(i, i ^ mask) for i in range(tp)])

    works = [add_own, forward_outputs]
    for bit in range(0, tp.bit_length() - 1, 2):
        masks = [m << bit for m in (1, 2, 3) if m << bit < tp]
        shares = [tp_swap(square, mask) for mask in masks]
        after = square
        while works:
            after = works.pop(0)(after)
        square = plus(after, square, *shares)
    share = swap(square, 0)
    after = square
    for work in works + [adjoint_outputs]:
        after = work(after)
    operator_out, grad_queries, scanned, early_keys, early_values = kept["final"]
    grad_residues, grad_keys, grad_values = pl.pallas_call(
        partial(last_outputs_kernel, math.sqrt(channels * tp * modes)),
        in_specs=[VMEM] * 14,
        out_specs=[HBM] * 3,
        out_shape=[table_shape] + [line_shape] * 2,
        scratch_shapes=[
            late_scratch,
            late_scratch,
            table_scratch,
            states_scratch,
            pltpu.SemaphoreType.DMA((2 * parts + 3,)),
        ],
        compiler_params=KERNEL,
        cost_estimate=pl.CostEstimate(
            flops=elements, bytes_accessed=8 * seq * channels, transcendentals=0
        ),
        name="last_outputs",
    )(
        q,
        k,
        v,
        ct,
        scanned,
        skip,
        early_keys,
        early_values,
        mine,
        other,
        from_scan,
        after,
        square,
        share,
    )
    return (operator_out, grad_queries, grad_keys, grad_values, grad_residues.T)


def solution(mesh):
    lines, tables = P("ctx", "tp"), P("tp", None)
    in_specs = (lines, lines, lines, tables, tables, P("tp"), lines)
    out_specs = (lines, lines, lines, lines, tables)
    return jax.shard_map(shards, mesh=mesh, in_specs=in_specs, out_specs=out_specs, check_vma=False)
```

```python
from functools import partial
import math

import jax
import jax.numpy as jnp
from jax import lax
from jax.experimental import pallas as pl
from jax.experimental.pallas import tpu as pltpu
from jax.sharding import PartitionSpec as P

F32 = jnp.float32
WIRE = jnp.bfloat16
LANES = 128
UNROLL = 8
GROUP = 16
STEP_ROWS = 32
KERNEL = pltpu.CompilerParams(vmem_limit_bytes=24 * 1024 * 1024)
HBM = pl.BlockSpec(memory_space=pltpu.HBM)
VMEM = pl.BlockSpec(memory_space=pltpu.VMEM)


def reorder(rows, inner):
    outer = rows // inner
    first = lax.broadcasted_iota(jnp.int32, (rows, rows), 0)
    second = lax.broadcasted_iota(jnp.int32, (rows, rows), 1)

    def matrix(to, fro):
        if inner & (inner - 1) == 0 and outer & (outer - 1) == 0:
            low, high = inner.bit_length() - 1, outer.bit_length() - 1
            same = (fro & (inner - 1)) * outer + (fro >> low) == to
        else:
            same = (fro % inner) * outer + fro // inner == to
        return jnp.where(same, 1.0, 0.0).astype(jnp.bfloat16)

    return matrix(first, second), matrix(second, first)


def tree_sum(items):
    items = list(items)
    while len(items) > 1:
        items = [
            items[i] + items[i + 1] if i + 1 < len(items) else items[i]
            for i in range(0, len(items), 2)
        ]
    return items[0]


def spread(source, target, modes, sub):
    for group in range(source.shape[1] // LANES):
        cols = slice(group * LANES, (group + 1) * LANES)
        first = group // sub * (modes * sub) + group % sub
        target[pl.ds(first, modes, stride=sub), :] = source[:, cols]


def half_units(which, blocks, modes, sub):
    if blocks == 1:
        return [(0, which * (modes // 2 * sub), modes // 2)]
    count = blocks // 2
    return [
        (which * count + j, (which * count + j) * (modes * sub), modes) for j in range(count)
    ]


def to_scan_order(to_scan, pairs, part, i, block, targets):
    size, sub = to_scan.shape[0], to_scan.shape[0] // part
    rows = slice(i * part, (i + 1) * part)
    sides = []
    for left, right in pairs:
        stacked = []
        for s in range(sub):
            cols = pl.ds(pl.multiple_of((block * sub + s) * LANES, LANES), LANES)
            product = left[rows, cols].astype(F32) * right[rows, cols].astype(F32)
            stacked.append(product.astype(jnp.bfloat16))
        sides.append(jnp.concatenate(stacked, axis=0))
    ordered = jnp.dot(
        to_scan[...], jnp.concatenate(sides, axis=1), preferred_element_type=F32
    )
    for j, target in enumerate(targets):
        target[block, i * size : (i + 1) * size, :] = ordered[:, j * LANES : (j + 1) * LANES]


def exchange_rows(items):
    size = len(items)
    row = lax.broadcasted_iota(jnp.int32, items[0].shape, 0)
    step = size // 2
    while step:
        low = (row & step) == 0
        for i in range(size):
            if i & step == 0:
                first, second = items[i], items[i + step]
                items[i] = jnp.where(low, first, pltpu.roll(second, step, 0))
                items[i + step] = jnp.where(low, pltpu.roll(first, size - step, 0), second)
        step //= 2
    return items


def fill_group(left, right, group, block, target):
    rows = pl.ds(pl.multiple_of(group * GROUP, GROUP), GROUP)
    products = []
    for s in range(8):
        cols = pl.ds(pl.multiple_of((block * 8 + s) * LANES, LANES), LANES)
        product = left[rows, cols].astype(F32) * right[rows, cols].astype(F32)
        products.append(product.astype(jnp.bfloat16).astype(F32))
    for at in range(0, GROUP, 8):
        ordered = exchange_rows([product[at : at + 8, :] for product in products])
        for t in range(8):
            where = pl.ds(pl.multiple_of((group * GROUP + at + t) * 8, 8), 8)
            target[block, where, :] = ordered[t]


def scan_states(unit, sub, gated_ref, pulled_ref, decay_ref, out_ref, at_row, pairs, waits):
    block, base, modes = unit
    seq = gated_ref.shape[1] // sub
    decay = [
        decay_ref[pl.ds(pl.multiple_of(base + n * sub, sub), sub), :] for n in range(modes)
    ]
    first = tuple(jnp.zeros((sub, LANES), F32) for _ in range(modes))

    def forward(j, carry):
        held, inner = list(carry[0]), list(carry[1])
        for u in range(UNROLL):
            at = pl.ds(pl.multiple_of((j * UNROLL + u) * sub, sub), sub)
            x = gated_ref[block, at, :]
            p = pulled_ref[block, at, :]
            for n in range(modes):
                held[n] = decay[n] * held[n] + x
                inner[n] = inner[n] + p * held[n]
        return tuple(held), tuple(inner)

    def backward(step, fill, last, j, carry):
        held = list(carry)
        group = last - j
        for u in reversed(range(step)):
            at = pl.ds(pl.multiple_of((group * step + u) * sub, sub), sub)
            p = pulled_ref[block, at, :]
            for n in range(modes):
                held[n] = decay[n] * held[n] + p
            if fill and u in (12, 6):
                left, right, target = pairs[0 if u == 12 else 1]
                fill_group(left, right, jnp.maximum(group - 1, 0), block, target)
        return tuple(held)

    if pairs is None:
        last = seq // UNROLL - 1
        starts = lax.fori_loop(0, last + 1, partial(backward, UNROLL, False, last), first)
    else:
        starts = first
        groups = seq // GROUP // len(waits)
        waits[-1]()
        for left, right, target in pairs:
            fill_group(left, right, seq // GROUP - 1, block, target)
        for i in reversed(range(len(waits))):
            if i > 0:
                waits[i - 1]()
            last = (i + 1) * groups - 1
            starts = lax.fori_loop(0, groups, partial(backward, GROUP, True, last), starts)
    for n in range(modes):
        out_ref[1, at_row + n * sub : at_row + (n + 1) * sub, :] = starts[n]
    ends, inner = lax.fori_loop(0, seq // UNROLL, forward, (first, first))
    for n in range(modes):
        rows = slice(at_row + n * sub, at_row + (n + 1) * sub)
        out_ref[0, rows, :] = ends[n]
        out_ref[2, rows, :] = inner[n]


def can_exchange(sub, part, units):
    return sub == 8 and part % GROUP == 0 and len(units) == 1


def send_kernel(
    q_hbm,
    k_hbm,
    v_hbm,
    ct_hbm,
    rate_hbm,
    res_hbm,
    skip_hbm,
    send_ref,
    q_ref,
    k_ref,
    v_ref,
    ct_ref,
    gated_ref,
    pulled_ref,
    rate_ref,
    decay_ref,
    to_scan,
    from_scan,
    res_cols,
    skip_ref,
    rate_cols,
    sems,
):
    seq, channels = q_ref.shape
    modes = rate_cols.shape[0]
    blocks = gated_ref.shape[0]
    sub = channels // (blocks * LANES)
    part = math.gcd(seq, STEP_ROWS)
    parts = seq // part
    which = 1 - lax.axis_index("ctx") % 2
    pairs = ((k_hbm, k_ref), (v_hbm, v_ref), (ct_hbm, ct_ref), (q_hbm, q_ref))
    copies = []

    def start(source, target):
        copy = pltpu.make_async_copy(source, target, sems.at[len(copies)])
        copy.start()
        copies.append(copy)

    width = channels // min(blocks, 2)
    cols = pl.ds(pl.multiple_of(which * width, LANES) if blocks > 1 else 0, width)
    start(rate_hbm, rate_cols)
    for i in reversed(range(parts)):
        rows = pl.ds(i * part, part)
        for source, target in pairs:
            start(source.at[rows, cols], target.at[rows, cols])
    if blocks > 1:
        cols = pl.ds(pl.multiple_of((1 - which) * width, LANES), width)
        for source, target in pairs:
            start(source.at[:, cols], target.at[:, cols])
    start(res_hbm, res_cols)
    start(skip_hbm, skip_ref)
    to_scan[...], from_scan[...] = reorder(part * sub, part)
    copies[0].wait()
    spread(rate_cols, rate_ref, modes, sub)
    decay_ref[...] = jnp.exp(-rate_ref[...])
    units = half_units(which, blocks, modes, sub)

    def wait_part(i):
        for copy in copies[4 * (parts - 1 - i) + 1 : 4 * (parts - i) + 1]:
            copy.wait()

    if can_exchange(sub, part, units):
        waits = [partial(wait_part, i) for i in range(parts)]
        lines = ((k_ref, v_ref, gated_ref), (ct_ref, q_ref, pulled_ref))
    else:
        waits, lines = None, None
        for i in reversed(range(parts)):
            wait_part(i)
            for unit in units:
                both = ((k_ref, v_ref), (ct_ref, q_ref))
                to_scan_order(to_scan, both, part, i, unit[0], (gated_ref, pulled_ref))
    for at, unit in enumerate(units):
        at_row = at * unit[2] * sub
        scan_states(
            unit, sub, gated_ref, pulled_ref, decay_ref, send_ref, at_row, lines, waits
        )
    for copy in copies[4 * parts + 1 :]:
        copy.wait()


def keep_kernel(
    q_ref,
    k_ref,
    v_ref,
    ct_ref,
    decay_ref,
    to_scan,
    gated_in,
    pulled_in,
    keep_ref,
    gated_ref,
    pulled_ref,
    sems,
):
    seq, channels = q_ref.shape
    blocks = gated_ref.shape[0]
    sub = channels // (blocks * LANES)
    modes = decay_ref.shape[0] // (blocks * sub)
    part = math.gcd(seq, STEP_ROWS)
    which = lax.axis_index("ctx") % 2
    count = max(blocks // 2, 1)
    done = pl.ds((1 - which) * count if blocks > 1 else 0, count)
    copies = [
        pltpu.make_async_copy(gated_in.at[done], gated_ref.at[done], sems.at[0]),
        pltpu.make_async_copy(pulled_in.at[done], pulled_ref.at[done], sems.at[1]),
    ]
    for copy in copies:
        copy.start()
    units = half_units(which, blocks, modes, sub)
    lines, pairs = (gated_in, pulled_in), None
    if blocks > 1:
        lines = (gated_ref, pulled_ref)
        if can_exchange(sub, part, units):
            pairs = ((k_ref, v_ref, gated_ref), (ct_ref, q_ref, pulled_ref))
        else:
            for i in range(seq // part):
                for unit in units:
                    both = ((k_ref, v_ref), (ct_ref, q_ref))
                    to_scan_order(to_scan, both, part, i, unit[0], lines)
    for at, unit in enumerate(units):
        at_row = at * unit[2] * sub
        scan_states(
            unit, sub, *lines, decay_ref, keep_ref, at_row, pairs, [lambda: None]
        )
    for copy in copies:
        copy.wait()


def own_rows(rate_ref, half):
    core = lax.axis_index("ctx") % 2
    return rate_ref[pl.ds(pl.multiple_of(core * half, half), half), :]


def joined(is_right, mine, other, span, step):
    left = [jnp.where(is_right, o, m) for m, o in zip(mine, other)]
    right = [jnp.where(is_right, m, o) for m, o in zip(mine, other)]
    return (
        span * left[0] + right[0],
        left[1] + span * right[1],
        left[2] + right[2] + step * right[1] * left[0],
    )


def put_wire(wire_ref, is_last, next_right, block):
    if is_last:
        wire_ref[0] = jnp.where(next_right, block[1], block[0]).astype(wire_ref.dtype)
        wire_ref[1] = block[2].astype(wire_ref.dtype)
    else:
        for kind in range(3):
            wire_ref[kind] = block[kind].astype(wire_ref.dtype)


def pair_kernel(seq, is_last, keep_ref, got_ref, rate_ref, after_ref, block_ref, wire_ref):
    rate = own_rows(rate_ref, keep_ref.shape[1])
    place = lax.axis_index("ctx")
    block = joined(
        place % 2 == 1,
        [keep_ref[i] for i in range(3)],
        [got_ref[i] for i in range(3)],
        jnp.exp(-rate * seq),
        jnp.exp(-rate),
    )
    for kind in range(3):
        block_ref[kind] = block[kind]
    block_ref[3] = jnp.zeros_like(rate)
    block_ref[4] = jnp.zeros_like(rate)
    put_wire(wire_ref, is_last, (place // 2) % 2 == 1, block)


def carries_with(block_ref, end_state, start_state, level, seq, rate):
    place = lax.axis_index("ctx")
    is_right = (place >> level) % 2 == 1
    chips = 1 << (level - 1)
    at = (place // 2) % chips
    before = at * (2 * seq)
    behind = (chips - 1 - at) * (2 * seq)
    ahead = block_ref[3] + jnp.where(
        is_right, jnp.exp(-rate * before.astype(F32)) * end_state, 0.0
    )
    after = block_ref[4] + jnp.where(
        is_right, 0.0, jnp.exp(-rate * behind.astype(F32)) * start_state
    )
    return is_right, ahead, after


def level_kernel(
    seq, level, is_last, block_ref, got_ref, rate_ref, after_ref, out_ref, wire_ref
):
    rate = own_rows(rate_ref, block_ref.shape[1])
    got = [got_ref[i].astype(F32) for i in range(3)]
    is_right, ahead, after = carries_with(block_ref, got[0], got[1], level, seq, rate)
    block = joined(
        is_right,
        [block_ref[i] for i in range(3)],
        got,
        jnp.exp(-rate * (seq << level)),
        jnp.exp(-rate),
    )
    for kind in range(3):
        out_ref[kind] = block[kind]
    out_ref[3] = ahead
    out_ref[4] = after
    next_right = (lax.axis_index("ctx") >> (level + 1)) % 2 == 1
    put_wire(wire_ref, is_last, next_right, block)


def last_kernel(
    seq,
    level,
    block_ref,
    got_ref,
    rate_ref,
    keep_ref,
    sibling_ref,
    after_ref,
    mine_ref,
    other_ref,
    share_ref,
):
    half = block_ref.shape[1]
    rate = own_rows(rate_ref, half)
    edge, inner = got_ref[0].astype(F32), got_ref[1].astype(F32)
    is_right, ahead, after = carries_with(block_ref, edge, edge, level, seq, rate)
    own_edge = jnp.where(is_right, block_ref[1], block_ref[0])
    total = block_ref[2] + inner + jnp.exp(-rate) * own_edge * edge
    raw = jnp.sqrt(1.0 - jnp.exp(-2.0 * rate)) * total
    core = lax.axis_index("ctx") % 2
    first = core == 0
    span = jnp.exp(-rate * seq)
    end_first = jnp.where(first, keep_ref[0], sibling_ref[0])
    start_second = jnp.where(first, sibling_ref[1], keep_ref[1])
    ahead_second = span * ahead + end_first
    after_first = span * after + start_second
    mine_ref[0:half, :] = jnp.where(first, ahead, ahead_second)
    mine_ref[half : 2 * half, :] = jnp.where(first, after_first, after)
    other_ref[0:half, :] = jnp.where(first, ahead_second, ahead)
    other_ref[half : 2 * half, :] = jnp.where(first, after, after_first)
    squares = raw * raw
    share_ref[...] = tree_sum([squares[i : i + 8, :] for i in range(0, half, 8)])
    mine_ref[2 * half : 3 * half, :] = raw
    other_ref[2 * half : 3 * half, :] = raw


def place_halves(mine_ref, other_ref, first, target):
    half = target.shape[0] // 2
    core = lax.axis_index("ctx") % 2
    for ref, at in ((mine_ref, core), (other_ref, 1 - core)):
        rows = pl.ds(pl.multiple_of(at * half, half), half)
        target[rows, :] = ref[first : first + half, :]


def mode_rows(block, modes, sub):
    return [slice((block * modes + n) * sub, (block * modes + n + 1) * sub) for n in range(modes)]


def first_local_kernel(modes, lines_ref, decay_ref, rate_ref, res_cols, after_ref, out_ref, coef_ref):
    sub = decay_ref.shape[0] // (lines_ref.shape[0] * modes)
    spread(res_cols, coef_ref, modes, sub)
    coef_ref[...] = coef_ref[...] * jnp.sqrt(1.0 - jnp.exp(-2.0 * rate_ref[...]))
    local_kernel(False, modes, lines_ref, decay_ref, coef_ref, after_ref, out_ref)


def local_kernel(reverse, modes, lines_ref, decay_ref, coef_ref, after_ref, out_ref):
    blocks = lines_ref.shape[0]
    sub = decay_ref.shape[0] // (blocks * modes)
    seq = lines_ref.shape[1] // sub
    for b in range(blocks):
        rows = mode_rows(b, modes, sub)
        decay = [decay_ref[r, :] for r in rows]
        coef = [coef_ref[r, :] for r in rows]

        def body(j, carry):
            held = list(carry)
            for u in range(UNROLL):
                t = j * UNROLL + u
                if reverse:
                    t = seq - 1 - t
                at = pl.ds(pl.multiple_of(t * sub, sub), sub)
                x = lines_ref[b, at, :]
                total = [None] * 4
                for n in range(modes):
                    held[n] = decay[n] * held[n] + x
                    term = coef[n] * held[n]
                    total[n % 4] = term if n < 4 else total[n % 4] + term
                out_ref[b, at, :] = tree_sum(total)
            return tuple(held)

        first = tuple(jnp.zeros((sub, LANES), F32) for _ in range(modes))
        lax.fori_loop(0, seq // UNROLL, body, first)


def add_carries(reverse, unit, sub, decay_ref, coef_ref, states_ref, at_row, source, target, at):
    _, base, modes = unit
    seq = target.shape[1] // sub
    rows = [pl.ds(pl.multiple_of(base + n * sub, sub), sub) for n in range(modes)]
    decay = [decay_ref[r, :] for r in rows]
    first = tuple(
        coef_ref[r, :] * states_ref[at_row + n * sub : at_row + (n + 1) * sub, :]
        for n, r in enumerate(rows)
    )

    def body(j, carry):
        held = list(carry)
        for u in range(UNROLL):
            t = j * UNROLL + u
            if reverse:
                t = seq - 1 - t
            where = pl.ds(pl.multiple_of(t * sub, sub), sub)
            total = [source[where, :], None, None, None]
            for n in range(modes):
                held[n] = decay[n] * held[n]
                total[n % 4] = held[n] if total[n % 4] is None else total[n % 4] + held[n]
            target[at, where, :] = tree_sum(total)
        return tuple(held)

    lax.fori_loop(0, seq // UNROLL, body, first)


def own_kernel(modes, conv_ref, adj_ref, decay_ref, coef_ref, mine_ref, conv_own, adj_own):
    blocks = conv_ref.shape[0]
    sub = decay_ref.shape[0] // (blocks * modes)
    half = decay_ref.shape[0] // 2
    core = lax.axis_index("ctx") % 2
    for i, unit in enumerate(half_units(core, blocks, modes, sub)):
        at_row = i * unit[2] * sub
        for reverse, source, target in ((False, conv_ref, conv_own), (True, adj_ref, adj_own)):
            add_carries(
                reverse,
                unit,
                sub,
                decay_ref,
                coef_ref,
                mine_ref,
                at_row + half * reverse,
                source.at[unit[0]],
                target,
                i,
            )


def other_carries(reverse, modes, decay_ref, coef_ref, other_ref, local_ref, own_ref, whole, sem):
    blocks, own_blocks = local_ref.shape[0], own_ref.shape[0]
    sub = decay_ref.shape[0] // (blocks * modes)
    half = decay_ref.shape[0] // 2
    core = lax.axis_index("ctx") % 2
    copy = pltpu.make_async_copy(own_ref, whole.at[pl.ds(core * own_blocks, own_blocks)], sem)
    if blocks > 1:
        copy.start()
    for i, unit in enumerate(half_units(1 - core, blocks, modes, sub)):
        source = local_ref.at[unit[0]] if blocks > 1 else own_ref.at[0]
        at_row = i * unit[2] * sub + half * reverse
        add_carries(
            reverse, unit, sub, decay_ref, coef_ref, other_ref, at_row, source, whole, unit[0]
        )
    if blocks > 1:
        copy.wait()


def line_outputs(
    from_scan, left, right, scales, skip_ref, scanned, targets, which, done_with=None
):
    seq, channels = left.shape
    blocks = scanned.shape[0]
    sub = channels // (blocks * LANES)
    part = math.gcd(seq, STEP_ROWS)
    for i in which:
        rows = slice(i * part, (i + 1) * part)
        to_rows = slice((i - which[0]) * part, (i - which[0] + 1) * part)
        stacked = jnp.concatenate(
            [scanned[b, i * part * sub : (i + 1) * part * sub, :] for b in range(blocks)], axis=1
        ).astype(jnp.bfloat16)
        ordered = jnp.dot(from_scan[...], stacked, preferred_element_type=F32)
        for b in range(blocks):
            for s in range(sub):
                cols = slice((b * sub + s) * LANES, (b * sub + s + 1) * LANES)
                own = ordered[s * part : (s + 1) * part, b * LANES : (b + 1) * LANES]
                line = left[rows, cols].astype(F32) * right[rows, cols].astype(F32)
                mixed = own + skip_ref[:, cols] * line.astype(jnp.bfloat16).astype(F32)
                for scale, target in zip(scales, targets):
                    target[to_rows, cols] = (scale[rows, cols].astype(F32) * mixed).astype(
                        jnp.bfloat16
                    )
        if done_with is not None:
            done_with(pl.ds((i - which[0]) * part, part), pl.ds(i * part, part))


def forward_kernel(
    modes,
    q_ref,
    k_ref,
    v_ref,
    ct_ref,
    decay_ref,
    coef_ref,
    skip_ref,
    other_ref,
    from_scan,
    conv_ref,
    conv_own,
    after_ref,
    out_ref,
    gq_ref,
    token_ref,
    scanned,
    sem,
):
    token_ref[...] = jnp.zeros_like(token_ref)
    other_carries(
        False, modes, decay_ref, coef_ref, other_ref, conv_ref, conv_own, scanned, sem
    )
    line_outputs(
        from_scan,
        k_ref,
        v_ref,
        (q_ref, ct_ref),
        skip_ref,
        scanned,
        (out_ref, gq_ref),
        range(k_ref.shape[0] // math.gcd(k_ref.shape[0], STEP_ROWS)),
    )


def early_parts(seq):
    parts = seq // math.gcd(seq, STEP_ROWS)
    return range((parts + 1) // 2), range((parts + 1) // 2, parts)


def adjoint_kernel(
    modes,
    q_ref,
    k_ref,
    v_ref,
    ct_ref,
    decay_ref,
    coef_ref,
    skip_ref,
    other_ref,
    from_scan,
    adj_ref,
    adj_own,
    out_rows,
    gq_rows,
    after_ref,
    out_hbm,
    gq_hbm,
    scanned,
    gk_ref,
    gv_ref,
    token_ref,
    sems,
):
    token_ref[...] = jnp.zeros_like(token_ref)
    copies = [
        pltpu.make_async_copy(out_rows, out_hbm, sems.at[0]),
        pltpu.make_async_copy(gq_rows, gq_hbm, sems.at[1]),
    ]
    for copy in copies:
        copy.start()
    other_carries(
        True, modes, decay_ref, coef_ref, other_ref, adj_ref, adj_own, scanned, sems.at[2]
    )
    line_outputs(
        from_scan,
        ct_ref,
        q_ref,
        (v_ref, k_ref),
        skip_ref,
        scanned,
        (gk_ref, gv_ref),
        early_parts(q_ref.shape[0])[0],
    )
    for copy in copies:
        copy.wait()


def last_outputs_kernel(limit, *refs):
    q_ref, k_ref, v_ref, ct_ref, scanned, skip_ref, gk_early, gv_early = refs[:8]
    mine_ref, other_ref, from_scan = refs[8:11]
    share_refs = refs[12:-8]
    raw_hbm, gk_hbm, gv_hbm, gk_rows, gv_rows, raw_cols, states, sems = refs[-8:]
    copies = []

    def start(source, target):
        copy = pltpu.make_async_copy(source, target, sems.at[len(copies)])
        copy.start()
        copies.append(copy)

    early = pl.ds(0, gk_early.shape[0])
    start(gk_early, gk_hbm.at[early])
    start(gv_early, gv_hbm.at[early])
    clip(limit, scanned.shape[0], mine_ref, other_ref, share_refs, raw_cols, states)
    start(raw_cols, raw_hbm)

    def send(at, to):
        start(gk_rows.at[at], gk_hbm.at[to])
        start(gv_rows.at[at], gv_hbm.at[to])

    late = early_parts(q_ref.shape[0])[1]
    if len(late) > 0:
        sides, targets = (v_ref, k_ref), (gk_rows, gv_rows)
        line_outputs(
            from_scan, ct_ref, q_ref, sides, skip_ref, scanned, targets, late, send
        )
    for copy in copies:
        copy.wait()


def add_kernel(after_ref, *refs):
    refs[-1][...] = tree_sum([ref[...] for ref in refs[:-1]])


def clip(limit, blocks, mine_ref, other_ref, share_refs, out_ref, states):
    modes = out_ref.shape[0]
    sub = out_ref.shape[1] // (blocks * LANES)
    half = states.shape[0] // 2
    place_halves(mine_ref, other_ref, 2 * half, states)
    square = jnp.sum(tree_sum([ref[...] for ref in share_refs]))
    factor = jnp.minimum(1.0, limit * lax.rsqrt(jnp.full((1, LANES), square + 1e-06, F32)))
    for b in range(blocks):
        for s in range(sub):
            cols = slice((b * sub + s) * LANES, (b * sub + s + 1) * LANES)
            rows = pl.ds(b * modes * sub + s, modes, stride=sub)
            out_ref[:, cols] = states[rows, :] * factor


def shards(queries, keys_in, values_in, decay_rates, residues, skip_gain, cotangent):
    seq, channels = queries.shape
    modes = decay_rates.shape[1]
    ctx = lax.axis_size("ctx")
    tp = lax.axis_size("tp")
    levels = ctx.bit_length() - 1
    groups = channels // LANES
    sub = math.gcd(groups, 8)
    blocks = groups // sub
    half = modes * groups // 2
    part = math.gcd(seq, STEP_ROWS)
    parts, size = seq // part, part * sub

    def swap(value, bit):
        return lax.ppermute(value, "ctx", [(i, i ^ (1 << bit)) for i in range(ctx)])

    def rows(*shape, dtype=F32):
        return jax.ShapeDtypeStruct((*shape, LANES), dtype)

    line_shape = jax.ShapeDtypeStruct((seq, channels), jnp.bfloat16)
    table_shape = jax.ShapeDtypeStruct((modes, channels), F32)
    line_scratch = pltpu.VMEM((seq, channels), jnp.bfloat16)
    table_scratch = pltpu.VMEM((modes, channels), F32)
    elements = seq * channels * modes
    tables = (decay_rates.T, residues.T, skip_gain.reshape(1, channels))
    sources = (queries, keys_in, values_in, cotangent, *tables)

    (
        send,
        q,
        k,
        v,
        ct,
        gated,
        pulled,
        row_rates,
        row_decay,
        to_scan,
        from_scan,
        res_cols,
        skip,
    ) = pl.pallas_call(
        send_kernel,
        in_specs=[HBM] * 7,
        out_specs=[VMEM] * 13,
        out_shape=[rows(3, half)]
        + [line_shape] * 4
        + [rows(blocks, seq * sub)] * 2
        + [rows(2 * half)] * 2
        + [jax.ShapeDtypeStruct((size, size), jnp.bfloat16)] * 2
        + [table_shape, jax.ShapeDtypeStruct((1, channels), F32)],
        scratch_shapes=[table_scratch, pltpu.SemaphoreType.DMA((4 * parts + 7,))],
        compiler_params=KERNEL,
        cost_estimate=pl.CostEstimate(
            flops=3 * elements, bytes_accessed=8 * seq * channels, transcendentals=0
        ),
        name="sent_states",
    )(*[pltpu.with_memory_space_constraint(item, pltpu.HBM) for item in sources])
    sibling = swap(send, 0)
    keep, gated, pulled = pl.pallas_call(
        keep_kernel,
        out_shape=[rows(3, half)] + [rows(blocks, seq * sub)] * 2,
        scratch_shapes=[pltpu.SemaphoreType.DMA((2,))],
        compiler_params=KERNEL,
        cost_estimate=pl.CostEstimate(
            flops=3 * elements, bytes_accessed=8 * seq * channels, transcendentals=0
        ),
        name="kept_states",
    )(q, k, v, ct, row_decay, to_scan, gated, pulled)

    def wire(level):
        return rows(2 if level == levels - 1 else 3, half, dtype=WIRE)

    whole = rows(blocks, seq * sub)
    whole_scratch = pltpu.VMEM((blocks, seq * sub, LANES), F32)
    states_scratch = pltpu.VMEM((2 * half, LANES), F32)
    local_cost = pl.CostEstimate(
        flops=4 * elements, bytes_accessed=8 * seq * channels, transcendentals=0
    )

    block, packed = pl.pallas_call(
        partial(pair_kernel, seq, levels == 2),
        out_shape=[rows(5, half), wire(1)],
        compiler_params=KERNEL,
        name="chip_states",
    )(keep, sibling, row_rates, row_rates[:8])
    got = swap(packed, 1)
    conv, row_coefs = pl.pallas_call(
        partial(first_local_kernel, modes),
        out_shape=[whole, rows(2 * half)],
        compiler_params=KERNEL,
        cost_estimate=local_cost,
        name="local_conv",
    )(gated, row_decay, row_rates, res_cols, block[4, :8])
    for level in range(1, levels - 1):
        block, packed = pl.pallas_call(
            partial(level_kernel, seq, level, level + 1 == levels - 1),
            out_shape=[rows(5, half), wire(level + 1)],
            compiler_params=KERNEL,
            name="block_states",
        )(block, got, row_rates, conv[0, :8])
        got = swap(packed, level + 1)
    adj = pl.pallas_call(
        partial(local_kernel, True, modes),
        out_shape=whole,
        compiler_params=KERNEL,
        cost_estimate=local_cost,
        name="local_adjoint",
    )(pulled, row_decay, row_coefs, block[4, :8])
    mine, other, square = pl.pallas_call(
        partial(last_kernel, seq, levels - 1),
        out_shape=[rows(3 * half)] * 2 + [rows(8)],
        compiler_params=KERNEL,
        name="carries",
    )(block, got, row_rates, keep, sibling, adj[0, :8])
    other = swap(other, 0)
    early, late = early_parts(seq)
    early_shape = jax.ShapeDtypeStruct((seq * len(early) // parts, channels), jnp.bfloat16)
    late_scratch = pltpu.VMEM((seq * max(len(late), 1) // parts, channels), jnp.bfloat16)
    own_shape = rows(max(blocks // 2, 1), seq * sub)
    kept = {}

    def add_own(after):
        kept["conv"], kept["adj"] = pl.pallas_call(
            partial(own_kernel, modes),
            out_shape=[own_shape] * 2,
            compiler_params=KERNEL,
            cost_estimate=pl.CostEstimate(
                flops=2 * elements, bytes_accessed=8 * seq * channels, transcendentals=0
            ),
            name="own_carries",
        )(conv, adj, row_decay, row_coefs, mine)
        return kept["adj"][0, :8]

    def forward_outputs(after):
        kept["out"], kept["gq"], token = pl.pallas_call(
            partial(forward_kernel, modes),
            out_shape=[line_shape] * 2 + [rows(8)],
            scratch_shapes=[whole_scratch, pltpu.SemaphoreType.DMA],
            compiler_params=KERNEL,
            cost_estimate=pl.CostEstimate(
                flops=2 * elements, bytes_accessed=16 * seq * channels, transcendentals=0
            ),
            name="forward_outputs",
        )(
            q,
            k,
            v,
            ct,
            row_decay,
            row_coefs,
            skip,
            other,
            from_scan,
            conv,
            kept["conv"],
            after,
        )
        return token

    def adjoint_outputs(after):
        results = (
            pl.pallas_call(
                partial(adjoint_kernel, modes),
                in_specs=[VMEM] * 14,
                out_specs=[HBM] * 2 + [VMEM] * 4,
                out_shape=[line_shape] * 2 + [whole] + [early_shape] * 2 + [rows(8)],
                scratch_shapes=[pltpu.SemaphoreType.DMA((3,))],
                compiler_params=KERNEL,
                cost_estimate=pl.CostEstimate(
                    flops=2 * elements, bytes_accessed=8 * seq * channels, transcendentals=0
                ),
                name="adjoint_outputs",
            )(
                q,
                k,
                v,
                ct,
                row_decay,
                row_coefs,
                skip,
                other,
                from_scan,
                adj,
                kept["adj"],
                kept["out"],
                kept["gq"],
                after,
            )
        )
        kept["final"] = results[:-1]
        return results[-1]

    def plus(after, *shares):
        return pl.pallas_call(
            add_kernel,
            in_specs=[VMEM] * (1 + len(shares)),
            out_shape=rows(8),
            compiler_params=KERNEL,
            name="square_sum",
        )(after, *shares)

    def tp_swap(value, mask):
        return lax.ppermute(value, "tp", [(i, i ^ mask) for i in range(tp)])

    works = [add_own, forward_outputs]
    for bit in range(0, tp.bit_length() - 1, 2):
        masks = [m << bit for m in (1, 2, 3) if m << bit < tp]
        shares = [tp_swap(square, mask) for mask in masks]
        after = square
        while works:
            after = works.pop(0)(after)
        square = plus(after, square, *shares)
    share = swap(square, 0)
    after = square
    for work in works + [adjoint_outputs]:
        after = work(after)
    operator_out, grad_queries, scanned, early_keys, early_values = kept["final"]
    grad_residues, grad_keys, grad_values = pl.pallas_call(
        partial(last_outputs_kernel, math.sqrt(channels * tp * modes)),
        in_specs=[VMEM] * 14,
        out_specs=[HBM] * 3,
        out_shape=[table_shape] + [line_shape] * 2,
        scratch_shapes=[
            late_scratch,
            late_scratch,
            table_scratch,
            states_scratch,
            pltpu.SemaphoreType.DMA((2 * parts + 3,)),
        ],
        compiler_params=KERNEL,
        cost_estimate=pl.CostEstimate(
            flops=elements, bytes_accessed=8 * seq * channels, transcendentals=0
        ),
        name="last_outputs",
    )(
        q,
        k,
        v,
        ct,
        scanned,
        skip,
        early_keys,
        early_values,
        mine,
        other,
        from_scan,
        after,
        square,
        share,
    )
    return (operator_out, grad_queries, grad_keys, grad_values, grad_residues.T)


def solution(mesh):
    lines, tables = P("ctx", "tp"), P("tp", None)
    in_specs = (lines, lines, lines, tables, tables, P("tp"), lines)
    out_specs = (lines, lines, lines, lines, tables)
    return jax.shard_map(shards, mesh=mesh, in_specs=in_specs, out_specs=out_specs, check_vma=False)
```

```python
from functools import partial
import math

import jax
import jax.numpy as jnp
from jax import lax
from jax.experimental import pallas as pl
from jax.experimental.pallas import tpu as pltpu
from jax.sharding import PartitionSpec as P

F32 = jnp.float32
WIRE = jnp.bfloat16
LANES = 128
UNROLL = 8
GROUP = 16
STEP_ROWS = 32
KERNEL = pltpu.CompilerParams(vmem_limit_bytes=24 * 1024 * 1024)
HBM = pl.BlockSpec(memory_space=pltpu.HBM)
VMEM = pl.BlockSpec(memory_space=pltpu.VMEM)


def reorder(rows, inner):
    outer = rows // inner
    first = lax.broadcasted_iota(jnp.int32, (rows, rows), 0)
    second = lax.broadcasted_iota(jnp.int32, (rows, rows), 1)

    def matrix(to, fro):
        if inner & (inner - 1) == 0 and outer & (outer - 1) == 0:
            low, high = inner.bit_length() - 1, outer.bit_length() - 1
            same = (fro & (inner - 1)) * outer + (fro >> low) == to
        else:
            same = (fro % inner) * outer + fro // inner == to
        return jnp.where(same, 1.0, 0.0).astype(jnp.bfloat16)

    return matrix(first, second), matrix(second, first)


def tree_sum(items):
    items = list(items)
    while len(items) > 1:
        items = [
            items[i] + items[i + 1] if i + 1 < len(items) else items[i]
            for i in range(0, len(items), 2)
        ]
    return items[0]


def spread(source, target, modes, sub):
    for group in range(source.shape[1] // LANES):
        cols = slice(group * LANES, (group + 1) * LANES)
        first = group // sub * (modes * sub) + group % sub
        target[pl.ds(first, modes, stride=sub), :] = source[:, cols]


def half_units(which, blocks, modes, sub):
    if blocks == 1:
        return [(0, which * (modes // 2 * sub), modes // 2)]
    count = blocks // 2
    return [
        (which * count + j, (which * count + j) * (modes * sub), modes) for j in range(count)
    ]


def to_scan_order(to_scan, pairs, part, i, block, targets, slot):
    size, sub = to_scan.shape[0], to_scan.shape[0] // part
    rows = slice(i * part, (i + 1) * part)
    sides = []
    for left, right in pairs:
        stacked = []
        for s in range(sub):
            cols = pl.ds(pl.multiple_of((block * sub + s) * LANES, LANES), LANES)
            product = left[rows, cols].astype(F32) * right[rows, cols].astype(F32)
            stacked.append(product.astype(jnp.bfloat16))
        sides.append(jnp.concatenate(stacked, axis=0))
    ordered = jnp.dot(
        to_scan[...], jnp.concatenate(sides, axis=1), preferred_element_type=F32
    )
    for j, target in enumerate(targets):
        target[slot, i * size : (i + 1) * size, :] = ordered[:, j * LANES : (j + 1) * LANES]


def exchange_rows(items):
    size = len(items)
    row = lax.broadcasted_iota(jnp.int32, items[0].shape, 0)
    step = size // 2
    while step:
        low = (row & step) == 0
        for i in range(size):
            if i & step == 0:
                first, second = items[i], items[i + step]
                items[i] = jnp.where(low, first, pltpu.roll(second, step, 0))
                items[i + step] = jnp.where(low, pltpu.roll(first, size - step, 0), second)
        step //= 2
    return items


def fill_group(left, right, group, block, target, slot):
    rows = pl.ds(pl.multiple_of(group * GROUP, GROUP), GROUP)
    products = []
    for s in range(8):
        cols = pl.ds(pl.multiple_of((block * 8 + s) * LANES, LANES), LANES)
        product = left[rows, cols].astype(F32) * right[rows, cols].astype(F32)
        products.append(product.astype(jnp.bfloat16).astype(F32))
    for at in range(0, GROUP, 8):
        ordered = exchange_rows([product[at : at + 8, :] for product in products])
        for t in range(8):
            where = pl.ds(pl.multiple_of((group * GROUP + at + t) * 8, 8), 8)
            target[slot, where, :] = ordered[t]


def scan_states(unit, slot, sub, gated_ref, pulled_ref, decay_ref, out_ref, pairs, waits):
    block, base, modes = unit
    at_row = slot * modes * sub
    seq = gated_ref.shape[1] // sub
    slot = slot % gated_ref.shape[0]
    decay = [
        decay_ref[pl.ds(pl.multiple_of(base + n * sub, sub), sub), :] for n in range(modes)
    ]
    first = tuple(jnp.zeros((sub, LANES), F32) for _ in range(modes))

    def forward(j, carry):
        held, inner = list(carry[0]), list(carry[1])
        for u in range(UNROLL):
            at = pl.ds(pl.multiple_of((j * UNROLL + u) * sub, sub), sub)
            x = gated_ref[slot, at, :]
            p = pulled_ref[slot, at, :]
            for n in range(modes):
                held[n] = decay[n] * held[n] + x
                inner[n] = inner[n] + p * held[n]
        return tuple(held), tuple(inner)

    def backward(step, fill, last, j, carry):
        held = list(carry)
        group = last - j
        for u in reversed(range(step)):
            at = pl.ds(pl.multiple_of((group * step + u) * sub, sub), sub)
            p = pulled_ref[slot, at, :]
            for n in range(modes):
                held[n] = decay[n] * held[n] + p
            if fill and u in (12, 6):
                left, right, target = pairs[0 if u == 12 else 1]
                fill_group(left, right, jnp.maximum(group - 1, 0), block, target, slot)
        return tuple(held)

    if pairs is None:
        last = seq // UNROLL - 1
        starts = lax.fori_loop(0, last + 1, partial(backward, UNROLL, False, last), first)
    else:
        starts = first
        groups = seq // GROUP // len(waits)
        waits[-1]()
        for left, right, target in pairs:
            fill_group(left, right, seq // GROUP - 1, block, target, slot)
        for i in reversed(range(len(waits))):
            if i > 0:
                waits[i - 1]()
            last = (i + 1) * groups - 1
            starts = lax.fori_loop(0, groups, partial(backward, GROUP, True, last), starts)
    for n in range(modes):
        out_ref[1, at_row + n * sub : at_row + (n + 1) * sub, :] = starts[n]
    ends, inner = lax.fori_loop(0, seq // UNROLL, forward, (first, first))
    for n in range(modes):
        rows = slice(at_row + n * sub, at_row + (n + 1) * sub)
        out_ref[0, rows, :] = ends[n]
        out_ref[2, rows, :] = inner[n]


def can_exchange(sub, part, units):
    return sub == 8 and part % GROUP == 0 and len(units) == 1


def send_kernel(
    q_hbm,
    k_hbm,
    v_hbm,
    ct_hbm,
    rate_hbm,
    res_hbm,
    skip_hbm,
    send_ref,
    q_ref,
    k_ref,
    v_ref,
    ct_ref,
    gated_ref,
    pulled_ref,
    rate_ref,
    decay_ref,
    to_scan,
    from_scan,
    res_cols,
    skip_ref,
    rate_cols,
    sems,
):
    seq, channels = q_ref.shape
    modes = rate_cols.shape[0]
    sub = gated_ref.shape[1] // seq
    blocks = channels // (sub * LANES)
    part = math.gcd(seq, STEP_ROWS)
    parts = seq // part
    which = 1 - lax.axis_index("ctx") % 2
    pairs = ((k_hbm, k_ref), (v_hbm, v_ref), (ct_hbm, ct_ref), (q_hbm, q_ref))
    copies = []

    def start(source, target):
        copy = pltpu.make_async_copy(source, target, sems.at[len(copies)])
        copy.start()
        copies.append(copy)

    width = channels // min(blocks, 2)
    cols = pl.ds(pl.multiple_of(which * width, LANES) if blocks > 1 else 0, width)
    start(rate_hbm, rate_cols)
    for i in reversed(range(parts)):
        rows = pl.ds(i * part, part)
        for source, target in pairs:
            start(source.at[rows, cols], target.at[rows, cols])
    if blocks > 1:
        cols = pl.ds(pl.multiple_of((1 - which) * width, LANES), width)
        for source, target in pairs:
            start(source.at[:, cols], target.at[:, cols])
    start(res_hbm, res_cols)
    start(skip_hbm, skip_ref)
    to_scan[...], from_scan[...] = reorder(part * sub, part)
    copies[0].wait()
    spread(rate_cols, rate_ref, modes, sub)
    decay_ref[...] = jnp.exp(-rate_ref[...])
    units = half_units(which, blocks, modes, sub)

    def wait_part(i):
        for copy in copies[4 * (parts - 1 - i) + 1 : 4 * (parts - i) + 1]:
            copy.wait()

    if can_exchange(sub, part, units):
        waits = [partial(wait_part, i) for i in range(parts)]
        lines = ((k_ref, v_ref, gated_ref), (ct_ref, q_ref, pulled_ref))
    else:
        waits, lines = None, None
        for i in reversed(range(parts)):
            wait_part(i)
            for at, unit in enumerate(units):
                both = ((k_ref, v_ref), (ct_ref, q_ref))
                to_scan_order(to_scan, both, part, i, unit[0], (gated_ref, pulled_ref), at)
    for at, unit in enumerate(units):
        scan_states(unit, at, sub, gated_ref, pulled_ref, decay_ref, send_ref, lines, waits)
    for copy in copies[4 * parts + 1 :]:
        copy.wait()


def keep_kernel(
    q_ref, k_ref, v_ref, ct_ref, decay_ref, to_scan, gated_in, pulled_in, keep_ref, *line_refs
):
    seq, channels = q_ref.shape
    sub = gated_in.shape[1] // seq
    blocks = channels // (sub * LANES)
    modes = decay_ref.shape[0] // (blocks * sub)
    part = math.gcd(seq, STEP_ROWS)
    units = half_units(lax.axis_index("ctx") % 2, blocks, modes, sub)
    lines, pairs = (gated_in, pulled_in), None
    if blocks > 1:
        lines = line_refs
        if can_exchange(sub, part, units):
            pairs = ((k_ref, v_ref, line_refs[0]), (ct_ref, q_ref, line_refs[1]))
        else:
            for i in range(seq // part):
                for at, unit in enumerate(units):
                    both = ((k_ref, v_ref), (ct_ref, q_ref))
                    to_scan_order(to_scan, both, part, i, unit[0], lines, at)
    for at, unit in enumerate(units):
        scan_states(unit, at, sub, *lines, decay_ref, keep_ref, pairs, [lambda: None])


def own_rows(rate_ref, half):
    core = lax.axis_index("ctx") % 2
    return rate_ref[pl.ds(pl.multiple_of(core * half, half), half), :]


def joined(is_right, mine, other, span, step):
    left = [jnp.where(is_right, o, m) for m, o in zip(mine, other)]
    right = [jnp.where(is_right, m, o) for m, o in zip(mine, other)]
    return (
        span * left[0] + right[0],
        left[1] + span * right[1],
        left[2] + right[2] + step * right[1] * left[0],
    )


def put_wire(wire_ref, is_last, next_right, block):
    if is_last:
        wire_ref[0] = jnp.where(next_right, block[1], block[0]).astype(wire_ref.dtype)
        wire_ref[1] = block[2].astype(wire_ref.dtype)
    else:
        for kind in range(3):
            wire_ref[kind] = block[kind].astype(wire_ref.dtype)


def pair_kernel(seq, is_last, keep_ref, got_ref, rate_ref, after_ref, block_ref, wire_ref):
    rate = own_rows(rate_ref, keep_ref.shape[1])
    place = lax.axis_index("ctx")
    block = joined(
        place % 2 == 1,
        [keep_ref[i] for i in range(3)],
        [got_ref[i] for i in range(3)],
        jnp.exp(-rate * seq),
        jnp.exp(-rate),
    )
    for kind in range(3):
        block_ref[kind] = block[kind]
    block_ref[3] = jnp.zeros_like(rate)
    block_ref[4] = jnp.zeros_like(rate)
    put_wire(wire_ref, is_last, (place // 2) % 2 == 1, block)


def carries_with(block_ref, end_state, start_state, level, seq, rate):
    place = lax.axis_index("ctx")
    is_right = (place >> level) % 2 == 1
    chips = 1 << (level - 1)
    at = (place // 2) % chips
    before = at * (2 * seq)
    behind = (chips - 1 - at) * (2 * seq)
    ahead = block_ref[3] + jnp.where(
        is_right, jnp.exp(-rate * before.astype(F32)) * end_state, 0.0
    )
    after = block_ref[4] + jnp.where(
        is_right, 0.0, jnp.exp(-rate * behind.astype(F32)) * start_state
    )
    return is_right, ahead, after


def level_kernel(
    seq, level, is_last, block_ref, got_ref, rate_ref, after_ref, out_ref, wire_ref
):
    rate = own_rows(rate_ref, block_ref.shape[1])
    got = [got_ref[i].astype(F32) for i in range(3)]
    is_right, ahead, after = carries_with(block_ref, got[0], got[1], level, seq, rate)
    block = joined(
        is_right,
        [block_ref[i] for i in range(3)],
        got,
        jnp.exp(-rate * (seq << level)),
        jnp.exp(-rate),
    )
    for kind in range(3):
        out_ref[kind] = block[kind]
    out_ref[3] = ahead
    out_ref[4] = after
    next_right = (lax.axis_index("ctx") >> (level + 1)) % 2 == 1
    put_wire(wire_ref, is_last, next_right, block)


def last_kernel(
    seq,
    level,
    block_ref,
    got_ref,
    rate_ref,
    keep_ref,
    sibling_ref,
    after_ref,
    mine_ref,
    other_ref,
    share_ref,
):
    half = block_ref.shape[1]
    rate = own_rows(rate_ref, half)
    edge, inner = got_ref[0].astype(F32), got_ref[1].astype(F32)
    is_right, ahead, after = carries_with(block_ref, edge, edge, level, seq, rate)
    own_edge = jnp.where(is_right, block_ref[1], block_ref[0])
    total = block_ref[2] + inner + jnp.exp(-rate) * own_edge * edge
    raw = jnp.sqrt(1.0 - jnp.exp(-2.0 * rate)) * total
    core = lax.axis_index("ctx") % 2
    first = core == 0
    span = jnp.exp(-rate * seq)
    end_first = jnp.where(first, keep_ref[0], sibling_ref[0])
    start_second = jnp.where(first, sibling_ref[1], keep_ref[1])
    ahead_second = span * ahead + end_first
    after_first = span * after + start_second
    mine_ref[0:half, :] = jnp.where(first, ahead, ahead_second)
    mine_ref[half : 2 * half, :] = jnp.where(first, after_first, after)
    other_ref[0:half, :] = jnp.where(first, ahead_second, ahead)
    other_ref[half : 2 * half, :] = jnp.where(first, after, after_first)
    squares = raw * raw
    share_ref[...] = tree_sum([squares[i : i + 8, :] for i in range(0, half, 8)])
    mine_ref[2 * half : 3 * half, :] = raw
    other_ref[2 * half : 3 * half, :] = raw


def place_halves(mine_ref, other_ref, first, target):
    half = target.shape[0] // 2
    core = lax.axis_index("ctx") % 2
    for ref, at in ((mine_ref, core), (other_ref, 1 - core)):
        rows = pl.ds(pl.multiple_of(at * half, half), half)
        target[rows, :] = ref[first : first + half, :]


def first_local_kernel(modes, *refs):
    line_refs, (decay_ref, rate_ref, res_cols, after_ref, out_ref, coef_ref) = refs[:-6], refs[-6:]
    sub = decay_ref.shape[0] // (out_ref.shape[0] * modes)
    spread(res_cols, coef_ref, modes, sub)
    coef_ref[...] = coef_ref[...] * jnp.sqrt(1.0 - jnp.exp(-2.0 * rate_ref[...]))
    local_kernel(False, modes, *line_refs, decay_ref, coef_ref, after_ref, out_ref)


def local_kernel(reverse, modes, *refs):
    line_refs, (decay_ref, coef_ref, after_ref, out_ref) = refs[:-4], refs[-4:]
    blocks = out_ref.shape[0]
    sub = decay_ref.shape[0] // (blocks * modes)
    seq = out_ref.shape[1] // sub
    core = lax.axis_index("ctx") % 2
    for ref, which in zip(line_refs, (1 - core, core)):
        for slot in range(ref.shape[0]):
            block = which * ref.shape[0] + slot if blocks > 1 else 0
            rows = [
                pl.ds(pl.multiple_of((block * modes + n) * sub, sub), sub) for n in range(modes)
            ]
            decay = [decay_ref[r, :] for r in rows]
            coef = [coef_ref[r, :] for r in rows]

            def body(j, carry):
                held = list(carry)
                for u in range(UNROLL):
                    t = j * UNROLL + u
                    if reverse:
                        t = seq - 1 - t
                    at = pl.ds(pl.multiple_of(t * sub, sub), sub)
                    x = ref[slot, at, :]
                    total = [None] * 4
                    for n in range(modes):
                        held[n] = decay[n] * held[n] + x
                        term = coef[n] * held[n]
                        total[n % 4] = term if n < 4 else total[n % 4] + term
                    out_ref[block, at, :] = tree_sum(total)
                return tuple(held)

            first = tuple(jnp.zeros((sub, LANES), F32) for _ in range(modes))
            lax.fori_loop(0, seq // UNROLL, body, first)


def add_carries(reverse, unit, sub, decay_ref, coef_ref, states_ref, at_row, source, target, at):
    _, base, modes = unit
    seq = target.shape[1] // sub
    rows = [pl.ds(pl.multiple_of(base + n * sub, sub), sub) for n in range(modes)]
    decay = [decay_ref[r, :] for r in rows]
    first = tuple(
        coef_ref[r, :] * states_ref[at_row + n * sub : at_row + (n + 1) * sub, :]
        for n, r in enumerate(rows)
    )

    def body(j, carry):
        held = list(carry)
        for u in range(UNROLL):
            t = j * UNROLL + u
            if reverse:
                t = seq - 1 - t
            where = pl.ds(pl.multiple_of(t * sub, sub), sub)
            total = [source[where, :], None, None, None]
            for n in range(modes):
                held[n] = decay[n] * held[n]
                total[n % 4] = held[n] if total[n % 4] is None else total[n % 4] + held[n]
            target[at, where, :] = tree_sum(total)
        return tuple(held)

    lax.fori_loop(0, seq // UNROLL, body, first)


def own_kernel(modes, conv_ref, adj_ref, decay_ref, coef_ref, mine_ref, conv_own, adj_own):
    blocks = conv_ref.shape[0]
    sub = decay_ref.shape[0] // (blocks * modes)
    half = decay_ref.shape[0] // 2
    core = lax.axis_index("ctx") % 2
    for i, unit in enumerate(half_units(core, blocks, modes, sub)):
        at_row = i * unit[2] * sub
        for reverse, source, target in ((False, conv_ref, conv_own), (True, adj_ref, adj_own)):
            add_carries(
                reverse,
                unit,
                sub,
                decay_ref,
                coef_ref,
                mine_ref,
                at_row + half * reverse,
                source.at[unit[0]],
                target,
                i,
            )


def other_carries(reverse, modes, decay_ref, coef_ref, other_ref, local_ref, own_ref, whole, sem):
    blocks, own_blocks = local_ref.shape[0], own_ref.shape[0]
    sub = decay_ref.shape[0] // (blocks * modes)
    half = decay_ref.shape[0] // 2
    core = lax.axis_index("ctx") % 2
    copy = pltpu.make_async_copy(own_ref, whole.at[pl.ds(core * own_blocks, own_blocks)], sem)
    if blocks > 1:
        copy.start()
    for i, unit in enumerate(half_units(1 - core, blocks, modes, sub)):
        source = local_ref.at[unit[0]] if blocks > 1 else own_ref.at[0]
        at_row = i * unit[2] * sub + half * reverse
        add_carries(
            reverse, unit, sub, decay_ref, coef_ref, other_ref, at_row, source, whole, unit[0]
        )
    if blocks > 1:
        copy.wait()


def line_outputs(
    from_scan, left, right, scales, skip_ref, scanned, targets, which, done_with=None
):
    seq, channels = left.shape
    blocks = scanned.shape[0]
    sub = channels // (blocks * LANES)
    part = math.gcd(seq, STEP_ROWS)
    for i in which:
        rows = slice(i * part, (i + 1) * part)
        to_rows = slice((i - which[0]) * part, (i - which[0] + 1) * part)
        stacked = jnp.concatenate(
            [scanned[b, i * part * sub : (i + 1) * part * sub, :] for b in range(blocks)], axis=1
        ).astype(jnp.bfloat16)
        ordered = jnp.dot(from_scan[...], stacked, preferred_element_type=F32)
        for b in range(blocks):
            for s in range(sub):
                cols = slice((b * sub + s) * LANES, (b * sub + s + 1) * LANES)
                own = ordered[s * part : (s + 1) * part, b * LANES : (b + 1) * LANES]
                line = left[rows, cols].astype(F32) * right[rows, cols].astype(F32)
                mixed = own + skip_ref[:, cols] * line.astype(jnp.bfloat16).astype(F32)
                for scale, target in zip(scales, targets):
                    target[to_rows, cols] = (scale[rows, cols].astype(F32) * mixed).astype(
                        jnp.bfloat16
                    )
        if done_with is not None:
            done_with(pl.ds((i - which[0]) * part, part), pl.ds(i * part, part))


def forward_kernel(
    modes,
    q_ref,
    k_ref,
    v_ref,
    ct_ref,
    decay_ref,
    coef_ref,
    skip_ref,
    other_ref,
    from_scan,
    conv_ref,
    conv_own,
    after_ref,
    out_ref,
    gq_ref,
    token_ref,
    scanned,
    sem,
):
    token_ref[...] = jnp.zeros_like(token_ref)
    other_carries(
        False, modes, decay_ref, coef_ref, other_ref, conv_ref, conv_own, scanned, sem
    )
    line_outputs(
        from_scan,
        k_ref,
        v_ref,
        (q_ref, ct_ref),
        skip_ref,
        scanned,
        (out_ref, gq_ref),
        range(k_ref.shape[0] // math.gcd(k_ref.shape[0], STEP_ROWS)),
    )


def early_parts(seq):
    parts = seq // math.gcd(seq, STEP_ROWS)
    return range((parts + 1) // 2), range((parts + 1) // 2, parts)


def adjoint_kernel(
    modes,
    q_ref,
    k_ref,
    v_ref,
    ct_ref,
    decay_ref,
    coef_ref,
    skip_ref,
    other_ref,
    from_scan,
    adj_ref,
    adj_own,
    out_rows,
    gq_rows,
    after_ref,
    out_hbm,
    gq_hbm,
    scanned,
    gk_ref,
    gv_ref,
    token_ref,
    sems,
):
    token_ref[...] = jnp.zeros_like(token_ref)
    copies = [
        pltpu.make_async_copy(out_rows, out_hbm, sems.at[0]),
        pltpu.make_async_copy(gq_rows, gq_hbm, sems.at[1]),
    ]
    for copy in copies:
        copy.start()
    other_carries(
        True, modes, decay_ref, coef_ref, other_ref, adj_ref, adj_own, scanned, sems.at[2]
    )
    line_outputs(
        from_scan,
        ct_ref,
        q_ref,
        (v_ref, k_ref),
        skip_ref,
        scanned,
        (gk_ref, gv_ref),
        early_parts(q_ref.shape[0])[0],
    )
    for copy in copies:
        copy.wait()


def last_outputs_kernel(limit, *refs):
    q_ref, k_ref, v_ref, ct_ref, scanned, skip_ref, gk_early, gv_early = refs[:8]
    mine_ref, other_ref, from_scan = refs[8:11]
    share_refs = refs[12:-8]
    raw_hbm, gk_hbm, gv_hbm, gk_rows, gv_rows, raw_cols, states, sems = refs[-8:]
    copies = []

    def start(source, target):
        copy = pltpu.make_async_copy(source, target, sems.at[len(copies)])
        copy.start()
        copies.append(copy)

    early = pl.ds(0, gk_early.shape[0])
    start(gk_early, gk_hbm.at[early])
    start(gv_early, gv_hbm.at[early])
    clip(limit, scanned.shape[0], mine_ref, other_ref, share_refs, raw_cols, states)
    start(raw_cols, raw_hbm)

    def send(at, to):
        start(gk_rows.at[at], gk_hbm.at[to])
        start(gv_rows.at[at], gv_hbm.at[to])

    late = early_parts(q_ref.shape[0])[1]
    if len(late) > 0:
        sides, targets = (v_ref, k_ref), (gk_rows, gv_rows)
        line_outputs(
            from_scan, ct_ref, q_ref, sides, skip_ref, scanned, targets, late, send
        )
    for copy in copies:
        copy.wait()


def add_kernel(after_ref, *refs):
    refs[-1][...] = tree_sum([ref[...] for ref in refs[:-1]])


def clip(limit, blocks, mine_ref, other_ref, share_refs, out_ref, states):
    modes = out_ref.shape[0]
    sub = out_ref.shape[1] // (blocks * LANES)
    half = states.shape[0] // 2
    place_halves(mine_ref, other_ref, 2 * half, states)
    square = jnp.sum(tree_sum([ref[...] for ref in share_refs]))
    factor = jnp.minimum(1.0, limit * lax.rsqrt(jnp.full((1, LANES), square + 1e-06, F32)))
    for b in range(blocks):
        for s in range(sub):
            cols = slice((b * sub + s) * LANES, (b * sub + s + 1) * LANES)
            rows = pl.ds(b * modes * sub + s, modes, stride=sub)
            out_ref[:, cols] = states[rows, :] * factor


def shards(queries, keys_in, values_in, decay_rates, residues, skip_gain, cotangent):
    seq, channels = queries.shape
    modes = decay_rates.shape[1]
    ctx = lax.axis_size("ctx")
    tp = lax.axis_size("tp")
    levels = ctx.bit_length() - 1
    groups = channels // LANES
    sub = math.gcd(groups, 8)
    blocks = groups // sub
    half = modes * groups // 2
    part = math.gcd(seq, STEP_ROWS)
    parts, size = seq // part, part * sub

    def swap(value, bit):
        return lax.ppermute(value, "ctx", [(i, i ^ (1 << bit)) for i in range(ctx)])

    def rows(*shape, dtype=F32):
        return jax.ShapeDtypeStruct((*shape, LANES), dtype)

    line_shape = jax.ShapeDtypeStruct((seq, channels), jnp.bfloat16)
    table_shape = jax.ShapeDtypeStruct((modes, channels), F32)
    line_scratch = pltpu.VMEM((seq, channels), jnp.bfloat16)
    table_scratch = pltpu.VMEM((modes, channels), F32)
    own_shape = rows(max(blocks // 2, 1), seq * sub)
    elements = seq * channels * modes
    tables = (decay_rates.T, residues.T, skip_gain.reshape(1, channels))
    sources = (queries, keys_in, values_in, cotangent, *tables)

    (
        send,
        q,
        k,
        v,
        ct,
        gated,
        pulled,
        row_rates,
        row_decay,
        to_scan,
        from_scan,
        res_cols,
        skip,
    ) = pl.pallas_call(
        send_kernel,
        in_specs=[HBM] * 7,
        out_specs=[VMEM] * 13,
        out_shape=[rows(3, half)]
        + [line_shape] * 4
        + [own_shape] * 2
        + [rows(2 * half)] * 2
        + [jax.ShapeDtypeStruct((size, size), jnp.bfloat16)] * 2
        + [table_shape, jax.ShapeDtypeStruct((1, channels), F32)],
        scratch_shapes=[table_scratch, pltpu.SemaphoreType.DMA((4 * parts + 7,))],
        compiler_params=KERNEL,
        cost_estimate=pl.CostEstimate(
            flops=3 * elements, bytes_accessed=8 * seq * channels, transcendentals=0
        ),
        name="sent_states",
    )(*[pltpu.with_memory_space_constraint(item, pltpu.HBM) for item in sources])
    sibling = swap(send, 0)
    keep, *kept_lines = pl.pallas_call(
        keep_kernel,
        out_shape=[rows(3, half)] + [own_shape] * (2 if blocks > 1 else 0),
        compiler_params=KERNEL,
        cost_estimate=pl.CostEstimate(
            flops=3 * elements, bytes_accessed=8 * seq * channels, transcendentals=0
        ),
        name="kept_states",
    )(q, k, v, ct, row_decay, to_scan, gated, pulled)
    gated, pulled = (gated, *kept_lines[:1]), (pulled, *kept_lines[1:])

    def wire(level):
        return rows(2 if level == levels - 1 else 3, half, dtype=WIRE)

    whole = rows(blocks, seq * sub)
    whole_scratch = pltpu.VMEM((blocks, seq * sub, LANES), F32)
    states_scratch = pltpu.VMEM((2 * half, LANES), F32)
    local_cost = pl.CostEstimate(
        flops=4 * elements, bytes_accessed=8 * seq * channels, transcendentals=0
    )

    block, packed = pl.pallas_call(
        partial(pair_kernel, seq, levels == 2),
        out_shape=[rows(5, half), wire(1)],
        compiler_params=KERNEL,
        name="chip_states",
    )(keep, sibling, row_rates, row_rates[:8])
    got = swap(packed, 1)
    conv, row_coefs = pl.pallas_call(
        partial(first_local_kernel, modes),
        out_shape=[whole, rows(2 * half)],
        compiler_params=KERNEL,
        cost_estimate=local_cost,
        name="local_conv",
    )(*gated, row_decay, row_rates, res_cols, block[4, :8])
    for level in range(1, levels - 1):
        block, packed = pl.pallas_call(
            partial(level_kernel, seq, level, level + 1 == levels - 1),
            out_shape=[rows(5, half), wire(level + 1)],
            compiler_params=KERNEL,
            name="block_states",
        )(block, got, row_rates, conv[0, :8])
        got = swap(packed, level + 1)
    adj = pl.pallas_call(
        partial(local_kernel, True, modes),
        out_shape=whole,
        compiler_params=KERNEL,
        cost_estimate=local_cost,
        name="local_adjoint",
    )(*pulled, row_decay, row_coefs, block[4, :8])
    mine, other, square = pl.pallas_call(
        partial(last_kernel, seq, levels - 1),
        out_shape=[rows(3 * half)] * 2 + [rows(8)],
        compiler_params=KERNEL,
        name="carries",
    )(block, got, row_rates, keep, sibling, adj[0, :8])
    other = swap(other, 0)
    early, late = early_parts(seq)
    early_shape = jax.ShapeDtypeStruct((seq * len(early) // parts, channels), jnp.bfloat16)
    late_scratch = pltpu.VMEM((seq * max(len(late), 1) // parts, channels), jnp.bfloat16)
    kept = {}

    def add_own(after):
        kept["conv"], kept["adj"] = pl.pallas_call(
            partial(own_kernel, modes),
            out_shape=[own_shape] * 2,
            compiler_params=KERNEL,
            cost_estimate=pl.CostEstimate(
                flops=2 * elements, bytes_accessed=8 * seq * channels, transcendentals=0
            ),
            name="own_carries",
        )(conv, adj, row_decay, row_coefs, mine)
        return kept["adj"][0, :8]

    def forward_outputs(after):
        kept["out"], kept["gq"], token = pl.pallas_call(
            partial(forward_kernel, modes),
            out_shape=[line_shape] * 2 + [rows(8)],
            scratch_shapes=[whole_scratch, pltpu.SemaphoreType.DMA],
            compiler_params=KERNEL,
            cost_estimate=pl.CostEstimate(
                flops=2 * elements, bytes_accessed=16 * seq * channels, transcendentals=0
            ),
            name="forward_outputs",
        )(
            q,
            k,
            v,
            ct,
            row_decay,
            row_coefs,
            skip,
            other,
            from_scan,
            conv,
            kept["conv"],
            after,
        )
        return token

    def adjoint_outputs(after):
        results = (
            pl.pallas_call(
                partial(adjoint_kernel, modes),
                in_specs=[VMEM] * 14,
                out_specs=[HBM] * 2 + [VMEM] * 4,
                out_shape=[line_shape] * 2 + [whole] + [early_shape] * 2 + [rows(8)],
                scratch_shapes=[pltpu.SemaphoreType.DMA((3,))],
                compiler_params=KERNEL,
                cost_estimate=pl.CostEstimate(
                    flops=2 * elements, bytes_accessed=8 * seq * channels, transcendentals=0
                ),
                name="adjoint_outputs",
            )(
                q,
                k,
                v,
                ct,
                row_decay,
                row_coefs,
                skip,
                other,
                from_scan,
                adj,
                kept["adj"],
                kept["out"],
                kept["gq"],
                after,
            )
        )
        kept["final"] = results[:-1]
        return results[-1]

    def plus(after, *shares):
        return pl.pallas_call(
            add_kernel,
            in_specs=[VMEM] * (1 + len(shares)),
            out_shape=rows(8),
            compiler_params=KERNEL,
            name="square_sum",
        )(after, *shares)

    def tp_swap(value, mask):
        return lax.ppermute(value, "tp", [(i, i ^ mask) for i in range(tp)])

    works = [add_own, forward_outputs]
    for bit in range(0, tp.bit_length() - 1, 2):
        masks = [m << bit for m in (1, 2, 3) if m << bit < tp]
        shares = [tp_swap(square, mask) for mask in masks]
        after = square
        while works:
            after = works.pop(0)(after)
        square = plus(after, square, *shares)
    share = swap(square, 0)
    after = square
    for work in works + [adjoint_outputs]:
        after = work(after)
    operator_out, grad_queries, scanned, early_keys, early_values = kept["final"]
    grad_residues, grad_keys, grad_values = pl.pallas_call(
        partial(last_outputs_kernel, math.sqrt(channels * tp * modes)),
        in_specs=[VMEM] * 14,
        out_specs=[HBM] * 3,
        out_shape=[table_shape] + [line_shape] * 2,
        scratch_shapes=[
            late_scratch,
            late_scratch,
            table_scratch,
            states_scratch,
            pltpu.SemaphoreType.DMA((2 * parts + 3,)),
        ],
        compiler_params=KERNEL,
        cost_estimate=pl.CostEstimate(
            flops=elements, bytes_accessed=8 * seq * channels, transcendentals=0
        ),
        name="last_outputs",
    )(
        q,
        k,
        v,
        ct,
        scanned,
        skip,
        early_keys,
        early_values,
        mine,
        other,
        from_scan,
        after,
        square,
        share,
    )
    return (operator_out, grad_queries, grad_keys, grad_values, grad_residues.T)


def solution(mesh):
    lines, tables = P("ctx", "tp"), P("tp", None)
    in_specs = (lines, lines, lines, tables, tables, P("tp"), lines)
    out_specs = (lines, lines, lines, lines, tables)
    return jax.shard_map(shards, mesh=mesh, in_specs=in_specs, out_specs=out_specs, check_vma=False)
```

```python
from functools import partial
import math

import jax
import jax.numpy as jnp
from jax import lax
from jax.experimental import pallas as pl
from jax.experimental.pallas import tpu as pltpu
from jax.sharding import PartitionSpec as P

F32 = jnp.float32
WIRE = jnp.bfloat16
LANES = 128
UNROLL = 8
GROUP = 16
STEP_ROWS = 32
KERNEL = pltpu.CompilerParams(vmem_limit_bytes=24 * 1024 * 1024)
HBM = pl.BlockSpec(memory_space=pltpu.HBM)
VMEM = pl.BlockSpec(memory_space=pltpu.VMEM)


def reorder(rows, inner):
    outer = rows // inner
    first = lax.broadcasted_iota(jnp.int32, (rows, rows), 0)
    second = lax.broadcasted_iota(jnp.int32, (rows, rows), 1)

    def matrix(to, fro):
        if inner & (inner - 1) == 0 and outer & (outer - 1) == 0:
            low, high = inner.bit_length() - 1, outer.bit_length() - 1
            same = (fro & (inner - 1)) * outer + (fro >> low) == to
        else:
            same = (fro % inner) * outer + fro // inner == to
        return jnp.where(same, 1.0, 0.0).astype(jnp.bfloat16)

    return matrix(first, second), matrix(second, first)


def tree_sum(items):
    items = list(items)
    while len(items) > 1:
        items = [
            items[i] + items[i + 1] if i + 1 < len(items) else items[i]
            for i in range(0, len(items), 2)
        ]
    return items[0]


def spread(source, target, modes, sub):
    for group in range(source.shape[1] // LANES):
        cols = slice(group * LANES, (group + 1) * LANES)
        first = group // sub * (modes * sub) + group % sub
        target[pl.ds(first, modes, stride=sub), :] = source[:, cols]


def half_units(which, blocks, modes, sub):
    if blocks == 1:
        return [(0, which * (modes // 2 * sub), modes // 2)]
    count = blocks // 2
    return [
        (which * count + j, (which * count + j) * (modes * sub), modes) for j in range(count)
    ]


def to_scan_order(to_scan, pairs, part, i, block, targets, slot):
    size, sub = to_scan.shape[0], to_scan.shape[0] // part
    rows = slice(i * part, (i + 1) * part)
    sides = []
    for left, right in pairs:
        stacked = []
        for s in range(sub):
            cols = pl.ds(pl.multiple_of((block * sub + s) * LANES, LANES), LANES)
            product = left[rows, cols].astype(F32) * right[rows, cols].astype(F32)
            stacked.append(product.astype(jnp.bfloat16))
        sides.append(jnp.concatenate(stacked, axis=0))
    ordered = jnp.dot(
        to_scan[...], jnp.concatenate(sides, axis=1), preferred_element_type=F32
    )
    for j, target in enumerate(targets):
        target[slot, i * size : (i + 1) * size, :] = ordered[:, j * LANES : (j + 1) * LANES]


def exchange_rows(items):
    size = len(items)
    row = lax.broadcasted_iota(jnp.int32, items[0].shape, 0)
    step = size // 2
    while step:
        low = (row & step) == 0
        for i in range(size):
            if i & step == 0:
                first, second = items[i], items[i + step]
                items[i] = jnp.where(low, first, pltpu.roll(second, step, 0))
                items[i + step] = jnp.where(low, pltpu.roll(first, size - step, 0), second)
        step //= 2
    return items


def fill_group(left, right, group, block, target, slot):
    rows = pl.ds(pl.multiple_of(group * GROUP, GROUP), GROUP)
    products = []
    for s in range(8):
        cols = pl.ds(pl.multiple_of((block * 8 + s) * LANES, LANES), LANES)
        product = left[rows, cols].astype(F32) * right[rows, cols].astype(F32)
        products.append(product.astype(jnp.bfloat16).astype(F32))
    for at in range(0, GROUP, 8):
        ordered = exchange_rows([product[at : at + 8, :] for product in products])
        for t in range(8):
            where = pl.ds(pl.multiple_of((group * GROUP + at + t) * 8, 8), 8)
            target[slot, where, :] = ordered[t]


def scan_states(unit, slot, sub, gated_ref, pulled_ref, decay_ref, out_ref, pairs, waits):
    block, base, modes = unit
    at_row = slot * modes * sub
    seq = gated_ref.shape[1] // sub
    slot = slot % gated_ref.shape[0]
    decay = [
        decay_ref[pl.ds(pl.multiple_of(base + n * sub, sub), sub), :] for n in range(modes)
    ]
    first = tuple(jnp.zeros((sub, LANES), F32) for _ in range(modes))

    def forward(j, carry):
        held, inner = list(carry[0]), list(carry[1])
        for u in range(UNROLL):
            at = pl.ds(pl.multiple_of((j * UNROLL + u) * sub, sub), sub)
            x = gated_ref[slot, at, :]
            p = pulled_ref[slot, at, :]
            for n in range(modes):
                held[n] = decay[n] * held[n] + x
                inner[n] = inner[n] + p * held[n]
        return tuple(held), tuple(inner)

    def backward(step, fill, last, j, carry):
        held = list(carry)
        group = last - j
        for u in reversed(range(step)):
            at = pl.ds(pl.multiple_of((group * step + u) * sub, sub), sub)
            p = pulled_ref[slot, at, :]
            for n in range(modes):
                held[n] = decay[n] * held[n] + p
            if fill and u in (12, 6):
                left, right, target = pairs[0 if u == 12 else 1]
                fill_group(left, right, jnp.maximum(group - 1, 0), block, target, slot)
        return tuple(held)

    if pairs is None:
        last = seq // UNROLL - 1
        starts = lax.fori_loop(0, last + 1, partial(backward, UNROLL, False, last), first)
    else:
        starts = first
        groups = seq // GROUP // len(waits)
        waits[-1]()
        for left, right, target in pairs:
            fill_group(left, right, seq // GROUP - 1, block, target, slot)
        for i in reversed(range(len(waits))):
            if i > 0:
                waits[i - 1]()
            last = (i + 1) * groups - 1
            starts = lax.fori_loop(0, groups, partial(backward, GROUP, True, last), starts)
    for n in range(modes):
        out_ref[1, at_row + n * sub : at_row + (n + 1) * sub, :] = starts[n]
    ends, inner = lax.fori_loop(0, seq // UNROLL, forward, (first, first))
    for n in range(modes):
        rows = slice(at_row + n * sub, at_row + (n + 1) * sub)
        out_ref[0, rows, :] = ends[n]
        out_ref[2, rows, :] = inner[n]


def can_exchange(sub, part, units):
    return sub == 8 and part % GROUP == 0 and len(units) == 1


def send_kernel(
    q_hbm,
    k_hbm,
    v_hbm,
    ct_hbm,
    rate_hbm,
    res_hbm,
    skip_hbm,
    send_ref,
    q_ref,
    k_ref,
    v_ref,
    ct_ref,
    gated_ref,
    pulled_ref,
    rate_ref,
    decay_ref,
    to_scan,
    from_scan,
    res_cols,
    skip_ref,
    rate_cols,
    sems,
):
    seq, channels = q_ref.shape
    modes = rate_cols.shape[0]
    sub = gated_ref.shape[1] // seq
    blocks = channels // (sub * LANES)
    part = math.gcd(seq, STEP_ROWS)
    parts = seq // part
    which = 1 - lax.axis_index("ctx") % 2
    pairs = ((k_hbm, k_ref), (v_hbm, v_ref), (ct_hbm, ct_ref), (q_hbm, q_ref))
    copies = []

    def start(source, target):
        copy = pltpu.make_async_copy(source, target, sems.at[len(copies)])
        copy.start()
        copies.append(copy)

    width = channels // min(blocks, 2)
    cols = pl.ds(pl.multiple_of(which * width, LANES) if blocks > 1 else 0, width)
    start(rate_hbm, rate_cols)
    for i in reversed(range(parts)):
        rows = pl.ds(i * part, part)
        for source, target in pairs:
            start(source.at[rows, cols], target.at[rows, cols])
    if blocks > 1:
        cols = pl.ds(pl.multiple_of((1 - which) * width, LANES), width)
        for source, target in pairs:
            start(source.at[:, cols], target.at[:, cols])
    start(res_hbm, res_cols)
    start(skip_hbm, skip_ref)
    to_scan[...], from_scan[...] = reorder(part * sub, part)
    copies[0].wait()
    spread(rate_cols, rate_ref, modes, sub)
    decay_ref[...] = jnp.exp(-rate_ref[...])
    units = half_units(which, blocks, modes, sub)

    def wait_part(i):
        for copy in copies[4 * (parts - 1 - i) + 1 : 4 * (parts - i) + 1]:
            copy.wait()

    if can_exchange(sub, part, units):
        waits = [partial(wait_part, i) for i in range(parts)]
        lines = ((k_ref, v_ref, gated_ref), (ct_ref, q_ref, pulled_ref))
    else:
        waits, lines = None, None
        for i in reversed(range(parts)):
            wait_part(i)
            for at, unit in enumerate(units):
                both = ((k_ref, v_ref), (ct_ref, q_ref))
                to_scan_order(to_scan, both, part, i, unit[0], (gated_ref, pulled_ref), at)
    for at, unit in enumerate(units):
        scan_states(unit, at, sub, gated_ref, pulled_ref, decay_ref, send_ref, lines, waits)
    for copy in copies[4 * parts + 1 :]:
        copy.wait()


def keep_kernel(
    q_ref, k_ref, v_ref, ct_ref, decay_ref, to_scan, gated_in, pulled_in, keep_ref, *line_refs
):
    seq, channels = q_ref.shape
    sub = gated_in.shape[1] // seq
    blocks = channels // (sub * LANES)
    modes = decay_ref.shape[0] // (blocks * sub)
    part = math.gcd(seq, STEP_ROWS)
    units = half_units(lax.axis_index("ctx") % 2, blocks, modes, sub)
    lines, pairs = (gated_in, pulled_in), None
    if blocks > 1:
        lines = line_refs
        if can_exchange(sub, part, units):
            pairs = ((k_ref, v_ref, line_refs[0]), (ct_ref, q_ref, line_refs[1]))
        else:
            for i in range(seq // part):
                for at, unit in enumerate(units):
                    both = ((k_ref, v_ref), (ct_ref, q_ref))
                    to_scan_order(to_scan, both, part, i, unit[0], lines, at)
    for at, unit in enumerate(units):
        scan_states(unit, at, sub, *lines, decay_ref, keep_ref, pairs, [lambda: None])


def own_rows(rate_ref, half):
    core = lax.axis_index("ctx") % 2
    return rate_ref[pl.ds(pl.multiple_of(core * half, half), half), :]


def joined(is_right, mine, other, span, step):
    left = [jnp.where(is_right, o, m) for m, o in zip(mine, other)]
    right = [jnp.where(is_right, m, o) for m, o in zip(mine, other)]
    return (
        span * left[0] + right[0],
        left[1] + span * right[1],
        left[2] + right[2] + step * right[1] * left[0],
    )


def put_wire(wire_ref, is_last, next_right, block):
    if is_last:
        wire_ref[0] = jnp.where(next_right, block[1], block[0]).astype(wire_ref.dtype)
        wire_ref[1] = block[2].astype(wire_ref.dtype)
    else:
        for kind in range(3):
            wire_ref[kind] = block[kind].astype(wire_ref.dtype)


def pair_kernel(seq, is_last, keep_ref, got_ref, rate_ref, after_ref, block_ref, wire_ref):
    rate = own_rows(rate_ref, keep_ref.shape[1])
    place = lax.axis_index("ctx")
    block = joined(
        place % 2 == 1,
        [keep_ref[i] for i in range(3)],
        [got_ref[i] for i in range(3)],
        jnp.exp(-rate * seq),
        jnp.exp(-rate),
    )
    for kind in range(3):
        block_ref[kind] = block[kind]
    block_ref[3] = jnp.zeros_like(rate)
    block_ref[4] = jnp.zeros_like(rate)
    put_wire(wire_ref, is_last, (place // 2) % 2 == 1, block)


def carries_with(block_ref, end_state, start_state, level, seq, rate):
    place = lax.axis_index("ctx")
    is_right = (place >> level) % 2 == 1
    chips = 1 << (level - 1)
    at = (place // 2) % chips
    before = at * (2 * seq)
    behind = (chips - 1 - at) * (2 * seq)
    ahead = block_ref[3] + jnp.where(
        is_right, jnp.exp(-rate * before.astype(F32)) * end_state, 0.0
    )
    after = block_ref[4] + jnp.where(
        is_right, 0.0, jnp.exp(-rate * behind.astype(F32)) * start_state
    )
    return is_right, ahead, after


def level_kernel(
    seq, level, is_last, block_ref, got_ref, rate_ref, after_ref, out_ref, wire_ref
):
    rate = own_rows(rate_ref, block_ref.shape[1])
    got = [got_ref[i].astype(F32) for i in range(3)]
    is_right, ahead, after = carries_with(block_ref, got[0], got[1], level, seq, rate)
    block = joined(
        is_right,
        [block_ref[i] for i in range(3)],
        got,
        jnp.exp(-rate * (seq << level)),
        jnp.exp(-rate),
    )
    for kind in range(3):
        out_ref[kind] = block[kind]
    out_ref[3] = ahead
    out_ref[4] = after
    next_right = (lax.axis_index("ctx") >> (level + 1)) % 2 == 1
    put_wire(wire_ref, is_last, next_right, block)


def last_kernel(
    seq,
    level,
    block_ref,
    got_ref,
    rate_ref,
    keep_ref,
    sibling_ref,
    after_ref,
    mine_ref,
    other_ref,
):
    half = block_ref.shape[1]
    rate = own_rows(rate_ref, half)
    edge, inner = got_ref[0].astype(F32), got_ref[1].astype(F32)
    is_right, ahead, after = carries_with(block_ref, edge, edge, level, seq, rate)
    own_edge = jnp.where(is_right, block_ref[1], block_ref[0])
    total = block_ref[2] + inner + jnp.exp(-rate) * own_edge * edge
    raw = jnp.sqrt(1.0 - jnp.exp(-2.0 * rate)) * total
    core = lax.axis_index("ctx") % 2
    first = core == 0
    span = jnp.exp(-rate * seq)
    end_first = jnp.where(first, keep_ref[0], sibling_ref[0])
    start_second = jnp.where(first, sibling_ref[1], keep_ref[1])
    ahead_second = span * ahead + end_first
    after_first = span * after + start_second
    mine_ref[0:half, :] = jnp.where(first, ahead, ahead_second)
    mine_ref[half : 2 * half, :] = jnp.where(first, after_first, after)
    other_ref[0:half, :] = jnp.where(first, ahead_second, ahead)
    other_ref[half : 2 * half, :] = jnp.where(first, after, after_first)
    squares = raw * raw
    share = tree_sum([squares[i : i + 8, :] for i in range(0, half, 8)])
    for ref in (mine_ref, other_ref):
        ref[2 * half : 3 * half, :] = raw
        ref[3 * half : 3 * half + 8, :] = share


def place_halves(mine_ref, other_ref, first, target):
    half = target.shape[0] // 2
    core = lax.axis_index("ctx") % 2
    for ref, at in ((mine_ref, core), (other_ref, 1 - core)):
        rows = pl.ds(pl.multiple_of(at * half, half), half)
        target[rows, :] = ref[first : first + half, :]


def first_local_kernel(modes, *refs):
    line_refs, (decay_ref, rate_ref, res_cols, after_ref, out_ref, coef_ref) = refs[:-6], refs[-6:]
    sub = decay_ref.shape[0] // (out_ref.shape[0] * modes)
    spread(res_cols, coef_ref, modes, sub)
    coef_ref[...] = coef_ref[...] * jnp.sqrt(1.0 - jnp.exp(-2.0 * rate_ref[...]))
    local_kernel(False, modes, *line_refs, decay_ref, coef_ref, after_ref, out_ref)


def local_kernel(reverse, modes, *refs):
    line_refs, (decay_ref, coef_ref, after_ref, out_ref) = refs[:-4], refs[-4:]
    blocks = out_ref.shape[0]
    sub = decay_ref.shape[0] // (blocks * modes)
    seq = out_ref.shape[1] // sub
    core = lax.axis_index("ctx") % 2
    for ref, which in zip(line_refs, (1 - core, core)):
        for slot in range(ref.shape[0]):
            block = which * ref.shape[0] + slot if blocks > 1 else 0
            rows = [
                pl.ds(pl.multiple_of((block * modes + n) * sub, sub), sub) for n in range(modes)
            ]
            decay = [decay_ref[r, :] for r in rows]
            coef = [coef_ref[r, :] for r in rows]

            def body(j, carry):
                held = list(carry)
                for u in range(UNROLL):
                    t = j * UNROLL + u
                    if reverse:
                        t = seq - 1 - t
                    at = pl.ds(pl.multiple_of(t * sub, sub), sub)
                    x = ref[slot, at, :]
                    total = [None] * 4
                    for n in range(modes):
                        held[n] = decay[n] * held[n] + x
                        term = coef[n] * held[n]
                        total[n % 4] = term if n < 4 else total[n % 4] + term
                    out_ref[block, at, :] = tree_sum(total)
                return tuple(held)

            first = tuple(jnp.zeros((sub, LANES), F32) for _ in range(modes))
            lax.fori_loop(0, seq // UNROLL, body, first)


def add_carries(reverse, unit, sub, decay_ref, coef_ref, states_ref, at_row, source, target, at):
    _, base, modes = unit
    seq = target.shape[1] // sub
    rows = [pl.ds(pl.multiple_of(base + n * sub, sub), sub) for n in range(modes)]
    decay = [decay_ref[r, :] for r in rows]
    first = tuple(
        coef_ref[r, :] * states_ref[at_row + n * sub : at_row + (n + 1) * sub, :]
        for n, r in enumerate(rows)
    )

    def body(j, carry):
        held = list(carry)
        for u in range(UNROLL):
            t = j * UNROLL + u
            if reverse:
                t = seq - 1 - t
            where = pl.ds(pl.multiple_of(t * sub, sub), sub)
            total = [source[where, :], None, None, None]
            for n in range(modes):
                held[n] = decay[n] * held[n]
                total[n % 4] = held[n] if total[n % 4] is None else total[n % 4] + held[n]
            target[at, where, :] = tree_sum(total)
        return tuple(held)

    lax.fori_loop(0, seq // UNROLL, body, first)


def own_kernel(modes, conv_ref, adj_ref, decay_ref, coef_ref, mine_ref, conv_own, adj_own):
    blocks = conv_ref.shape[0]
    sub = decay_ref.shape[0] // (blocks * modes)
    half = decay_ref.shape[0] // 2
    core = lax.axis_index("ctx") % 2
    for i, unit in enumerate(half_units(core, blocks, modes, sub)):
        at_row = i * unit[2] * sub
        for reverse, source, target in ((False, conv_ref, conv_own), (True, adj_ref, adj_own)):
            add_carries(
                reverse,
                unit,
                sub,
                decay_ref,
                coef_ref,
                mine_ref,
                at_row + half * reverse,
                source.at[unit[0]],
                target,
                i,
            )


def other_carries(reverse, modes, decay_ref, coef_ref, other_ref, local_ref, own_ref, whole, sem):
    blocks, own_blocks = local_ref.shape[0], own_ref.shape[0]
    sub = decay_ref.shape[0] // (blocks * modes)
    half = decay_ref.shape[0] // 2
    core = lax.axis_index("ctx") % 2
    copy = pltpu.make_async_copy(own_ref, whole.at[pl.ds(core * own_blocks, own_blocks)], sem)
    if blocks > 1:
        copy.start()
    for i, unit in enumerate(half_units(1 - core, blocks, modes, sub)):
        source = local_ref.at[unit[0]] if blocks > 1 else own_ref.at[0]
        at_row = i * unit[2] * sub + half * reverse
        add_carries(
            reverse, unit, sub, decay_ref, coef_ref, other_ref, at_row, source, whole, unit[0]
        )
    if blocks > 1:
        copy.wait()


def line_outputs(
    from_scan, left, right, scales, skip_ref, scanned, targets, which, done_with=None
):
    seq, channels = left.shape
    blocks = scanned.shape[0]
    sub = channels // (blocks * LANES)
    part = math.gcd(seq, STEP_ROWS)
    for i in which:
        rows = slice(i * part, (i + 1) * part)
        to_rows = slice((i - which[0]) * part, (i - which[0] + 1) * part)
        stacked = jnp.concatenate(
            [scanned[b, i * part * sub : (i + 1) * part * sub, :] for b in range(blocks)], axis=1
        ).astype(jnp.bfloat16)
        ordered = jnp.dot(from_scan[...], stacked, preferred_element_type=F32)
        for b in range(blocks):
            for s in range(sub):
                cols = slice((b * sub + s) * LANES, (b * sub + s + 1) * LANES)
                own = ordered[s * part : (s + 1) * part, b * LANES : (b + 1) * LANES]
                line = left[rows, cols].astype(F32) * right[rows, cols].astype(F32)
                mixed = own + skip_ref[:, cols] * line.astype(jnp.bfloat16).astype(F32)
                for scale, target in zip(scales, targets):
                    target[to_rows, cols] = (scale[rows, cols].astype(F32) * mixed).astype(
                        jnp.bfloat16
                    )
        if done_with is not None:
            done_with(pl.ds((i - which[0]) * part, part), pl.ds(i * part, part))


def forward_kernel(
    modes,
    q_ref,
    k_ref,
    v_ref,
    ct_ref,
    decay_ref,
    coef_ref,
    skip_ref,
    other_ref,
    from_scan,
    conv_ref,
    conv_own,
    after_ref,
    out_ref,
    gq_ref,
    token_ref,
    scanned,
    sem,
):
    token_ref[...] = jnp.zeros_like(token_ref)
    other_carries(
        False, modes, decay_ref, coef_ref, other_ref, conv_ref, conv_own, scanned, sem
    )
    line_outputs(
        from_scan,
        k_ref,
        v_ref,
        (q_ref, ct_ref),
        skip_ref,
        scanned,
        (out_ref, gq_ref),
        range(k_ref.shape[0] // math.gcd(k_ref.shape[0], STEP_ROWS)),
    )


def early_parts(seq):
    parts = seq // math.gcd(seq, STEP_ROWS)
    return range((parts + 1) // 2), range((parts + 1) // 2, parts)


def adjoint_kernel(
    modes,
    q_ref,
    k_ref,
    v_ref,
    ct_ref,
    decay_ref,
    coef_ref,
    skip_ref,
    other_ref,
    from_scan,
    adj_ref,
    adj_own,
    out_rows,
    gq_rows,
    after_ref,
    out_hbm,
    gq_hbm,
    scanned,
    gk_ref,
    gv_ref,
    token_ref,
    sems,
):
    token_ref[...] = jnp.zeros_like(token_ref)
    copies = [
        pltpu.make_async_copy(out_rows, out_hbm, sems.at[0]),
        pltpu.make_async_copy(gq_rows, gq_hbm, sems.at[1]),
    ]
    for copy in copies:
        copy.start()
    other_carries(
        True, modes, decay_ref, coef_ref, other_ref, adj_ref, adj_own, scanned, sems.at[2]
    )
    line_outputs(
        from_scan,
        ct_ref,
        q_ref,
        (v_ref, k_ref),
        skip_ref,
        scanned,
        (gk_ref, gv_ref),
        early_parts(q_ref.shape[0])[0],
    )
    for copy in copies:
        copy.wait()


def late_kernel(
    q_ref,
    k_ref,
    v_ref,
    ct_ref,
    scanned,
    skip_ref,
    gk_early,
    gv_early,
    from_scan,
    after_ref,
    gk_hbm,
    gv_hbm,
    token_ref,
    gk_rows,
    gv_rows,
    sems,
):
    token_ref[...] = jnp.zeros_like(token_ref)
    copies = []

    def start(source, target):
        copy = pltpu.make_async_copy(source, target, sems.at[len(copies)])
        copy.start()
        copies.append(copy)

    early = pl.ds(0, gk_early.shape[0])
    start(gk_early, gk_hbm.at[early])
    start(gv_early, gv_hbm.at[early])

    def send(at, to):
        start(gk_rows.at[at], gk_hbm.at[to])
        start(gv_rows.at[at], gv_hbm.at[to])

    late = early_parts(q_ref.shape[0])[1]
    if len(late) > 0:
        sides, targets = (v_ref, k_ref), (gk_rows, gv_rows)
        line_outputs(
            from_scan, ct_ref, q_ref, sides, skip_ref, scanned, targets, late, send
        )
    for copy in copies:
        copy.wait()


def add_kernel(first_core_only, after_ref, *refs):
    first, others, out_ref = refs[0][...], refs[1:-1], refs[-1]
    if first_core_only:
        first = jnp.where(lax.axis_index("ctx") % 2 == 0, first, 0.0)
    out_ref[...] = tree_sum([first] + [ref[...] for ref in others])


def clip_kernel(limit, blocks, mine_ref, other_ref, after_ref, *refs):
    share_refs, (out_ref, states) = refs[:-2], refs[-2:]
    modes = out_ref.shape[0]
    sub = out_ref.shape[1] // (blocks * LANES)
    half = states.shape[0] // 2
    place_halves(mine_ref, other_ref, 2 * half, states)
    square = jnp.sum(tree_sum([ref[...] for ref in share_refs]))
    factor = jnp.minimum(1.0, limit * lax.rsqrt(jnp.full((1, LANES), square + 1e-06, F32)))
    for b in range(blocks):
        for s in range(sub):
            cols = slice((b * sub + s) * LANES, (b * sub + s + 1) * LANES)
            rows = pl.ds(b * modes * sub + s, modes, stride=sub)
            out_ref[:, cols] = states[rows, :] * factor


def shards(queries, keys_in, values_in, decay_rates, residues, skip_gain, cotangent):
    seq, channels = queries.shape
    modes = decay_rates.shape[1]
    ctx = lax.axis_size("ctx")
    tp = lax.axis_size("tp")
    levels = ctx.bit_length() - 1
    groups = channels // LANES
    sub = math.gcd(groups, 8)
    blocks = groups // sub
    half = modes * groups // 2
    part = math.gcd(seq, STEP_ROWS)
    parts, size = seq // part, part * sub

    def swap(value, bit):
        return lax.ppermute(value, "ctx", [(i, i ^ (1 << bit)) for i in range(ctx)])

    def rows(*shape, dtype=F32):
        return jax.ShapeDtypeStruct((*shape, LANES), dtype)

    line_shape = jax.ShapeDtypeStruct((seq, channels), jnp.bfloat16)
    table_shape = jax.ShapeDtypeStruct((modes, channels), F32)
    line_scratch = pltpu.VMEM((seq, channels), jnp.bfloat16)
    table_scratch = pltpu.VMEM((modes, channels), F32)
    own_shape = rows(max(blocks // 2, 1), seq * sub)
    elements = seq * channels * modes
    tables = (decay_rates.T, residues.T, skip_gain.reshape(1, channels))
    sources = (queries, keys_in, values_in, cotangent, *tables)

    (
        send,
        q,
        k,
        v,
        ct,
        gated,
        pulled,
        row_rates,
        row_decay,
        to_scan,
        from_scan,
        res_cols,
        skip,
    ) = pl.pallas_call(
        send_kernel,
        in_specs=[HBM] * 7,
        out_specs=[VMEM] * 13,
        out_shape=[rows(3, half)]
        + [line_shape] * 4
        + [own_shape] * 2
        + [rows(2 * half)] * 2
        + [jax.ShapeDtypeStruct((size, size), jnp.bfloat16)] * 2
        + [table_shape, jax.ShapeDtypeStruct((1, channels), F32)],
        scratch_shapes=[table_scratch, pltpu.SemaphoreType.DMA((4 * parts + 7,))],
        compiler_params=KERNEL,
        cost_estimate=pl.CostEstimate(
            flops=3 * elements, bytes_accessed=8 * seq * channels, transcendentals=0
        ),
        name="sent_states",
    )(*[pltpu.with_memory_space_constraint(item, pltpu.HBM) for item in sources])
    sibling = swap(send, 0)
    keep, *kept_lines = pl.pallas_call(
        keep_kernel,
        out_shape=[rows(3, half)] + [own_shape] * (2 if blocks > 1 else 0),
        compiler_params=KERNEL,
        cost_estimate=pl.CostEstimate(
            flops=3 * elements, bytes_accessed=8 * seq * channels, transcendentals=0
        ),
        name="kept_states",
    )(q, k, v, ct, row_decay, to_scan, gated, pulled)
    gated, pulled = (gated, *kept_lines[:1]), (pulled, *kept_lines[1:])

    def wire(level):
        return rows(2 if level == levels - 1 else 3, half, dtype=WIRE)

    whole = rows(blocks, seq * sub)
    whole_scratch = pltpu.VMEM((blocks, seq * sub, LANES), F32)
    states_scratch = pltpu.VMEM((2 * half, LANES), F32)
    local_cost = pl.CostEstimate(
        flops=4 * elements, bytes_accessed=8 * seq * channels, transcendentals=0
    )

    block, packed = pl.pallas_call(
        partial(pair_kernel, seq, levels == 2),
        out_shape=[rows(5, half), wire(1)],
        compiler_params=KERNEL,
        name="chip_states",
    )(keep, sibling, row_rates, row_rates[:8])
    got = swap(packed, 1)
    conv, row_coefs = pl.pallas_call(
        partial(first_local_kernel, modes),
        out_shape=[whole, rows(2 * half)],
        compiler_params=KERNEL,
        cost_estimate=local_cost,
        name="local_conv",
    )(*gated, row_decay, row_rates, res_cols, block[4, :8])
    for level in range(1, levels - 1):
        block, packed = pl.pallas_call(
            partial(level_kernel, seq, level, level + 1 == levels - 1),
            out_shape=[rows(5, half), wire(level + 1)],
            compiler_params=KERNEL,
            name="block_states",
        )(block, got, row_rates, conv[0, :8])
        got = swap(packed, level + 1)
    adj = pl.pallas_call(
        partial(local_kernel, True, modes),
        out_shape=whole,
        compiler_params=KERNEL,
        cost_estimate=local_cost,
        name="local_adjoint",
    )(*pulled, row_decay, row_coefs, block[4, :8])
    mine, other = pl.pallas_call(
        partial(last_kernel, seq, levels - 1),
        out_shape=[rows(3 * half + 8)] * 2,
        compiler_params=KERNEL,
        name="carries",
    )(block, got, row_rates, keep, sibling, adj[0, :8])
    other = swap(other, 0)
    early, late = early_parts(seq)
    early_shape = jax.ShapeDtypeStruct((seq * len(early) // parts, channels), jnp.bfloat16)
    late_scratch = pltpu.VMEM((seq * max(len(late), 1) // parts, channels), jnp.bfloat16)
    kept = {}

    def add_own(after):
        kept["conv"], kept["adj"] = pl.pallas_call(
            partial(own_kernel, modes),
            out_shape=[own_shape] * 2,
            compiler_params=KERNEL,
            cost_estimate=pl.CostEstimate(
                flops=2 * elements, bytes_accessed=8 * seq * channels, transcendentals=0
            ),
            name="own_carries",
        )(conv, adj, row_decay, row_coefs, mine)
        return kept["adj"]

    def forward_outputs(after):
        kept["out"], kept["gq"], token = pl.pallas_call(
            partial(forward_kernel, modes),
            out_shape=[line_shape] * 2 + [rows(8)],
            scratch_shapes=[whole_scratch, pltpu.SemaphoreType.DMA],
            compiler_params=KERNEL,
            cost_estimate=pl.CostEstimate(
                flops=2 * elements, bytes_accessed=16 * seq * channels, transcendentals=0
            ),
            name="forward_outputs",
        )(
            q,
            k,
            v,
            ct,
            row_decay,
            row_coefs,
            skip,
            other,
            from_scan,
            conv,
            kept["conv"],
            after,
        )
        return token

    def adjoint_outputs(after):
        results = (
            pl.pallas_call(
                partial(adjoint_kernel, modes),
                in_specs=[VMEM] * 14,
                out_specs=[HBM] * 2 + [VMEM] * 4,
                out_shape=[line_shape] * 2 + [whole] + [early_shape] * 2 + [rows(8)],
                scratch_shapes=[pltpu.SemaphoreType.DMA((3,))],
                compiler_params=KERNEL,
                cost_estimate=pl.CostEstimate(
                    flops=2 * elements, bytes_accessed=8 * seq * channels, transcendentals=0
                ),
                name="adjoint_outputs",
            )(
                q,
                k,
                v,
                ct,
                row_decay,
                row_coefs,
                skip,
                other,
                from_scan,
                adj,
                kept["adj"],
                kept["out"],
                kept["gq"],
                after,
            )
        )
        kept["final"] = results[:-1]
        return results[-1]

    def plus(first_core_only, after, *shares):
        return pl.pallas_call(
            partial(add_kernel, first_core_only),
            in_specs=[VMEM] * (1 + len(shares)),
            out_shape=rows(8),
            compiler_params=KERNEL,
            name="square_sum",
        )(after, *shares)

    def core_swap(value, masks):
        pairs = [
            (i * tp + j, i * tp + (j ^ masks[i % 2]))
            for i in range(ctx)
            if i % 2 < len(masks)
            for j in range(tp)
        ]
        return lax.ppermute(value, ("ctx", "tp"), pairs)

    after = add_own(mine[:8])
    square = plus(False, after, mine[3 * half :], other[3 * half :])
    shares, after = [square], square
    works = [forward_outputs, adjoint_outputs]
    for bit in range(0, tp.bit_length() - 1, 2):
        if bit > 0:
            square = plus(False, after, *shares)
        masks = [m << bit for m in (1, 2, 3) if m << bit < tp]
        got = [core_swap(square, masks[at : at + 2]) for at in range(0, len(masks), 2)]
        for work in works:
            after = work(after)
        works = []
        square = plus(True, after, square, *got)
        shares = [square, swap(square, 0)]
        after = square
    for work in works:
        after = work(after)
    operator_out, grad_queries, scanned, early_keys, early_values = kept["final"]
    grad_keys, grad_values, after = pl.pallas_call(
        late_kernel,
        in_specs=[VMEM] * 10,
        out_specs=[HBM] * 2 + [VMEM],
        out_shape=[line_shape] * 2 + [rows(8)],
        scratch_shapes=[
            late_scratch,
            late_scratch,
            pltpu.SemaphoreType.DMA((2 * parts + 2,)),
        ],
        compiler_params=KERNEL,
        cost_estimate=pl.CostEstimate(
            flops=elements, bytes_accessed=8 * seq * channels, transcendentals=0
        ),
        name="late_outputs",
    )(q, k, v, ct, scanned, skip, early_keys, early_values, from_scan, after)
    grad_residues = pl.pallas_call(
        partial(clip_kernel, math.sqrt(channels * tp * modes), blocks),
        out_shape=table_shape,
        scratch_shapes=[pltpu.VMEM((2 * half, LANES), F32)],
        compiler_params=KERNEL,
        name="clip",
    )(mine, other, after, *shares)
    return (operator_out, grad_queries, grad_keys, grad_values, grad_residues.T)


def solution(mesh):
    lines, tables = P("ctx", "tp"), P("tp", None)
    in_specs = (lines, lines, lines, tables, tables, P("tp"), lines)
    out_specs = (lines, lines, lines, lines, tables)
    return jax.shard_map(shards, mesh=mesh, in_specs=in_specs, out_specs=out_specs, check_vma=False)
```

```python
from functools import partial
import math

import jax
import jax.numpy as jnp
from jax import lax
from jax.experimental import pallas as pl
from jax.experimental.pallas import tpu as pltpu
from jax.sharding import PartitionSpec as P

F32 = jnp.float32
WIRE = jnp.bfloat16
LANES = 128
UNROLL = 8
GROUP = 16
STEP_ROWS = 32
KERNEL = pltpu.CompilerParams(vmem_limit_bytes=24 * 1024 * 1024)
HBM = pl.BlockSpec(memory_space=pltpu.HBM)
VMEM = pl.BlockSpec(memory_space=pltpu.VMEM)


def reorder(rows, inner):
    outer = rows // inner
    first = lax.broadcasted_iota(jnp.int32, (rows, rows), 0)
    second = lax.broadcasted_iota(jnp.int32, (rows, rows), 1)

    def matrix(to, fro):
        if inner & (inner - 1) == 0 and outer & (outer - 1) == 0:
            low, high = inner.bit_length() - 1, outer.bit_length() - 1
            same = (fro & (inner - 1)) * outer + (fro >> low) == to
        else:
            same = (fro % inner) * outer + fro // inner == to
        return jnp.where(same, 1.0, 0.0).astype(jnp.bfloat16)

    return matrix(first, second), matrix(second, first)


def tree_sum(items):
    items = list(items)
    while len(items) > 1:
        items = [
            items[i] + items[i + 1] if i + 1 < len(items) else items[i]
            for i in range(0, len(items), 2)
        ]
    return items[0]


def spread(source, target, modes, sub):
    for group in range(source.shape[1] // LANES):
        cols = slice(group * LANES, (group + 1) * LANES)
        first = group // sub * (modes * sub) + group % sub
        target[pl.ds(first, modes, stride=sub), :] = source[:, cols]


def half_units(which, blocks, modes, sub):
    if blocks == 1:
        return [(0, which * (modes // 2 * sub), modes // 2)]
    count = blocks // 2
    return [
        (which * count + j, (which * count + j) * (modes * sub), modes) for j in range(count)
    ]


def to_scan_order(to_scan, pairs, part, i, block, targets, slot):
    size, sub = to_scan.shape[0], to_scan.shape[0] // part
    rows = slice(i * part, (i + 1) * part)
    sides = []
    for left, right in pairs:
        stacked = []
        for s in range(sub):
            cols = pl.ds(pl.multiple_of((block * sub + s) * LANES, LANES), LANES)
            product = left[rows, cols].astype(F32) * right[rows, cols].astype(F32)
            stacked.append(product.astype(jnp.bfloat16))
        sides.append(jnp.concatenate(stacked, axis=0))
    ordered = jnp.dot(
        to_scan[...], jnp.concatenate(sides, axis=1), preferred_element_type=F32
    )
    for j, target in enumerate(targets):
        target[slot, i * size : (i + 1) * size, :] = ordered[:, j * LANES : (j + 1) * LANES]


def exchange_rows(items):
    size = len(items)
    row = lax.broadcasted_iota(jnp.int32, items[0].shape, 0)
    step = size // 2
    while step:
        low = (row & step) == 0
        for i in range(size):
            if i & step == 0:
                first, second = items[i], items[i + step]
                items[i] = jnp.where(low, first, pltpu.roll(second, step, 0))
                items[i + step] = jnp.where(low, pltpu.roll(first, size - step, 0), second)
        step //= 2
    return items


def fill_group(left, right, group, block, target, slot):
    rows = pl.ds(pl.multiple_of(group * GROUP, GROUP), GROUP)
    products = []
    for s in range(8):
        cols = pl.ds(pl.multiple_of((block * 8 + s) * LANES, LANES), LANES)
        product = left[rows, cols].astype(F32) * right[rows, cols].astype(F32)
        products.append(product.astype(jnp.bfloat16).astype(F32))
    for at in range(0, GROUP, 8):
        ordered = exchange_rows([product[at : at + 8, :] for product in products])
        for t in range(8):
            where = pl.ds(pl.multiple_of((group * GROUP + at + t) * 8, 8), 8)
            target[slot, where, :] = ordered[t]


def scan_states(unit, slot, sub, gated_ref, pulled_ref, decay_ref, out_ref, pairs, waits):
    block, base, modes = unit
    at_row = slot * modes * sub
    seq = gated_ref.shape[1] // sub
    slot = slot % gated_ref.shape[0]
    decay = [
        decay_ref[pl.ds(pl.multiple_of(base + n * sub, sub), sub), :] for n in range(modes)
    ]
    first = tuple(jnp.zeros((sub, LANES), F32) for _ in range(modes))

    def forward(j, carry):
        held, inner = list(carry[0]), list(carry[1])
        for u in range(UNROLL):
            at = pl.ds(pl.multiple_of((j * UNROLL + u) * sub, sub), sub)
            x = gated_ref[slot, at, :]
            p = pulled_ref[slot, at, :]
            for n in range(modes):
                held[n] = decay[n] * held[n] + x
                inner[n] = inner[n] + p * held[n]
        return tuple(held), tuple(inner)

    def backward(step, fill, last, j, carry):
        held = list(carry)
        group = last - j
        for u in reversed(range(step)):
            at = pl.ds(pl.multiple_of((group * step + u) * sub, sub), sub)
            p = pulled_ref[slot, at, :]
            for n in range(modes):
                held[n] = decay[n] * held[n] + p
            if fill and u in (12, 6):
                left, right, target = pairs[0 if u == 12 else 1]
                fill_group(left, right, jnp.maximum(group - 1, 0), block, target, slot)
        return tuple(held)

    if pairs is None:
        last = seq // UNROLL - 1
        starts = lax.fori_loop(0, last + 1, partial(backward, UNROLL, False, last), first)
    else:
        starts = first
        groups = seq // GROUP // len(waits)
        waits[-1]()
        for left, right, target in pairs:
            fill_group(left, right, seq // GROUP - 1, block, target, slot)
        for i in reversed(range(len(waits))):
            if i > 0:
                waits[i - 1]()
            last = (i + 1) * groups - 1
            starts = lax.fori_loop(0, groups, partial(backward, GROUP, True, last), starts)
    for n in range(modes):
        out_ref[1, at_row + n * sub : at_row + (n + 1) * sub, :] = starts[n]
    ends, inner = lax.fori_loop(0, seq // UNROLL, forward, (first, first))
    for n in range(modes):
        rows = slice(at_row + n * sub, at_row + (n + 1) * sub)
        out_ref[0, rows, :] = ends[n]
        out_ref[2, rows, :] = inner[n]


def can_exchange(sub, part, units):
    return sub == 8 and part % GROUP == 0 and len(units) == 1


def send_kernel(
    q_hbm,
    k_hbm,
    v_hbm,
    ct_hbm,
    rate_hbm,
    res_hbm,
    skip_hbm,
    send_ref,
    q_ref,
    k_ref,
    v_ref,
    ct_ref,
    gated_ref,
    pulled_ref,
    rate_ref,
    decay_ref,
    to_scan,
    from_scan,
    res_cols,
    skip_ref,
    rate_cols,
    sems,
):
    seq, channels = q_ref.shape
    modes = rate_cols.shape[0]
    sub = gated_ref.shape[1] // seq
    blocks = channels // (sub * LANES)
    part = math.gcd(seq, STEP_ROWS)
    parts = seq // part
    which = 1 - lax.axis_index("ctx") % 2
    pairs = ((k_hbm, k_ref), (v_hbm, v_ref), (ct_hbm, ct_ref), (q_hbm, q_ref))
    copies = []

    def start(source, target):
        copy = pltpu.make_async_copy(source, target, sems.at[len(copies)])
        copy.start()
        copies.append(copy)

    width = channels // min(blocks, 2)
    cols = pl.ds(pl.multiple_of(which * width, LANES) if blocks > 1 else 0, width)
    start(rate_hbm, rate_cols)
    for i in reversed(range(parts)):
        rows = pl.ds(i * part, part)
        for source, target in pairs:
            start(source.at[rows, cols], target.at[rows, cols])
    if blocks > 1:
        cols = pl.ds(pl.multiple_of((1 - which) * width, LANES), width)
        for source, target in pairs:
            start(source.at[:, cols], target.at[:, cols])
    start(res_hbm, res_cols)
    start(skip_hbm, skip_ref)
    to_scan[...], from_scan[...] = reorder(part * sub, part)
    copies[0].wait()
    spread(rate_cols, rate_ref, modes, sub)
    decay_ref[...] = jnp.exp(-rate_ref[...])
    units = half_units(which, blocks, modes, sub)

    def wait_part(i):
        for copy in copies[4 * (parts - 1 - i) + 1 : 4 * (parts - i) + 1]:
            copy.wait()

    if can_exchange(sub, part, units):
        waits = [partial(wait_part, i) for i in range(parts)]
        lines = ((k_ref, v_ref, gated_ref), (ct_ref, q_ref, pulled_ref))
    else:
        waits, lines = None, None
        for i in reversed(range(parts)):
            wait_part(i)
            for at, unit in enumerate(units):
                both = ((k_ref, v_ref), (ct_ref, q_ref))
                to_scan_order(to_scan, both, part, i, unit[0], (gated_ref, pulled_ref), at)
    for at, unit in enumerate(units):
        scan_states(unit, at, sub, gated_ref, pulled_ref, decay_ref, send_ref, lines, waits)
    for copy in copies[4 * parts + 1 :]:
        copy.wait()


def keep_kernel(
    q_ref, k_ref, v_ref, ct_ref, decay_ref, to_scan, gated_in, pulled_in, keep_ref, *line_refs
):
    seq, channels = q_ref.shape
    sub = gated_in.shape[1] // seq
    blocks = channels // (sub * LANES)
    modes = decay_ref.shape[0] // (blocks * sub)
    part = math.gcd(seq, STEP_ROWS)
    units = half_units(lax.axis_index("ctx") % 2, blocks, modes, sub)
    lines, pairs = (gated_in, pulled_in), None
    if blocks > 1:
        lines = line_refs
        if can_exchange(sub, part, units):
            pairs = ((k_ref, v_ref, line_refs[0]), (ct_ref, q_ref, line_refs[1]))
        else:
            for i in range(seq // part):
                for at, unit in enumerate(units):
                    both = ((k_ref, v_ref), (ct_ref, q_ref))
                    to_scan_order(to_scan, both, part, i, unit[0], lines, at)
    for at, unit in enumerate(units):
        scan_states(unit, at, sub, *lines, decay_ref, keep_ref, pairs, [lambda: None])


def own_rows(rate_ref, half):
    core = lax.axis_index("ctx") % 2
    return rate_ref[pl.ds(pl.multiple_of(core * half, half), half), :]


def joined(is_right, mine, other, span, step):
    left = [jnp.where(is_right, o, m) for m, o in zip(mine, other)]
    right = [jnp.where(is_right, m, o) for m, o in zip(mine, other)]
    return (
        span * left[0] + right[0],
        left[1] + span * right[1],
        left[2] + right[2] + step * right[1] * left[0],
    )


def put_wire(wire_ref, is_last, next_right, block):
    if is_last:
        wire_ref[0] = jnp.where(next_right, block[1], block[0]).astype(wire_ref.dtype)
        wire_ref[1] = block[2].astype(wire_ref.dtype)
    else:
        for kind in range(3):
            wire_ref[kind] = block[kind].astype(wire_ref.dtype)


def pair_kernel(seq, is_last, keep_ref, got_ref, rate_ref, after_ref, block_ref, wire_ref):
    rate = own_rows(rate_ref, keep_ref.shape[1])
    place = lax.axis_index("ctx")
    block = joined(
        place % 2 == 1,
        [keep_ref[i] for i in range(3)],
        [got_ref[i] for i in range(3)],
        jnp.exp(-rate * seq),
        jnp.exp(-rate),
    )
    for kind in range(3):
        block_ref[kind] = block[kind]
    block_ref[3] = jnp.zeros_like(rate)
    block_ref[4] = jnp.zeros_like(rate)
    put_wire(wire_ref, is_last, (place // 2) % 2 == 1, block)


def carries_with(block_ref, end_state, start_state, level, seq, rate):
    place = lax.axis_index("ctx")
    is_right = (place >> level) % 2 == 1
    chips = 1 << (level - 1)
    at = (place // 2) % chips
    before = at * (2 * seq)
    behind = (chips - 1 - at) * (2 * seq)
    ahead = block_ref[3] + jnp.where(
        is_right, jnp.exp(-rate * before.astype(F32)) * end_state, 0.0
    )
    after = block_ref[4] + jnp.where(
        is_right, 0.0, jnp.exp(-rate * behind.astype(F32)) * start_state
    )
    return is_right, ahead, after


def level_kernel(
    seq, level, is_last, block_ref, got_ref, rate_ref, after_ref, out_ref, wire_ref
):
    rate = own_rows(rate_ref, block_ref.shape[1])
    got = [got_ref[i].astype(F32) for i in range(3)]
    is_right, ahead, after = carries_with(block_ref, got[0], got[1], level, seq, rate)
    block = joined(
        is_right,
        [block_ref[i] for i in range(3)],
        got,
        jnp.exp(-rate * (seq << level)),
        jnp.exp(-rate),
    )
    for kind in range(3):
        out_ref[kind] = block[kind]
    out_ref[3] = ahead
    out_ref[4] = after
    next_right = (lax.axis_index("ctx") >> (level + 1)) % 2 == 1
    put_wire(wire_ref, is_last, next_right, block)


def last_kernel(
    seq,
    level,
    block_ref,
    got_ref,
    rate_ref,
    keep_ref,
    sibling_ref,
    after_ref,
    mine_ref,
    other_ref,
    share_ref,
):
    half = block_ref.shape[1]
    rate = own_rows(rate_ref, half)
    edge, inner = got_ref[0].astype(F32), got_ref[1].astype(F32)
    is_right, ahead, after = carries_with(block_ref, edge, edge, level, seq, rate)
    own_edge = jnp.where(is_right, block_ref[1], block_ref[0])
    total = block_ref[2] + inner + jnp.exp(-rate) * own_edge * edge
    raw = jnp.sqrt(1.0 - jnp.exp(-2.0 * rate)) * total
    core = lax.axis_index("ctx") % 2
    first = core == 0
    span = jnp.exp(-rate * seq)
    end_first = jnp.where(first, keep_ref[0], sibling_ref[0])
    start_second = jnp.where(first, sibling_ref[1], keep_ref[1])
    ahead_second = span * ahead + end_first
    after_first = span * after + start_second
    mine_ref[0:half, :] = jnp.where(first, ahead, ahead_second)
    mine_ref[half : 2 * half, :] = jnp.where(first, after_first, after)
    other_ref[0:half, :] = jnp.where(first, ahead_second, ahead)
    other_ref[half : 2 * half, :] = jnp.where(first, after, after_first)
    squares = raw * raw
    share_ref[...] = tree_sum([squares[i : i + 8, :] for i in range(0, half, 8)])
    mine_ref[2 * half : 3 * half, :] = raw
    other_ref[2 * half : 3 * half, :] = raw


def place_halves(mine_ref, other_ref, first, target):
    half = target.shape[0] // 2
    core = lax.axis_index("ctx") % 2
    for ref, at in ((mine_ref, core), (other_ref, 1 - core)):
        rows = pl.ds(pl.multiple_of(at * half, half), half)
        target[rows, :] = ref[first : first + half, :]


def first_local_kernel(modes, *refs):
    line_refs, (decay_ref, rate_ref, res_cols, after_ref, out_ref, coef_ref) = refs[:-6], refs[-6:]
    sub = decay_ref.shape[0] // (out_ref.shape[0] * modes)
    spread(res_cols, coef_ref, modes, sub)
    coef_ref[...] = coef_ref[...] * jnp.sqrt(1.0 - jnp.exp(-2.0 * rate_ref[...]))
    local_kernel(False, modes, *line_refs, decay_ref, coef_ref, after_ref, out_ref)


def local_kernel(reverse, modes, *refs):
    line_refs, (decay_ref, coef_ref, after_ref, out_ref) = refs[:-4], refs[-4:]
    blocks = out_ref.shape[0]
    sub = decay_ref.shape[0] // (blocks * modes)
    seq = out_ref.shape[1] // sub
    core = lax.axis_index("ctx") % 2
    for ref, which in zip(line_refs, (1 - core, core)):
        for slot in range(ref.shape[0]):
            block = which * ref.shape[0] + slot if blocks > 1 else 0
            rows = [
                pl.ds(pl.multiple_of((block * modes + n) * sub, sub), sub) for n in range(modes)
            ]
            decay = [decay_ref[r, :] for r in rows]
            coef = [coef_ref[r, :] for r in rows]

            def body(j, carry):
                held = list(carry)
                for u in range(UNROLL):
                    t = j * UNROLL + u
                    if reverse:
                        t = seq - 1 - t
                    at = pl.ds(pl.multiple_of(t * sub, sub), sub)
                    x = ref[slot, at, :]
                    total = [None] * 4
                    for n in range(modes):
                        held[n] = decay[n] * held[n] + x
                        term = coef[n] * held[n]
                        total[n % 4] = term if n < 4 else total[n % 4] + term
                    out_ref[block, at, :] = tree_sum(total)
                return tuple(held)

            first = tuple(jnp.zeros((sub, LANES), F32) for _ in range(modes))
            lax.fori_loop(0, seq // UNROLL, body, first)


def second_local_kernel(modes, *refs):
    line_refs, refs = refs[:-11], refs[-11:]
    decay_ref, coef_ref, q_ref, k_ref, v_ref, ct_ref, skip_ref, after_ref = refs[:8]
    out_ref, gated_term, pulled_term = refs[8:]
    local_kernel(True, modes, *line_refs, decay_ref, coef_ref, after_ref, out_ref)
    pairs = ((k_ref, v_ref, gated_term), (ct_ref, q_ref, pulled_term))
    for left, right, target in pairs:
        for at in range(0, q_ref.shape[1], LANES):
            cols = slice(at, at + LANES)
            line = left[:, cols].astype(F32) * right[:, cols].astype(F32)
            target[:, cols] = skip_ref[:, cols] * line.astype(jnp.bfloat16).astype(F32)


def add_carries(reverse, unit, sub, decay_ref, coef_ref, states_ref, at_row, source, target, at):
    _, base, modes = unit
    seq = target.shape[1] // sub
    rows = [pl.ds(pl.multiple_of(base + n * sub, sub), sub) for n in range(modes)]
    decay = [decay_ref[r, :] for r in rows]
    first = tuple(
        coef_ref[r, :] * states_ref[at_row + n * sub : at_row + (n + 1) * sub, :]
        for n, r in enumerate(rows)
    )

    def body(j, carry):
        held = list(carry)
        for u in range(UNROLL):
            t = j * UNROLL + u
            if reverse:
                t = seq - 1 - t
            where = pl.ds(pl.multiple_of(t * sub, sub), sub)
            total = [source[where, :], None, None, None]
            for n in range(modes):
                held[n] = decay[n] * held[n]
                total[n % 4] = held[n] if total[n % 4] is None else total[n % 4] + held[n]
            target[at, where, :] = tree_sum(total)
        return tuple(held)

    lax.fori_loop(0, seq // UNROLL, body, first)


def own_kernel(modes, conv_ref, adj_ref, decay_ref, coef_ref, mine_ref, conv_own, adj_own):
    blocks = conv_ref.shape[0]
    sub = decay_ref.shape[0] // (blocks * modes)
    half = decay_ref.shape[0] // 2
    core = lax.axis_index("ctx") % 2
    for i, unit in enumerate(half_units(core, blocks, modes, sub)):
        at_row = i * unit[2] * sub
        for reverse, source, target in ((False, conv_ref, conv_own), (True, adj_ref, adj_own)):
            add_carries(
                reverse,
                unit,
                sub,
                decay_ref,
                coef_ref,
                mine_ref,
                at_row + half * reverse,
                source.at[unit[0]],
                target,
                i,
            )


def other_carries(reverse, modes, decay_ref, coef_ref, other_ref, local_ref, own_ref, whole, sem):
    blocks, own_blocks = local_ref.shape[0], own_ref.shape[0]
    sub = decay_ref.shape[0] // (blocks * modes)
    half = decay_ref.shape[0] // 2
    core = lax.axis_index("ctx") % 2
    copy = pltpu.make_async_copy(own_ref, whole.at[pl.ds(core * own_blocks, own_blocks)], sem)
    if blocks > 1:
        copy.start()
    for i, unit in enumerate(half_units(1 - core, blocks, modes, sub)):
        source = local_ref.at[unit[0]] if blocks > 1 else own_ref.at[0]
        at_row = i * unit[2] * sub + half * reverse
        add_carries(
            reverse, unit, sub, decay_ref, coef_ref, other_ref, at_row, source, whole, unit[0]
        )
    if blocks > 1:
        copy.wait()


def line_outputs(from_scan, term, scales, scanned, targets, which, done_with=None):
    seq, channels = term.shape
    blocks = scanned.shape[0]
    sub = channels // (blocks * LANES)
    part = math.gcd(seq, STEP_ROWS)
    for i in which:
        rows = slice(i * part, (i + 1) * part)
        to_rows = slice((i - which[0]) * part, (i - which[0] + 1) * part)
        stacked = jnp.concatenate(
            [scanned[b, i * part * sub : (i + 1) * part * sub, :] for b in range(blocks)], axis=1
        ).astype(jnp.bfloat16)
        ordered = jnp.dot(from_scan[...], stacked, preferred_element_type=F32)
        for b in range(blocks):
            for s in range(sub):
                cols = slice((b * sub + s) * LANES, (b * sub + s + 1) * LANES)
                own = ordered[s * part : (s + 1) * part, b * LANES : (b + 1) * LANES]
                mixed = own + term[rows, cols]
                for scale, target in zip(scales, targets):
                    target[to_rows, cols] = (scale[rows, cols].astype(F32) * mixed).astype(
                        jnp.bfloat16
                    )
        if done_with is not None:
            done_with(pl.ds((i - which[0]) * part, part), pl.ds(i * part, part))


def forward_kernel(
    modes,
    q_ref,
    ct_ref,
    term_ref,
    decay_ref,
    coef_ref,
    other_ref,
    from_scan,
    conv_ref,
    conv_own,
    after_ref,
    out_ref,
    gq_ref,
    token_ref,
    scanned,
    sem,
):
    token_ref[...] = jnp.zeros_like(token_ref)
    other_carries(
        False, modes, decay_ref, coef_ref, other_ref, conv_ref, conv_own, scanned, sem
    )
    line_outputs(
        from_scan,
        term_ref,
        (q_ref, ct_ref),
        scanned,
        (out_ref, gq_ref),
        range(q_ref.shape[0] // math.gcd(q_ref.shape[0], STEP_ROWS)),
    )


def early_parts(seq):
    parts = seq // math.gcd(seq, STEP_ROWS)
    return range((parts + 1) // 2), range((parts + 1) // 2, parts)


def adjoint_kernel(
    modes,
    k_ref,
    v_ref,
    term_ref,
    decay_ref,
    coef_ref,
    other_ref,
    from_scan,
    adj_ref,
    adj_own,
    out_rows,
    gq_rows,
    after_ref,
    out_hbm,
    gq_hbm,
    scanned,
    gk_ref,
    gv_ref,
    token_ref,
    sems,
):
    token_ref[...] = jnp.zeros_like(token_ref)
    copies = [
        pltpu.make_async_copy(out_rows, out_hbm, sems.at[0]),
        pltpu.make_async_copy(gq_rows, gq_hbm, sems.at[1]),
    ]
    for copy in copies:
        copy.start()
    other_carries(
        True, modes, decay_ref, coef_ref, other_ref, adj_ref, adj_own, scanned, sems.at[2]
    )
    line_outputs(
        from_scan,
        term_ref,
        (v_ref, k_ref),
        scanned,
        (gk_ref, gv_ref),
        early_parts(k_ref.shape[0])[0],
    )
    for copy in copies:
        copy.wait()


def last_outputs_kernel(limit, *refs):
    k_ref, v_ref, term_ref, scanned, gk_early, gv_early = refs[:6]
    mine_ref, other_ref, from_scan = refs[6:9]
    share_refs = refs[10:-8]
    raw_hbm, gk_hbm, gv_hbm, gk_rows, gv_rows, raw_cols, states, sems = refs[-8:]
    copies = []

    def start(source, target):
        copy = pltpu.make_async_copy(source, target, sems.at[len(copies)])
        copy.start()
        copies.append(copy)

    early = pl.ds(0, gk_early.shape[0])
    start(gk_early, gk_hbm.at[early])
    start(gv_early, gv_hbm.at[early])
    clip(limit, scanned.shape[0], mine_ref, other_ref, share_refs, raw_cols, states)
    start(raw_cols, raw_hbm)

    def send(at, to):
        start(gk_rows.at[at], gk_hbm.at[to])
        start(gv_rows.at[at], gv_hbm.at[to])

    late = early_parts(k_ref.shape[0])[1]
    if len(late) > 0:
        sides, targets = (v_ref, k_ref), (gk_rows, gv_rows)
        line_outputs(from_scan, term_ref, sides, scanned, targets, late, send)
    for copy in copies:
        copy.wait()


def add_kernel(after_ref, *refs):
    refs[-1][...] = tree_sum([ref[...] for ref in refs[:-1]])


def clip(limit, blocks, mine_ref, other_ref, share_refs, out_ref, states):
    modes = out_ref.shape[0]
    sub = out_ref.shape[1] // (blocks * LANES)
    half = states.shape[0] // 2
    place_halves(mine_ref, other_ref, 2 * half, states)
    square = jnp.sum(tree_sum([ref[...] for ref in share_refs]))
    factor = jnp.minimum(1.0, limit * lax.rsqrt(jnp.full((1, LANES), square + 1e-06, F32)))
    for b in range(blocks):
        for s in range(sub):
            cols = slice((b * sub + s) * LANES, (b * sub + s + 1) * LANES)
            rows = pl.ds(b * modes * sub + s, modes, stride=sub)
            out_ref[:, cols] = states[rows, :] * factor


def shards(queries, keys_in, values_in, decay_rates, residues, skip_gain, cotangent):
    seq, channels = queries.shape
    modes = decay_rates.shape[1]
    ctx = lax.axis_size("ctx")
    tp = lax.axis_size("tp")
    levels = ctx.bit_length() - 1
    groups = channels // LANES
    sub = math.gcd(groups, 8)
    blocks = groups // sub
    half = modes * groups // 2
    part = math.gcd(seq, STEP_ROWS)
    parts, size = seq // part, part * sub

    def swap(value, bit):
        return lax.ppermute(value, "ctx", [(i, i ^ (1 << bit)) for i in range(ctx)])

    def rows(*shape, dtype=F32):
        return jax.ShapeDtypeStruct((*shape, LANES), dtype)

    line_shape = jax.ShapeDtypeStruct((seq, channels), jnp.bfloat16)
    table_shape = jax.ShapeDtypeStruct((modes, channels), F32)
    line_scratch = pltpu.VMEM((seq, channels), jnp.bfloat16)
    table_scratch = pltpu.VMEM((modes, channels), F32)
    own_shape = rows(max(blocks // 2, 1), seq * sub)
    elements = seq * channels * modes
    tables = (decay_rates.T, residues.T, skip_gain.reshape(1, channels))
    sources = (queries, keys_in, values_in, cotangent, *tables)

    (
        send,
        q,
        k,
        v,
        ct,
        gated,
        pulled,
        row_rates,
        row_decay,
        to_scan,
        from_scan,
        res_cols,
        skip,
    ) = pl.pallas_call(
        send_kernel,
        in_specs=[HBM] * 7,
        out_specs=[VMEM] * 13,
        out_shape=[rows(3, half)]
        + [line_shape] * 4
        + [own_shape] * 2
        + [rows(2 * half)] * 2
        + [jax.ShapeDtypeStruct((size, size), jnp.bfloat16)] * 2
        + [table_shape, jax.ShapeDtypeStruct((1, channels), F32)],
        scratch_shapes=[table_scratch, pltpu.SemaphoreType.DMA((4 * parts + 7,))],
        compiler_params=KERNEL,
        cost_estimate=pl.CostEstimate(
            flops=3 * elements, bytes_accessed=8 * seq * channels, transcendentals=0
        ),
        name="sent_states",
    )(*[pltpu.with_memory_space_constraint(item, pltpu.HBM) for item in sources])
    sibling = swap(send, 0)
    keep, *kept_lines = pl.pallas_call(
        keep_kernel,
        out_shape=[rows(3, half)] + [own_shape] * (2 if blocks > 1 else 0),
        compiler_params=KERNEL,
        cost_estimate=pl.CostEstimate(
            flops=3 * elements, bytes_accessed=8 * seq * channels, transcendentals=0
        ),
        name="kept_states",
    )(q, k, v, ct, row_decay, to_scan, gated, pulled)
    gated, pulled = (gated, *kept_lines[:1]), (pulled, *kept_lines[1:])

    def wire(level):
        return rows(2 if level == levels - 1 else 3, half, dtype=WIRE)

    whole = rows(blocks, seq * sub)
    whole_scratch = pltpu.VMEM((blocks, seq * sub, LANES), F32)
    states_scratch = pltpu.VMEM((2 * half, LANES), F32)
    local_cost = pl.CostEstimate(
        flops=4 * elements, bytes_accessed=8 * seq * channels, transcendentals=0
    )

    block, packed = pl.pallas_call(
        partial(pair_kernel, seq, levels == 2),
        out_shape=[rows(5, half), wire(1)],
        compiler_params=KERNEL,
        name="chip_states",
    )(keep, sibling, row_rates, row_rates[:8])
    got = swap(packed, 1)
    conv, row_coefs = pl.pallas_call(
        partial(first_local_kernel, modes),
        out_shape=[whole, rows(2 * half)],
        compiler_params=KERNEL,
        cost_estimate=local_cost,
        name="local_conv",
    )(*gated, row_decay, row_rates, res_cols, block[4, :8])
    for level in range(1, levels - 1):
        block, packed = pl.pallas_call(
            partial(level_kernel, seq, level, level + 1 == levels - 1),
            out_shape=[rows(5, half), wire(level + 1)],
            compiler_params=KERNEL,
            name="block_states",
        )(block, got, row_rates, conv[0, :8])
        got = swap(packed, level + 1)
    term_shape = jax.ShapeDtypeStruct((seq, channels), F32)
    adj, gated_term, pulled_term = pl.pallas_call(
        partial(second_local_kernel, modes),
        out_shape=[whole] + [term_shape] * 2,
        compiler_params=KERNEL,
        cost_estimate=local_cost,
        name="local_adjoint",
    )(*pulled, row_decay, row_coefs, q, k, v, ct, skip, block[4, :8])
    mine, other, square = pl.pallas_call(
        partial(last_kernel, seq, levels - 1),
        out_shape=[rows(3 * half)] * 2 + [rows(8)],
        compiler_params=KERNEL,
        name="carries",
    )(block, got, row_rates, keep, sibling, adj[0, :8])
    other = swap(other, 0)
    early, late = early_parts(seq)
    early_shape = jax.ShapeDtypeStruct((seq * len(early) // parts, channels), jnp.bfloat16)
    late_scratch = pltpu.VMEM((seq * max(len(late), 1) // parts, channels), jnp.bfloat16)
    kept = {}

    def add_own(after):
        kept["conv"], kept["adj"] = pl.pallas_call(
            partial(own_kernel, modes),
            out_shape=[own_shape] * 2,
            compiler_params=KERNEL,
            cost_estimate=pl.CostEstimate(
                flops=2 * elements, bytes_accessed=8 * seq * channels, transcendentals=0
            ),
            name="own_carries",
        )(conv, adj, row_decay, row_coefs, mine)
        return kept["adj"][0, :8]

    def forward_outputs(after):
        kept["out"], kept["gq"], token = pl.pallas_call(
            partial(forward_kernel, modes),
            out_shape=[line_shape] * 2 + [rows(8)],
            scratch_shapes=[whole_scratch, pltpu.SemaphoreType.DMA],
            compiler_params=KERNEL,
            cost_estimate=pl.CostEstimate(
                flops=2 * elements, bytes_accessed=16 * seq * channels, transcendentals=0
            ),
            name="forward_outputs",
        )(
            q,
            ct,
            gated_term,
            row_decay,
            row_coefs,
            other,
            from_scan,
            conv,
            kept["conv"],
            after,
        )
        return token

    def adjoint_outputs(after):
        results = (
            pl.pallas_call(
                partial(adjoint_kernel, modes),
                in_specs=[VMEM] * 12,
                out_specs=[HBM] * 2 + [VMEM] * 4,
                out_shape=[line_shape] * 2 + [whole] + [early_shape] * 2 + [rows(8)],
                scratch_shapes=[pltpu.SemaphoreType.DMA((3,))],
                compiler_params=KERNEL,
                cost_estimate=pl.CostEstimate(
                    flops=2 * elements, bytes_accessed=8 * seq * channels, transcendentals=0
                ),
                name="adjoint_outputs",
            )(
                k,
                v,
                pulled_term,
                row_decay,
                row_coefs,
                other,
                from_scan,
                adj,
                kept["adj"],
                kept["out"],
                kept["gq"],
                after,
            )
        )
        kept["final"] = results[:-1]
        return results[-1]

    def plus(after, *shares):
        return pl.pallas_call(
            add_kernel,
            in_specs=[VMEM] * (1 + len(shares)),
            out_shape=rows(8),
            compiler_params=KERNEL,
            name="square_sum",
        )(after, *shares)

    def tp_swap(value, mask):
        return lax.ppermute(value, "tp", [(i, i ^ mask) for i in range(tp)])

    works = [add_own, forward_outputs]
    for bit in range(0, tp.bit_length() - 1, 2):
        masks = [m << bit for m in (1, 2, 3) if m << bit < tp]
        shares = [tp_swap(square, mask) for mask in masks]
        after = square
        while works:
            after = works.pop(0)(after)
        square = plus(after, square, *shares)
    share = swap(square, 0)
    after = square
    for work in works + [adjoint_outputs]:
        after = work(after)
    operator_out, grad_queries, scanned, early_keys, early_values = kept["final"]
    grad_residues, grad_keys, grad_values = pl.pallas_call(
        partial(last_outputs_kernel, math.sqrt(channels * tp * modes)),
        in_specs=[VMEM] * 12,
        out_specs=[HBM] * 3,
        out_shape=[table_shape] + [line_shape] * 2,
        scratch_shapes=[
            late_scratch,
            late_scratch,
            table_scratch,
            states_scratch,
            pltpu.SemaphoreType.DMA((2 * parts + 3,)),
        ],
        compiler_params=KERNEL,
        cost_estimate=pl.CostEstimate(
            flops=elements, bytes_accessed=8 * seq * channels, transcendentals=0
        ),
        name="last_outputs",
    )(
        k,
        v,
        pulled_term,
        scanned,
        early_keys,
        early_values,
        mine,
        other,
        from_scan,
        after,
        square,
        share,
    )
    return (operator_out, grad_queries, grad_keys, grad_values, grad_residues.T)


def solution(mesh):
    lines, tables = P("ctx", "tp"), P("tp", None)
    in_specs = (lines, lines, lines, tables, tables, P("tp"), lines)
    out_specs = (lines, lines, lines, lines, tables)
    return jax.shard_map(shards, mesh=mesh, in_specs=in_specs, out_specs=out_specs, check_vma=False)
```

```python
from functools import partial
import math

import jax
import jax.numpy as jnp
from jax import lax
from jax.experimental import pallas as pl
from jax.experimental.pallas import tpu as pltpu
from jax.sharding import PartitionSpec as P

F32 = jnp.float32
WIRE = jnp.bfloat16
LANES = 128
UNROLL = 8
GROUP = 16
STEP_ROWS = 32
KERNEL = pltpu.CompilerParams(vmem_limit_bytes=24 * 1024 * 1024)
HBM = pl.BlockSpec(memory_space=pltpu.HBM)
VMEM = pl.BlockSpec(memory_space=pltpu.VMEM)


def reorder(rows, inner):
    outer = rows // inner
    first = lax.broadcasted_iota(jnp.int32, (rows, rows), 0)
    second = lax.broadcasted_iota(jnp.int32, (rows, rows), 1)

    def matrix(to, fro):
        if inner & (inner - 1) == 0 and outer & (outer - 1) == 0:
            low, high = inner.bit_length() - 1, outer.bit_length() - 1
            same = (fro & (inner - 1)) * outer + (fro >> low) == to
        else:
            same = (fro % inner) * outer + fro // inner == to
        return jnp.where(same, 1.0, 0.0).astype(jnp.bfloat16)

    return matrix(first, second), matrix(second, first)


def tree_sum(items):
    items = list(items)
    while len(items) > 1:
        items = [
            items[i] + items[i + 1] if i + 1 < len(items) else items[i]
            for i in range(0, len(items), 2)
        ]
    return items[0]


def spread(source, target, modes, sub):
    for group in range(source.shape[1] // LANES):
        cols = slice(group * LANES, (group + 1) * LANES)
        first = group // sub * (modes * sub) + group % sub
        target[pl.ds(first, modes, stride=sub), :] = source[:, cols]


def half_units(which, blocks, modes, sub):
    if blocks == 1:
        return [(0, which * (modes // 2 * sub), modes // 2)]
    count = blocks // 2
    return [
        (which * count + j, (which * count + j) * (modes * sub), modes) for j in range(count)
    ]


def to_scan_order(to_scan, pairs, part, i, block, targets, slot):
    size, sub = to_scan.shape[0], to_scan.shape[0] // part
    rows = slice(i * part, (i + 1) * part)
    sides = []
    for left, right in pairs:
        stacked = []
        for s in range(sub):
            cols = pl.ds(pl.multiple_of((block * sub + s) * LANES, LANES), LANES)
            product = left[rows, cols].astype(F32) * right[rows, cols].astype(F32)
            stacked.append(product.astype(jnp.bfloat16))
        sides.append(jnp.concatenate(stacked, axis=0))
    ordered = jnp.dot(
        to_scan[...], jnp.concatenate(sides, axis=1), preferred_element_type=F32
    )
    for j, target in enumerate(targets):
        target[slot, i * size : (i + 1) * size, :] = ordered[:, j * LANES : (j + 1) * LANES]


def exchange_rows(items):
    size = len(items)
    row = lax.broadcasted_iota(jnp.int32, items[0].shape, 0)
    step = size // 2
    while step:
        low = (row & step) == 0
        for i in range(size):
            if i & step == 0:
                first, second = items[i], items[i + step]
                items[i] = jnp.where(low, first, pltpu.roll(second, step, 0))
                items[i + step] = jnp.where(low, pltpu.roll(first, size - step, 0), second)
        step //= 2
    return items


def fill_group(left, right, group, block, target, slot):
    rows = pl.ds(pl.multiple_of(group * GROUP, GROUP), GROUP)
    products = []
    for s in range(8):
        cols = pl.ds(pl.multiple_of((block * 8 + s) * LANES, LANES), LANES)
        product = left[rows, cols].astype(F32) * right[rows, cols].astype(F32)
        products.append(product.astype(jnp.bfloat16).astype(F32))
    for at in range(0, GROUP, 8):
        ordered = exchange_rows([product[at : at + 8, :] for product in products])
        for t in range(8):
            where = pl.ds(pl.multiple_of((group * GROUP + at + t) * 8, 8), 8)
            target[slot, where, :] = ordered[t]


def scan_states(unit, slot, sub, gated_ref, pulled_ref, decay_ref, out_ref, pairs, waits):
    block, base, modes = unit
    at_row = slot * modes * sub
    seq = gated_ref.shape[1] // sub
    slot = slot % gated_ref.shape[0]
    decay = [
        decay_ref[pl.ds(pl.multiple_of(base + n * sub, sub), sub), :] for n in range(modes)
    ]
    first = tuple(jnp.zeros((sub, LANES), F32) for _ in range(modes))

    def forward(j, carry):
        held, inner = list(carry[0]), list(carry[1])
        for u in range(UNROLL):
            at = pl.ds(pl.multiple_of((j * UNROLL + u) * sub, sub), sub)
            x = gated_ref[slot, at, :]
            p = pulled_ref[slot, at, :]
            for n in range(modes):
                held[n] = decay[n] * held[n] + x
                inner[n] = inner[n] + p * held[n]
        return tuple(held), tuple(inner)

    def backward(step, fill, last, j, carry):
        held = list(carry)
        group = last - j
        for u in reversed(range(step)):
            at = pl.ds(pl.multiple_of((group * step + u) * sub, sub), sub)
            p = pulled_ref[slot, at, :]
            for n in range(modes):
                held[n] = decay[n] * held[n] + p
            if fill and u in (12, 6):
                left, right, target = pairs[0 if u == 12 else 1]
                fill_group(left, right, jnp.maximum(group - 1, 0), block, target, slot)
        return tuple(held)

    if pairs is None:
        last = seq // UNROLL - 1
        starts = lax.fori_loop(0, last + 1, partial(backward, UNROLL, False, last), first)
    else:
        starts = first
        groups = seq // GROUP // len(waits)
        waits[-1]()
        for left, right, target in pairs:
            fill_group(left, right, seq // GROUP - 1, block, target, slot)
        for i in reversed(range(len(waits))):
            if i > 0:
                waits[i - 1]()
            last = (i + 1) * groups - 1
            starts = lax.fori_loop(0, groups, partial(backward, GROUP, True, last), starts)
    for n in range(modes):
        out_ref[1, at_row + n * sub : at_row + (n + 1) * sub, :] = starts[n]
    ends, inner = lax.fori_loop(0, seq // UNROLL, forward, (first, first))
    for n in range(modes):
        rows = slice(at_row + n * sub, at_row + (n + 1) * sub)
        out_ref[0, rows, :] = ends[n]
        out_ref[2, rows, :] = inner[n]


def can_exchange(sub, part, units):
    return sub == 8 and part % GROUP == 0 and len(units) == 1


def send_kernel(
    q_hbm,
    k_hbm,
    v_hbm,
    ct_hbm,
    rate_hbm,
    res_hbm,
    skip_hbm,
    send_ref,
    q_ref,
    k_ref,
    v_ref,
    ct_ref,
    gated_ref,
    pulled_ref,
    rate_ref,
    decay_ref,
    to_scan,
    from_scan,
    res_cols,
    skip_ref,
    rate_cols,
    sems,
):
    seq, channels = q_ref.shape
    modes = rate_cols.shape[0]
    sub = gated_ref.shape[1] // seq
    blocks = channels // (sub * LANES)
    part = math.gcd(seq, STEP_ROWS)
    parts = seq // part
    which = 1 - lax.axis_index("ctx") % 2
    pairs = ((k_hbm, k_ref), (v_hbm, v_ref), (ct_hbm, ct_ref), (q_hbm, q_ref))
    copies = []

    def start(source, target):
        copy = pltpu.make_async_copy(source, target, sems.at[len(copies)])
        copy.start()
        copies.append(copy)

    width = channels // min(blocks, 2)
    cols = pl.ds(pl.multiple_of(which * width, LANES) if blocks > 1 else 0, width)
    start(rate_hbm, rate_cols)
    for i in reversed(range(parts)):
        rows = pl.ds(i * part, part)
        for source, target in pairs:
            start(source.at[rows, cols], target.at[rows, cols])
    if blocks > 1:
        cols = pl.ds(pl.multiple_of((1 - which) * width, LANES), width)
        for source, target in pairs:
            start(source.at[:, cols], target.at[:, cols])
    start(res_hbm, res_cols)
    start(skip_hbm, skip_ref)
    to_scan[...], from_scan[...] = reorder(part * sub, part)
    copies[0].wait()
    spread(rate_cols, rate_ref, modes, sub)
    decay_ref[...] = jnp.exp(-rate_ref[...])
    units = half_units(which, blocks, modes, sub)

    def wait_part(i):
        for copy in copies[4 * (parts - 1 - i) + 1 : 4 * (parts - i) + 1]:
            copy.wait()

    if can_exchange(sub, part, units):
        waits = [partial(wait_part, i) for i in range(parts)]
        lines = ((k_ref, v_ref, gated_ref), (ct_ref, q_ref, pulled_ref))
    else:
        waits, lines = None, None
        for i in reversed(range(parts)):
            wait_part(i)
            for at, unit in enumerate(units):
                both = ((k_ref, v_ref), (ct_ref, q_ref))
                to_scan_order(to_scan, both, part, i, unit[0], (gated_ref, pulled_ref), at)
    for at, unit in enumerate(units):
        scan_states(unit, at, sub, gated_ref, pulled_ref, decay_ref, send_ref, lines, waits)
    for copy in copies[4 * parts + 1 :]:
        copy.wait()


def keep_kernel(
    q_ref, k_ref, v_ref, ct_ref, decay_ref, to_scan, gated_in, pulled_in, keep_ref, *line_refs
):
    seq, channels = q_ref.shape
    sub = gated_in.shape[1] // seq
    blocks = channels // (sub * LANES)
    modes = decay_ref.shape[0] // (blocks * sub)
    part = math.gcd(seq, STEP_ROWS)
    units = half_units(lax.axis_index("ctx") % 2, blocks, modes, sub)
    lines, pairs = (gated_in, pulled_in), None
    if blocks > 1:
        lines = line_refs
        if can_exchange(sub, part, units):
            pairs = ((k_ref, v_ref, line_refs[0]), (ct_ref, q_ref, line_refs[1]))
        else:
            for i in range(seq // part):
                for at, unit in enumerate(units):
                    both = ((k_ref, v_ref), (ct_ref, q_ref))
                    to_scan_order(to_scan, both, part, i, unit[0], lines, at)
    for at, unit in enumerate(units):
        scan_states(unit, at, sub, *lines, decay_ref, keep_ref, pairs, [lambda: None])


def own_rows(rate_ref, half):
    core = lax.axis_index("ctx") % 2
    return rate_ref[pl.ds(pl.multiple_of(core * half, half), half), :]


def joined(is_right, mine, other, span, step):
    left = [jnp.where(is_right, o, m) for m, o in zip(mine, other)]
    right = [jnp.where(is_right, m, o) for m, o in zip(mine, other)]
    return (
        span * left[0] + right[0],
        left[1] + span * right[1],
        left[2] + right[2] + step * right[1] * left[0],
    )


def put_wire(wire_ref, is_last, next_right, block):
    if is_last:
        wire_ref[0] = jnp.where(next_right, block[1], block[0]).astype(wire_ref.dtype)
        wire_ref[1] = block[2].astype(wire_ref.dtype)
    else:
        for kind in range(3):
            wire_ref[kind] = block[kind].astype(wire_ref.dtype)


def pair_kernel(seq, is_last, keep_ref, got_ref, rate_ref, after_ref, block_ref, wire_ref):
    rate = own_rows(rate_ref, keep_ref.shape[1])
    place = lax.axis_index("ctx")
    block = joined(
        place % 2 == 1,
        [keep_ref[i] for i in range(3)],
        [got_ref[i] for i in range(3)],
        jnp.exp(-rate * seq),
        jnp.exp(-rate),
    )
    for kind in range(3):
        block_ref[kind] = block[kind]
    block_ref[3] = jnp.zeros_like(rate)
    block_ref[4] = jnp.zeros_like(rate)
    put_wire(wire_ref, is_last, (place // 2) % 2 == 1, block)


def carries_with(block_ref, end_state, start_state, level, seq, rate):
    place = lax.axis_index("ctx")
    is_right = (place >> level) % 2 == 1
    chips = 1 << (level - 1)
    at = (place // 2) % chips
    before = at * (2 * seq)
    behind = (chips - 1 - at) * (2 * seq)
    ahead = block_ref[3] + jnp.where(
        is_right, jnp.exp(-rate * before.astype(F32)) * end_state, 0.0
    )
    after = block_ref[4] + jnp.where(
        is_right, 0.0, jnp.exp(-rate * behind.astype(F32)) * start_state
    )
    return is_right, ahead, after


def level_kernel(
    seq, level, is_last, block_ref, got_ref, rate_ref, after_ref, out_ref, wire_ref
):
    rate = own_rows(rate_ref, block_ref.shape[1])
    got = [got_ref[i].astype(F32) for i in range(3)]
    is_right, ahead, after = carries_with(block_ref, got[0], got[1], level, seq, rate)
    block = joined(
        is_right,
        [block_ref[i] for i in range(3)],
        got,
        jnp.exp(-rate * (seq << level)),
        jnp.exp(-rate),
    )
    for kind in range(3):
        out_ref[kind] = block[kind]
    out_ref[3] = ahead
    out_ref[4] = after
    next_right = (lax.axis_index("ctx") >> (level + 1)) % 2 == 1
    put_wire(wire_ref, is_last, next_right, block)


def last_kernel(
    seq,
    level,
    block_ref,
    got_ref,
    rate_ref,
    keep_ref,
    sibling_ref,
    after_ref,
    mine_ref,
    other_ref,
    share_ref,
):
    half = block_ref.shape[1]
    rate = own_rows(rate_ref, half)
    edge, inner = got_ref[0].astype(F32), got_ref[1].astype(F32)
    is_right, ahead, after = carries_with(block_ref, edge, edge, level, seq, rate)
    own_edge = jnp.where(is_right, block_ref[1], block_ref[0])
    total = block_ref[2] + inner + jnp.exp(-rate) * own_edge * edge
    raw = jnp.sqrt(1.0 - jnp.exp(-2.0 * rate)) * total
    core = lax.axis_index("ctx") % 2
    first = core == 0
    span = jnp.exp(-rate * seq)
    end_first = jnp.where(first, keep_ref[0], sibling_ref[0])
    start_second = jnp.where(first, sibling_ref[1], keep_ref[1])
    ahead_second = span * ahead + end_first
    after_first = span * after + start_second
    mine_ref[0:half, :] = jnp.where(first, ahead, ahead_second)
    mine_ref[half : 2 * half, :] = jnp.where(first, after_first, after)
    other_ref[0:half, :] = jnp.where(first, ahead_second, ahead)
    other_ref[half : 2 * half, :] = jnp.where(first, after, after_first)
    squares = raw * raw
    share_ref[...] = tree_sum([squares[i : i + 8, :] for i in range(0, half, 8)])
    mine_ref[2 * half : 3 * half, :] = raw
    other_ref[2 * half : 3 * half, :] = raw


def place_halves(mine_ref, other_ref, first, target):
    half = target.shape[0] // 2
    core = lax.axis_index("ctx") % 2
    for ref, at in ((mine_ref, core), (other_ref, 1 - core)):
        rows = pl.ds(pl.multiple_of(at * half, half), half)
        target[rows, :] = ref[first : first + half, :]


def first_local_kernel(modes, *refs):
    line_refs, (decay_ref, rate_ref, res_cols, after_ref, out_ref, coef_ref) = refs[:-6], refs[-6:]
    sub = decay_ref.shape[0] // (out_ref.shape[0] * modes)
    spread(res_cols, coef_ref, modes, sub)
    coef_ref[...] = coef_ref[...] * jnp.sqrt(1.0 - jnp.exp(-2.0 * rate_ref[...]))
    local_kernel(False, modes, *line_refs, decay_ref, coef_ref, after_ref, out_ref)


def local_kernel(reverse, modes, *refs):
    line_refs, (decay_ref, coef_ref, after_ref, out_ref) = refs[:-4], refs[-4:]
    blocks = out_ref.shape[0]
    sub = decay_ref.shape[0] // (blocks * modes)
    seq = out_ref.shape[1] // sub
    core = lax.axis_index("ctx") % 2
    for ref, which in zip(line_refs, (1 - core, core)):
        for slot in range(ref.shape[0]):
            block = which * ref.shape[0] + slot if blocks > 1 else 0
            rows = [
                pl.ds(pl.multiple_of((block * modes + n) * sub, sub), sub) for n in range(modes)
            ]
            decay = [decay_ref[r, :] for r in rows]
            coef = [coef_ref[r, :] for r in rows]

            def body(j, carry):
                held = list(carry)
                for u in range(UNROLL):
                    t = j * UNROLL + u
                    if reverse:
                        t = seq - 1 - t
                    at = pl.ds(pl.multiple_of(t * sub, sub), sub)
                    x = ref[slot, at, :]
                    total = [None] * 4
                    for n in range(modes):
                        held[n] = decay[n] * held[n] + x
                        term = coef[n] * held[n]
                        total[n % 4] = term if n < 4 else total[n % 4] + term
                    out_ref[block, at, :] = tree_sum(total)
                return tuple(held)

            first = tuple(jnp.zeros((sub, LANES), F32) for _ in range(modes))
            lax.fori_loop(0, seq // UNROLL, body, first)


def second_local_kernel(modes, *refs):
    line_refs, refs = refs[:-11], refs[-11:]
    decay_ref, coef_ref, q_ref, k_ref, v_ref, ct_ref, skip_ref, after_ref = refs[:8]
    out_ref, gated_term, pulled_term = refs[8:]
    local_kernel(True, modes, *line_refs, decay_ref, coef_ref, after_ref, out_ref)
    pairs = ((k_ref, v_ref, gated_term), (ct_ref, q_ref, pulled_term))
    for left, right, target in pairs:
        for at in range(0, q_ref.shape[1], LANES):
            cols = slice(at, at + LANES)
            line = left[:, cols].astype(F32) * right[:, cols].astype(F32)
            target[:, cols] = skip_ref[:, cols] * line.astype(jnp.bfloat16).astype(F32)


def add_carries(reverse, unit, sub, decay_ref, coef_ref, states_ref, at_row, source, target, at):
    _, base, modes = unit
    seq = target.shape[1] // sub
    rows = [pl.ds(pl.multiple_of(base + n * sub, sub), sub) for n in range(modes)]
    decay = [decay_ref[r, :] for r in rows]
    first = tuple(
        coef_ref[r, :] * states_ref[at_row + n * sub : at_row + (n + 1) * sub, :]
        for n, r in enumerate(rows)
    )

    def body(j, carry):
        held = list(carry)
        for u in range(UNROLL):
            t = j * UNROLL + u
            if reverse:
                t = seq - 1 - t
            where = pl.ds(pl.multiple_of(t * sub, sub), sub)
            total = [source[where, :], None, None, None]
            for n in range(modes):
                held[n] = decay[n] * held[n]
                total[n % 4] = held[n] if total[n % 4] is None else total[n % 4] + held[n]
            target[at, where, :] = tree_sum(total)
        return tuple(held)

    lax.fori_loop(0, seq // UNROLL, body, first)


def own_kernel(modes, conv_ref, adj_ref, decay_ref, coef_ref, mine_ref, conv_own, adj_own):
    blocks = conv_ref.shape[0]
    sub = decay_ref.shape[0] // (blocks * modes)
    half = decay_ref.shape[0] // 2
    core = lax.axis_index("ctx") % 2
    for i, unit in enumerate(half_units(core, blocks, modes, sub)):
        at_row = i * unit[2] * sub
        for reverse, source, target in ((False, conv_ref, conv_own), (True, adj_ref, adj_own)):
            add_carries(
                reverse,
                unit,
                sub,
                decay_ref,
                coef_ref,
                mine_ref,
                at_row + half * reverse,
                source.at[unit[0]],
                target,
                i,
            )


def other_carries(reverse, modes, decay_ref, coef_ref, other_ref, local_ref, own_ref, whole, sem):
    blocks, own_blocks = local_ref.shape[0], own_ref.shape[0]
    sub = decay_ref.shape[0] // (blocks * modes)
    half = decay_ref.shape[0] // 2
    core = lax.axis_index("ctx") % 2
    copy = pltpu.make_async_copy(own_ref, whole.at[pl.ds(core * own_blocks, own_blocks)], sem)
    if blocks > 1:
        copy.start()
    for i, unit in enumerate(half_units(1 - core, blocks, modes, sub)):
        source = local_ref.at[unit[0]] if blocks > 1 else own_ref.at[0]
        at_row = i * unit[2] * sub + half * reverse
        add_carries(
            reverse, unit, sub, decay_ref, coef_ref, other_ref, at_row, source, whole, unit[0]
        )
    if blocks > 1:
        copy.wait()


def line_outputs(from_scan, term, scales, scanned, targets, which, done_with=None):
    seq, channels = term.shape
    blocks = scanned.shape[0]
    sub = channels // (blocks * LANES)
    part = math.gcd(seq, STEP_ROWS)
    for i in which:
        rows = slice(i * part, (i + 1) * part)
        to_rows = slice((i - which[0]) * part, (i - which[0] + 1) * part)
        stacked = jnp.concatenate(
            [scanned[b, i * part * sub : (i + 1) * part * sub, :] for b in range(blocks)], axis=1
        ).astype(jnp.bfloat16)
        ordered = jnp.dot(from_scan[...], stacked, preferred_element_type=F32)
        for b in range(blocks):
            for s in range(sub):
                cols = slice((b * sub + s) * LANES, (b * sub + s + 1) * LANES)
                own = ordered[s * part : (s + 1) * part, b * LANES : (b + 1) * LANES]
                mixed = own + term[rows, cols]
                for scale, target in zip(scales, targets):
                    target[to_rows, cols] = (scale[rows, cols].astype(F32) * mixed).astype(
                        jnp.bfloat16
                    )
        if done_with is not None:
            done_with(pl.ds((i - which[0]) * part, part), pl.ds(i * part, part))


def forward_kernel(
    modes,
    q_ref,
    ct_ref,
    term_ref,
    decay_ref,
    coef_ref,
    other_ref,
    from_scan,
    conv_ref,
    conv_own,
    after_ref,
    out_ref,
    gq_ref,
    token_ref,
    scanned,
    sem,
):
    token_ref[...] = jnp.zeros_like(token_ref)
    other_carries(
        False, modes, decay_ref, coef_ref, other_ref, conv_ref, conv_own, scanned, sem
    )
    line_outputs(
        from_scan,
        term_ref,
        (q_ref, ct_ref),
        scanned,
        (out_ref, gq_ref),
        range(q_ref.shape[0] // math.gcd(q_ref.shape[0], STEP_ROWS)),
    )


def early_parts(seq):
    parts = seq // math.gcd(seq, STEP_ROWS)
    return range((parts + 1) // 2), range((parts + 1) // 2, parts)


def adjoint_kernel(
    modes,
    k_ref,
    v_ref,
    term_ref,
    decay_ref,
    coef_ref,
    other_ref,
    from_scan,
    adj_ref,
    adj_own,
    out_rows,
    gq_rows,
    after_ref,
    out_hbm,
    gq_hbm,
    scanned,
    gk_ref,
    gv_ref,
    token_ref,
    sems,
):
    token_ref[...] = jnp.zeros_like(token_ref)
    copies = [
        pltpu.make_async_copy(out_rows, out_hbm, sems.at[0]),
        pltpu.make_async_copy(gq_rows, gq_hbm, sems.at[1]),
    ]
    for copy in copies:
        copy.start()
    other_carries(
        True, modes, decay_ref, coef_ref, other_ref, adj_ref, adj_own, scanned, sems.at[2]
    )
    line_outputs(
        from_scan,
        term_ref,
        (v_ref, k_ref),
        scanned,
        (gk_ref, gv_ref),
        early_parts(k_ref.shape[0])[0],
    )
    for copy in copies:
        copy.wait()


def last_outputs_kernel(limit, *refs):
    k_ref, v_ref, term_ref, scanned, gk_early, gv_early = refs[:6]
    mine_ref, other_ref, from_scan = refs[6:9]
    share_refs = refs[10:-8]
    raw_hbm, gk_hbm, gv_hbm, gk_rows, gv_rows, raw_cols, states, sems = refs[-8:]
    copies = []

    def start(source, target):
        copy = pltpu.make_async_copy(source, target, sems.at[len(copies)])
        copy.start()
        copies.append(copy)

    early = pl.ds(0, gk_early.shape[0])
    start(gk_early, gk_hbm.at[early])
    start(gv_early, gv_hbm.at[early])
    clip(limit, scanned.shape[0], mine_ref, other_ref, share_refs, raw_cols, states)
    start(raw_cols, raw_hbm)

    def send(at, to):
        start(gk_rows.at[at], gk_hbm.at[to])
        start(gv_rows.at[at], gv_hbm.at[to])

    late = early_parts(k_ref.shape[0])[1]
    if len(late) > 0:
        sides, targets = (v_ref, k_ref), (gk_rows, gv_rows)
        line_outputs(from_scan, term_ref, sides, scanned, targets, late, send)
    for copy in copies:
        copy.wait()


def add_kernel(after_ref, *refs):
    refs[-1][...] = tree_sum([ref[...] for ref in refs[:-1]])


def clip(limit, blocks, mine_ref, other_ref, share_refs, out_ref, states):
    modes = out_ref.shape[0]
    sub = out_ref.shape[1] // (blocks * LANES)
    half = states.shape[0] // 2
    place_halves(mine_ref, other_ref, 2 * half, states)
    square = jnp.sum(tree_sum([ref[...] for ref in share_refs]))
    factor = jnp.minimum(1.0, limit * lax.rsqrt(jnp.full((1, LANES), square + 1e-06, F32)))
    for b in range(blocks):
        for s in range(sub):
            cols = slice((b * sub + s) * LANES, (b * sub + s + 1) * LANES)
            rows = pl.ds(b * modes * sub + s, modes, stride=sub)
            out_ref[:, cols] = states[rows, :] * factor


def shards(queries, keys_in, values_in, decay_rates, residues, skip_gain, cotangent):
    seq, channels = queries.shape
    modes = decay_rates.shape[1]
    ctx = lax.axis_size("ctx")
    tp = lax.axis_size("tp")
    levels = ctx.bit_length() - 1
    groups = channels // LANES
    sub = math.gcd(groups, 8)
    blocks = groups // sub
    half = modes * groups // 2
    part = math.gcd(seq, STEP_ROWS)
    parts, size = seq // part, part * sub

    def swap(value, bit):
        return lax.ppermute(value, "ctx", [(i, i ^ (1 << bit)) for i in range(ctx)])

    def rows(*shape, dtype=F32):
        return jax.ShapeDtypeStruct((*shape, LANES), dtype)

    line_shape = jax.ShapeDtypeStruct((seq, channels), jnp.bfloat16)
    table_shape = jax.ShapeDtypeStruct((modes, channels), F32)
    line_scratch = pltpu.VMEM((seq, channels), jnp.bfloat16)
    table_scratch = pltpu.VMEM((modes, channels), F32)
    own_shape = rows(max(blocks // 2, 1), seq * sub)
    elements = seq * channels * modes
    tables = (decay_rates.T, residues.T, skip_gain.reshape(1, channels))
    sources = (queries, keys_in, values_in, cotangent, *tables)

    (
        send,
        q,
        k,
        v,
        ct,
        gated,
        pulled,
        row_rates,
        row_decay,
        to_scan,
        from_scan,
        res_cols,
        skip,
    ) = pl.pallas_call(
        send_kernel,
        in_specs=[HBM] * 7,
        out_specs=[VMEM] * 13,
        out_shape=[rows(3, half)]
        + [line_shape] * 4
        + [own_shape] * 2
        + [rows(2 * half)] * 2
        + [jax.ShapeDtypeStruct((size, size), jnp.bfloat16)] * 2
        + [table_shape, jax.ShapeDtypeStruct((1, channels), F32)],
        scratch_shapes=[table_scratch, pltpu.SemaphoreType.DMA((4 * parts + 7,))],
        compiler_params=KERNEL,
        cost_estimate=pl.CostEstimate(
            flops=3 * elements, bytes_accessed=8 * seq * channels, transcendentals=0
        ),
        name="sent_states",
    )(*[pltpu.with_memory_space_constraint(item, pltpu.HBM) for item in sources])
    sibling = swap(send, 0)
    keep, *kept_lines = pl.pallas_call(
        keep_kernel,
        out_shape=[rows(3, half)] + [own_shape] * (2 if blocks > 1 else 0),
        compiler_params=KERNEL,
        cost_estimate=pl.CostEstimate(
            flops=3 * elements, bytes_accessed=8 * seq * channels, transcendentals=0
        ),
        name="kept_states",
    )(q, k, v, ct, row_decay, to_scan, gated, pulled)
    gated, pulled = (gated, *kept_lines[:1]), (pulled, *kept_lines[1:])

    def wire(level):
        return rows(2 if level == levels - 1 else 3, half, dtype=WIRE)

    whole = rows(blocks, seq * sub)
    whole_scratch = pltpu.VMEM((blocks, seq * sub, LANES), F32)
    states_scratch = pltpu.VMEM((2 * half, LANES), F32)
    local_cost = pl.CostEstimate(
        flops=4 * elements, bytes_accessed=8 * seq * channels, transcendentals=0
    )

    block, packed = pl.pallas_call(
        partial(pair_kernel, seq, levels == 2),
        out_shape=[rows(5, half), wire(1)],
        compiler_params=KERNEL,
        name="chip_states",
    )(keep, sibling, row_rates, row_rates[:8])
    got = swap(packed, 1)
    conv, row_coefs = pl.pallas_call(
        partial(first_local_kernel, modes),
        out_shape=[whole, rows(2 * half)],
        compiler_params=KERNEL,
        cost_estimate=local_cost,
        name="local_conv",
    )(*gated, row_decay, row_rates, res_cols, block[4, :8])
    for level in range(1, levels - 1):
        block, packed = pl.pallas_call(
            partial(level_kernel, seq, level, level + 1 == levels - 1),
            out_shape=[rows(5, half), wire(level + 1)],
            compiler_params=KERNEL,
            name="block_states",
        )(block, got, row_rates, conv[0, :8])
        got = swap(packed, level + 1)
    term_shape = jax.ShapeDtypeStruct((seq, channels), F32)
    adj, gated_term, pulled_term = pl.pallas_call(
        partial(second_local_kernel, modes),
        out_shape=[whole] + [term_shape] * 2,
        compiler_params=KERNEL,
        cost_estimate=local_cost,
        name="local_adjoint",
    )(*pulled, row_decay, row_coefs, q, k, v, ct, skip, block[4, :8])
    mine, other, square = pl.pallas_call(
        partial(last_kernel, seq, levels - 1),
        out_shape=[rows(3 * half)] * 2 + [rows(8)],
        compiler_params=KERNEL,
        name="carries",
    )(block, got, row_rates, keep, sibling, adj[0, :8])
    other = swap(other, 0)
    early, late = early_parts(seq)
    early_shape = jax.ShapeDtypeStruct((seq * len(early) // parts, channels), jnp.bfloat16)
    late_scratch = pltpu.VMEM((seq * max(len(late), 1) // parts, channels), jnp.bfloat16)
    kept = {}

    def add_own(after):
        kept["conv"], kept["adj"] = pl.pallas_call(
            partial(own_kernel, modes),
            out_shape=[own_shape] * 2,
            compiler_params=KERNEL,
            cost_estimate=pl.CostEstimate(
                flops=2 * elements, bytes_accessed=8 * seq * channels, transcendentals=0
            ),
            name="own_carries",
        )(conv, adj, row_decay, row_coefs, mine)
        return kept["adj"][0, :8]

    def forward_outputs(after):
        kept["out"], kept["gq"], token = pl.pallas_call(
            partial(forward_kernel, modes),
            out_shape=[line_shape] * 2 + [rows(8)],
            scratch_shapes=[whole_scratch, pltpu.SemaphoreType.DMA],
            compiler_params=KERNEL,
            cost_estimate=pl.CostEstimate(
                flops=2 * elements, bytes_accessed=16 * seq * channels, transcendentals=0
            ),
            name="forward_outputs",
        )(
            q,
            ct,
            gated_term,
            row_decay,
            row_coefs,
            other,
            from_scan,
            conv,
            kept["conv"],
            after,
        )
        return token

    def adjoint_outputs(after):
        results = (
            pl.pallas_call(
                partial(adjoint_kernel, modes),
                in_specs=[VMEM] * 12,
                out_specs=[HBM] * 2 + [VMEM] * 4,
                out_shape=[line_shape] * 2 + [whole] + [early_shape] * 2 + [rows(8)],
                scratch_shapes=[pltpu.SemaphoreType.DMA((3,))],
                compiler_params=KERNEL,
                cost_estimate=pl.CostEstimate(
                    flops=2 * elements, bytes_accessed=8 * seq * channels, transcendentals=0
                ),
                name="adjoint_outputs",
            )(
                k,
                v,
                pulled_term,
                row_decay,
                row_coefs,
                other,
                from_scan,
                adj,
                kept["adj"],
                kept["out"],
                kept["gq"],
                after,
            )
        )
        kept["final"] = results[:-1]
        return results[-1]

    def plus(after, *shares):
        return pl.pallas_call(
            add_kernel,
            in_specs=[VMEM] * (1 + len(shares)),
            out_shape=rows(8),
            compiler_params=KERNEL,
            name="square_sum",
        )(after, *shares)

    def tp_swap(value, mask):
        return lax.ppermute(value, "tp", [(i, i ^ mask) for i in range(tp)])

    works = [add_own, forward_outputs]
    for bit in range(0, tp.bit_length() - 1, 2):
        masks = [m << bit for m in (3, 2, 1) if m << bit < tp]
        shares = [tp_swap(square, mask) for mask in masks]
        after = square
        while works:
            after = works.pop(0)(after)
        square = plus(after, square, *shares)
    share = swap(square, 0)
    after = square
    for work in works + [adjoint_outputs]:
        after = work(after)
    operator_out, grad_queries, scanned, early_keys, early_values = kept["final"]
    grad_residues, grad_keys, grad_values = pl.pallas_call(
        partial(last_outputs_kernel, math.sqrt(channels * tp * modes)),
        in_specs=[VMEM] * 12,
        out_specs=[HBM] * 3,
        out_shape=[table_shape] + [line_shape] * 2,
        scratch_shapes=[
            late_scratch,
            late_scratch,
            table_scratch,
            states_scratch,
            pltpu.SemaphoreType.DMA((2 * parts + 3,)),
        ],
        compiler_params=KERNEL,
        cost_estimate=pl.CostEstimate(
            flops=elements, bytes_accessed=8 * seq * channels, transcendentals=0
        ),
        name="last_outputs",
    )(
        k,
        v,
        pulled_term,
        scanned,
        early_keys,
        early_values,
        mine,
        other,
        from_scan,
        after,
        square,
        share,
    )
    return (operator_out, grad_queries, grad_keys, grad_values, grad_residues.T)


def solution(mesh):
    lines, tables = P("ctx", "tp"), P("tp", None)
    in_specs = (lines, lines, lines, tables, tables, P("tp"), lines)
    out_specs = (lines, lines, lines, lines, tables)
    return jax.shard_map(shards, mesh=mesh, in_specs=in_specs, out_specs=out_specs, check_vma=False)
```
